32 devices in a mesh: grp: 4 (over x, core), dev: 8 (over z, y).
Axes of the slice: x: 2, y: 2, z: 4, core: 2. Of those that a mesh axis runs over, the one named last changes fastest.
Arguments:
- parent_state: float32 [24, 256, 1024], P(None, 'grp', 'dev'), may hold values from -6 to 6
- nest_state: float32 [8, 24, 192, 384], P('grp', None, 'dev'), may hold values from -6 to 6
- nest_anchor: int32 [8, 2], replicated, may hold values from 0 to 896, as said below
- diffusion: float32 [2, 24], replicated, may hold values from 0.02 to 0.05
- courant: float32 [2, 24], replicated, may hold values from 0.05 to 0.15
Outputs:
- parent_out: float32 [24, 256, 1024], P(None, 'grp', 'dev')
- nest_out: float32 [8, 24, 192, 384], P('grp', None, 'dev')
The draws below stay inside these ranges and needn't reach their ends.
Inputs may be any that keep to these rules, and one draw needn't show every extreme that they name: `nest_anchor`: the parent grid is cut into 2 x 8 / 2 disjoint bands of 128 x 256 cells; each nest lies in a band of its own, its 64 x 128 covered cells inside that band.
All inputs are finite; a program needn't handle non-finite values.
Results may differ from the reference program's by a relative error of at most 0.0003.
Values sent between devices are 32-bit elements; how exact they have to be, the bound alone decides.
No kernel may reach another device: no remote copies, remote signals or barrier semaphores. Data moves between devices by JAX's collectives and lax.ppermute only.
A program may use at most 320 MiB of HBM per device.

```python
import jax
import jax.numpy as jnp
from jax import lax

NCOL = 384
C = 24
NESTS = 8
PY = 256
PX = 1024
NROWS = 192
FP_R = 64
FP_C = 128
BAND_R = 128
BAND_C = 256


def draw_nest_anchor(key, part):
    band_key, row_key, col_key = jax.random.split(key, 3)
    band_order = jax.random.permutation(band_key, NESTS)
    band_row = band_order // (NESTS // 2)
    band_col = band_order % (NESTS // 2)
    offset_row = jax.random.randint(row_key, (NESTS,), 0, BAND_R - FP_R + 1)
    offset_col = jax.random.randint(col_key, (NESTS,), 0, BAND_C - FP_C + 1)
    return jnp.stack([band_row * BAND_R + offset_row, band_col * BAND_C + offset_col], axis=1).astype(jnp.int32)


def levels(key, dims, cuts, least, top_value):
    loudness, own = 1.0, jax.random.fold_in(key, 6)
    for position, parts in cuts:
        heights = jnp.exp(jax.random.uniform(jax.random.fold_in(own, position), (parts,), jnp.float32, least / len(cuts), top_value / len(cuts)))
        loudness = loudness * jnp.repeat(heights, dims[position] // parts).reshape([-1 if axis == position else 1 for axis in range(len(dims))])
    return loudness


def gaussian(rng, shape, deviation, limit, shards=(), held_as=jnp.bfloat16):
    drawn = deviation * jax.random.normal(rng, shape, jnp.float32)
    if shards:
        drawn = drawn * levels(rng, shape, shards, -0.22, 0.18)
    return jnp.clip(drawn, -limit, limit).astype(held_as)


def setup_inputs(seed: int = 0) -> dict:
    arg_keys = jax.random.split(jax.random.key(seed), 6)
    parent_state = gaussian(arg_keys[0], (C, PY, PX), 1.0, 6.0, ((1, 4), (2, 8)), jnp.float32)
    nest_state = gaussian(arg_keys[1], (NESTS, C, NROWS, NCOL), 1.0, 6.0, ((0, 4), (2, 8)), jnp.float32)
    nest_anchor = draw_nest_anchor(jax.random.fold_in(arg_keys[5], 71), 0)
    diffusion = jnp.clip(jax.random.uniform(arg_keys[3], (2, C), jnp.float32, 0.02, 0.05), 0.02, 0.05)
    courant = jnp.clip(jax.random.uniform(arg_keys[4], (2, C), jnp.float32, 0.05, 0.15), 0.05, 0.15)
    return dict(parent_state=parent_state, nest_state=nest_state, nest_anchor=nest_anchor, diffusion=diffusion, courant=courant)


def stencil(padded, diff_x, diff_y, adv_x, adv_y):
    centre = padded[..., 1:-1, 1:-1]
    eastern = padded[..., 1:-1, 2:]
    western = padded[..., 1:-1, :-2]
    northern = padded[..., 2:, 1:-1]
    southern = padded[..., :-2, 1:-1]
    return (centre + diff_x * (eastern - 2.0 * centre + western)
            + diff_y * (northern - 2.0 * centre + southern)
            - adv_x * (centre - western) - adv_y * (centre - southern))


def reference(parent_state, nest_state, nest_anchor, diffusion, courant):
    channels = parent_state.shape[0]
    diff_x = diffusion[0][:, None, None]
    diff_y = diffusion[1][:, None, None]
    adv_x = courant[0][:, None, None]
    adv_y = courant[1][:, None, None]
    parent_pad = jnp.pad(parent_state, ((0, 0), (1, 1), (1, 1)))
    advanced = stencil(parent_pad, diff_x, diff_y, adv_x, adv_y)

    def one_nest(inputs):
        fine_field, anchor = inputs
        row_start = anchor[0].astype(jnp.int32)
        col_start = anchor[1].astype(jnp.int32)
        zero_start = jnp.zeros((), jnp.int32)
        west_cycle = lax.dynamic_slice(parent_pad, (zero_start, row_start + 1, col_start), (channels, FP_R, 1))[:, :, 0]
        east_cycle = lax.dynamic_slice(parent_pad, (zero_start, row_start + 1, col_start + FP_C + 1), (channels, FP_R, 1))[:, :, 0]
        south_cycle = lax.dynamic_slice(parent_pad, (zero_start, row_start, col_start + 1), (channels, 1, FP_C))[:, 0, :]
        north_cycle = lax.dynamic_slice(parent_pad, (zero_start, row_start + FP_R + 1, col_start + 1), (channels, 1, FP_C))[:, 0, :]
        west_fine = jnp.repeat(west_cycle, 3, axis=1)
        east_fine = jnp.repeat(east_cycle, 3, axis=1)
        corner = jnp.zeros((channels, 1), jnp.float32)
        top_row = jnp.concatenate([corner, jnp.repeat(south_cycle, 3, axis=1), corner], axis=1)[:, None, :]
        bottom = jnp.concatenate([corner, jnp.repeat(north_cycle, 3, axis=1), corner], axis=1)[:, None, :]
        for substep in range(3):
            middle = jnp.concatenate([west_fine[:, :, None], fine_field, east_fine[:, :, None]], axis=2)
            padded = jnp.concatenate([top_row, middle, bottom], axis=1)
            fine_field = stencil(padded, 3.0 * diff_x, 3.0 * diff_y, adv_x, adv_y)
        average = fine_field.reshape(channels, FP_R, 3, FP_C, 3).mean(axis=(2, 4))
        return fine_field, average

    nest_out, averages = lax.map(one_nest, (nest_state, nest_anchor))

    def place(nest_index, parent_field):
        return lax.dynamic_update_slice(
            parent_field, averages[nest_index],
            (jnp.zeros((), jnp.int32), nest_anchor[nest_index, 0], nest_anchor[nest_index, 1]))

    parent_out = lax.fori_loop(0, NESTS, place, advanced)
    return parent_out, nest_out
```

```python
import functools

import jax
import jax.numpy as jnp
from jax import lax
from jax.experimental import pallas as pl
from jax.experimental.pallas import tpu as pltpu
from jax.sharding import PartitionSpec as P

F32 = jnp.float32
HIGH = lax.Precision.HIGHEST
LANES = 128
VMEM_LIMIT = 48 * 1024 * 1024


class Sizes:
    def __init__(self, parent, nest, anchor, grp_count, dev_count):
        self.C, self.TR, self.TC = parent.shape
        self.L, _, self.H, self.W = nest.shape
        self.N = anchor.shape[0]
        self.G, self.D = grp_count, dev_count
        self.M = self.H // 3
        self.FR, self.FC = self.M * self.D, self.W // 3
        self.S = self.G // 2
        self.NB = self.N // 2
        self.Y = self.D // self.NB
        self.CS = self.C // self.S
        self.BR, self.BC = self.S * self.TR, self.Y * self.TC
        self.R1 = self.L * self.CS * (self.M + 2)
        self.R2 = self.CS * (self.M + 2)
        self.RG1 = self.FR + self.L * 2 * self.C + self.C
        self.RG2 = 16 + self.L * self.C + self.TR + 8
        assert self.H == 24 and self.FC == LANES and self.TC == LANES
        assert self.FR >= self.TR and self.L == 2


def call(body, out_shape, n_smem, args, scratch=()):
    in_specs = [pl.BlockSpec(memory_space=pltpu.SMEM)] * n_smem
    in_specs += [pl.BlockSpec(memory_space=pltpu.VMEM)] * (len(args) - n_smem)
    many = isinstance(out_shape, (list, tuple))
    vm = pl.BlockSpec(memory_space=pltpu.VMEM)
    return pl.pallas_call(
        body,
        out_shape=out_shape,
        in_specs=in_specs,
        out_specs=[vm] * len(out_shape) if many else vm,
        scratch_shapes=list(scratch),
        compiler_params=pltpu.CompilerParams(vmem_limit_bytes=VMEM_LIMIT),
    )(*args)


def iota(shape, dim):
    return lax.broadcasted_iota(jnp.int32, shape, dim)


def nest_weights(diff, cour, c):
    east = 3.0 * diff[0, c]
    north = 3.0 * diff[1, c]
    west = east + cour[0, c]
    south = north + cour[1, c]
    return 1.0 - (east + west) - (north + south), east, west, north, south


def partial_averages(z, tab, diff, cour, nest, out, halo_up, halo_dn, t_s, vm, ve):
    d = tab[1]
    C, L, M, CS = z.C, z.L, z.M, z.CS
    sub = iota((8, z.W), 0)
    lo_ok = jnp.where(d > 0, 1.0, 0.0)
    hi_ok = jnp.where(d < z.D - 1, 1.0, 0.0)
    keep = jnp.where(sub >= 5, lo_ok, jnp.where(sub < 3, hi_ok, 0.0)).astype(F32)
    lane = iota((z.H + 8, z.W), 1)
    rows = z.H + 8

    def channel(c, _):
        mid, east, west, north, south = nest_weights(diff, cour, c)
        for l in range(L):
            strip = nest[l, c]
            at = (l * C + c) * 3
            for j in range(3):
                lanes = slice(j * LANES, (j + 1) * LANES)
                halo_up[j, pl.ds(at, 3), :] = strip[z.H - 3 :, lanes]
                halo_dn[j, pl.ds(at, 3), :] = strip[:3, lanes]
            u = jnp.concatenate([strip, jnp.zeros((8, z.W), F32)], axis=0)
            for _step in range(3):
                e = jnp.where(lane == z.W - 1, 0.0, pltpu.roll(u, z.W - 1, 1))
                w = jnp.where(lane == 0, 0.0, pltpu.roll(u, 1, 1))
                n = pltpu.roll(u, rows - 1, 0)
                s = pltpu.roll(u, 1, 0)
                v = mid * u + east * e + west * w + north * n + south * s
                u = jnp.concatenate([v[: z.H], v[z.H :] * keep], axis=0)
            t = u + pltpu.roll(u, rows - 1, 0) + pltpu.roll(u, rows - 2, 0)
            for j in range(3):
                t_s[j] = t[:, j * LANES : (j + 1) * LANES]
                vm[j, pl.ds(pl.multiple_of((l * C + c) * M, M), M), :] = t_s[j, pl.ds(0, M, 3), :]
                ve[j, pl.ds((l * 2) * C + c, 1), :] = t_s[j, pl.ds(z.H + 5, 1), :]
                ve[j, pl.ds((l * 2 + 1) * C + c, 1), :] = t_s[j, pl.ds(z.H, 1), :]
        return 0

    lax.fori_loop(0, C, channel, 0)
    main = jnp.zeros((L * C * M, LANES), F32)
    edge = jnp.zeros((L * 2 * C, LANES), F32)
    fine = iota((LANES, LANES), 0)
    coarse = iota((LANES, LANES), 1) * 3
    for j in range(3):
        x = fine + j * LANES
        pool = jnp.where((x >= coarse) & (x < coarse + 3), 1.0, 0.0).astype(F32)
        main += jnp.dot(vm[j], pool, precision=HIGH, preferred_element_type=F32)
        edge += jnp.dot(ve[j], pool, precision=HIGH, preferred_element_type=F32)
    main = main * (1.0 / 9.0)
    edge = edge * (1.0 / 9.0)
    base = L * CS * M
    for g in range(z.G):
        part = g % z.S
        for l in range(L):
            first = (l * C + part * CS) * M
            out[g, l * CS * M : (l + 1) * CS * M, :] = main[first : first + CS * M]
            for side in range(2):
                k = l * 2 + side
                out[g, base + k * CS : base + (k + 1) * CS, :] = edge[
                    k * C + part * CS : k * C + part * CS + CS
                ]


def pick_band(z, tab, got, out):
    top = tab[0] // z.S * z.NB
    base, size = z.L * z.CS * z.M, z.CS * z.M
    for band in range(z.NB):
        n = tab[2 + top + band]
        g = n // z.L
        first = n - g * z.L == 0
        main = jnp.where(first, got[g, :size, :], got[g, size : 2 * size, :])
        edge = jnp.where(
            first,
            got[g, base : base + 2 * z.CS, :],
            got[g, base + 2 * z.CS : base + 4 * z.CS, :],
        )
        for y in range(z.Y):
            out[band * z.Y + y, :size, :] = main
            out[band * z.Y + y, size:, :] = edge


def ring_parts(z, tab, anc, parent, out):
    g, d = tab[0], tab[1]
    row_base, col_base = g * z.TR, d * z.TC
    lane_t = iota((z.TR, LANES), 1)
    lane_f = iota((z.FR, LANES), 1)
    row_f = iota((z.FR, LANES), 0)
    lane_c = iota((z.C, LANES), 1)
    for to in range(z.G):
        out[to, : z.RG1 - z.C, :] = jnp.zeros((z.RG1 - z.C, LANES), F32)
        edge_row = jnp.where(to > g, z.TR - 1, 0)

        def put_edge(c, _, to=to, edge_row=edge_row):
            out[to, pl.ds(z.RG1 - z.C + c, 1), :] = parent[c, pl.ds(edge_row, 1), :]
            return 0

        lax.fori_loop(0, z.C, put_edge, 0)
        for l in range(z.L):
            n = to * z.L + l
            r, q = anc[n, 0], anc[n, 1]
            rows_meet = (r < row_base + z.TR) & (r + z.FR > row_base)
            cols_meet = (q < col_base + z.TC) & (q + z.FC > col_base)
            shift_r = lax.rem(row_base - r + 2 * z.G * z.TR, z.FR)
            shift_q = lax.rem(col_base - q + 2 * z.D * z.TC, z.FC)
            for side in range(2):
                col = (q - 1 if side == 0 else q + z.FC) - col_base
                first = (l * 2 + side) * z.C

                @pl.when(rows_meet & (col >= 0) & (col < z.TC))
                def _(col=col, first=first, r=r, shift_r=shift_r, to=to):
                    def take(c, acc):
                        at = first + c
                        moved = pltpu.roll(parent[c], lax.rem(at - col + LANES, LANES), 1)
                        return jnp.where(lane_t == at, moved, acc)

                    acc = lax.fori_loop(0, z.C, take, jnp.zeros((z.TR, LANES), F32))
                    if z.FR > z.TR:
                        acc = jnp.concatenate([acc, jnp.zeros((z.FR - z.TR, LANES), F32)], axis=0)
                    acc = pltpu.roll(acc, shift_r, 0)
                    y = row_f + (r - row_base)
                    good = (y >= 0) & (y < z.TR) & (lane_f >= first) & (lane_f < first + z.C)
                    out[to, : z.FR, :] = jnp.where(good, acc, out[to, : z.FR, :])

                row = (r - 1 if side == 0 else r + z.FR) - row_base

                @pl.when(cols_meet & (row >= 0) & (row < z.TR))
                def _(row=row, l=l, side=side, q=q, shift_q=shift_q, to=to):
                    at = z.FR + (l * 2 + side) * z.C

                    def take(c, _):
                        out[to, pl.ds(at + c, 1), :] = parent[c, pl.ds(row, 1), :]
                        return 0

                    lax.fori_loop(0, z.C, take, 0)
                    x = lane_c + (q - col_base)
                    moved = pltpu.roll(out[to, at : at + z.C, :], shift_q, 1)
                    out[to, at : at + z.C, :] = jnp.where((x >= 0) & (x < z.TC), moved, 0.0)


def ring_next(z, tab, got, parent, out, edges, tile):
    g, d = tab[0], tab[1]
    C, L, FR, M = z.C, z.L, z.FR, z.M
    sides = got[0, :FR, :]
    ends = got[0, FR : FR + 2 * L * C, :]
    for k in range(1, z.G):
        sides = sides + got[k, :FR, :]
        ends = ends + got[k, FR : FR + 2 * L * C, :]
    before = jnp.where(g > 0, got[jnp.maximum(g - 1, 0), z.RG1 - C :, :], 0.0)
    after = jnp.where(g < z.G - 1, got[jnp.minimum(g + 1, z.G - 1), z.RG1 - C :, :], 0.0)
    edges[:C, :] = before
    edges[C:, :] = after
    rows = z.TR + 8
    lane = iota((rows, LANES), 1)
    sub = iota((8, LANES), 0)

    def take(c, acc):
        first, last = acc
        lo = edges[pl.ds(c, 1), :]
        hi = edges[pl.ds(C + c, 1), :]
        cap = jnp.where(sub == 0, hi, jnp.where(sub == 7, lo, 0.0))
        full = jnp.concatenate([parent[c], cap], axis=0)
        first = jnp.where(lane == c, pltpu.roll(full, c, 1), first)
        last = jnp.where(lane == c, pltpu.roll(full, c + 1, 1), last)
        return first, last

    blank = jnp.zeros((rows, LANES), F32)
    first, last = lax.fori_loop(0, C, take, (blank, blank))
    tile[:FR, :] = sides
    tile[FR:, :] = jnp.zeros((8, LANES), F32)
    for to in range(z.D):
        out[to, :M, :] = tile[to * M : (to + 1) * M, :]
        hi = tile[(to + 1) * M : (to + 1) * M + 1, :]
        lo = tile[max(to * M - 1, 0) : max(to * M - 1, 0) + 1, :]
        out[to, M:16, :] = jnp.where(sub == 0, hi, jnp.where(sub == 7, lo, 0.0))
        for l in range(L):
            at = 16 + l * C
            if to == 0 or to == z.D - 1:
                k = l * 2 + (0 if to == 0 else 1)
                out[to, at : at + C, :] = ends[k * C : (k + 1) * C]
            else:
                out[to, at : at + C, :] = jnp.zeros((C, LANES), F32)
        out[to, 16 + L * C :, :] = jnp.where(to > d, last, first)


def nest_steps(z, tab, diff, cour, nest, got, up, dn, out, side_s, end_s, cap_s):
    d = tab[1]
    C, L, M = z.C, z.L, z.M
    rows = z.H + 8
    sides = got[0, :16, :]
    ends = got[0, 16 : 16 + L * C, :]
    for k in range(1, z.D):
        sides = sides + got[k, :16, :]
        ends = ends + got[k, 16 : 16 + L * C, :]
    i = iota((rows, 16), 0)
    k = iota((rows, 16), 1)
    own = (i < z.H) & (i >= 3 * k) & (i < 3 * k + 3)
    spread = own | ((i >= z.H) & (i < z.H + 3) & (k == M)) | ((i >= z.H + 5) & (k == 15))
    side_s[...] = jnp.dot(
        jnp.where(spread, 1.0, 0.0).astype(F32), sides, precision=HIGH, preferred_element_type=F32
    )
    x = iota((LANES, z.W), 1)
    k = iota((LANES, z.W), 0) * 3
    widen = jnp.where((x >= k) & (x < k + 3), 1.0, 0.0).astype(F32)
    wide = jnp.dot(ends, widen, precision=HIGH, preferred_element_type=F32)
    for j in range(3):
        end_s[j] = wide[:, j * LANES : (j + 1) * LANES]
    sub = iota((8, z.W), 0)
    at_low, at_high = d == 0, d == z.D - 1
    held = ((sub >= 5) & at_low) | ((sub < 3) & at_high)
    carry = ((sub == 7) & at_low) | ((sub == 0) & at_high)
    lane = iota((rows, LANES), 1)
    cap_s[...] = jnp.zeros((8, z.W), F32)

    def channel(c, _):
        mid, east, west, north, south = nest_weights(diff, cour, c)
        for l in range(L):
            at = (l * C + c) * 3
            for j in range(3):
                lanes = slice(j * LANES, (j + 1) * LANES)
                cap_s[0:3, lanes] = dn[j, pl.ds(at, 3), :]
                cap_s[5:8, lanes] = up[j, pl.ds(at, 3), :]
            end = jnp.concatenate([end_s[j, pl.ds(l * C + c, 1), :] for j in range(3)], axis=1)
            ghost = jnp.where(carry, end, 0.0)
            cap = jnp.where(held, ghost, cap_s[...])
            u = jnp.concatenate([nest[l, c], cap], axis=0)
            place = 2 * l * C + c
            w_col = pltpu.roll(side_s[...], LANES - place, 1)
            e_col = pltpu.roll(side_s[...], LANES - 1 - (place + C), 1)
            for _step in range(3):
                e = pltpu.roll(u, z.W - 1, 1)
                w = pltpu.roll(u, 1, 1)
                cut = z.W - LANES
                e = jnp.concatenate(
                    [e[:, :cut], jnp.where(lane == LANES - 1, e_col, e[:, cut:])], axis=1
                )
                w = jnp.concatenate(
                    [jnp.where(lane == 0, w_col, w[:, :LANES]), w[:, LANES:]], axis=1
                )
                n = pltpu.roll(u, rows - 1, 0)
                s = pltpu.roll(u, 1, 0)
                v = mid * u + east * e + west * w + north * n + south * s
                u = jnp.concatenate([v[: z.H], jnp.where(held, ghost, v[z.H :])], axis=0)
            out[l, c] = u[: z.H]
        return 0

    lax.fori_loop(0, C, channel, 0)


def ghost_share(inject, back, mid, plus, minus):
    stay = mid + inject
    m0 = inject * (1.0 + stay + mid * stay + inject * (stay + back) + 2.0 * plus * minus)
    p1 = inject * plus * (1.0 + 2.0 * stay)
    p2 = inject * plus * plus
    n1 = inject * minus * (1.0 + 2.0 * stay)
    n2 = inject * minus * minus
    ninth = 1.0 / 9.0
    same = (3.0 * m0 + 2.0 * p1 + p2 + 2.0 * n1 + n2) * ninth
    return same, (p1 + 2.0 * p2) * ninth, (n1 + 2.0 * n2) * ninth, inject * plus * minus * ninth


def parent_step(z, tab, anc, diff, cour, parent, edges, got, out):
    g, d = tab[0], tab[1]
    C = z.C
    rows = z.TR + 8
    n = tab[2 + g // z.S * z.NB + d // z.Y]
    i = iota((z.TR, LANES), 0) + (g * z.TR - anc[n, 0])
    j = iota((z.TR, LANES), 1) + (d * z.TC - anc[n, 1])
    inside = (i >= 0) & (i < z.FR) & (j >= 0) & (j < z.FC)
    one = lambda cond: jnp.where(cond, 1.0, 0.0).astype(F32)
    on_w, on_e = one(inside & (j == 0)), one(inside & (j == z.FC - 1))
    on_s, on_n = one(inside & (i == 0)), one(inside & (i == z.FR - 1))
    i_end, j_end = one((i == 0) | (i == z.FR - 1)), one((j == 0) | (j == z.FC - 1))
    i_lo, i_hi = one(i > 0), one(i < z.FR - 1)
    j_lo, j_hi = one(j > 0), one(j < z.FC - 1)
    lane = iota((rows, LANES), 1)
    sub = iota((8, LANES), 0)
    at = 16 + z.L * C
    col_w = jnp.where(d > 0, got[jnp.maximum(d - 1, 0), at:, :], 0.0)
    col_e = jnp.where(d < z.D - 1, got[jnp.minimum(d + 1, z.D - 1), at:, :], 0.0)

    def channel(c, _):
        lo = edges[pl.ds(c, 1), :]
        hi = edges[pl.ds(C + c, 1), :]
        cap = jnp.where(sub == 0, hi, jnp.where(sub == 7, lo, 0.0))
        full = jnp.concatenate([parent[c], cap], axis=0)
        w_in = pltpu.roll(col_w, lax.rem(LANES - c, LANES), 1)
        e_in = pltpu.roll(col_e, LANES - 1 - c, 1)
        w_all = jnp.where(lane == 0, w_in, pltpu.roll(full, 1, 1))
        e_all = jnp.where(lane == LANES - 1, e_in, pltpu.roll(full, LANES - 1, 1))
        up = lambda x: pltpu.roll(x, rows - 1, 0)[: z.TR]
        down = lambda x: pltpu.roll(x, 1, 0)[: z.TR]
        mid = full[: z.TR]
        w, e, nn, s = w_all[: z.TR], e_all[: z.TR], up(full), down(full)
        kx, ky, ax, ay = diff[0, c], diff[1, c], cour[0, c], cour[1, c]
        step = (
            mid
            + kx * (e - 2.0 * mid + w)
            + ky * (nn - 2.0 * mid + s)
            - ax * (mid - w)
            - ay * (mid - s)
        )
        m, fe, fw, fn, fs = nest_weights(diff, cour, c)
        a, b, k, x = ghost_share(fw, fe, m, fs, fn)
        share = on_w * ((a - x * i_end) * w + b * i_lo * down(w_all) + k * i_hi * up(w_all))
        a, b, k, x = ghost_share(fe, fw, m, fs, fn)
        share += on_e * ((a - x * i_end) * e + b * i_lo * down(e_all) + k * i_hi * up(e_all))
        a, b, k, x = ghost_share(fs, fn, m, fw, fe)
        share += on_s * ((a - x * j_end) * s + b * j_lo * down(w_all) + k * j_hi * down(e_all))
        a, b, k, x = ghost_share(fn, fs, m, fw, fe)
        share += on_n * ((a - x * j_end) * nn + b * j_lo * up(w_all) + k * j_hi * up(e_all))
        out[c] = jnp.where(inside, share, step)
        return 0

    lax.fori_loop(0, C, channel, 0)


def merge(z, tab, anc, base, *refs):
    pieces, out = refs[: z.S], refs[z.S]
    g, d = tab[0], tab[1]
    n = tab[2 + g // z.S * z.NB + d // z.Y]
    r, q = anc[n, 0], anc[n, 1]
    shift_r = lax.rem(r - g * z.TR + 2 * z.G * z.TR, z.FR)
    shift_q = lax.rem(q - d * z.TC + 2 * z.D * z.TC, z.FC)
    i = iota((z.TR, LANES), 0) + (g * z.TR - r)
    j = iota((z.TR, LANES), 1) + (d * z.TC - q)
    inside = (i >= 0) & (i < z.FR) & (j >= 0) & (j < z.FC)
    sub = iota((z.M, LANES), 0)
    part = lax.rem(g, z.S)
    size = z.CS * z.M
    for k in range(z.S):
        piece = pieces[k]
        first = lax.rem(part - k + z.S, z.S) * z.CS

        def channel(c, _, piece=piece, first=first):
            blocks = []
            for m in range(z.D):
                x = piece[m, pl.ds(pl.multiple_of(c * z.M, z.M), z.M), :]
                if m + 1 < z.D:
                    x += jnp.where(sub == z.M - 1, piece[m + 1, pl.ds(size + c, 1), :], 0.0)
                if m > 0:
                    x += jnp.where(sub == 0, piece[m - 1, pl.ds(size + z.CS + c, 1), :], 0.0)
                blocks.append(x)
            x = jnp.concatenate(blocks, axis=0)
            x = pltpu.roll(pltpu.roll(x, shift_r, 0), shift_q, 1)[: z.TR]
            out[first + c] = base[first + c] + jnp.where(inside, x, 0.0)
            return 0

        lax.fori_loop(0, z.CS, channel, 0)


def shards(parent, nest, anchor, diff, cour):
    z = Sizes(parent, nest, anchor, lax.axis_size("grp"), lax.axis_size("dev"))
    g, d = lax.axis_index("grp"), lax.axis_index("dev")
    every = jnp.arange(z.N, dtype=jnp.int32)
    band = anchor[:, 0] // z.BR * z.NB + anchor[:, 1] // z.BC
    nest_at = jnp.sum(jnp.where(band[None, :] == every[:, None], every[None, :], 0), axis=1)
    place = jnp.stack([g, d]).astype(jnp.int32)
    tab = jnp.concatenate([place, nest_at.astype(jnp.int32)])
    sds = lambda *shape: jax.ShapeDtypeStruct(shape, F32)
    vmem = lambda *shape: pltpu.VMEM(shape, F32)

    halo = sds(3, z.L * z.C * 3, LANES)
    avg, last3, first3 = call(
        functools.partial(partial_averages, z),
        [sds(z.G, z.R1, LANES), halo, halo],
        3,
        (place, diff, cour, nest),
        [
            vmem(3, z.H + 8, LANES),
            vmem(3, z.L * z.C * z.M, LANES),
            vmem(3, z.L * 2 * z.C, LANES),
        ],
    )
    avg = lax.all_to_all(avg, "grp", 0, 0, tiled=True)
    ring = call(functools.partial(ring_parts, z), sds(z.G, z.RG1, LANES), 2, (place, anchor, parent))
    ring = lax.all_to_all(ring, "grp", 0, 0, tiled=True)
    forward = [(k, k + 1) for k in range(z.D - 1)]
    up = lax.ppermute(last3, "dev", forward)
    dn = lax.ppermute(first3, "dev", [(b, a) for a, b in forward])

    avg = call(functools.partial(pick_band, z), sds(z.D, z.R2, LANES), 1, (tab, avg))
    avg = lax.all_to_all(avg, "dev", 0, 0, tiled=True)
    ring, edges = call(
        functools.partial(ring_next, z),
        [sds(z.D, z.RG2, LANES), sds(2 * z.C, LANES)],
        1,
        (place, ring, parent),
        [vmem(z.FR + 8, LANES)],
    )
    ring = lax.all_to_all(ring, "dev", 0, 0, tiled=True)

    pieces = [avg]
    for k in range(1, z.S):
        pairs = [(a, a // z.S * z.S + (a + k) % z.S) for a in range(z.G)]
        pieces.append(lax.ppermute(avg, "grp", pairs))
    nest_out = call(
        functools.partial(nest_steps, z),
        jax.ShapeDtypeStruct(nest.shape, F32),
        3,
        (place, diff, cour, nest, ring, up, dn),
        [vmem(z.H + 8, LANES), vmem(3, z.L * z.C, LANES), vmem(8, z.W)],
    )
    base = call(
        functools.partial(parent_step, z),
        jax.ShapeDtypeStruct(parent.shape, F32),
        4,
        (tab, anchor, diff, cour, parent, edges, ring),
    )
    parent_out = call(
        functools.partial(merge, z),
        jax.ShapeDtypeStruct(parent.shape, F32),
        2,
        (tab, anchor, base, *pieces),
    )
    return parent_out, nest_out


def solution(mesh):
    placed = (P(None, "grp", "dev"), P("grp", None, "dev", None), P(), P(), P())
    return jax.shard_map(
        shards,
        mesh=mesh,
        in_specs=placed,
        out_specs=(P(None, "grp", "dev"), P("grp", None, "dev", None)),
        check_vma=False,
    )
```

```python
import functools

import jax
import jax.numpy as jnp
from jax import lax
from jax.experimental import pallas as pl
from jax.experimental.pallas import tpu as pltpu
from jax.sharding import PartitionSpec as P

F32 = jnp.float32
BF16 = jnp.bfloat16
LANES = 128
VMEM_LIMIT = 48 * 1024 * 1024
MID, EAST, WEST, NORTH, SOUTH = range(5)
P_MID, P_EAST, P_WEST, P_NORTH, P_SOUTH = range(5)
SHARE = 8


class Sizes:
    def __init__(self, parent, nest, anchor, grp_count, dev_count):
        self.C, self.TR, self.TC = parent.shape
        self.L, _, self.H, self.W = nest.shape
        self.N = anchor.shape[0]
        self.G, self.D = grp_count, dev_count
        self.M = self.H // 3
        self.FR, self.FC = self.M * self.D, self.W // 3
        self.S = self.G // 2
        self.NB = self.N // 2
        self.Y = self.D // self.NB
        self.CS = self.C // self.S
        self.BR, self.BC = self.S * self.TR, self.Y * self.TC
        self.R1 = self.L * self.CS * (self.M + 2)
        self.R2 = self.CS * (self.M + 2)
        self.RING = self.FR + self.L * 2 * self.C
        self.RG = self.RING + 2 * self.C
        assert self.H == 24 and self.FC == LANES and self.TC == LANES
        assert self.FR >= self.TR and self.L == 2


def call(body, out_shape, n_smem, args, scratch=(), aliases=None):
    in_specs = [pl.BlockSpec(memory_space=pltpu.SMEM)] * n_smem
    in_specs += [pl.BlockSpec(memory_space=pltpu.VMEM)] * (len(args) - n_smem)
    many = isinstance(out_shape, (list, tuple))
    vm = pl.BlockSpec(memory_space=pltpu.VMEM)
    return pl.pallas_call(
        body,
        out_shape=out_shape,
        in_specs=in_specs,
        out_specs=[vm] * len(out_shape) if many else vm,
        scratch_shapes=list(scratch),
        input_output_aliases=aliases or {},
        compiler_params=pltpu.CompilerParams(vmem_limit_bytes=VMEM_LIMIT),
    )(*args)


def iota(shape, dim):
    return lax.broadcasted_iota(jnp.int32, shape, dim)


def split_dot(x, table):
    high = x.astype(BF16)
    low = (x - high.astype(F32)).astype(BF16)
    return jnp.dot(jnp.concatenate([high, low], axis=1), table, preferred_element_type=F32)


def weights(diff, cour, times):
    east = times * diff[0]
    north = times * diff[1]
    west = east + cour[0]
    south = north + cour[1]
    return 1.0 - (east + west) - (north + south), east, west, north, south


def ghost_share(inject, back, mid, plus, minus):
    stay = mid + inject
    m0 = inject * (1.0 + stay + mid * stay + inject * (stay + back) + 2.0 * plus * minus)
    p1 = inject * plus * (1.0 + 2.0 * stay)
    p2 = inject * plus * plus
    n1 = inject * minus * (1.0 + 2.0 * stay)
    n2 = inject * minus * minus
    ninth = 1.0 / 9.0
    same = (3.0 * m0 + 2.0 * p1 + p2 + 2.0 * n1 + n2) * ninth
    return same, (p1 + 2.0 * p2) * ninth, (n1 + 2.0 * n2) * ninth, inject * plus * minus * ninth


def rows_of(table, c, count):
    return [table[c, pl.ds(k, 1), :] for k in range(count)]


class Strip:
    def __init__(self):
        sub = iota((8, LANES), 0)
        lane = iota((8, LANES), 1)
        self.high = [sub == 0, sub == 4]
        self.low = [sub == 7, sub == 3]
        self.any_high = (sub == 0) | (sub == 4)
        self.any_low = (sub == 7) | (sub == 3)
        self.first, self.last = lane == 0, lane == LANES - 1

    def east(self, x, ghost):
        return jnp.where(self.last, ghost, pltpu.roll(x, LANES - 1, 1))

    def west(self, x, ghost):
        return jnp.where(self.first, ghost, pltpu.roll(x, 1, 1))

    def north(self, mains, cap):
        up = [pltpu.roll(m, 7, 0) for m in mains]
        cap_up = pltpu.roll(cap, 7, 0)
        new = [jnp.where(self.low[l], cap_up, up[l]) for l in range(2)]
        return new, jnp.where(self.low[0], up[0], jnp.where(self.low[1], up[1], 0.0))

    def south(self, mains, cap):
        down = [pltpu.roll(m, 1, 0) for m in mains]
        cap_down = pltpu.roll(cap, 1, 0)
        new = [jnp.where(self.high[l], cap_down, down[l]) for l in range(2)]
        return new, jnp.where(self.high[0], down[0], jnp.where(self.high[1], down[1], 0.0))

    def step(self, u, co, west_ghost, east_ghost):
        n_in = [self.north([u[0][0][x], u[1][0][x]], u[2][0][x]) for x in range(3)]
        s_in = [self.south([u[0][2][x], u[1][2][x]], u[2][2][x]) for x in range(3)]
        pick = lambda pair, k: pair[1] if k == 2 else pair[0][k]
        new = []
        for k in range(3):
            rows = []
            for y in range(3):
                row = u[k][y]
                e = [row[1], row[2], self.east(row[0], east_ghost[k])]
                w = [self.west(row[2], west_ghost[k]), row[0], row[1]]
                cells = []
                for x in range(3):
                    n = u[k][y + 1][x] if y < 2 else pick(n_in[x], k)
                    s = u[k][y - 1][x] if y > 0 else pick(s_in[x], k)
                    cells.append(
                        co[MID] * row[x]
                        + (co[EAST] * e[x] + co[WEST] * w[x])
                        + (co[NORTH] * n + co[SOUTH] * s)
                    )
                rows.append(cells)
            new.append(rows)
        return new

    def pooled_step(self, u, co):
        ends = []
        for k in range(3):
            row = [u[k][y][0] + u[k][y][1] + u[k][y][2] for y in range(3)]
            col = [u[k][0][x] + u[k][1][x] + u[k][2][x] for x in (0, 2)]
            ends.append((row[0], row[2], col[0], col[1], row[0] + row[1] + row[2]))
        n_in = self.north([ends[0][0], ends[1][0]], ends[2][0])
        s_in = self.south([ends[0][1], ends[1][1]], ends[2][1])
        pick = lambda pair, k: pair[1] if k == 2 else pair[0][k]
        out = []
        for k in range(3):
            row0, row2, col0, col2, total = ends[k]
            flux_x = co[EAST] * (self.east(col0, 0.0) - col0)
            flux_x += co[WEST] * (self.west(col2, 0.0) - col2)
            flux_y = co[NORTH] * (pick(n_in, k) - row0) + co[SOUTH] * (pick(s_in, k) - row2)
            out.append(total + (flux_x + flux_y))
        return out


def phase_rows(z, ref, l, c, y, x):
    got = ref[x, pl.ds((l * z.C + c) * z.H + y, z.M, 3), :]
    return got if l == 0 else pltpu.roll(got, 4, 0)


def partial_averages(z, nest, table, out, phases):
    d = lax.axis_index("dev")
    C, M, CS = z.C, z.M, z.CS
    fine = lax.rem(iota((2 * z.W, z.W), 0), z.W)
    place = iota((2 * z.W, z.W), 1)
    at = lax.rem(place, LANES) * 3 + place // LANES
    deal = jnp.where(fine == at, 1.0, 0.0).astype(BF16)
    dealt = split_dot(nest[...].reshape(z.L * C * z.H, z.W), deal)
    for x in range(3):
        phases[x] = dealt[:, x * LANES : (x + 1) * LANES]
    strip = Strip()
    keep_high = strip.any_low | (strip.any_high & (d < z.D - 1))
    keep_low = strip.any_high | (strip.any_low & (d > 0))
    zero = jnp.zeros((8, LANES), F32)
    ghosts = [0.0] * 3
    base = z.L * CS * M

    def hold(u):
        cap = [
            [jnp.where(keep_high, v, 0.0) for v in u[2][0]],
            u[2][1],
            [jnp.where(keep_low, v, 0.0) for v in u[2][2]],
        ]
        return [u[0], u[1], cap]

    for part in range(z.S):

        def channel(i, _, part=part):
            c = part * CS + i
            co = rows_of(table, c, 5)
            u = [
                [[phase_rows(z, phases, l, c, y, x) for x in range(3)] for y in range(3)]
                for l in range(2)
            ]
            u.append([[zero] * 3] * 3)
            for _step in range(2):
                u = hold(strip.step(u, co, ghosts, ghosts))
            got = [v * (1.0 / 9.0) for v in strip.pooled_step(u, co)]
            got[1] = pltpu.roll(got[1], 4, 0)
            for half in range(2):
                g = half * z.S + part
                for l in range(2):
                    row = pl.multiple_of((l * CS + i) * M, M)
                    out[g, pl.ds(row, M), :] = got[l]
                    for side, sub in enumerate(((7, 3), (0, 4))):
                        row = base + (l * 2 + side) * CS + i
                        out[g, pl.ds(row, 1), :] = got[2][sub[l] : sub[l] + 1]
            return 0

        lax.fori_loop(0, CS, channel, 0, unroll=2)


def halo_rows(z, phases, up, dn):
    for k in range(z.L * z.C):
        for x in range(3):
            up[x, 3 * k : 3 * k + 3, :] = phases[x, (k + 1) * z.H - 3 : (k + 1) * z.H, :]
            dn[x, 3 * k : 3 * k + 3, :] = phases[x, k * z.H : k * z.H + 3, :]


def pick_band(z, tab, got, out):
    top = lax.axis_index("grp") // z.S * z.NB
    base, size = z.L * z.CS * z.M, z.CS * z.M
    for band in range(z.NB):
        n = tab[2 * z.N + top + band]
        g = n // z.L
        first = n - g * z.L == 0
        main = jnp.where(first, got[g, :size, :], got[g, size : 2 * size, :])
        edge = jnp.where(
            first,
            got[g, base : base + 2 * z.CS, :],
            got[g, base + 2 * z.CS : base + 4 * z.CS, :],
        )
        for y in range(z.Y):
            out[band * z.Y + y, :size, :] = main
            out[band * z.Y + y, size:, :] = edge


def ring_parts(z, tab, parent, keep, send, buf):
    g, d = lax.axis_index("grp"), lax.axis_index("dev")
    row_base, col_base = g * z.TR, d * z.TC
    lane_t = iota((z.TR, LANES), 1)
    lane_f = iota((z.FR, LANES), 1)
    row_f = iota((z.FR, LANES), 0)
    lane_c = iota((z.C, LANES), 1)
    buf[...] = jnp.zeros_like(buf)

    def nest_ring(n, _):
        to = n // z.L
        l = n - to * z.L
        slot = jnp.bitwise_xor(to, g)
        r, q = tab[2 * n], tab[2 * n + 1]
        rows_meet = (r < row_base + z.TR) & (r + z.FR > row_base)
        cols_meet = (q < col_base + z.TC) & (q + z.FC > col_base)
        shift_r = lax.rem(row_base - r + 2 * z.G * z.TR, z.FR)
        shift_q = lax.rem(col_base - q + 2 * z.D * z.TC, z.FC)
        for side in range(2):
            col = (q - 1 if side == 0 else q + z.FC) - col_base
            first = (l * 2 + side) * z.C

            @pl.when(rows_meet & (col >= 0) & (col < z.TC))
            def _(col=col, first=first):
                acc = jnp.zeros((z.TR, LANES), F32)
                for c in range(z.C):
                    at = first + c
                    moved = pltpu.roll(parent[c], lax.rem(at - col + LANES, LANES), 1)
                    acc = jnp.where(lane_t == at, moved, acc)
                if z.FR > z.TR:
                    acc = jnp.concatenate([acc, jnp.zeros((z.FR - z.TR, LANES), F32)], axis=0)
                acc = pltpu.roll(acc, shift_r, 0)
                y = row_f + (r - row_base)
                good = (y >= 0) & (y < z.TR) & (lane_f >= first) & (lane_f < first + z.C)
                buf[slot, : z.FR, :] = jnp.where(good, acc, buf[slot, : z.FR, :])

            row = (r - 1 if side == 0 else r + z.FR) - row_base

            @pl.when(cols_meet & (row >= 0) & (row < z.TR))
            def _(row=row, first=first):
                rows = jnp.concatenate(
                    [parent[c, pl.ds(row, 1), :] for c in range(z.C)], axis=0
                )
                x = lane_c + (q - col_base)
                moved = jnp.where((x >= 0) & (x < z.TC), pltpu.roll(rows, shift_q, 1), 0.0)
                buf[slot, pl.ds(pl.multiple_of(z.FR + first, 8), z.C), :] = moved

        return 0

    lax.fori_loop(0, z.N, nest_ring, 0)
    for step, edge in ((1, z.TR - 1), (-1, 0)):
        to = g + step
        at = z.RING if step == 1 else z.RING + z.C

        @pl.when((to >= 0) & (to < z.G))
        def _(to=to, edge=edge, at=at):
            slot = jnp.bitwise_xor(to, g)
            for c in range(z.C):
                buf[slot, at + c : at + c + 1, :] = parent[c, edge : edge + 1, :]

    half = z.G // 2
    keep[...] = buf[:half]
    send[...] = buf[half:]


def edge_columns(z, parent, edges, first_out, last_out):
    C = z.C
    rows = z.TR + 8
    lane = iota((rows, LANES), 1)
    sub = iota((8, LANES), 0)
    first = jnp.zeros((rows, LANES), F32)
    last = first
    for c in range(C):
        lo = edges[c : c + 1, :]
        hi = edges[C + c : C + c + 1, :]
        cap = jnp.where(sub == 0, hi, jnp.where(sub == 7, lo, 0.0))
        full = jnp.concatenate([parent[c], cap], axis=0)
        first = jnp.where(lane == c, pltpu.roll(full, c, 1) if c else full, first)
        last = jnp.where(lane == c, pltpu.roll(full, c + 1, 1), last)
    first_out[...] = first
    last_out[...] = last


def nest_steps(z, phases, table, ring, up, dn, out, back):
    d = lax.axis_index("dev")
    C, M = z.C, z.M
    strip = Strip()
    side_main = ring[pl.ds(pl.multiple_of(d * M, M), M), :]
    side_hi = ring[pl.ds(jnp.minimum(d * M + M, z.FR - 1), 1), :]
    side_lo = ring[pl.ds(jnp.maximum(d * M - 1, 0), 1), :]
    side_main = [side_main, pltpu.roll(side_main, 4, 0)]
    side_cap = jnp.where(strip.any_high, side_hi, jnp.where(strip.any_low, side_lo, 0.0))
    hold_low, hold_high = strip.any_low & (d == 0), strip.any_high & (d == z.D - 1)
    nest_1 = strip.high[1] | strip.low[1]

    def channel(c, _):
        co = rows_of(table, c, 5)
        u = [
            [[phase_rows(z, phases, l, c, y, x) for x in range(3)] for y in range(3)]
            for l in range(2)
        ]
        cap = []
        for y in range(3):
            row = []
            for x in range(3):
                v = jnp.zeros((8, LANES), F32)
                for l in range(2):
                    at = (l * C + c) * 3 + y
                    v = jnp.where(strip.high[l], dn[x, pl.ds(at, 1), :], v)
                    v = jnp.where(strip.low[l], up[x, pl.ds(at, 1), :], v)
                row.append(v)
            cap.append(row)
        u.append(cap)
        end = []
        for side in range(2):
            at = z.FR + side * C + c
            end.append(
                jnp.where(nest_1, ring[pl.ds(at + 2 * C, 1), :], ring[pl.ds(at, 1), :])
            )
        west, east = [], []
        for side, lane, ghosts in ((0, 0, west), (1, LANES - 1, east)):
            turn = [lax.rem(lane - ((l * 2 + side) * C + c) + LANES, LANES) for l in range(2)]
            for l in range(2):
                ghosts.append(pltpu.roll(side_main[l], turn[l], 1))
            caps = [pltpu.roll(side_cap, turn[l], 1) for l in range(2)]
            ghosts.append(jnp.where(nest_1, caps[1], caps[0]))

        def hold(u):
            cap = [
                [jnp.where(hold_high, end[1], v) for v in u[2][0]],
                u[2][1],
                [jnp.where(hold_low, end[0], v) for v in u[2][2]],
            ]
            return [u[0], u[1], cap]

        u = hold(u)
        for k in range(3):
            u = strip.step(u, co, west, east)
            if k < 2:
                u = hold(u)
        for l in range(2):
            for y in range(3):
                for x in range(3):
                    v = u[l][y][x]
                    v = v if l == 0 else pltpu.roll(v, 4, 0)
                    back[x, pl.ds((l * C + c) * z.H + y, M, 3), :] = v
        return 0

    lax.fori_loop(0, C, channel, 0, unroll=2)
    fine = iota((2 * z.W, z.W), 1)
    place = lax.rem(iota((2 * z.W, z.W), 0), z.W)
    at = lax.rem(place, LANES) * 3 + place // LANES
    undeal = jnp.where(fine == at, 1.0, 0.0).astype(BF16)
    done = split_dot(jnp.concatenate([back[0], back[1], back[2]], axis=1), undeal)
    out[...] = done.reshape(z.L, C, z.H, z.W)


def parent_step(z, tab, parent, table, edges, col_w, col_e, out):
    g, d = lax.axis_index("grp"), lax.axis_index("dev")
    C = z.C
    rows = z.TR + 8
    n = tab[2 * z.N + g // z.S * z.NB + d // z.Y]
    i = iota((z.TR, LANES), 0) + (g * z.TR - tab[2 * n])
    j = iota((z.TR, LANES), 1) + (d * z.TC - tab[2 * n + 1])
    inside = (i >= 0) & (i < z.FR) & (j >= 0) & (j < z.FC)
    one = lambda cond: jnp.where(cond, 1.0, 0.0).astype(F32)
    on_w, on_e = one(inside & (j == 0)), one(inside & (j == z.FC - 1))
    on_s, on_n = one(inside & (i == 0)), one(inside & (i == z.FR - 1))
    i_end, j_end = one((i == 0) | (i == z.FR - 1)), one((j == 0) | (j == z.FC - 1))
    i_lo, i_hi = one(i > 0), one(i < z.FR - 1)
    j_lo, j_hi = one(j > 0), one(j < z.FC - 1)
    lane = iota((rows, LANES), 1)
    sub = iota((8, LANES), 0)

    def channel(c, _):
        co = rows_of(table, c, SHARE + 16)
        lo = edges[pl.ds(c, 1), :]
        hi = edges[pl.ds(C + c, 1), :]
        cap = jnp.where(sub == 0, hi, jnp.where(sub == 7, lo, 0.0))
        full = jnp.concatenate([parent[c], cap], axis=0)
        w_in = pltpu.roll(col_w[...], lax.rem(LANES - c, LANES), 1)
        e_in = pltpu.roll(col_e[...], LANES - 1 - c, 1)
        w_all = jnp.where(lane == 0, w_in, pltpu.roll(full, 1, 1))
        e_all = jnp.where(lane == LANES - 1, e_in, pltpu.roll(full, LANES - 1, 1))
        up = lambda x: pltpu.roll(x, rows - 1, 0)[: z.TR]
        down = lambda x: pltpu.roll(x, 1, 0)[: z.TR]
        mid = full[: z.TR]
        w, e, n, s = w_all[: z.TR], e_all[: z.TR], up(full), down(full)
        w_up, w_down, e_up, e_down = up(w_all), down(w_all), up(e_all), down(e_all)
        step = (
            co[P_MID] * mid
            + (co[P_EAST] * e + co[P_WEST] * w)
            + (co[P_NORTH] * n + co[P_SOUTH] * s)
        )
        a, b, k, x = co[SHARE : SHARE + 4]
        share = on_w * ((a - x * i_end) * w + (b * i_lo) * w_down + (k * i_hi) * w_up)
        a, b, k, x = co[SHARE + 4 : SHARE + 8]
        share += on_e * ((a - x * i_end) * e + (b * i_lo) * e_down + (k * i_hi) * e_up)
        a, b, k, x = co[SHARE + 8 : SHARE + 12]
        share += on_s * ((a - x * j_end) * s + (b * j_lo) * w_down + (k * j_hi) * e_down)
        a, b, k, x = co[SHARE + 12 : SHARE + 16]
        share += on_n * ((a - x * j_end) * n + (b * j_lo) * w_up + (k * j_hi) * e_up)
        out[c] = jnp.where(inside, share, step)
        return 0

    lax.fori_loop(0, C, channel, 0)


def merge(z, which, tab, base, *refs):
    pieces, out, twice = refs[:-2], refs[-2], refs[-1]
    g, d = lax.axis_index("grp"), lax.axis_index("dev")
    n = tab[2 * z.N + g // z.S * z.NB + d // z.Y]
    r, q = tab[2 * n], tab[2 * n + 1]
    start = lax.rem(g * z.TR - r + 2 * z.G * z.TR, z.FR)
    shift_q = lax.rem(q - d * z.TC + 2 * z.D * z.TC, z.FC)
    i = iota((z.TR, LANES), 0) + (g * z.TR - r)
    j = iota((z.TR, LANES), 1) + (d * z.TC - q)
    inside = (i >= 0) & (i < z.FR) & (j >= 0) & (j < z.FC)
    sub = iota((z.M, LANES), 0)
    part = lax.rem(g, z.S)
    size = z.CS * z.M
    for k in range(z.S):
        if k not in which:
            other = lax.rem(part - k + z.S, z.S) * z.CS
            out[pl.ds(other, z.CS)] = base[pl.ds(other, z.CS)]
    for piece, k in zip(pieces, which):
        first = lax.rem(part - k + z.S, z.S) * z.CS
        for c in range(z.CS):
            for m in range(z.D):
                x = piece[m, c * z.M : (c + 1) * z.M, :]
                if m + 1 < z.D:
                    row = piece[m + 1, size + c : size + c + 1, :]
                    x += jnp.where(sub == z.M - 1, row, 0.0)
                if m > 0:
                    row = piece[m - 1, size + z.CS + c : size + z.CS + c + 1, :]
                    x += jnp.where(sub == 0, row, 0.0)
                twice[c % 4, m * z.M : (m + 1) * z.M, :] = x
                if m * z.M < z.TR:
                    twice[c % 4, z.FR + m * z.M : z.FR + (m + 1) * z.M, :] = x
            x = pltpu.roll(twice[c % 4, pl.ds(start, z.TR), :], shift_q, 1)
            out[first + c] = base[first + c] + jnp.where(inside, x, 0.0)


def shards(parent, nest, anchor, diff, cour):
    z = Sizes(parent, nest, anchor, lax.axis_size("grp"), lax.axis_size("dev"))
    every = jnp.arange(z.N, dtype=jnp.int32)
    band = anchor[:, 0] // z.BR * z.NB + anchor[:, 1] // z.BC
    nest_at = jnp.sum(jnp.where(band[None, :] == every[:, None], every[None, :], 0), axis=1)
    tab = jnp.concatenate([anchor.reshape(-1), nest_at.astype(jnp.int32)])
    sds = lambda *shape: jax.ShapeDtypeStruct(shape, F32)
    vmem = lambda *shape: pltpu.VMEM(shape, F32)
    spread = lambda rows, count: jnp.broadcast_to(
        jnp.stack(rows + [jnp.zeros_like(rows[0])] * (count - len(rows)), axis=1)[:, :, None],
        (z.C, count, LANES),
    )
    fine = weights(diff, cour, 3.0)
    mid, east, west, north, south = fine
    shares = [
        *ghost_share(west, east, mid, south, north),
        *ghost_share(east, west, mid, south, north),
        *ghost_share(south, north, mid, west, east),
        *ghost_share(north, south, mid, west, east),
    ]
    blank = jnp.zeros_like(mid)
    fine_table = spread(list(fine), 8)
    coarse_table = spread([*weights(diff, cour, 1.0), blank, blank, blank, *shares], 24)

    half = z.G // 2
    keep, send = call(
        functools.partial(ring_parts, z),
        [sds(half, z.RG, LANES), sds(z.G - half, z.RG, LANES)],
        1,
        (tab, parent),
        [vmem(z.G, z.RG, LANES)],
    )
    swap = lambda x, axis, size, bit: lax.ppermute(x, axis, [(a, a ^ bit) for a in range(size)])
    ring = keep + swap(send, "grp", z.G, half)
    avg, phases = call(
        functools.partial(partial_averages, z),
        [sds(z.G, z.R1, LANES), sds(3, z.L * z.C * z.H, LANES)],
        0,
        (nest, fine_table),
    )
    avg = lax.all_to_all(avg, "grp", 0, 0, tiled=True)
    bit = half // 2
    while bit:
        ring = ring[:bit] + swap(ring[bit:], "grp", z.G, bit)
        bit //= 2
    ring = ring[0]
    edges = ring[z.RING :]
    ring = ring[: z.RING]
    halo = sds(3, z.L * z.C * 3, LANES)
    last3, first3 = call(functools.partial(halo_rows, z), [halo, halo], 0, (phases,))
    forward = [(k, k + 1) for k in range(z.D - 1)]
    backward = [(b, a) for a, b in forward]
    up = lax.ppermute(last3, "dev", forward)
    dn = lax.ppermute(first3, "dev", backward)

    avg = call(functools.partial(pick_band, z), sds(z.D, z.R2, LANES), 1, (tab, avg))
    avg = lax.all_to_all(avg, "dev", 0, 0, tiled=True)
    first, last = call(
        functools.partial(edge_columns, z),
        [sds(z.TR + 8, LANES), sds(z.TR + 8, LANES)],
        0,
        (parent, edges),
    )
    col_w = lax.ppermute(last, "dev", forward)
    col_e = lax.ppermute(first, "dev", backward)
    bit = 1
    while bit < z.D:
        ring = ring + swap(ring, "dev", z.D, bit)
        bit *= 2

    pieces = [avg]
    for k in range(1, z.S):
        pairs = [(a, a // z.S * z.S + (a + k) % z.S) for a in range(z.G)]
        pieces.append(lax.ppermute(avg, "grp", pairs))
    nest_out = call(
        functools.partial(nest_steps, z),
        jax.ShapeDtypeStruct(nest.shape, F32),
        0,
        (phases, fine_table, ring, up, dn),
        [vmem(3, z.L * z.C * z.H, LANES)],
    )
    out = call(
        functools.partial(parent_step, z),
        jax.ShapeDtypeStruct(parent.shape, F32),
        1,
        (tab, parent, coarse_table, edges, col_w, col_e),
    )
    for which in ([0], list(range(1, z.S))):
        out = call(
            functools.partial(merge, z, which),
            jax.ShapeDtypeStruct(parent.shape, F32),
            1,
            (tab, out, *[pieces[k] for k in which]),
            [vmem(4, z.FR + z.TR, LANES)],
            {1: 0},
        )
    return out, nest_out


def solution(mesh):
    placed = (P(None, "grp", "dev"), P("grp", None, "dev", None), P(), P(), P())
    return jax.shard_map(
        shards,
        mesh=mesh,
        in_specs=placed,
        out_specs=(P(None, "grp", "dev"), P("grp", None, "dev", None)),
        check_vma=False,
    )
```

```python
import functools

import jax
import jax.numpy as jnp
from jax import lax
from jax.experimental import pallas as pl
from jax.experimental.pallas import tpu as pltpu
from jax.sharding import PartitionSpec as P

F32 = jnp.float32
BF16 = jnp.bfloat16
LANES = 128
VMEM_LIMIT = 48 * 1024 * 1024
MID, EAST, WEST, NORTH, SOUTH = range(5)


class Sizes:
    def __init__(self, parent, nest, anchor, grp_count, dev_count):
        self.C, self.TR, self.TC = parent.shape
        self.L, _, self.H, self.W = nest.shape
        self.N = anchor.shape[0]
        self.G, self.D = grp_count, dev_count
        self.M = self.H // 3
        self.FR, self.FC = self.M * self.D, self.W // 3
        self.S = self.G // 2
        self.NB = self.N // 2
        self.Y = self.D // self.NB
        self.CS = self.C // self.S
        self.BR, self.BC = self.S * self.TR, self.Y * self.TC
        self.R1 = self.L * self.CS * (self.M + 2)
        self.R2 = self.CS * (self.M + 2)
        self.RING = self.FR + self.L * 2 * self.C
        self.RG = self.RING + self.C
        self.RG2 = 16 + self.L * self.C
        self.HALO = self.L * self.C * 3
        self.EDGE = 3 * self.HALO
        assert self.H == 24 and self.FC == LANES and self.TC == LANES
        assert self.FR >= self.TR and self.L == 2


def call(body, out_shape, n_smem, args, scratch=(), aliases=None):
    in_specs = [pl.BlockSpec(memory_space=pltpu.SMEM)] * n_smem
    in_specs += [pl.BlockSpec(memory_space=pltpu.VMEM)] * (len(args) - n_smem)
    many = isinstance(out_shape, (list, tuple))
    vm = pl.BlockSpec(memory_space=pltpu.VMEM)
    return pl.pallas_call(
        body,
        out_shape=out_shape,
        in_specs=in_specs,
        out_specs=[vm] * len(out_shape) if many else vm,
        scratch_shapes=list(scratch),
        input_output_aliases=aliases or {},
        compiler_params=pltpu.CompilerParams(vmem_limit_bytes=VMEM_LIMIT),
    )(*args)


def iota(shape, dim):
    return lax.broadcasted_iota(jnp.int32, shape, dim)


def split_dot(x, table):
    high = x.astype(BF16)
    low = (x - high.astype(F32)).astype(BF16)
    return jnp.dot(jnp.concatenate([high, low], axis=1), table, preferred_element_type=F32)


def weights(coef, c, times):
    east = times * coef[0, c]
    north = times * coef[1, c]
    west = east + coef[2, c]
    south = north + coef[3, c]
    return 1.0 - (east + west) - (north + south), east, west, north, south


def ghost_share(inject, back, mid, plus, minus):
    stay = mid + inject
    m0 = inject * (1.0 + stay + mid * stay + inject * (stay + back) + 2.0 * plus * minus)
    p1 = inject * plus * (1.0 + 2.0 * stay)
    p2 = inject * plus * plus
    n1 = inject * minus * (1.0 + 2.0 * stay)
    n2 = inject * minus * minus
    ninth = 1.0 / 9.0
    same = (3.0 * m0 + 2.0 * p1 + p2 + 2.0 * n1 + n2) * ninth
    return same, (p1 + 2.0 * p2) * ninth, (n1 + 2.0 * n2) * ninth, inject * plus * minus * ninth


class Strip:
    def __init__(self):
        sub = iota((8, LANES), 0)
        lane = iota((8, LANES), 1)
        self.high = [sub == 0, sub == 4]
        self.low = [sub == 7, sub == 3]
        self.any_high = (sub == 0) | (sub == 4)
        self.any_low = (sub == 7) | (sub == 3)
        self.first, self.last = lane == 0, lane == LANES - 1

    def east(self, x, ghost):
        return jnp.where(self.last, ghost, pltpu.roll(x, LANES - 1, 1))

    def west(self, x, ghost):
        return jnp.where(self.first, ghost, pltpu.roll(x, 1, 1))

    def north(self, mains, cap):
        up = [pltpu.roll(m, 7, 0) for m in mains]
        cap_up = pltpu.roll(cap, 7, 0)
        new = [jnp.where(self.low[l], cap_up, up[l]) for l in range(2)]
        return new, jnp.where(self.low[0], up[0], jnp.where(self.low[1], up[1], 0.0))

    def south(self, mains, cap):
        down = [pltpu.roll(m, 1, 0) for m in mains]
        cap_down = pltpu.roll(cap, 1, 0)
        new = [jnp.where(self.high[l], cap_down, down[l]) for l in range(2)]
        return new, jnp.where(self.high[0], down[0], jnp.where(self.high[1], down[1], 0.0))

    def step(self, u, co, west_ghost, east_ghost):
        n_in = [self.north([u[0][0][x], u[1][0][x]], u[2][0][x]) for x in range(3)]
        s_in = [self.south([u[0][2][x], u[1][2][x]], u[2][2][x]) for x in range(3)]
        pick = lambda pair, k: pair[1] if k == 2 else pair[0][k]
        new = []
        for k in range(3):
            rows = []
            for y in range(3):
                row = u[k][y]
                e = [row[1], row[2], self.east(row[0], east_ghost[k])]
                w = [self.west(row[2], west_ghost[k]), row[0], row[1]]
                cells = []
                for x in range(3):
                    n = u[k][y + 1][x] if y < 2 else pick(n_in[x], k)
                    s = u[k][y - 1][x] if y > 0 else pick(s_in[x], k)
                    cells.append(
                        co[MID] * row[x]
                        + (co[EAST] * e[x] + co[WEST] * w[x])
                        + (co[NORTH] * n + co[SOUTH] * s)
                    )
                rows.append(cells)
            new.append(rows)
        return new

    def pooled_step(self, u, co):
        ends = []
        for k in range(3):
            row = [u[k][y][0] + u[k][y][1] + u[k][y][2] for y in range(3)]
            col = [u[k][0][x] + u[k][1][x] + u[k][2][x] for x in (0, 2)]
            ends.append((row[0], row[2], col[0], col[1], row[0] + row[1] + row[2]))
        n_in = self.north([ends[0][0], ends[1][0]], ends[2][0])
        s_in = self.south([ends[0][1], ends[1][1]], ends[2][1])
        pick = lambda pair, k: pair[1] if k == 2 else pair[0][k]
        out = []
        for k in range(3):
            row0, row2, col0, col2, total = ends[k]
            flux_x = co[EAST] * (self.east(col0, 0.0) - col0)
            flux_x += co[WEST] * (self.west(col2, 0.0) - col2)
            flux_y = co[NORTH] * (pick(n_in, k) - row0) + co[SOUTH] * (pick(s_in, k) - row2)
            out.append(total + (flux_x + flux_y))
        return out


def phase_rows(z, ref, l, c, y, x):
    got = ref[x, pl.ds((l * z.C + c) * z.H + y, z.M, 3), :]
    return got if l == 0 else pltpu.roll(got, 4, 0)


def partial_averages(z, coef, nest, *refs):
    out, phases = refs[: z.S], refs[z.S]
    d = lax.axis_index("dev")
    own = lax.rem(lax.axis_index("grp"), z.S)
    C, M, CS = z.C, z.M, z.CS
    fine = lax.rem(iota((2 * z.W, z.W), 0), z.W)
    place = iota((2 * z.W, z.W), 1)
    at = lax.rem(place, LANES) * 3 + place // LANES
    deal = jnp.where(fine == at, 1.0, 0.0).astype(BF16)
    dealt = split_dot(nest[...].reshape(z.L * C * z.H, z.W), deal)
    for x in range(3):
        phases[x] = dealt[:, x * LANES : (x + 1) * LANES]
    strip = Strip()
    keep_high = strip.any_low | (strip.any_high & (d < z.D - 1))
    keep_low = strip.any_high | (strip.any_low & (d > 0))
    zero = jnp.zeros((8, LANES), F32)
    ghosts = [0.0] * 3
    base = z.L * CS * M

    def hold(u):
        cap = [
            [jnp.where(keep_high, v, 0.0) for v in u[2][0]],
            u[2][1],
            [jnp.where(keep_low, v, 0.0) for v in u[2][2]],
        ]
        return [u[0], u[1], cap]

    for part in range(z.S):

        def channel(i, _, to=out[part], first=jnp.bitwise_xor(own, part) * CS):
            c = first + i
            co = weights(coef, c, 3.0)
            u = [
                [[phase_rows(z, phases, l, c, y, x) for x in range(3)] for y in range(3)]
                for l in range(2)
            ]
            u.append([[zero] * 3] * 3)
            for _step in range(2):
                u = hold(strip.step(u, co, ghosts, ghosts))
            got = [v * (1.0 / 9.0) for v in strip.pooled_step(u, co)]
            got[1] = pltpu.roll(got[1], 4, 0)
            for l in range(2):
                row = pl.multiple_of((l * CS + i) * M, M)
                to[pl.ds(row, M), :] = got[l]
                for side, sub in enumerate(((7, 3), (0, 4))):
                    row = base + (l * 2 + side) * CS + i
                    to[pl.ds(row, 1), :] = got[2][sub[l] : sub[l] + 1]
            return 0

        lax.fori_loop(0, CS, channel, 0, unroll=2)


def pick_band(z, tab, *refs):
    got, out = refs[: z.G], refs[z.G]
    g = lax.axis_index("grp")
    top = g // z.S * z.NB
    base, size = z.L * z.CS * z.M, z.CS * z.M
    for band in range(z.NB):
        n = tab[2 * z.N + top + band]
        of = n // z.L
        slot = jnp.bitwise_xor(of, g)
        first = n - of * z.L == 0
        for k in range(z.G):

            @pl.when(slot == k)
            def _(k=k, first=first, band=band):
                main = jnp.where(first, got[k][:size, :], got[k][size : 2 * size, :])
                edge = jnp.where(
                    first,
                    got[k][base : base + 2 * z.CS, :],
                    got[k][base + 2 * z.CS : base + 4 * z.CS, :],
                )
                for y in range(z.Y):
                    out[band * z.Y + y, :size, :] = main
                    out[band * z.Y + y, size:, :] = edge


def ring_parts(z, tab, parent, buf):
    g, d = lax.axis_index("grp"), lax.axis_index("dev")
    row_base, col_base = g * z.TR, d * z.TC
    lane_t = iota((z.TR, LANES), 1)
    lane_f = iota((z.FR, LANES), 1)
    row_f = iota((z.FR, LANES), 0)
    lane_c = iota((z.C, LANES), 1)
    buf[...] = jnp.zeros_like(buf)

    def nest_ring(n, _):
        to = n // z.L
        l = n - to * z.L
        slot = to
        r, q = tab[2 * n], tab[2 * n + 1]
        rows_meet = (r < row_base + z.TR) & (r + z.FR > row_base)
        cols_meet = (q < col_base + z.TC) & (q + z.FC > col_base)
        shift_r = lax.rem(row_base - r + 2 * z.G * z.TR, z.FR)
        shift_q = lax.rem(col_base - q + 2 * z.D * z.TC, z.FC)
        for side in range(2):
            col = (q - 1 if side == 0 else q + z.FC) - col_base
            first = (l * 2 + side) * z.C

            @pl.when(rows_meet & (col >= 0) & (col < z.TC))
            def _(col=col, first=first):
                acc = jnp.zeros((z.TR, LANES), F32)
                for c in range(z.C):
                    at = first + c
                    moved = pltpu.roll(parent[c], lax.rem(at - col + LANES, LANES), 1)
                    acc = jnp.where(lane_t == at, moved, acc)
                if z.FR > z.TR:
                    acc = jnp.concatenate([acc, jnp.zeros((z.FR - z.TR, LANES), F32)], axis=0)
                acc = pltpu.roll(acc, shift_r, 0)
                y = row_f + (r - row_base)
                good = (y >= 0) & (y < z.TR) & (lane_f >= first) & (lane_f < first + z.C)
                buf[slot, : z.FR, :] = jnp.where(good, acc, buf[slot, : z.FR, :])

            row = (r - 1 if side == 0 else r + z.FR) - row_base

            @pl.when(cols_meet & (row >= 0) & (row < z.TR))
            def _(row=row, first=first):
                rows = jnp.concatenate(
                    [parent[c, pl.ds(row, 1), :] for c in range(z.C)], axis=0
                )
                x = lane_c + (q - col_base)
                moved = jnp.where((x >= 0) & (x < z.TC), pltpu.roll(rows, shift_q, 1), 0.0)
                buf[slot, pl.ds(pl.multiple_of(z.FR + first, 8), z.C), :] = moved

        return 0

    lax.fori_loop(0, z.N, nest_ring, 0)
    for to in range(z.G):
        edge = jnp.where(to > g, z.TR - 1, 0)
        for c in range(z.C):
            buf[to, z.RING + c : z.RING + c + 1, :] = parent[c, pl.ds(edge, 1), :]


def ring_next(z, got, parent, phases, out, edges, up, dn, slab):
    g = lax.axis_index("grp")
    C, L, FR, M = z.C, z.L, z.FR, z.M
    total = got[0, : z.RING, :]
    for k in range(1, z.G):
        total = total + got[k, : z.RING, :]
    slab[...] = total
    sub = iota((8, LANES), 0)
    for to in range(z.D):
        out[to, :M, :] = slab[to * M : (to + 1) * M, :]
        hi = min(to * M + M, FR - 1)
        lo = max(to * M - 1, 0)
        hi, lo = slab[hi : hi + 1, :], slab[lo : lo + 1, :]
        out[to, M:16, :] = jnp.where(sub == 0, hi, jnp.where(sub == 7, lo, 0.0))
        for l in range(L):
            at = 16 + l * C
            if to == 0 or to == z.D - 1:
                k = FR + (l * 2 + (0 if to == 0 else 1)) * C
                out[to, at : at + C, :] = slab[k : k + C, :]
            else:
                out[to, at : at + C, :] = jnp.zeros((C, LANES), F32)
    before, after = jnp.maximum(g - 1, 0), jnp.minimum(g + 1, z.G - 1)
    edges[:C, :] = jnp.where(g > 0, got[before, z.RING :, :], 0.0)
    edges[C:, :] = jnp.where(g < z.G - 1, got[after, z.RING :, :], 0.0)
    rows = z.TR + 8
    lane = iota((rows, LANES), 1)
    first = jnp.zeros((rows, LANES), F32)
    last = first
    for c in range(C):
        lo = edges[c : c + 1, :]
        hi = edges[C + c : C + c + 1, :]
        cap = jnp.where(sub == 0, hi, jnp.where(sub == 7, lo, 0.0))
        full = jnp.concatenate([parent[c], cap], axis=0)
        first = jnp.where(lane == c, pltpu.roll(full, c, 1) if c else full, first)
        last = jnp.where(lane == c, pltpu.roll(full, c + 1, 1), last)
    up[z.EDGE :, :] = last
    dn[z.EDGE :, :] = first
    for x in range(3):
        for k in range(L * C):
            at = x * z.HALO + 3 * k
            up[at : at + 3, :] = phases[x, (k + 1) * z.H - 3 : (k + 1) * z.H, :]
            dn[at : at + 3, :] = phases[x, k * z.H : k * z.H + 3, :]


def nest_steps(z, coef, phases, got, up, dn, out, back, ring):
    d = lax.axis_index("dev")
    C, M = z.C, z.M
    strip = Strip()
    total = got[0]
    for k in range(1, z.D):
        total = total + got[k]
    ring[...] = total
    side_main = [ring[:M, :], pltpu.roll(ring[:M, :], 4, 0)]
    side_cap = jnp.where(
        strip.any_high, ring[M : M + 1, :], jnp.where(strip.any_low, ring[15:16, :], 0.0)
    )
    hold_low, hold_high = strip.any_low & (d == 0), strip.any_high & (d == z.D - 1)
    nest_1 = strip.high[1] | strip.low[1]

    def channel(c, _):
        co = weights(coef, c, 3.0)
        u = [
            [[phase_rows(z, phases, l, c, y, x) for x in range(3)] for y in range(3)]
            for l in range(2)
        ]
        cap = []
        for y in range(3):
            row = []
            for x in range(3):
                v = jnp.zeros((8, LANES), F32)
                for l in range(2):
                    at = x * z.HALO + (l * C + c) * 3 + y
                    v = jnp.where(strip.high[l], dn[pl.ds(at, 1), :], v)
                    v = jnp.where(strip.low[l], up[pl.ds(at, 1), :], v)
                row.append(v)
            cap.append(row)
        u.append(cap)
        end = jnp.where(nest_1, ring[pl.ds(16 + C + c, 1), :], ring[pl.ds(16 + c, 1), :])
        west, east = [], []
        for side, lane, ghosts in ((0, 0, west), (1, LANES - 1, east)):
            turn = [lax.rem(lane - ((l * 2 + side) * C + c) + LANES, LANES) for l in range(2)]
            for l in range(2):
                ghosts.append(pltpu.roll(side_main[l], turn[l], 1))
            caps = [pltpu.roll(side_cap, turn[l], 1) for l in range(2)]
            ghosts.append(jnp.where(nest_1, caps[1], caps[0]))

        def hold(u):
            cap = [
                [jnp.where(hold_high, end, v) for v in u[2][0]],
                u[2][1],
                [jnp.where(hold_low, end, v) for v in u[2][2]],
            ]
            return [u[0], u[1], cap]

        u = hold(u)
        for k in range(3):
            u = strip.step(u, co, west, east)
            if k < 2:
                u = hold(u)
        for l in range(2):
            for y in range(3):
                for x in range(3):
                    v = u[l][y][x]
                    v = v if l == 0 else pltpu.roll(v, 4, 0)
                    back[x, pl.ds((l * C + c) * z.H + y, M, 3), :] = v
        return 0

    lax.fori_loop(0, C, channel, 0, unroll=2)
    fine = iota((2 * z.W, z.W), 1)
    place = lax.rem(iota((2 * z.W, z.W), 0), z.W)
    at = lax.rem(place, LANES) * 3 + place // LANES
    undeal = jnp.where(fine == at, 1.0, 0.0).astype(BF16)
    done = split_dot(jnp.concatenate([back[0], back[1], back[2]], axis=1), undeal)
    out[...] = done.reshape(z.L, C, z.H, z.W)


def parent_step(z, tab, coef, parent, edges, up_in, dn_in, out):
    g, d = lax.axis_index("grp"), lax.axis_index("dev")
    C = z.C
    rows = z.TR + 8
    n = tab[2 * z.N + g // z.S * z.NB + d // z.Y]
    i = iota((z.TR, LANES), 0) + (g * z.TR - tab[2 * n])
    j = iota((z.TR, LANES), 1) + (d * z.TC - tab[2 * n + 1])
    inside = (i >= 0) & (i < z.FR) & (j >= 0) & (j < z.FC)
    one = lambda cond: jnp.where(cond, 1.0, 0.0).astype(F32)
    on_w, on_e = one(inside & (j == 0)), one(inside & (j == z.FC - 1))
    on_s, on_n = one(inside & (i == 0)), one(inside & (i == z.FR - 1))
    i_end, j_end = one((i == 0) | (i == z.FR - 1)), one((j == 0) | (j == z.FC - 1))
    i_lo, i_hi = one(i > 0), one(i < z.FR - 1)
    j_lo, j_hi = one(j > 0), one(j < z.FC - 1)
    lane = iota((rows, LANES), 1)
    sub = iota((8, LANES), 0)

    col_w, col_e = up_in[z.EDGE :, :], dn_in[z.EDGE :, :]

    def channel(c, _):
        co = weights(coef, c, 1.0)
        fm, fe, fw, fn, fs = [
            jnp.full((1, LANES), v, F32) for v in weights(coef, c, 3.0)
        ]
        lo = edges[pl.ds(c, 1), :]
        hi = edges[pl.ds(C + c, 1), :]
        cap = jnp.where(sub == 0, hi, jnp.where(sub == 7, lo, 0.0))
        full = jnp.concatenate([parent[c], cap], axis=0)
        w_in = pltpu.roll(col_w, lax.rem(LANES - c, LANES), 1)
        e_in = pltpu.roll(col_e, LANES - 1 - c, 1)
        w_all = jnp.where(lane == 0, w_in, pltpu.roll(full, 1, 1))
        e_all = jnp.where(lane == LANES - 1, e_in, pltpu.roll(full, LANES - 1, 1))
        up = lambda x: pltpu.roll(x, rows - 1, 0)[: z.TR]
        down = lambda x: pltpu.roll(x, 1, 0)[: z.TR]
        mid = full[: z.TR]
        w, e, n, s = w_all[: z.TR], e_all[: z.TR], up(full), down(full)
        w_up, w_down, e_up, e_down = up(w_all), down(w_all), up(e_all), down(e_all)
        step = (
            co[MID] * mid
            + (co[EAST] * e + co[WEST] * w)
            + (co[NORTH] * n + co[SOUTH] * s)
        )
        a, b, k, x = ghost_share(fw, fe, fm, fs, fn)
        share = on_w * ((a - x * i_end) * w + (b * i_lo) * w_down + (k * i_hi) * w_up)
        a, b, k, x = ghost_share(fe, fw, fm, fs, fn)
        share += on_e * ((a - x * i_end) * e + (b * i_lo) * e_down + (k * i_hi) * e_up)
        a, b, k, x = ghost_share(fs, fn, fm, fw, fe)
        share += on_s * ((a - x * j_end) * s + (b * j_lo) * w_down + (k * j_hi) * e_down)
        a, b, k, x = ghost_share(fn, fs, fm, fw, fe)
        share += on_n * ((a - x * j_end) * n + (b * j_lo) * w_up + (k * j_hi) * e_up)
        out[c] = jnp.where(inside, share, step)
        return 0

    lax.fori_loop(0, C, channel, 0, unroll=2)


def merge(z, which, tab, base, *refs):
    pieces, out, twice = refs[:-2], refs[-2], refs[-1]
    g, d = lax.axis_index("grp"), lax.axis_index("dev")
    n = tab[2 * z.N + g // z.S * z.NB + d // z.Y]
    r, q = tab[2 * n], tab[2 * n + 1]
    start = lax.rem(g * z.TR - r + 2 * z.G * z.TR, z.FR)
    shift_q = lax.rem(q - d * z.TC + 2 * z.D * z.TC, z.FC)
    i = iota((z.TR, LANES), 0) + (g * z.TR - r)
    j = iota((z.TR, LANES), 1) + (d * z.TC - q)
    inside = (i >= 0) & (i < z.FR) & (j >= 0) & (j < z.FC)
    sub = iota((z.M, LANES), 0)
    part = lax.rem(g, z.S)
    size = z.CS * z.M
    for k in range(z.S):
        if k not in which:
            other = lax.rem(part - k + z.S, z.S) * z.CS
            out[pl.ds(other, z.CS)] = base[pl.ds(other, z.CS)]
    for piece, k in zip(pieces, which):
        first = lax.rem(part - k + z.S, z.S) * z.CS
        for c in range(z.CS):
            for m in range(z.D):
                x = piece[m, c * z.M : (c + 1) * z.M, :]
                if m + 1 < z.D:
                    row = piece[m + 1, size + c : size + c + 1, :]
                    x += jnp.where(sub == z.M - 1, row, 0.0)
                if m > 0:
                    row = piece[m - 1, size + z.CS + c : size + z.CS + c + 1, :]
                    x += jnp.where(sub == 0, row, 0.0)
                twice[c % 4, m * z.M : (m + 1) * z.M, :] = x
                if m * z.M < z.TR:
                    twice[c % 4, z.FR + m * z.M : z.FR + (m + 1) * z.M, :] = x
            x = pltpu.roll(twice[c % 4, pl.ds(start, z.TR), :], shift_q, 1)
            out[first + c] = base[first + c] + jnp.where(inside, x, 0.0)


def shards(parent, nest, anchor, diff, cour):
    z = Sizes(parent, nest, anchor, lax.axis_size("grp"), lax.axis_size("dev"))
    every = jnp.arange(z.N, dtype=jnp.int32)
    band = anchor[:, 0] // z.BR * z.NB + anchor[:, 1] // z.BC
    nest_at = jnp.sum(jnp.where(band[None, :] == every[:, None], every[None, :], 0), axis=1)
    tab = jnp.concatenate([anchor.reshape(-1), nest_at.astype(jnp.int32)])
    sds = lambda *shape: jax.ShapeDtypeStruct(shape, F32)
    vmem = lambda *shape: pltpu.VMEM(shape, F32)
    coef = jnp.concatenate([diff, cour])
    to_grp = lambda x, k: lax.ppermute(x, "grp", [(a, a ^ k) for a in range(z.G)])

    ring = call(functools.partial(ring_parts, z), sds(z.G, z.RG, LANES), 1, (tab, parent))
    nest, coef, ring = lax.optimization_barrier((nest, coef, ring))
    ring = lax.all_to_all(ring, "grp", 0, 0, tiled=True)
    *chunks, phases = call(
        functools.partial(partial_averages, z),
        [sds(z.R1, LANES)] * z.S + [sds(3, z.L * z.C * z.H, LANES)],
        1,
        (coef, nest),
    )
    got = [chunks[0]] + [to_grp(chunks[k % z.S], k) for k in range(1, z.G)]

    message = sds(z.EDGE + z.TR + 8, LANES)
    ring, edges, up, dn = call(
        functools.partial(ring_next, z),
        [sds(z.D, z.RG2, LANES), sds(2 * z.C, LANES), message, message],
        0,
        (ring, parent, phases),
        [vmem(z.RING, LANES)],
    )
    tab, ring, up, dn = lax.optimization_barrier((tab, ring, up, dn))
    ring = lax.all_to_all(ring, "dev", 0, 0, tiled=True)
    forward = [(k, k + 1) for k in range(z.D - 1)]
    up = lax.ppermute(up, "dev", forward)
    dn = lax.ppermute(dn, "dev", [(b, a) for a, b in forward])

    avg = call(functools.partial(pick_band, z), sds(z.D, z.R2, LANES), 1, (tab, *got))
    avg = lax.all_to_all(avg, "dev", 0, 0, tiled=True)
    pieces = [avg]
    for k in range(1, z.S):
        pairs = [(a, a // z.S * z.S + (a + k) % z.S) for a in range(z.G)]
        pieces.append(lax.ppermute(avg, "grp", pairs))
    nest_out = call(
        functools.partial(nest_steps, z),
        jax.ShapeDtypeStruct(nest.shape, F32),
        1,
        (coef, phases, ring, up, dn),
        [vmem(3, z.L * z.C * z.H, LANES), vmem(z.RG2, LANES)],
    )
    out = call(
        functools.partial(parent_step, z),
        jax.ShapeDtypeStruct(parent.shape, F32),
        2,
        (tab, coef, parent, edges, up, dn),
    )
    for which in ([0], list(range(1, z.S))):
        out = call(
            functools.partial(merge, z, which),
            jax.ShapeDtypeStruct(parent.shape, F32),
            1,
            (tab, out, *[pieces[k] for k in which]),
            [vmem(4, z.FR + z.TR, LANES)],
            {1: 0},
        )
    return out, nest_out


def solution(mesh):
    placed = (P(None, "grp", "dev"), P("grp", None, "dev", None), P(), P(), P())
    return jax.shard_map(
        shards,
        mesh=mesh,
        in_specs=placed,
        out_specs=(P(None, "grp", "dev"), P("grp", None, "dev", None)),
        check_vma=False,
    )
```

```python
import functools

import jax
import jax.numpy as jnp
from jax import lax
from jax.experimental import pallas as pl
from jax.experimental.pallas import tpu as pltpu
from jax.sharding import PartitionSpec as P

F32 = jnp.float32
BF16 = jnp.bfloat16
LANES = 128
VMEM_LIMIT = 48 * 1024 * 1024
MID, EAST, WEST, NORTH, SOUTH = range(5)


class Sizes:
    def __init__(self, parent, nest, anchor, grp_count, dev_count):
        self.C, self.TR, self.TC = parent.shape
        self.L, _, self.H, self.W = nest.shape
        self.N = anchor.shape[0]
        self.G, self.D = grp_count, dev_count
        self.M = self.H // 3
        self.FR, self.FC = self.M * self.D, self.W // 3
        self.S = self.G // 2
        self.NB = self.N // 2
        self.Y = self.D // self.NB
        self.CS = self.C // self.S
        self.BR, self.BC = self.S * self.TR, self.Y * self.TC
        self.R1 = self.L * self.CS * (self.M + 2)
        self.R2 = self.CS * (self.M + 2)
        self.RING = self.FR + self.L * 2 * self.C
        self.RG = self.RING + self.C
        self.RG2 = 16 + self.L * self.C
        self.HALO = self.L * self.C * 3
        self.EDGE = 3 * self.HALO
        assert self.H == 24 and self.FC == LANES and self.TC == LANES
        assert self.FR >= self.TR and self.L == 2


def call(body, out_shape, smem, args, scratch=(), raw=()):
    moved = [*smem, *args]
    n_in, n_raw, n_out = len(moved), len(raw), len(out_shape)
    anywhere = pl.BlockSpec(memory_space=pl.ANY)

    def kernel(*refs):
        source, refs = refs[:n_in], refs[n_in:]
        stay, refs = refs[:n_raw], refs[n_raw:]
        target, refs = refs[:n_out], refs[n_out:]
        inner, refs = refs[:n_in], refs[n_in:]
        result, refs = refs[:n_out], refs[n_out:]
        extra, sem = refs[:-1], refs[-1]
        fetch = [pltpu.make_async_copy(a, b, sem.at[k]) for k, (a, b) in enumerate(zip(source, inner))]
        for copy in fetch:
            copy.start()
        for copy in fetch:
            copy.wait()
        body(*inner, *stay, *result, *extra)
        store = [
            pltpu.make_async_copy(a, b, sem.at[n_in + k]) for k, (a, b) in enumerate(zip(result, target))
        ]
        for copy in store:
            copy.start()
        for copy in store:
            copy.wait()

    return pl.pallas_call(
        kernel,
        out_shape=list(out_shape),
        in_specs=[anywhere] * (n_in + n_raw),
        out_specs=[anywhere] * n_out,
        scratch_shapes=[
            *[pltpu.SMEM(x.shape, x.dtype) for x in smem],
            *[pltpu.VMEM(x.shape, x.dtype) for x in args],
            *[pltpu.VMEM(x.shape, x.dtype) for x in out_shape],
            *scratch,
            pltpu.SemaphoreType.DMA((n_in + n_out,)),
        ],
        compiler_params=pltpu.CompilerParams(vmem_limit_bytes=VMEM_LIMIT),
    )(*moved, *raw)


def iota(shape, dim):
    return lax.broadcasted_iota(jnp.int32, shape, dim)


def split_dot(x, table):
    high = x.astype(BF16)
    low = (x - high.astype(F32)).astype(BF16)
    return jnp.dot(jnp.concatenate([high, low], axis=1), table, preferred_element_type=F32)


def nest_at(z, anc, band):
    found = 0
    for n in range(z.N):
        found += jnp.where(anc[n, 0] // z.BR * z.NB + anc[n, 1] // z.BC == band, n, 0)
    return found


def weights(diff, cour, c, times):
    splat = lambda ref, k: jnp.full((8, LANES), ref[k, c], F32)
    east = times * splat(diff, 0)
    north = times * splat(diff, 1)
    west = east + splat(cour, 0)
    south = north + splat(cour, 1)
    return 1.0 - (east + west) - (north + south), east, west, north, south


def ghost_share(inject, back, mid, plus, minus):
    stay = mid + inject
    m0 = inject * (1.0 + stay + mid * stay + inject * (stay + back) + 2.0 * plus * minus)
    p1 = inject * plus * (1.0 + 2.0 * stay)
    p2 = inject * plus * plus
    n1 = inject * minus * (1.0 + 2.0 * stay)
    n2 = inject * minus * minus
    ninth = 1.0 / 9.0
    same = (3.0 * m0 + 2.0 * p1 + p2 + 2.0 * n1 + n2) * ninth
    return same, (p1 + 2.0 * p2) * ninth, (n1 + 2.0 * n2) * ninth, inject * plus * minus * ninth


class Strip:
    def __init__(self):
        sub = iota((8, LANES), 0)
        lane = iota((8, LANES), 1)
        self.high = [sub == 0, sub == 4]
        self.low = [sub == 7, sub == 3]
        self.any_high = (sub == 0) | (sub == 4)
        self.any_low = (sub == 7) | (sub == 3)
        self.first, self.last = lane == 0, lane == LANES - 1

    def east(self, x, ghost):
        return jnp.where(self.last, ghost, pltpu.roll(x, LANES - 1, 1))

    def west(self, x, ghost):
        return jnp.where(self.first, ghost, pltpu.roll(x, 1, 1))

    def north(self, mains, cap):
        up = [pltpu.roll(m, 7, 0) for m in mains]
        cap_up = pltpu.roll(cap, 7, 0)
        new = [jnp.where(self.low[l], cap_up, up[l]) for l in range(2)]
        return new, jnp.where(self.low[0], up[0], jnp.where(self.low[1], up[1], 0.0))

    def south(self, mains, cap):
        down = [pltpu.roll(m, 1, 0) for m in mains]
        cap_down = pltpu.roll(cap, 1, 0)
        new = [jnp.where(self.high[l], cap_down, down[l]) for l in range(2)]
        return new, jnp.where(self.high[0], down[0], jnp.where(self.high[1], down[1], 0.0))

    def step(self, u, co, west_ghost, east_ghost):
        n_in = [self.north([u[0][0][x], u[1][0][x]], u[2][0][x]) for x in range(3)]
        s_in = [self.south([u[0][2][x], u[1][2][x]], u[2][2][x]) for x in range(3)]
        pick = lambda pair, k: pair[1] if k == 2 else pair[0][k]
        new = []
        for k in range(3):
            rows = []
            for y in range(3):
                row = u[k][y]
                e = [row[1], row[2], self.east(row[0], east_ghost[k])]
                w = [self.west(row[2], west_ghost[k]), row[0], row[1]]
                cells = []
                for x in range(3):
                    n = u[k][y + 1][x] if y < 2 else pick(n_in[x], k)
                    s = u[k][y - 1][x] if y > 0 else pick(s_in[x], k)
                    cells.append(
                        co[MID] * row[x]
                        + (co[EAST] * e[x] + co[WEST] * w[x])
                        + (co[NORTH] * n + co[SOUTH] * s)
                    )
                rows.append(cells)
            new.append(rows)
        return new

    def pooled_step(self, u, co):
        ends = []
        for k in range(3):
            row = [u[k][y][0] + u[k][y][1] + u[k][y][2] for y in range(3)]
            col = [u[k][0][x] + u[k][1][x] + u[k][2][x] for x in (0, 2)]
            ends.append((row[0], row[2], col[0], col[1], row[0] + row[1] + row[2]))
        n_in = self.north([ends[0][0], ends[1][0]], ends[2][0])
        s_in = self.south([ends[0][1], ends[1][1]], ends[2][1])
        pick = lambda pair, k: pair[1] if k == 2 else pair[0][k]
        out = []
        for k in range(3):
            row0, row2, col0, col2, total = ends[k]
            flux_x = co[EAST] * (self.east(col0, 0.0) - col0)
            flux_x += co[WEST] * (self.west(col2, 0.0) - col2)
            flux_y = co[NORTH] * (pick(n_in, k) - row0) + co[SOUTH] * (pick(s_in, k) - row2)
            out.append(total + (flux_x + flux_y))
        return out


def phase_rows(z, ref, l, c, y, x):
    got = ref[x, pl.ds((l * z.C + c) * z.H + y, z.M, 3), :]
    return got if l == 0 else pltpu.roll(got, 4, 0)


def partial_averages(z, diff, cour, nest, *refs):
    out, phases, strips, sem = refs[: z.S], refs[z.S], refs[z.S + 1], refs[z.S + 2]
    fetch = [pltpu.make_async_copy(nest.at[l], strips.at[l], sem.at[l]) for l in range(z.L)]
    for copy in fetch:
        copy.start()
    d = lax.axis_index("dev")
    own = lax.rem(lax.axis_index("grp"), z.S)
    C, M, CS = z.C, z.M, z.CS
    fine = lax.rem(iota((2 * z.W, z.W), 0), z.W)
    place = iota((2 * z.W, z.W), 1)
    at = lax.rem(place, LANES) * 3 + place // LANES
    deal = jnp.where(fine == at, 1.0, 0.0).astype(BF16)
    rows = C * z.H
    for l in range(z.L):
        fetch[l].wait()
        dealt = split_dot(strips[l].reshape(rows, z.W), deal)
        for x in range(3):
            phases[x, l * rows : (l + 1) * rows, :] = dealt[:, x * LANES : (x + 1) * LANES]
    strip = Strip()
    keep_high = strip.any_low | (strip.any_high & (d < z.D - 1))
    keep_low = strip.any_high | (strip.any_low & (d > 0))
    zero = jnp.zeros((8, LANES), F32)
    ghosts = [0.0] * 3
    base = z.L * CS * M

    def hold(u):
        cap = [
            [jnp.where(keep_high, v, 0.0) for v in u[2][0]],
            u[2][1],
            [jnp.where(keep_low, v, 0.0) for v in u[2][2]],
        ]
        return [u[0], u[1], cap]

    for part in range(z.S):

        def channel(i, _, to=out[part], first=jnp.bitwise_xor(own, part) * CS):
            c = first + i
            co = weights(diff, cour, c, 3.0)
            u = [
                [[phase_rows(z, phases, l, c, y, x) for x in range(3)] for y in range(3)]
                for l in range(2)
            ]
            u.append([[zero] * 3] * 3)
            for _step in range(2):
                u = hold(strip.step(u, co, ghosts, ghosts))
            got = [v * (1.0 / 9.0) for v in strip.pooled_step(u, co)]
            got[1] = pltpu.roll(got[1], 4, 0)
            for l in range(2):
                row = pl.multiple_of((l * CS + i) * M, M)
                to[pl.ds(row, M), :] = got[l]
                for side, sub in enumerate(((7, 3), (0, 4))):
                    row = base + (l * 2 + side) * CS + i
                    to[pl.ds(row, 1), :] = got[2][sub[l] : sub[l] + 1]
            return 0

        lax.fori_loop(0, CS, channel, 0, unroll=2)


def pick_band(z, anc, *refs):
    got, out = refs[: z.G], refs[z.G]
    g = lax.axis_index("grp")
    top = g // z.S * z.NB
    base, size = z.L * z.CS * z.M, z.CS * z.M
    for band in range(z.NB):
        n = nest_at(z, anc, top + band)
        of = n // z.L
        slot = jnp.bitwise_xor(of, g)
        first = n - of * z.L == 0
        for k in range(z.G):

            @pl.when(slot == k)
            def _(k=k, first=first, band=band):
                main = jnp.where(first, got[k][:size, :], got[k][size : 2 * size, :])
                edge = jnp.where(
                    first,
                    got[k][base : base + 2 * z.CS, :],
                    got[k][base + 2 * z.CS : base + 4 * z.CS, :],
                )
                for y in range(z.Y):
                    out[band * z.Y + y, :size, :] = main
                    out[band * z.Y + y, size:, :] = edge


def ring_parts(z, anc, parent, buf):
    g, d = lax.axis_index("grp"), lax.axis_index("dev")
    row_base, col_base = g * z.TR, d * z.TC
    lane_t = iota((z.TR, LANES), 1)
    lane_f = iota((z.FR, LANES), 1)
    row_f = iota((z.FR, LANES), 0)
    lane_c = iota((z.C, LANES), 1)
    buf[...] = jnp.zeros_like(buf)

    def nest_ring(n, _):
        to = n // z.L
        l = n - to * z.L
        slot = to
        r, q = anc[n, 0], anc[n, 1]
        rows_meet = (r < row_base + z.TR) & (r + z.FR > row_base)
        cols_meet = (q < col_base + z.TC) & (q + z.FC > col_base)
        shift_r = lax.rem(row_base - r + 2 * z.G * z.TR, z.FR)
        shift_q = lax.rem(col_base - q + 2 * z.D * z.TC, z.FC)
        for side in range(2):
            col = (q - 1 if side == 0 else q + z.FC) - col_base
            first = (l * 2 + side) * z.C

            @pl.when(rows_meet & (col >= 0) & (col < z.TC))
            def _(col=col, first=first):
                acc = jnp.zeros((z.TR, LANES), F32)
                for c in range(z.C):
                    at = first + c
                    moved = pltpu.roll(parent[c], lax.rem(at - col + LANES, LANES), 1)
                    acc = jnp.where(lane_t == at, moved, acc)
                if z.FR > z.TR:
                    acc = jnp.concatenate([acc, jnp.zeros((z.FR - z.TR, LANES), F32)], axis=0)
                acc = pltpu.roll(acc, shift_r, 0)
                y = row_f + (r - row_base)
                good = (y >= 0) & (y < z.TR) & (lane_f >= first) & (lane_f < first + z.C)
                buf[slot, : z.FR, :] = jnp.where(good, acc, buf[slot, : z.FR, :])

            row = (r - 1 if side == 0 else r + z.FR) - row_base

            @pl.when(cols_meet & (row >= 0) & (row < z.TR))
            def _(row=row, first=first):
                rows = jnp.concatenate(
                    [parent[c, pl.ds(row, 1), :] for c in range(z.C)], axis=0
                )
                x = lane_c + (q - col_base)
                moved = jnp.where((x >= 0) & (x < z.TC), pltpu.roll(rows, shift_q, 1), 0.0)
                buf[slot, pl.ds(pl.multiple_of(z.FR + first, 8), z.C), :] = moved

        return 0

    lax.fori_loop(0, z.N, nest_ring, 0)
    for to in range(z.G):
        edge = jnp.where(to > g, z.TR - 1, 0)
        for c in range(z.C):
            buf[to, z.RING + c : z.RING + c + 1, :] = parent[c, pl.ds(edge, 1), :]


def ring_next(z, got, parent, phases, out, edges, up, dn, slab):
    g = lax.axis_index("grp")
    C, L, FR, M = z.C, z.L, z.FR, z.M
    total = got[0, : z.RING, :]
    for k in range(1, z.G):
        total = total + got[k, : z.RING, :]
    slab[...] = total
    sub = iota((8, LANES), 0)
    for to in range(z.D):
        out[to, :M, :] = slab[to * M : (to + 1) * M, :]
        hi = min(to * M + M, FR - 1)
        lo = max(to * M - 1, 0)
        hi, lo = slab[hi : hi + 1, :], slab[lo : lo + 1, :]
        out[to, M:16, :] = jnp.where(sub == 0, hi, jnp.where(sub == 7, lo, 0.0))
        for l in range(L):
            at = 16 + l * C
            if to == 0 or to == z.D - 1:
                k = FR + (l * 2 + (0 if to == 0 else 1)) * C
                out[to, at : at + C, :] = slab[k : k + C, :]
            else:
                out[to, at : at + C, :] = jnp.zeros((C, LANES), F32)
    before, after = jnp.maximum(g - 1, 0), jnp.minimum(g + 1, z.G - 1)
    edges[:C, :] = jnp.where(g > 0, got[before, z.RING :, :], 0.0)
    edges[C:, :] = jnp.where(g < z.G - 1, got[after, z.RING :, :], 0.0)
    rows = z.TR + 8
    lane = iota((rows, LANES), 1)
    first = jnp.zeros((rows, LANES), F32)
    last = first
    for c in range(C):
        lo = edges[c : c + 1, :]
        hi = edges[C + c : C + c + 1, :]
        cap = jnp.where(sub == 0, hi, jnp.where(sub == 7, lo, 0.0))
        full = jnp.concatenate([parent[c], cap], axis=0)
        first = jnp.where(lane == c, pltpu.roll(full, c, 1) if c else full, first)
        last = jnp.where(lane == c, pltpu.roll(full, c + 1, 1), last)
    up[z.EDGE :, :] = last
    dn[z.EDGE :, :] = first
    for x in range(3):
        for k in range(L * C):
            at = x * z.HALO + 3 * k
            up[at : at + 3, :] = phases[x, (k + 1) * z.H - 3 : (k + 1) * z.H, :]
            dn[at : at + 3, :] = phases[x, k * z.H : k * z.H + 3, :]


def nest_steps(z, diff, cour, phases, got, up, dn, out, back, ring):
    d = lax.axis_index("dev")
    C, M = z.C, z.M
    strip = Strip()
    total = got[0]
    for k in range(1, z.D):
        total = total + got[k]
    ring[...] = total
    side_main = [ring[:M, :], pltpu.roll(ring[:M, :], 4, 0)]
    side_cap = jnp.where(
        strip.any_high, ring[M : M + 1, :], jnp.where(strip.any_low, ring[15:16, :], 0.0)
    )
    hold_low, hold_high = strip.any_low & (d == 0), strip.any_high & (d == z.D - 1)
    nest_1 = strip.high[1] | strip.low[1]

    def channel(c, _):
        co = weights(diff, cour, c, 3.0)
        u = [
            [[phase_rows(z, phases, l, c, y, x) for x in range(3)] for y in range(3)]
            for l in range(2)
        ]
        cap = []
        for y in range(3):
            row = []
            for x in range(3):
                v = jnp.zeros((8, LANES), F32)
                for l in range(2):
                    at = x * z.HALO + (l * C + c) * 3 + y
                    v = jnp.where(strip.high[l], dn[pl.ds(at, 1), :], v)
                    v = jnp.where(strip.low[l], up[pl.ds(at, 1), :], v)
                row.append(v)
            cap.append(row)
        u.append(cap)
        end = jnp.where(nest_1, ring[pl.ds(16 + C + c, 1), :], ring[pl.ds(16 + c, 1), :])
        west, east = [], []
        for side, lane, ghosts in ((0, 0, west), (1, LANES - 1, east)):
            turn = [lax.rem(lane - ((l * 2 + side) * C + c) + LANES, LANES) for l in range(2)]
            for l in range(2):
                ghosts.append(pltpu.roll(side_main[l], turn[l], 1))
            caps = [pltpu.roll(side_cap, turn[l], 1) for l in range(2)]
            ghosts.append(jnp.where(nest_1, caps[1], caps[0]))

        def hold(u):
            cap = [
                [jnp.where(hold_high, end, v) for v in u[2][0]],
                u[2][1],
                [jnp.where(hold_low, end, v) for v in u[2][2]],
            ]
            return [u[0], u[1], cap]

        u = hold(u)
        for k in range(3):
            u = strip.step(u, co, west, east)
            if k < 2:
                u = hold(u)
        for l in range(2):
            for y in range(3):
                for x in range(3):
                    v = u[l][y][x]
                    v = v if l == 0 else pltpu.roll(v, 4, 0)
                    back[x, pl.ds((l * C + c) * z.H + y, M, 3), :] = v
        return 0

    lax.fori_loop(0, C, channel, 0, unroll=2)
    fine = iota((2 * z.W, z.W), 1)
    place = lax.rem(iota((2 * z.W, z.W), 0), z.W)
    at = lax.rem(place, LANES) * 3 + place // LANES
    undeal = jnp.where(fine == at, 1.0, 0.0).astype(BF16)
    done = split_dot(jnp.concatenate([back[0], back[1], back[2]], axis=1), undeal)
    out[...] = done.reshape(z.L, C, z.H, z.W)


def parent_step(z, anc, diff, cour, parent, edges, up_in, dn_in, out):
    g, d = lax.axis_index("grp"), lax.axis_index("dev")
    C = z.C
    rows = z.TR + 8
    n = nest_at(z, anc, g // z.S * z.NB + d // z.Y)
    i = iota((z.TR, LANES), 0) + (g * z.TR - anc[n, 0])
    j = iota((z.TR, LANES), 1) + (d * z.TC - anc[n, 1])
    inside = (i >= 0) & (i < z.FR) & (j >= 0) & (j < z.FC)
    one = lambda cond: jnp.where(cond, 1.0, 0.0).astype(F32)
    on_w, on_e = one(inside & (j == 0)), one(inside & (j == z.FC - 1))
    on_s, on_n = one(inside & (i == 0)), one(inside & (i == z.FR - 1))
    i_end, j_end = one((i == 0) | (i == z.FR - 1)), one((j == 0) | (j == z.FC - 1))
    i_lo, i_hi = one(i > 0), one(i < z.FR - 1)
    j_lo, j_hi = one(j > 0), one(j < z.FC - 1)
    lane = iota((rows, LANES), 1)
    sub = iota((8, LANES), 0)

    col_w, col_e = up_in[z.EDGE :, :], dn_in[z.EDGE :, :]

    def channel(c, _):
        co = [v[:1] for v in weights(diff, cour, c, 1.0)]
        fm, fe, fw, fn, fs = [v[:1] for v in weights(diff, cour, c, 3.0)]
        lo = edges[pl.ds(c, 1), :]
        hi = edges[pl.ds(C + c, 1), :]
        cap = jnp.where(sub == 0, hi, jnp.where(sub == 7, lo, 0.0))
        full = jnp.concatenate([parent[c], cap], axis=0)
        w_in = pltpu.roll(col_w, lax.rem(LANES - c, LANES), 1)
        e_in = pltpu.roll(col_e, LANES - 1 - c, 1)
        w_all = jnp.where(lane == 0, w_in, pltpu.roll(full, 1, 1))
        e_all = jnp.where(lane == LANES - 1, e_in, pltpu.roll(full, LANES - 1, 1))
        up = lambda x: pltpu.roll(x, rows - 1, 0)[: z.TR]
        down = lambda x: pltpu.roll(x, 1, 0)[: z.TR]
        mid = full[: z.TR]
        w, e, n, s = w_all[: z.TR], e_all[: z.TR], up(full), down(full)
        w_up, w_down, e_up, e_down = up(w_all), down(w_all), up(e_all), down(e_all)
        step = (
            co[MID] * mid
            + (co[EAST] * e + co[WEST] * w)
            + (co[NORTH] * n + co[SOUTH] * s)
        )
        a, b, k, x = ghost_share(fw, fe, fm, fs, fn)
        share = on_w * ((a - x * i_end) * w + (b * i_lo) * w_down + (k * i_hi) * w_up)
        a, b, k, x = ghost_share(fe, fw, fm, fs, fn)
        share += on_e * ((a - x * i_end) * e + (b * i_lo) * e_down + (k * i_hi) * e_up)
        a, b, k, x = ghost_share(fs, fn, fm, fw, fe)
        share += on_s * ((a - x * j_end) * s + (b * j_lo) * w_down + (k * j_hi) * e_down)
        a, b, k, x = ghost_share(fn, fs, fm, fw, fe)
        share += on_n * ((a - x * j_end) * n + (b * j_lo) * w_up + (k * j_hi) * e_up)
        out[c] = jnp.where(inside, share, step)
        return 0

    lax.fori_loop(0, C, channel, 0, unroll=2)


def merge(z, which, anc, base, *refs):
    pieces, out, twice = refs[:-2], refs[-2], refs[-1]
    g, d = lax.axis_index("grp"), lax.axis_index("dev")
    n = nest_at(z, anc, g // z.S * z.NB + d // z.Y)
    r, q = anc[n, 0], anc[n, 1]
    start = lax.rem(g * z.TR - r + 2 * z.G * z.TR, z.FR)
    shift_q = lax.rem(q - d * z.TC + 2 * z.D * z.TC, z.FC)
    i = iota((z.TR, LANES), 0) + (g * z.TR - r)
    j = iota((z.TR, LANES), 1) + (d * z.TC - q)
    inside = (i >= 0) & (i < z.FR) & (j >= 0) & (j < z.FC)
    sub = iota((z.M, LANES), 0)
    part = lax.rem(g, z.S)
    size = z.CS * z.M
    for k in range(z.S):
        if k not in which:
            other = lax.rem(part - k + z.S, z.S) * z.CS
            out[pl.ds(other, z.CS)] = base[pl.ds(other, z.CS)]
    for piece, k in zip(pieces, which):
        first = lax.rem(part - k + z.S, z.S) * z.CS
        for c in range(z.CS):
            for m in range(z.D):
                x = piece[m, c * z.M : (c + 1) * z.M, :]
                if m + 1 < z.D:
                    row = piece[m + 1, size + c : size + c + 1, :]
                    x += jnp.where(sub == z.M - 1, row, 0.0)
                if m > 0:
                    row = piece[m - 1, size + z.CS + c : size + z.CS + c + 1, :]
                    x += jnp.where(sub == 0, row, 0.0)
                twice[c % 4, m * z.M : (m + 1) * z.M, :] = x
                if m * z.M < z.TR:
                    twice[c % 4, z.FR + m * z.M : z.FR + (m + 1) * z.M, :] = x
            x = pltpu.roll(twice[c % 4, pl.ds(start, z.TR), :], shift_q, 1)
            out[first + c] = base[first + c] + jnp.where(inside, x, 0.0)


def shards(parent, nest, anchor, diff, cour):
    z = Sizes(parent, nest, anchor, lax.axis_size("grp"), lax.axis_size("dev"))
    sds = lambda *shape: jax.ShapeDtypeStruct(shape, F32)
    vmem = lambda *shape: pltpu.VMEM(shape, F32)
    to_grp = lambda x, k: lax.ppermute(x, "grp", [(a, a ^ k) for a in range(z.G)])

    (ring,) = call(
        functools.partial(ring_parts, z), [sds(z.G, z.RG, LANES)], (anchor,), (parent,)
    )
    nest, ring = lax.optimization_barrier((nest, ring))
    ring = lax.all_to_all(ring, "grp", 0, 0, tiled=True)
    *chunks, phases = call(
        functools.partial(partial_averages, z),
        [sds(z.R1, LANES)] * z.S + [sds(3, z.L * z.C * z.H, LANES)],
        (diff, cour),
        (),
        [pltpu.VMEM(nest.shape, F32), pltpu.SemaphoreType.DMA((z.L,))],
        (nest,),
    )
    got = [chunks[0]] + [to_grp(chunks[k % z.S], k) for k in range(1, z.G)]

    message = sds(z.EDGE + z.TR + 8, LANES)
    ring, edges, up, dn = call(
        functools.partial(ring_next, z),
        [sds(z.D, z.RG2, LANES), sds(2 * z.C, LANES), message, message],
        (),
        (ring, parent, phases),
        [vmem(z.RING, LANES)],
    )
    forward = [(k, k + 1) for k in range(z.D - 1)]
    up = lax.ppermute(up, "dev", forward)
    dn = lax.ppermute(dn, "dev", [(b, a) for a, b in forward])
    ring = lax.all_to_all(ring, "dev", 0, 0, tiled=True)
    got, ring, up, dn = lax.optimization_barrier((got, ring, up, dn))

    (avg,) = call(functools.partial(pick_band, z), [sds(z.D, z.R2, LANES)], (anchor,), got)
    avg = lax.all_to_all(avg, "dev", 0, 0, tiled=True)
    pieces = [avg]
    for k in range(1, z.S):
        pairs = [(a, a // z.S * z.S + (a + k) % z.S) for a in range(z.G)]
        pieces.append(lax.ppermute(avg, "grp", pairs))
    (nest_out,) = call(
        functools.partial(nest_steps, z),
        [jax.ShapeDtypeStruct(nest.shape, F32)],
        (diff, cour),
        (phases, ring, up, dn),
        [vmem(3, z.L * z.C * z.H, LANES), vmem(z.RG2, LANES)],
    )
    (out,) = call(
        functools.partial(parent_step, z),
        [jax.ShapeDtypeStruct(parent.shape, F32)],
        (anchor, diff, cour),
        (parent, edges, up, dn),
    )
    for which in ([0], list(range(1, z.S))):
        (out,) = call(
            functools.partial(merge, z, which),
            [jax.ShapeDtypeStruct(parent.shape, F32)],
            (anchor,),
            (out, *[pieces[k] for k in which]),
            [vmem(4, z.FR + z.TR, LANES)],
        )
    return out, nest_out


def solution(mesh):
    placed = (P(None, "grp", "dev"), P("grp", None, "dev", None), P(), P(), P())
    return jax.shard_map(
        shards,
        mesh=mesh,
        in_specs=placed,
        out_specs=(P(None, "grp", "dev"), P("grp", None, "dev", None)),
        check_vma=False,
    )
```

```python
import functools

import jax
import jax.numpy as jnp
from jax import lax
from jax.experimental import pallas as pl
from jax.experimental.pallas import tpu as pltpu
from jax.sharding import PartitionSpec as P

F32 = jnp.float32
BF16 = jnp.bfloat16
LANES = 128
VMEM_LIMIT = 48 * 1024 * 1024
MID, EAST, WEST, NORTH, SOUTH = range(5)


class Sizes:
    def __init__(self, parent, nest, anchor, grp_count, dev_count):
        self.C, self.TR, self.TC = parent.shape
        self.L, _, self.H, self.W = nest.shape
        self.N = anchor.shape[0]
        self.G, self.D = grp_count, dev_count
        self.M = self.H // 3
        self.FR, self.FC = self.M * self.D, self.W // 3
        self.S = self.G // 2
        self.NB = self.N // 2
        self.Y = self.D // self.NB
        self.CS = self.C // self.S
        self.BR, self.BC = self.S * self.TR, self.Y * self.TC
        self.R1 = self.L * self.CS * (self.M + 2)
        self.R2 = self.CS * (self.M + 2)
        self.RING = self.FR + self.L * 2 * self.C
        self.RG = self.RING + self.C
        self.RG2 = 16 + self.L * self.C
        self.HALO = self.L * self.C * 3
        self.EDGE = 3 * self.HALO
        assert self.H == 24 and self.FC == LANES and self.TC == LANES
        assert self.FR >= self.TR and self.L == 2


def call(body, out_shape, smem, args, scratch=(), raw=()):
    moved = [*smem, *args]
    n_in, n_raw, n_out = len(moved), len(raw), len(out_shape)
    place = pl.BlockSpec(memory_space=pltpu.HBM)

    def kernel(*refs):
        source, refs = refs[:n_in], refs[n_in:]
        stay, refs = refs[:n_raw], refs[n_raw:]
        target, refs = refs[:n_out], refs[n_out:]
        inner, refs = refs[:n_in], refs[n_in:]
        result, refs = refs[:n_out], refs[n_out:]
        extra, sem = refs[:-1], refs[-1]
        fetch = [pltpu.make_async_copy(a, b, sem.at[k]) for k, (a, b) in enumerate(zip(source, inner))]
        for copy in fetch:
            copy.start()
        for copy in fetch:
            copy.wait()
        body(*inner, *stay, *result, *extra)
        store = [
            pltpu.make_async_copy(a, b, sem.at[n_in + k]) for k, (a, b) in enumerate(zip(result, target))
        ]
        for copy in store:
            copy.start()
        for copy in store:
            copy.wait()

    return pl.pallas_call(
        kernel,
        out_shape=list(out_shape),
        in_specs=[place] * (n_in + n_raw),
        out_specs=[place] * n_out,
        scratch_shapes=[
            *[pltpu.SMEM(x.shape, x.dtype) for x in smem],
            *[pltpu.VMEM(x.shape, x.dtype) for x in args],
            *[pltpu.VMEM(x.shape, x.dtype) for x in out_shape],
            *scratch,
            pltpu.SemaphoreType.DMA((n_in + n_out,)),
        ],
        compiler_params=pltpu.CompilerParams(vmem_limit_bytes=VMEM_LIMIT),
    )(*moved, *raw)


def iota(shape, dim):
    return lax.broadcasted_iota(jnp.int32, shape, dim)


def split_dot(x, table):
    high = x.astype(BF16)
    low = (x - high.astype(F32)).astype(BF16)
    return jnp.dot(jnp.concatenate([high, low], axis=1), table, preferred_element_type=F32)


def nest_at(z, anc, band):
    found = 0
    for n in range(z.N):
        found += jnp.where(anc[0, n] // z.BR * z.NB + anc[1, n] // z.BC == band, n, 0)
    return found


def weights(diff, cour, c, times):
    splat = lambda ref, k: jnp.full((8, LANES), ref[k, c], F32)
    east = times * splat(diff, 0)
    north = times * splat(diff, 1)
    west = east + splat(cour, 0)
    south = north + splat(cour, 1)
    return 1.0 - (east + west) - (north + south), east, west, north, south


def ghost_share(inject, back, mid, plus, minus):
    stay = mid + inject
    m0 = inject * (1.0 + stay + mid * stay + inject * (stay + back) + 2.0 * plus * minus)
    p1 = inject * plus * (1.0 + 2.0 * stay)
    p2 = inject * plus * plus
    n1 = inject * minus * (1.0 + 2.0 * stay)
    n2 = inject * minus * minus
    ninth = 1.0 / 9.0
    same = (3.0 * m0 + 2.0 * p1 + p2 + 2.0 * n1 + n2) * ninth
    return same, (p1 + 2.0 * p2) * ninth, (n1 + 2.0 * n2) * ninth, inject * plus * minus * ninth


class Strip:
    def __init__(self):
        sub = iota((8, LANES), 0)
        lane = iota((8, LANES), 1)
        self.high = [sub == 0, sub == 4]
        self.low = [sub == 7, sub == 3]
        self.any_high = (sub == 0) | (sub == 4)
        self.any_low = (sub == 7) | (sub == 3)
        self.first, self.last = lane == 0, lane == LANES - 1

    def east(self, x, ghost):
        return jnp.where(self.last, ghost, pltpu.roll(x, LANES - 1, 1))

    def west(self, x, ghost):
        return jnp.where(self.first, ghost, pltpu.roll(x, 1, 1))

    def north(self, mains, cap):
        up = [pltpu.roll(m, 7, 0) for m in mains]
        cap_up = pltpu.roll(cap, 7, 0)
        new = [jnp.where(self.low[l], cap_up, up[l]) for l in range(2)]
        return new, jnp.where(self.low[0], up[0], jnp.where(self.low[1], up[1], 0.0))

    def south(self, mains, cap):
        down = [pltpu.roll(m, 1, 0) for m in mains]
        cap_down = pltpu.roll(cap, 1, 0)
        new = [jnp.where(self.high[l], cap_down, down[l]) for l in range(2)]
        return new, jnp.where(self.high[0], down[0], jnp.where(self.high[1], down[1], 0.0))

    def step(self, u, co, west_ghost, east_ghost):
        n_in = [self.north([u[0][0][x], u[1][0][x]], u[2][0][x]) for x in range(3)]
        s_in = [self.south([u[0][2][x], u[1][2][x]], u[2][2][x]) for x in range(3)]
        pick = lambda pair, k: pair[1] if k == 2 else pair[0][k]
        new = []
        for k in range(3):
            rows = []
            for y in range(3):
                row = u[k][y]
                e = [row[1], row[2], self.east(row[0], east_ghost[k])]
                w = [self.west(row[2], west_ghost[k]), row[0], row[1]]
                cells = []
                for x in range(3):
                    n = u[k][y + 1][x] if y < 2 else pick(n_in[x], k)
                    s = u[k][y - 1][x] if y > 0 else pick(s_in[x], k)
                    cells.append(
                        co[MID] * row[x]
                        + (co[EAST] * e[x] + co[WEST] * w[x])
                        + (co[NORTH] * n + co[SOUTH] * s)
                    )
                rows.append(cells)
            new.append(rows)
        return new

    def pooled_step(self, u, co):
        ends = []
        for k in range(3):
            row = [u[k][y][0] + u[k][y][1] + u[k][y][2] for y in range(3)]
            col = [u[k][0][x] + u[k][1][x] + u[k][2][x] for x in (0, 2)]
            ends.append((row[0], row[2], col[0], col[1], row[0] + row[1] + row[2]))
        n_in = self.north([ends[0][0], ends[1][0]], ends[2][0])
        s_in = self.south([ends[0][1], ends[1][1]], ends[2][1])
        pick = lambda pair, k: pair[1] if k == 2 else pair[0][k]
        out = []
        for k in range(3):
            row0, row2, col0, col2, total = ends[k]
            flux_x = co[EAST] * (self.east(col0, 0.0) - col0)
            flux_x += co[WEST] * (self.west(col2, 0.0) - col2)
            flux_y = co[NORTH] * (pick(n_in, k) - row0) + co[SOUTH] * (pick(s_in, k) - row2)
            out.append(total + (flux_x + flux_y))
        return out


def phase_rows(z, ref, l, c, y, x):
    got = ref[x, pl.ds((l * z.C + c) * z.H + y, z.M, 3), :]
    return got if l == 0 else pltpu.roll(got, 4, 0)


def partial_averages(z, diff, cour, nest, *refs):
    out, phases, strips, sem = refs[: z.S], refs[z.S], refs[z.S + 1], refs[z.S + 2]
    fetch = [pltpu.make_async_copy(nest.at[l], strips.at[l], sem.at[l]) for l in range(z.L)]
    for copy in fetch:
        copy.start()
    d = lax.axis_index("dev")
    own = lax.rem(lax.axis_index("grp"), z.S)
    C, M, CS = z.C, z.M, z.CS
    fine = lax.rem(iota((2 * z.W, z.W), 0), z.W)
    place = iota((2 * z.W, z.W), 1)
    at = lax.rem(place, LANES) * 3 + place // LANES
    deal = jnp.where(fine == at, 1.0, 0.0).astype(BF16)
    rows = C * z.H
    for l in range(z.L):
        fetch[l].wait()
        dealt = split_dot(strips[l].reshape(rows, z.W), deal)
        for x in range(3):
            phases[x, l * rows : (l + 1) * rows, :] = dealt[:, x * LANES : (x + 1) * LANES]
    strip = Strip()
    keep_high = strip.any_low | (strip.any_high & (d < z.D - 1))
    keep_low = strip.any_high | (strip.any_low & (d > 0))
    zero = jnp.zeros((8, LANES), F32)
    ghosts = [0.0] * 3
    base = z.L * CS * M

    def hold(u):
        cap = [
            [jnp.where(keep_high, v, 0.0) for v in u[2][0]],
            u[2][1],
            [jnp.where(keep_low, v, 0.0) for v in u[2][2]],
        ]
        return [u[0], u[1], cap]

    for part in range(z.S):

        def channel(i, _, to=out[part], first=jnp.bitwise_xor(own, part) * CS):
            c = first + i
            co = weights(diff, cour, c, 3.0)
            u = [
                [[phase_rows(z, phases, l, c, y, x) for x in range(3)] for y in range(3)]
                for l in range(2)
            ]
            u.append([[zero] * 3] * 3)
            for _step in range(2):
                u = hold(strip.step(u, co, ghosts, ghosts))
            got = [v * (1.0 / 9.0) for v in strip.pooled_step(u, co)]
            got[1] = pltpu.roll(got[1], 4, 0)
            for l in range(2):
                row = pl.multiple_of((l * CS + i) * M, M)
                to[pl.ds(row, M), :] = got[l]
                for side, sub in enumerate(((7, 3), (0, 4))):
                    row = base + (l * 2 + side) * CS + i
                    to[pl.ds(row, 1), :] = got[2][sub[l] : sub[l] + 1]
            return 0

        lax.fori_loop(0, CS, channel, 0, unroll=2)


def pick_band(z, anc, *refs):
    got, out = refs[: z.G], refs[z.G]
    g = lax.axis_index("grp")
    top = g // z.S * z.NB
    base, size = z.L * z.CS * z.M, z.CS * z.M
    for band in range(z.NB):
        n = nest_at(z, anc, top + band)
        of = n // z.L
        slot = jnp.bitwise_xor(of, g)
        first = n - of * z.L == 0
        for k in range(z.G):

            @pl.when(slot == k)
            def _(k=k, first=first, band=band):
                main = jnp.where(first, got[k][:size, :], got[k][size : 2 * size, :])
                edge = jnp.where(
                    first,
                    got[k][base : base + 2 * z.CS, :],
                    got[k][base + 2 * z.CS : base + 4 * z.CS, :],
                )
                for y in range(z.Y):
                    out[band * z.Y + y, :size, :] = main
                    out[band * z.Y + y, size:, :] = edge


def ring_parts(z, anc, parent, buf):
    g, d = lax.axis_index("grp"), lax.axis_index("dev")
    row_base, col_base = g * z.TR, d * z.TC
    lane_t = iota((z.TR, LANES), 1)
    lane_f = iota((z.FR, LANES), 1)
    row_f = iota((z.FR, LANES), 0)
    lane_c = iota((z.C, LANES), 1)
    buf[...] = jnp.zeros_like(buf)

    def nest_ring(n, _):
        to = n // z.L
        l = n - to * z.L
        slot = to
        r, q = anc[0, n], anc[1, n]
        rows_meet = (r < row_base + z.TR) & (r + z.FR > row_base)
        cols_meet = (q < col_base + z.TC) & (q + z.FC > col_base)
        shift_r = lax.rem(row_base - r + 2 * z.G * z.TR, z.FR)
        shift_q = lax.rem(col_base - q + 2 * z.D * z.TC, z.FC)
        for side in range(2):
            col = (q - 1 if side == 0 else q + z.FC) - col_base
            first = (l * 2 + side) * z.C

            @pl.when(rows_meet & (col >= 0) & (col < z.TC))
            def _(col=col, first=first):
                acc = jnp.zeros((z.TR, LANES), F32)
                for c in range(z.C):
                    at = first + c
                    moved = pltpu.roll(parent[c], lax.rem(at - col + LANES, LANES), 1)
                    acc = jnp.where(lane_t == at, moved, acc)
                if z.FR > z.TR:
                    acc = jnp.concatenate([acc, jnp.zeros((z.FR - z.TR, LANES), F32)], axis=0)
                acc = pltpu.roll(acc, shift_r, 0)
                y = row_f + (r - row_base)
                good = (y >= 0) & (y < z.TR) & (lane_f >= first) & (lane_f < first + z.C)
                buf[slot, : z.FR, :] = jnp.where(good, acc, buf[slot, : z.FR, :])

            row = (r - 1 if side == 0 else r + z.FR) - row_base

            @pl.when(cols_meet & (row >= 0) & (row < z.TR))
            def _(row=row, first=first):
                rows = jnp.concatenate(
                    [parent[c, pl.ds(row, 1), :] for c in range(z.C)], axis=0
                )
                x = lane_c + (q - col_base)
                moved = jnp.where((x >= 0) & (x < z.TC), pltpu.roll(rows, shift_q, 1), 0.0)
                buf[slot, pl.ds(pl.multiple_of(z.FR + first, 8), z.C), :] = moved

        return 0

    lax.fori_loop(0, z.N, nest_ring, 0)
    for to in range(z.G):
        edge = jnp.where(to > g, z.TR - 1, 0)
        for c in range(z.C):
            buf[to, z.RING + c : z.RING + c + 1, :] = parent[c, pl.ds(edge, 1), :]


def ring_next(z, got, parent, phases, out, edges, up, dn, slab):
    g = lax.axis_index("grp")
    C, L, FR, M = z.C, z.L, z.FR, z.M
    total = got[0, : z.RING, :]
    for k in range(1, z.G):
        total = total + got[k, : z.RING, :]
    slab[...] = total
    sub = iota((8, LANES), 0)
    for to in range(z.D):
        out[to, :M, :] = slab[to * M : (to + 1) * M, :]
        hi = min(to * M + M, FR - 1)
        lo = max(to * M - 1, 0)
        hi, lo = slab[hi : hi + 1, :], slab[lo : lo + 1, :]
        out[to, M:16, :] = jnp.where(sub == 0, hi, jnp.where(sub == 7, lo, 0.0))
        for l in range(L):
            at = 16 + l * C
            if to == 0 or to == z.D - 1:
                k = FR + (l * 2 + (0 if to == 0 else 1)) * C
                out[to, at : at + C, :] = slab[k : k + C, :]
            else:
                out[to, at : at + C, :] = jnp.zeros((C, LANES), F32)
    before, after = jnp.maximum(g - 1, 0), jnp.minimum(g + 1, z.G - 1)
    edges[:C, :] = jnp.where(g > 0, got[before, z.RING :, :], 0.0)
    edges[C:, :] = jnp.where(g < z.G - 1, got[after, z.RING :, :], 0.0)
    rows = z.TR + 8
    lane = iota((rows, LANES), 1)
    first = jnp.zeros((rows, LANES), F32)
    last = first
    for c in range(C):
        lo = edges[c : c + 1, :]
        hi = edges[C + c : C + c + 1, :]
        cap = jnp.where(sub == 0, hi, jnp.where(sub == 7, lo, 0.0))
        full = jnp.concatenate([parent[c], cap], axis=0)
        first = jnp.where(lane == c, pltpu.roll(full, c, 1) if c else full, first)
        last = jnp.where(lane == c, pltpu.roll(full, c + 1, 1), last)
    up[z.EDGE :, :] = last
    dn[z.EDGE :, :] = first
    for x in range(3):
        for k in range(L * C):
            at = x * z.HALO + 3 * k
            up[at : at + 3, :] = phases[x, (k + 1) * z.H - 3 : (k + 1) * z.H, :]
            dn[at : at + 3, :] = phases[x, k * z.H : k * z.H + 3, :]


def nest_steps(z, diff, cour, phases, got, up, dn, out, back, ring):
    d = lax.axis_index("dev")
    C, M = z.C, z.M
    strip = Strip()
    total = got[0]
    for k in range(1, z.D):
        total = total + got[k]
    ring[...] = total
    side_main = [ring[:M, :], pltpu.roll(ring[:M, :], 4, 0)]
    side_cap = jnp.where(
        strip.any_high, ring[M : M + 1, :], jnp.where(strip.any_low, ring[15:16, :], 0.0)
    )
    hold_low, hold_high = strip.any_low & (d == 0), strip.any_high & (d == z.D - 1)
    nest_1 = strip.high[1] | strip.low[1]

    def channel(c, _):
        co = weights(diff, cour, c, 3.0)
        u = [
            [[phase_rows(z, phases, l, c, y, x) for x in range(3)] for y in range(3)]
            for l in range(2)
        ]
        cap = []
        for y in range(3):
            row = []
            for x in range(3):
                v = jnp.zeros((8, LANES), F32)
                for l in range(2):
                    at = x * z.HALO + (l * C + c) * 3 + y
                    v = jnp.where(strip.high[l], dn[pl.ds(at, 1), :], v)
                    v = jnp.where(strip.low[l], up[pl.ds(at, 1), :], v)
                row.append(v)
            cap.append(row)
        u.append(cap)
        end = jnp.where(nest_1, ring[pl.ds(16 + C + c, 1), :], ring[pl.ds(16 + c, 1), :])
        west, east = [], []
        for side, lane, ghosts in ((0, 0, west), (1, LANES - 1, east)):
            turn = [lax.rem(lane - ((l * 2 + side) * C + c) + LANES, LANES) for l in range(2)]
            for l in range(2):
                ghosts.append(pltpu.roll(side_main[l], turn[l], 1))
            caps = [pltpu.roll(side_cap, turn[l], 1) for l in range(2)]
            ghosts.append(jnp.where(nest_1, caps[1], caps[0]))

        def hold(u):
            cap = [
                [jnp.where(hold_high, end, v) for v in u[2][0]],
                u[2][1],
                [jnp.where(hold_low, end, v) for v in u[2][2]],
            ]
            return [u[0], u[1], cap]

        u = hold(u)
        for k in range(3):
            u = strip.step(u, co, west, east)
            if k < 2:
                u = hold(u)
        for l in range(2):
            for y in range(3):
                for x in range(3):
                    v = u[l][y][x]
                    v = v if l == 0 else pltpu.roll(v, 4, 0)
                    back[x, pl.ds((l * C + c) * z.H + y, M, 3), :] = v
        return 0

    lax.fori_loop(0, C, channel, 0, unroll=2)
    fine = iota((2 * z.W, z.W), 1)
    place = lax.rem(iota((2 * z.W, z.W), 0), z.W)
    at = lax.rem(place, LANES) * 3 + place // LANES
    undeal = jnp.where(fine == at, 1.0, 0.0).astype(BF16)
    done = split_dot(jnp.concatenate([back[0], back[1], back[2]], axis=1), undeal)
    out[...] = done.reshape(z.L, C, z.H, z.W)


def parent_step(z, anc, diff, cour, parent, edges, up_in, dn_in, out):
    g, d = lax.axis_index("grp"), lax.axis_index("dev")
    C = z.C
    rows = z.TR + 8
    n = nest_at(z, anc, g // z.S * z.NB + d // z.Y)
    i = iota((z.TR, LANES), 0) + (g * z.TR - anc[0, n])
    j = iota((z.TR, LANES), 1) + (d * z.TC - anc[1, n])
    inside = (i >= 0) & (i < z.FR) & (j >= 0) & (j < z.FC)
    one = lambda cond: jnp.where(cond, 1.0, 0.0).astype(F32)
    on_w, on_e = one(inside & (j == 0)), one(inside & (j == z.FC - 1))
    on_s, on_n = one(inside & (i == 0)), one(inside & (i == z.FR - 1))
    i_end, j_end = one((i == 0) | (i == z.FR - 1)), one((j == 0) | (j == z.FC - 1))
    i_lo, i_hi = one(i > 0), one(i < z.FR - 1)
    j_lo, j_hi = one(j > 0), one(j < z.FC - 1)
    lane = iota((rows, LANES), 1)
    sub = iota((8, LANES), 0)

    col_w, col_e = up_in[z.EDGE :, :], dn_in[z.EDGE :, :]

    def channel(c, _):
        co = [v[:1] for v in weights(diff, cour, c, 1.0)]
        fm, fe, fw, fn, fs = [v[:1] for v in weights(diff, cour, c, 3.0)]
        lo = edges[pl.ds(c, 1), :]
        hi = edges[pl.ds(C + c, 1), :]
        cap = jnp.where(sub == 0, hi, jnp.where(sub == 7, lo, 0.0))
        full = jnp.concatenate([parent[c], cap], axis=0)
        w_in = pltpu.roll(col_w, lax.rem(LANES - c, LANES), 1)
        e_in = pltpu.roll(col_e, LANES - 1 - c, 1)
        w_all = jnp.where(lane == 0, w_in, pltpu.roll(full, 1, 1))
        e_all = jnp.where(lane == LANES - 1, e_in, pltpu.roll(full, LANES - 1, 1))
        up = lambda x: pltpu.roll(x, rows - 1, 0)[: z.TR]
        down = lambda x: pltpu.roll(x, 1, 0)[: z.TR]
        mid = full[: z.TR]
        w, e, n, s = w_all[: z.TR], e_all[: z.TR], up(full), down(full)
        w_up, w_down, e_up, e_down = up(w_all), down(w_all), up(e_all), down(e_all)
        step = (
            co[MID] * mid
            + (co[EAST] * e + co[WEST] * w)
            + (co[NORTH] * n + co[SOUTH] * s)
        )
        a, b, k, x = ghost_share(fw, fe, fm, fs, fn)
        share = on_w * ((a - x * i_end) * w + (b * i_lo) * w_down + (k * i_hi) * w_up)
        a, b, k, x = ghost_share(fe, fw, fm, fs, fn)
        share += on_e * ((a - x * i_end) * e + (b * i_lo) * e_down + (k * i_hi) * e_up)
        a, b, k, x = ghost_share(fs, fn, fm, fw, fe)
        share += on_s * ((a - x * j_end) * s + (b * j_lo) * w_down + (k * j_hi) * e_down)
        a, b, k, x = ghost_share(fn, fs, fm, fw, fe)
        share += on_n * ((a - x * j_end) * n + (b * j_lo) * w_up + (k * j_hi) * e_up)
        out[c] = jnp.where(inside, share, step)
        return 0

    lax.fori_loop(0, C, channel, 0, unroll=2)


def merge(z, which, anc, base, *refs):
    pieces, out, twice = refs[:-2], refs[-2], refs[-1]
    g, d = lax.axis_index("grp"), lax.axis_index("dev")
    n = nest_at(z, anc, g // z.S * z.NB + d // z.Y)
    r, q = anc[0, n], anc[1, n]
    start = lax.rem(g * z.TR - r + 2 * z.G * z.TR, z.FR)
    shift_q = lax.rem(q - d * z.TC + 2 * z.D * z.TC, z.FC)
    i = iota((z.TR, LANES), 0) + (g * z.TR - r)
    j = iota((z.TR, LANES), 1) + (d * z.TC - q)
    inside = (i >= 0) & (i < z.FR) & (j >= 0) & (j < z.FC)
    sub = iota((z.M, LANES), 0)
    part = lax.rem(g, z.S)
    size = z.CS * z.M
    for k in range(z.S):
        if k not in which:
            other = lax.rem(part - k + z.S, z.S) * z.CS
            out[pl.ds(other, z.CS)] = base[pl.ds(other, z.CS)]
    for piece, k in zip(pieces, which):
        first = lax.rem(part - k + z.S, z.S) * z.CS
        for c in range(z.CS):
            for m in range(z.D):
                x = piece[m, c * z.M : (c + 1) * z.M, :]
                if m + 1 < z.D:
                    row = piece[m + 1, size + c : size + c + 1, :]
                    x += jnp.where(sub == z.M - 1, row, 0.0)
                if m > 0:
                    row = piece[m - 1, size + z.CS + c : size + z.CS + c + 1, :]
                    x += jnp.where(sub == 0, row, 0.0)
                twice[c % 4, m * z.M : (m + 1) * z.M, :] = x
                if m * z.M < z.TR:
                    twice[c % 4, z.FR + m * z.M : z.FR + (m + 1) * z.M, :] = x
            x = pltpu.roll(twice[c % 4, pl.ds(start, z.TR), :], shift_q, 1)
            out[first + c] = base[first + c] + jnp.where(inside, x, 0.0)


def shards(parent, nest, anchor, diff, cour):
    z = Sizes(parent, nest, anchor, lax.axis_size("grp"), lax.axis_size("dev"))
    sds = lambda *shape: jax.ShapeDtypeStruct(shape, F32)
    vmem = lambda *shape: pltpu.VMEM(shape, F32)
    to_grp = lambda x, k: lax.ppermute(x, "grp", [(a, a ^ k) for a in range(z.G)])

    anchor = anchor.T
    (ring,) = call(
        functools.partial(ring_parts, z), [sds(z.G, z.RG, LANES)], (anchor,), (parent,)
    )
    nest, ring = lax.optimization_barrier((nest, ring))
    ring = lax.all_to_all(ring, "grp", 0, 0, tiled=True)
    *chunks, phases = call(
        functools.partial(partial_averages, z),
        [sds(z.R1, LANES)] * z.S + [sds(3, z.L * z.C * z.H, LANES)],
        (diff, cour),
        (),
        [pltpu.VMEM(nest.shape, F32), pltpu.SemaphoreType.DMA((z.L,))],
        (nest,),
    )
    got = [chunks[0]] + [to_grp(chunks[k % z.S], k) for k in range(1, z.G)]

    message = sds(z.EDGE + z.TR + 8, LANES)
    ring, edges, up, dn = call(
        functools.partial(ring_next, z),
        [sds(z.D, z.RG2, LANES), sds(2 * z.C, LANES), message, message],
        (),
        (ring, parent, phases),
        [vmem(z.RING, LANES)],
    )
    forward = [(k, k + 1) for k in range(z.D - 1)]
    ring = lax.all_to_all(ring, "dev", 0, 0, tiled=True)
    got, up, dn = lax.optimization_barrier((got, up, dn))
    up = lax.ppermute(up, "dev", forward)
    dn = lax.ppermute(dn, "dev", [(b, a) for a, b in forward])
    got, ring, up, dn = lax.optimization_barrier((got, ring, up, dn))

    (avg,) = call(functools.partial(pick_band, z), [sds(z.D, z.R2, LANES)], (anchor,), got)
    avg = lax.all_to_all(avg, "dev", 0, 0, tiled=True)
    (nest_out,) = call(
        functools.partial(nest_steps, z),
        [jax.ShapeDtypeStruct(nest.shape, F32)],
        (diff, cour),
        (phases, ring, up, dn),
        [vmem(3, z.L * z.C * z.H, LANES), vmem(z.RG2, LANES)],
    )
    (out,) = call(
        functools.partial(parent_step, z),
        [jax.ShapeDtypeStruct(parent.shape, F32)],
        (anchor, diff, cour),
        (parent, edges, up, dn),
    )
    avg, nest_out, out = lax.optimization_barrier((avg, nest_out, out))
    pieces = [avg]
    for k in range(1, z.S):
        pairs = [(a, a // z.S * z.S + (a + k) % z.S) for a in range(z.G)]
        pieces.append(lax.ppermute(avg, "grp", pairs))
    for which in ([0], list(range(1, z.S))):
        (out,) = call(
            functools.partial(merge, z, which),
            [jax.ShapeDtypeStruct(parent.shape, F32)],
            (anchor,),
            (out, *[pieces[k] for k in which]),
            [vmem(4, z.FR + z.TR, LANES)],
        )
    return out, nest_out


def solution(mesh):
    placed = (P(None, "grp", "dev"), P("grp", None, "dev", None), P(), P(), P())
    return jax.shard_map(
        shards,
        mesh=mesh,
        in_specs=placed,
        out_specs=(P(None, "grp", "dev"), P("grp", None, "dev", None)),
        check_vma=False,
    )
```

```python
import functools

import jax
import jax.numpy as jnp
from jax import lax
from jax.experimental import pallas as pl
from jax.experimental.pallas import tpu as pltpu
from jax.sharding import PartitionSpec as P

F32 = jnp.float32
BF16 = jnp.bfloat16
LANES = 128
VMEM_LIMIT = 48 * 1024 * 1024
MID, EAST, WEST, NORTH, SOUTH = range(5)


class Sizes:
    def __init__(self, parent, nest, anchor, grp_count, dev_count):
        self.C, self.TR, self.TC = parent.shape
        self.L, _, self.H, self.W = nest.shape
        self.N = anchor.shape[0]
        self.G, self.D = grp_count, dev_count
        self.M = self.H // 3
        self.FR, self.FC = self.M * self.D, self.W // 3
        self.S = self.G // 2
        self.NB = self.N // 2
        self.Y = self.D // self.NB
        self.CS = self.C // self.S
        self.BR, self.BC = self.S * self.TR, self.Y * self.TC
        self.R1 = self.L * self.CS * (self.M + 2)
        self.R2 = self.CS * (self.M + 2)
        self.RING = self.FR + self.L * 2 * self.C
        self.RG = self.RING + self.C
        self.RG2 = 16 + self.L * self.C + 8
        self.HALO = self.L * self.C * 3
        self.EDGE = 3 * self.HALO
        assert self.H == 24 and self.FC == LANES and self.TC == LANES
        assert self.FR >= self.TR and self.L == 2


def call(body, out_shape, smem, args, scratch=(), raw=()):
    moved = [*smem, *args]
    n_in, n_raw, n_out = len(moved), len(raw), len(out_shape)
    place = pl.BlockSpec(memory_space=pltpu.HBM)

    def kernel(*refs):
        source, refs = refs[:n_in], refs[n_in:]
        stay, refs = refs[:n_raw], refs[n_raw:]
        target, refs = refs[:n_out], refs[n_out:]
        inner, refs = refs[:n_in], refs[n_in:]
        result, refs = refs[:n_out], refs[n_out:]
        extra, sem = refs[:-1], refs[-1]
        fetch = [pltpu.make_async_copy(a, b, sem.at[k]) for k, (a, b) in enumerate(zip(source, inner))]
        for copy in fetch:
            copy.start()
        for copy in fetch:
            copy.wait()
        body(*inner, *stay, *result, *extra)
        store = [
            pltpu.make_async_copy(a, b, sem.at[n_in + k]) for k, (a, b) in enumerate(zip(result, target))
        ]
        for copy in store:
            copy.start()
        for copy in store:
            copy.wait()

    return pl.pallas_call(
        kernel,
        out_shape=list(out_shape),
        in_specs=[place] * (n_in + n_raw),
        out_specs=[place] * n_out,
        scratch_shapes=[
            *[pltpu.SMEM(x.shape, x.dtype) for x in smem],
            *[pltpu.VMEM(x.shape, x.dtype) for x in args],
            *[pltpu.VMEM(x.shape, x.dtype) for x in out_shape],
            *scratch,
            pltpu.SemaphoreType.DMA((n_in + n_out,)),
        ],
        compiler_params=pltpu.CompilerParams(vmem_limit_bytes=VMEM_LIMIT),
    )(*moved, *raw)


def iota(shape, dim):
    return lax.broadcasted_iota(jnp.int32, shape, dim)


def split_dot(x, table):
    high = x.astype(BF16)
    low = (x - high.astype(F32)).astype(BF16)
    return jnp.dot(jnp.concatenate([high, low], axis=1), table, preferred_element_type=F32)


def nest_at(z, anc, band):
    found = 0
    for n in range(z.N):
        found += jnp.where(anc[0, n] // z.BR * z.NB + anc[1, n] // z.BC == band, n, 0)
    return found


def weights(diff, cour, c, times):
    splat = lambda ref, k: jnp.full((8, LANES), ref[k, c], F32)
    east = times * splat(diff, 0)
    north = times * splat(diff, 1)
    west = east + splat(cour, 0)
    south = north + splat(cour, 1)
    return 1.0 - (east + west) - (north + south), east, west, north, south


def ghost_share(inject, back, mid, plus, minus):
    stay = mid + inject
    m0 = inject * (1.0 + stay + mid * stay + inject * (stay + back) + 2.0 * plus * minus)
    p1 = inject * plus * (1.0 + 2.0 * stay)
    p2 = inject * plus * plus
    n1 = inject * minus * (1.0 + 2.0 * stay)
    n2 = inject * minus * minus
    ninth = 1.0 / 9.0
    same = (3.0 * m0 + 2.0 * p1 + p2 + 2.0 * n1 + n2) * ninth
    return same, (p1 + 2.0 * p2) * ninth, (n1 + 2.0 * n2) * ninth, inject * plus * minus * ninth


class Strip:
    def __init__(self):
        sub = iota((8, LANES), 0)
        lane = iota((8, LANES), 1)
        self.high = [sub == 0, sub == 4]
        self.low = [sub == 7, sub == 3]
        self.any_high = (sub == 0) | (sub == 4)
        self.any_low = (sub == 7) | (sub == 3)
        self.first, self.last = lane == 0, lane == LANES - 1

    def east(self, x, ghost):
        return jnp.where(self.last, ghost, pltpu.roll(x, LANES - 1, 1))

    def west(self, x, ghost):
        return jnp.where(self.first, ghost, pltpu.roll(x, 1, 1))

    def north(self, mains, cap):
        up = [pltpu.roll(m, 7, 0) for m in mains]
        cap_up = pltpu.roll(cap, 7, 0)
        new = [jnp.where(self.low[l], cap_up, up[l]) for l in range(2)]
        return new, jnp.where(self.low[0], up[0], jnp.where(self.low[1], up[1], 0.0))

    def south(self, mains, cap):
        down = [pltpu.roll(m, 1, 0) for m in mains]
        cap_down = pltpu.roll(cap, 1, 0)
        new = [jnp.where(self.high[l], cap_down, down[l]) for l in range(2)]
        return new, jnp.where(self.high[0], down[0], jnp.where(self.high[1], down[1], 0.0))

    def step(self, u, co, west_ghost, east_ghost):
        n_in = [self.north([u[0][0][x], u[1][0][x]], u[2][0][x]) for x in range(3)]
        s_in = [self.south([u[0][2][x], u[1][2][x]], u[2][2][x]) for x in range(3)]
        pick = lambda pair, k: pair[1] if k == 2 else pair[0][k]
        new = []
        for k in range(3):
            rows = []
            for y in range(3):
                row = u[k][y]
                e = [row[1], row[2], self.east(row[0], east_ghost[k])]
                w = [self.west(row[2], west_ghost[k]), row[0], row[1]]
                cells = []
                for x in range(3):
                    n = u[k][y + 1][x] if y < 2 else pick(n_in[x], k)
                    s = u[k][y - 1][x] if y > 0 else pick(s_in[x], k)
                    cells.append(
                        co[MID] * row[x]
                        + (co[EAST] * e[x] + co[WEST] * w[x])
                        + (co[NORTH] * n + co[SOUTH] * s)
                    )
                rows.append(cells)
            new.append(rows)
        return new

    def pooled_step(self, u, co):
        ends = []
        for k in range(3):
            row = [u[k][y][0] + u[k][y][1] + u[k][y][2] for y in range(3)]
            col = [u[k][0][x] + u[k][1][x] + u[k][2][x] for x in (0, 2)]
            ends.append((row[0], row[2], col[0], col[1], row[0] + row[1] + row[2]))
        n_in = self.north([ends[0][0], ends[1][0]], ends[2][0])
        s_in = self.south([ends[0][1], ends[1][1]], ends[2][1])
        pick = lambda pair, k: pair[1] if k == 2 else pair[0][k]
        out = []
        for k in range(3):
            row0, row2, col0, col2, total = ends[k]
            flux_x = co[EAST] * (self.east(col0, 0.0) - col0)
            flux_x += co[WEST] * (self.west(col2, 0.0) - col2)
            flux_y = co[NORTH] * (pick(n_in, k) - row0) + co[SOUTH] * (pick(s_in, k) - row2)
            out.append(total + (flux_x + flux_y))
        return out


def phase_rows(z, ref, l, c, y, x):
    got = ref[x, pl.ds((l * z.C + c) * z.H + y, z.M, 3), :]
    return got if l == 0 else pltpu.roll(got, 4, 0)


def partial_averages(z, diff, cour, nest, *refs):
    out, phases, strips, sem = refs[: z.S], refs[z.S], refs[z.S + 1], refs[z.S + 2]
    fetch = [pltpu.make_async_copy(nest.at[l], strips.at[l], sem.at[l]) for l in range(z.L)]
    for copy in fetch:
        copy.start()
    d = lax.axis_index("dev")
    own = lax.rem(lax.axis_index("grp"), z.S)
    C, M, CS = z.C, z.M, z.CS
    fine = lax.rem(iota((2 * z.W, z.W), 0), z.W)
    place = iota((2 * z.W, z.W), 1)
    at = lax.rem(place, LANES) * 3 + place // LANES
    deal = jnp.where(fine == at, 1.0, 0.0).astype(BF16)
    rows = C * z.H
    for l in range(z.L):
        fetch[l].wait()
        dealt = split_dot(strips[l].reshape(rows, z.W), deal)
        for x in range(3):
            phases[x, l * rows : (l + 1) * rows, :] = dealt[:, x * LANES : (x + 1) * LANES]
    strip = Strip()
    keep_high = strip.any_low | (strip.any_high & (d < z.D - 1))
    keep_low = strip.any_high | (strip.any_low & (d > 0))
    zero = jnp.zeros((8, LANES), F32)
    ghosts = [0.0] * 3
    base = z.L * CS * M

    def hold(u):
        cap = [
            [jnp.where(keep_high, v, 0.0) for v in u[2][0]],
            u[2][1],
            [jnp.where(keep_low, v, 0.0) for v in u[2][2]],
        ]
        return [u[0], u[1], cap]

    for part in range(z.S):

        def channel(i, _, to=out[part], first=jnp.bitwise_xor(own, part) * CS):
            c = first + i
            co = weights(diff, cour, c, 3.0)
            u = [
                [[phase_rows(z, phases, l, c, y, x) for x in range(3)] for y in range(3)]
                for l in range(2)
            ]
            u.append([[zero] * 3] * 3)
            for _step in range(2):
                u = hold(strip.step(u, co, ghosts, ghosts))
            got = [v * (1.0 / 9.0) for v in strip.pooled_step(u, co)]
            got[1] = pltpu.roll(got[1], 4, 0)
            for l in range(2):
                row = pl.multiple_of((l * CS + i) * M, M)
                to[pl.ds(row, M), :] = got[l]
                for side, sub in enumerate(((7, 3), (0, 4))):
                    row = base + (l * 2 + side) * CS + i
                    to[pl.ds(row, 1), :] = got[2][sub[l] : sub[l] + 1]
            return 0

        lax.fori_loop(0, CS, channel, 0, unroll=2)


def pick_band(z, anc, *refs):
    got, out = refs[: z.G], refs[z.G]
    g = lax.axis_index("grp")
    top = g // z.S * z.NB
    base, size = z.L * z.CS * z.M, z.CS * z.M
    for band in range(z.NB):
        n = nest_at(z, anc, top + band)
        of = n // z.L
        slot = jnp.bitwise_xor(of, g)
        first = n - of * z.L == 0
        for k in range(z.G):

            @pl.when(slot == k)
            def _(k=k, first=first, band=band):
                main = jnp.where(first, got[k][:size, :], got[k][size : 2 * size, :])
                edge = jnp.where(
                    first,
                    got[k][base : base + 2 * z.CS, :],
                    got[k][base + 2 * z.CS : base + 4 * z.CS, :],
                )
                for y in range(z.Y):
                    out[band * z.Y + y, :size, :] = main
                    out[band * z.Y + y, size:, :] = edge


def ring_parts(z, anc, parent, nest, buf, up, dn, tail, head, sem):
    fetch = [
        pltpu.make_async_copy(nest.at[:, :, z.H - 8 :, :], tail, sem.at[0]),
        pltpu.make_async_copy(nest.at[:, :, :8, :], head, sem.at[1]),
    ]
    for copy in fetch:
        copy.start()
    g, d = lax.axis_index("grp"), lax.axis_index("dev")
    row_base, col_base = g * z.TR, d * z.TC
    lane_t = iota((z.TR, LANES), 1)
    lane_f = iota((z.FR, LANES), 1)
    row_f = iota((z.FR, LANES), 0)
    lane_c = iota((z.C, LANES), 1)
    buf[...] = jnp.zeros_like(buf)

    def nest_ring(n, _):
        to = n // z.L
        l = n - to * z.L
        slot = to
        r, q = anc[0, n], anc[1, n]
        rows_meet = (r < row_base + z.TR) & (r + z.FR > row_base)
        cols_meet = (q < col_base + z.TC) & (q + z.FC > col_base)
        shift_r = lax.rem(row_base - r + 2 * z.G * z.TR, z.FR)
        shift_q = lax.rem(col_base - q + 2 * z.D * z.TC, z.FC)
        for side in range(2):
            col = (q - 1 if side == 0 else q + z.FC) - col_base
            first = (l * 2 + side) * z.C

            @pl.when(rows_meet & (col >= 0) & (col < z.TC))
            def _(col=col, first=first):
                acc = jnp.zeros((z.TR, LANES), F32)
                for c in range(z.C):
                    at = first + c
                    moved = pltpu.roll(parent[c], lax.rem(at - col + LANES, LANES), 1)
                    acc = jnp.where(lane_t == at, moved, acc)
                if z.FR > z.TR:
                    acc = jnp.concatenate([acc, jnp.zeros((z.FR - z.TR, LANES), F32)], axis=0)
                acc = pltpu.roll(acc, shift_r, 0)
                y = row_f + (r - row_base)
                good = (y >= 0) & (y < z.TR) & (lane_f >= first) & (lane_f < first + z.C)
                buf[slot, : z.FR, :] = jnp.where(good, acc, buf[slot, : z.FR, :])

            row = (r - 1 if side == 0 else r + z.FR) - row_base

            @pl.when(cols_meet & (row >= 0) & (row < z.TR))
            def _(row=row, first=first):
                rows = jnp.concatenate(
                    [parent[c, pl.ds(row, 1), :] for c in range(z.C)], axis=0
                )
                x = lane_c + (q - col_base)
                moved = jnp.where((x >= 0) & (x < z.TC), pltpu.roll(rows, shift_q, 1), 0.0)
                buf[slot, pl.ds(pl.multiple_of(z.FR + first, 8), z.C), :] = moved

        return 0

    lax.fori_loop(0, z.N, nest_ring, 0)
    for to in range(z.G):
        edge = jnp.where(to > g, z.TR - 1, 0)
        for c in range(z.C):
            buf[to, z.RING + c : z.RING + c + 1, :] = parent[c, pl.ds(edge, 1), :]
    first = jnp.zeros((z.TR, LANES), F32)
    last = first
    for c in range(z.C):
        first = jnp.where(lane_t == c, pltpu.roll(parent[c], c, 1) if c else parent[c], first)
        last = jnp.where(lane_t == c, pltpu.roll(parent[c], c + 1, 1), last)
    up[z.EDGE :, :] = last
    dn[z.EDGE :, :] = first
    for copy in fetch:
        copy.wait()
    for l in range(z.L):
        for c in range(z.C):
            for x in range(3):
                at = x * z.HALO + 3 * (l * z.C + c)
                lanes = slice(x * LANES, (x + 1) * LANES)
                up[at : at + 3, :] = tail[l, c, 5:8, lanes]
                dn[at : at + 3, :] = head[l, c, 0:3, lanes]


def ring_next(z, got, out, edges, slab):
    g, d = lax.axis_index("grp"), lax.axis_index("dev")
    C, L, FR, M = z.C, z.L, z.FR, z.M
    total = got[0, : z.RING, :]
    for k in range(1, z.G):
        total = total + got[k, : z.RING, :]
    slab[...] = total
    sub = iota((8, LANES), 0)
    for to in range(z.D):
        out[to, :M, :] = slab[to * M : (to + 1) * M, :]
        hi = min(to * M + M, FR - 1)
        lo = max(to * M - 1, 0)
        hi, lo = slab[hi : hi + 1, :], slab[lo : lo + 1, :]
        out[to, M:16, :] = jnp.where(sub == 0, hi, jnp.where(sub == 7, lo, 0.0))
        for l in range(L):
            at = 16 + l * C
            if to == 0 or to == z.D - 1:
                k = FR + (l * 2 + (0 if to == 0 else 1)) * C
                out[to, at : at + C, :] = slab[k : k + C, :]
            else:
                out[to, at : at + C, :] = jnp.zeros((C, LANES), F32)
    before, after = jnp.maximum(g - 1, 0), jnp.minimum(g + 1, z.G - 1)
    edges[:C, :] = jnp.where(g > 0, got[before, z.RING :, :], 0.0)
    edges[C:, :] = jnp.where(g < z.G - 1, got[after, z.RING :, :], 0.0)
    lane = iota((8, LANES), 1)
    first = jnp.zeros((8, LANES), F32)
    last = first
    for c in range(C):
        lo = edges[c : c + 1, :]
        hi = edges[C + c : C + c + 1, :]
        cap = jnp.where(sub == 0, hi, jnp.where(sub == 7, lo, 0.0))
        first = jnp.where(lane == c, pltpu.roll(cap, c, 1) if c else cap, first)
        last = jnp.where(lane == c, pltpu.roll(cap, c + 1, 1), last)
    for to in range(z.D):
        out[to, z.RG2 - 8 :, :] = jnp.where(to > d, last, first)


def nest_steps(z, diff, cour, phases, got, up_in, dn_in, out, back, ring, up, dn):
    d = lax.axis_index("dev")
    C, M = z.C, z.M
    strip = Strip()
    fine = lax.rem(iota((2 * z.W, z.W), 0), z.W)
    place = iota((2 * z.W, z.W), 1)
    deal = jnp.where(fine == lax.rem(place, LANES) * 3 + place // LANES, 1.0, 0.0).astype(BF16)
    for source, target in ((up_in, up), (dn_in, dn)):
        halo = [source[x * z.HALO : (x + 1) * z.HALO, :] for x in range(3)]
        dealt = split_dot(jnp.concatenate(halo, axis=1), deal)
        for x in range(3):
            target[x * z.HALO : (x + 1) * z.HALO, :] = dealt[:, x * LANES : (x + 1) * LANES]
    total = got[0]
    for k in range(1, z.D):
        total = total + got[k]
    ring[...] = total
    side_main = [ring[:M, :], pltpu.roll(ring[:M, :], 4, 0)]
    side_cap = jnp.where(
        strip.any_high, ring[M : M + 1, :], jnp.where(strip.any_low, ring[15:16, :], 0.0)
    )
    hold_low, hold_high = strip.any_low & (d == 0), strip.any_high & (d == z.D - 1)
    nest_1 = strip.high[1] | strip.low[1]

    def channel(c, _):
        co = weights(diff, cour, c, 3.0)
        u = [
            [[phase_rows(z, phases, l, c, y, x) for x in range(3)] for y in range(3)]
            for l in range(2)
        ]
        cap = []
        for y in range(3):
            row = []
            for x in range(3):
                v = jnp.zeros((8, LANES), F32)
                for l in range(2):
                    at = x * z.HALO + (l * C + c) * 3 + y
                    v = jnp.where(strip.high[l], dn[pl.ds(at, 1), :], v)
                    v = jnp.where(strip.low[l], up[pl.ds(at, 1), :], v)
                row.append(v)
            cap.append(row)
        u.append(cap)
        end = jnp.where(nest_1, ring[pl.ds(16 + C + c, 1), :], ring[pl.ds(16 + c, 1), :])
        west, east = [], []
        for side, lane, ghosts in ((0, 0, west), (1, LANES - 1, east)):
            turn = [lax.rem(lane - ((l * 2 + side) * C + c) + LANES, LANES) for l in range(2)]
            for l in range(2):
                ghosts.append(pltpu.roll(side_main[l], turn[l], 1))
            caps = [pltpu.roll(side_cap, turn[l], 1) for l in range(2)]
            ghosts.append(jnp.where(nest_1, caps[1], caps[0]))

        def hold(u):
            cap = [
                [jnp.where(hold_high, end, v) for v in u[2][0]],
                u[2][1],
                [jnp.where(hold_low, end, v) for v in u[2][2]],
            ]
            return [u[0], u[1], cap]

        u = hold(u)
        for k in range(3):
            u = strip.step(u, co, west, east)
            if k < 2:
                u = hold(u)
        for l in range(2):
            for y in range(3):
                for x in range(3):
                    v = u[l][y][x]
                    v = v if l == 0 else pltpu.roll(v, 4, 0)
                    back[x, pl.ds((l * C + c) * z.H + y, M, 3), :] = v
        return 0

    lax.fori_loop(0, C, channel, 0, unroll=2)
    fine = iota((2 * z.W, z.W), 1)
    place = lax.rem(iota((2 * z.W, z.W), 0), z.W)
    at = lax.rem(place, LANES) * 3 + place // LANES
    undeal = jnp.where(fine == at, 1.0, 0.0).astype(BF16)
    done = split_dot(jnp.concatenate([back[0], back[1], back[2]], axis=1), undeal)
    out[...] = done.reshape(z.L, C, z.H, z.W)


def parent_step(z, anc, diff, cour, parent, edges, up_in, dn_in, got, out):
    g, d = lax.axis_index("grp"), lax.axis_index("dev")
    C = z.C
    rows = z.TR + 8
    n = nest_at(z, anc, g // z.S * z.NB + d // z.Y)
    i = iota((z.TR, LANES), 0) + (g * z.TR - anc[0, n])
    j = iota((z.TR, LANES), 1) + (d * z.TC - anc[1, n])
    inside = (i >= 0) & (i < z.FR) & (j >= 0) & (j < z.FC)
    one = lambda cond: jnp.where(cond, 1.0, 0.0).astype(F32)
    on_w, on_e = one(inside & (j == 0)), one(inside & (j == z.FC - 1))
    on_s, on_n = one(inside & (i == 0)), one(inside & (i == z.FR - 1))
    i_end, j_end = one((i == 0) | (i == z.FR - 1)), one((j == 0) | (j == z.FC - 1))
    i_lo, i_hi = one(i > 0), one(i < z.FR - 1)
    j_lo, j_hi = one(j > 0), one(j < z.FC - 1)
    lane = iota((rows, LANES), 1)
    sub = iota((8, LANES), 0)

    cap_w = jnp.where(d > 0, got[jnp.maximum(d - 1, 0), z.RG2 - 8 :, :], 0.0)
    cap_e = jnp.where(d < z.D - 1, got[jnp.minimum(d + 1, z.D - 1), z.RG2 - 8 :, :], 0.0)
    col_w = jnp.concatenate([up_in[z.EDGE :, :], cap_w], axis=0)
    col_e = jnp.concatenate([dn_in[z.EDGE :, :], cap_e], axis=0)

    def channel(c, _):
        co = [v[:1] for v in weights(diff, cour, c, 1.0)]
        fm, fe, fw, fn, fs = [v[:1] for v in weights(diff, cour, c, 3.0)]
        lo = edges[pl.ds(c, 1), :]
        hi = edges[pl.ds(C + c, 1), :]
        cap = jnp.where(sub == 0, hi, jnp.where(sub == 7, lo, 0.0))
        full = jnp.concatenate([parent[c], cap], axis=0)
        w_in = pltpu.roll(col_w, lax.rem(LANES - c, LANES), 1)
        e_in = pltpu.roll(col_e, LANES - 1 - c, 1)
        w_all = jnp.where(lane == 0, w_in, pltpu.roll(full, 1, 1))
        e_all = jnp.where(lane == LANES - 1, e_in, pltpu.roll(full, LANES - 1, 1))
        up = lambda x: pltpu.roll(x, rows - 1, 0)[: z.TR]
        down = lambda x: pltpu.roll(x, 1, 0)[: z.TR]
        mid = full[: z.TR]
        w, e, n, s = w_all[: z.TR], e_all[: z.TR], up(full), down(full)
        w_up, w_down, e_up, e_down = up(w_all), down(w_all), up(e_all), down(e_all)
        step = (
            co[MID] * mid
            + (co[EAST] * e + co[WEST] * w)
            + (co[NORTH] * n + co[SOUTH] * s)
        )
        a, b, k, x = ghost_share(fw, fe, fm, fs, fn)
        share = on_w * ((a - x * i_end) * w + (b * i_lo) * w_down + (k * i_hi) * w_up)
        a, b, k, x = ghost_share(fe, fw, fm, fs, fn)
        share += on_e * ((a - x * i_end) * e + (b * i_lo) * e_down + (k * i_hi) * e_up)
        a, b, k, x = ghost_share(fs, fn, fm, fw, fe)
        share += on_s * ((a - x * j_end) * s + (b * j_lo) * w_down + (k * j_hi) * e_down)
        a, b, k, x = ghost_share(fn, fs, fm, fw, fe)
        share += on_n * ((a - x * j_end) * n + (b * j_lo) * w_up + (k * j_hi) * e_up)
        out[c] = jnp.where(inside, share, step)
        return 0

    lax.fori_loop(0, C, channel, 0, unroll=2)


def merge(z, which, anc, base, *refs):
    pieces, out, twice = refs[:-2], refs[-2], refs[-1]
    g, d = lax.axis_index("grp"), lax.axis_index("dev")
    n = nest_at(z, anc, g // z.S * z.NB + d // z.Y)
    r, q = anc[0, n], anc[1, n]
    start = lax.rem(g * z.TR - r + 2 * z.G * z.TR, z.FR)
    shift_q = lax.rem(q - d * z.TC + 2 * z.D * z.TC, z.FC)
    i = iota((z.TR, LANES), 0) + (g * z.TR - r)
    j = iota((z.TR, LANES), 1) + (d * z.TC - q)
    inside = (i >= 0) & (i < z.FR) & (j >= 0) & (j < z.FC)
    sub = iota((z.M, LANES), 0)
    part = lax.rem(g, z.S)
    size = z.CS * z.M
    for k in range(z.S):
        if k not in which:
            other = lax.rem(part - k + z.S, z.S) * z.CS
            out[pl.ds(other, z.CS)] = base[pl.ds(other, z.CS)]
    for piece, k in zip(pieces, which):
        first = lax.rem(part - k + z.S, z.S) * z.CS
        for c in range(z.CS):
            for m in range(z.D):
                x = piece[m, c * z.M : (c + 1) * z.M, :]
                if m + 1 < z.D:
                    row = piece[m + 1, size + c : size + c + 1, :]
                    x += jnp.where(sub == z.M - 1, row, 0.0)
                if m > 0:
                    row = piece[m - 1, size + z.CS + c : size + z.CS + c + 1, :]
                    x += jnp.where(sub == 0, row, 0.0)
                twice[c % 4, m * z.M : (m + 1) * z.M, :] = x
                if m * z.M < z.TR:
                    twice[c % 4, z.FR + m * z.M : z.FR + (m + 1) * z.M, :] = x
            x = pltpu.roll(twice[c % 4, pl.ds(start, z.TR), :], shift_q, 1)
            out[first + c] = base[first + c] + jnp.where(inside, x, 0.0)


def shards(parent, nest, anchor, diff, cour):
    z = Sizes(parent, nest, anchor, lax.axis_size("grp"), lax.axis_size("dev"))
    sds = lambda *shape: jax.ShapeDtypeStruct(shape, F32)
    vmem = lambda *shape: pltpu.VMEM(shape, F32)
    to_grp = lambda x, k: lax.ppermute(x, "grp", [(a, a ^ k) for a in range(z.G)])

    anchor = anchor.T
    message = sds(z.EDGE + z.TR, LANES)
    edge_tile = vmem(z.L, z.C, 8, z.W)
    ring, up, dn = call(
        functools.partial(ring_parts, z),
        [sds(z.G, z.RG, LANES), message, message],
        (anchor,),
        (parent,),
        [edge_tile, edge_tile, pltpu.SemaphoreType.DMA((2,))],
        (nest,),
    )
    forward = [(k, k + 1) for k in range(z.D - 1)]
    up = lax.ppermute(up, "dev", forward)
    dn = lax.ppermute(dn, "dev", [(b, a) for a, b in forward])
    ring = lax.all_to_all(ring, "grp", 0, 0, tiled=True)
    ring, edges = call(
        functools.partial(ring_next, z),
        [sds(z.D, z.RG2, LANES), sds(2 * z.C, LANES)],
        (),
        (ring,),
        [vmem(z.RING, LANES)],
    )
    nest, ring, edges = lax.optimization_barrier((nest, ring, edges))
    ring = lax.all_to_all(ring, "dev", 0, 0, tiled=True)
    *chunks, phases = call(
        functools.partial(partial_averages, z),
        [sds(z.R1, LANES)] * z.S + [sds(3, z.L * z.C * z.H, LANES)],
        (diff, cour),
        (),
        [pltpu.VMEM(nest.shape, F32), pltpu.SemaphoreType.DMA((z.L,))],
        (nest,),
    )
    chunks, ring, up, dn = lax.optimization_barrier((chunks, ring, up, dn))
    got = [chunks[0]] + [to_grp(chunks[k % z.S], k) for k in range(1, z.G)]

    (avg,) = call(functools.partial(pick_band, z), [sds(z.D, z.R2, LANES)], (anchor,), got)
    avg, phases, edges = lax.optimization_barrier((avg, phases, edges))
    avg = lax.all_to_all(avg, "dev", 0, 0, tiled=True)
    (nest_out,) = call(
        functools.partial(nest_steps, z),
        [jax.ShapeDtypeStruct(nest.shape, F32)],
        (diff, cour),
        (phases, ring, up, dn),
        [
            vmem(3, z.L * z.C * z.H, LANES),
            vmem(z.RG2, LANES),
            vmem(z.EDGE, LANES),
            vmem(z.EDGE, LANES),
        ],
    )
    (out,) = call(
        functools.partial(parent_step, z),
        [jax.ShapeDtypeStruct(parent.shape, F32)],
        (anchor, diff, cour),
        (parent, edges, up, dn, ring),
    )
    avg, nest_out, out = lax.optimization_barrier((avg, nest_out, out))
    pieces = [avg]
    for k in range(1, z.S):
        pairs = [(a, a // z.S * z.S + (a + k) % z.S) for a in range(z.G)]
        pieces.append(lax.ppermute(avg, "grp", pairs))
    for which in ([0], list(range(1, z.S))):
        (out,) = call(
            functools.partial(merge, z, which),
            [jax.ShapeDtypeStruct(parent.shape, F32)],
            (anchor,),
            (out, *[pieces[k] for k in which]),
            [vmem(4, z.FR + z.TR, LANES)],
        )
    return out, nest_out


def solution(mesh):
    placed = (P(None, "grp", "dev"), P("grp", None, "dev", None), P(), P(), P())
    return jax.shard_map(
        shards,
        mesh=mesh,
        in_specs=placed,
        out_specs=(P(None, "grp", "dev"), P("grp", None, "dev", None)),
        check_vma=False,
    )
```

```python
import functools

import jax
import jax.numpy as jnp
from jax import lax
from jax.experimental import pallas as pl
from jax.experimental.pallas import tpu as pltpu
from jax.sharding import PartitionSpec as P

F32 = jnp.float32
BF16 = jnp.bfloat16
LANES = 128
VMEM_LIMIT = 63 * 1024 * 1024
MID, EAST, WEST, NORTH, SOUTH = range(5)


class Sizes:
    def __init__(self, parent, nest, anchor, grp_count, dev_count):
        self.C, self.TR, self.TC = parent.shape
        self.L, _, self.H, self.W = nest.shape
        self.N = anchor.shape[0]
        self.G, self.D = grp_count, dev_count
        self.M = self.H // 3
        self.FR, self.FC = self.M * self.D, self.W // 3
        self.S = self.G // 2
        self.NB = self.N // 2
        self.Y = self.D // self.NB
        self.CS = self.C // self.S
        self.BR, self.BC = self.S * self.TR, self.Y * self.TC
        self.R1 = self.L * self.CS * (self.M + 2)
        self.R2 = self.CS * (self.M + 2)
        self.RING = self.FR + self.L * 2 * self.C
        self.RG = self.RING + self.C
        self.RG2 = 16 + self.L * self.C + 8
        self.HALO = self.L * self.C * 3
        self.EDGE = 3 * self.HALO
        assert self.H == 24 and self.FC == LANES and self.TC == LANES
        assert self.FR >= self.TR and self.L == 2


def call(body, out_shape, smem, args, scratch=(), raw=()):
    moved = [*smem, *args]
    n_in, n_raw, n_out = len(moved), len(raw), len(out_shape)
    place = pl.BlockSpec(memory_space=pltpu.HBM)

    def kernel(*refs):
        source, refs = refs[:n_in], refs[n_in:]
        stay, refs = refs[:n_raw], refs[n_raw:]
        target, refs = refs[:n_out], refs[n_out:]
        inner, refs = refs[:n_in], refs[n_in:]
        result, refs = refs[:n_out], refs[n_out:]
        extra, sem = refs[:-1], refs[-1]
        fetch = [pltpu.make_async_copy(a, b, sem.at[k]) for k, (a, b) in enumerate(zip(source, inner))]
        for copy in fetch:
            copy.start()
        for copy in fetch:
            copy.wait()
        body(*inner, *stay, *result, *extra)
        store = [
            pltpu.make_async_copy(a, b, sem.at[n_in + k]) for k, (a, b) in enumerate(zip(result, target))
        ]
        for copy in store:
            copy.start()
        for copy in store:
            copy.wait()

    return pl.pallas_call(
        kernel,
        out_shape=list(out_shape),
        in_specs=[place] * (n_in + n_raw),
        out_specs=[place] * n_out,
        scratch_shapes=[
            *[pltpu.SMEM(x.shape, x.dtype) for x in smem],
            *[pltpu.VMEM(x.shape, x.dtype) for x in args],
            *[pltpu.VMEM(x.shape, x.dtype) for x in out_shape],
            *scratch,
            pltpu.SemaphoreType.DMA((n_in + n_out,)),
        ],
        compiler_params=pltpu.CompilerParams(vmem_limit_bytes=VMEM_LIMIT),
    )(*moved, *raw)


def iota(shape, dim):
    return lax.broadcasted_iota(jnp.int32, shape, dim)


def split_dot(x, table):
    high = x.astype(BF16)
    low = (x - high.astype(F32)).astype(BF16)
    return jnp.dot(jnp.concatenate([high, low], axis=1), table, preferred_element_type=F32)


def nest_at(z, anc, band):
    found = 0
    for n in range(z.N):
        found += jnp.where(anc[0, n] // z.BR * z.NB + anc[1, n] // z.BC == band, n, 0)
    return found


def weights(diff, cour, c, times):
    splat = lambda ref, k: jnp.full((8, LANES), ref[k, c], F32)
    east = times * splat(diff, 0)
    north = times * splat(diff, 1)
    west = east + splat(cour, 0)
    south = north + splat(cour, 1)
    return 1.0 - (east + west) - (north + south), east, west, north, south


def ghost_share(inject, back, mid, plus, minus):
    stay = mid + inject
    m0 = inject * (1.0 + stay + mid * stay + inject * (stay + back) + 2.0 * plus * minus)
    p1 = inject * plus * (1.0 + 2.0 * stay)
    p2 = inject * plus * plus
    n1 = inject * minus * (1.0 + 2.0 * stay)
    n2 = inject * minus * minus
    ninth = 1.0 / 9.0
    same = (3.0 * m0 + 2.0 * p1 + p2 + 2.0 * n1 + n2) * ninth
    return same, (p1 + 2.0 * p2) * ninth, (n1 + 2.0 * n2) * ninth, inject * plus * minus * ninth


class Strip:
    def __init__(self):
        sub = iota((8, LANES), 0)
        lane = iota((8, LANES), 1)
        self.high = [sub == 0, sub == 4]
        self.low = [sub == 7, sub == 3]
        self.any_high = (sub == 0) | (sub == 4)
        self.any_low = (sub == 7) | (sub == 3)
        self.first, self.last = lane == 0, lane == LANES - 1

    def east(self, x, ghost):
        return jnp.where(self.last, ghost, pltpu.roll(x, LANES - 1, 1))

    def west(self, x, ghost):
        return jnp.where(self.first, ghost, pltpu.roll(x, 1, 1))

    def north(self, mains, cap):
        up = [pltpu.roll(m, 7, 0) for m in mains]
        cap_up = pltpu.roll(cap, 7, 0)
        new = [jnp.where(self.low[l], cap_up, up[l]) for l in range(2)]
        return new, jnp.where(self.low[0], up[0], jnp.where(self.low[1], up[1], 0.0))

    def south(self, mains, cap):
        down = [pltpu.roll(m, 1, 0) for m in mains]
        cap_down = pltpu.roll(cap, 1, 0)
        new = [jnp.where(self.high[l], cap_down, down[l]) for l in range(2)]
        return new, jnp.where(self.high[0], down[0], jnp.where(self.high[1], down[1], 0.0))

    def step(self, u, co, west_ghost, east_ghost):
        n_in = [self.north([u[0][0][x], u[1][0][x]], u[2][0][x]) for x in range(3)]
        s_in = [self.south([u[0][2][x], u[1][2][x]], u[2][2][x]) for x in range(3)]
        pick = lambda pair, k: pair[1] if k == 2 else pair[0][k]
        new = []
        for k in range(3):
            rows = []
            for y in range(3):
                row = u[k][y]
                e = [row[1], row[2], self.east(row[0], east_ghost[k])]
                w = [self.west(row[2], west_ghost[k]), row[0], row[1]]
                cells = []
                for x in range(3):
                    n = u[k][y + 1][x] if y < 2 else pick(n_in[x], k)
                    s = u[k][y - 1][x] if y > 0 else pick(s_in[x], k)
                    cells.append(
                        co[MID] * row[x]
                        + (co[EAST] * e[x] + co[WEST] * w[x])
                        + (co[NORTH] * n + co[SOUTH] * s)
                    )
                rows.append(cells)
            new.append(rows)
        return new

    def pooled_step(self, u, co):
        ends = []
        for k in range(3):
            row = [u[k][y][0] + u[k][y][1] + u[k][y][2] for y in range(3)]
            col = [u[k][0][x] + u[k][1][x] + u[k][2][x] for x in (0, 2)]
            ends.append((row[0], row[2], col[0], col[1], row[0] + row[1] + row[2]))
        n_in = self.north([ends[0][0], ends[1][0]], ends[2][0])
        s_in = self.south([ends[0][1], ends[1][1]], ends[2][1])
        pick = lambda pair, k: pair[1] if k == 2 else pair[0][k]
        out = []
        for k in range(3):
            row0, row2, col0, col2, total = ends[k]
            flux_x = co[EAST] * (self.east(col0, 0.0) - col0)
            flux_x += co[WEST] * (self.west(col2, 0.0) - col2)
            flux_y = co[NORTH] * (pick(n_in, k) - row0) + co[SOUTH] * (pick(s_in, k) - row2)
            out.append(total + (flux_x + flux_y))
        return out


def phase_rows(z, ref, l, c, y, x):
    got = ref[x, pl.ds((l * z.C + c) * z.H + y, z.M, 3), :]
    return got if l == 0 else pltpu.roll(got, 4, 0)


def partial_averages(z, diff, cour, nest, *refs):
    out, phases, strips, sem = refs[: z.S], refs[z.S], refs[z.S + 1], refs[z.S + 2]
    fetch = [pltpu.make_async_copy(nest.at[l], strips.at[l], sem.at[l]) for l in range(z.L)]
    for copy in fetch:
        copy.start()
    d = lax.axis_index("dev")
    own = lax.rem(lax.axis_index("grp"), z.S)
    C, M, CS = z.C, z.M, z.CS
    fine = lax.rem(iota((2 * z.W, z.W), 0), z.W)
    place = iota((2 * z.W, z.W), 1)
    at = lax.rem(place, LANES) * 3 + place // LANES
    deal = jnp.where(fine == at, 1.0, 0.0).astype(BF16)
    rows = C * z.H
    for l in range(z.L):
        fetch[l].wait()
        dealt = split_dot(strips[l].reshape(rows, z.W), deal)
        for x in range(3):
            phases[x, l * rows : (l + 1) * rows, :] = dealt[:, x * LANES : (x + 1) * LANES]
    strip = Strip()
    keep_high = strip.any_low | (strip.any_high & (d < z.D - 1))
    keep_low = strip.any_high | (strip.any_low & (d > 0))
    zero = jnp.zeros((8, LANES), F32)
    ghosts = [0.0] * 3
    base = z.L * CS * M

    def hold(u):
        cap = [
            [jnp.where(keep_high, v, 0.0) for v in u[2][0]],
            u[2][1],
            [jnp.where(keep_low, v, 0.0) for v in u[2][2]],
        ]
        return [u[0], u[1], cap]

    for part in range(z.S):

        def channel(i, _, to=out[part], first=jnp.bitwise_xor(own, part) * CS):
            c = first + i
            co = weights(diff, cour, c, 3.0)
            u = [
                [[phase_rows(z, phases, l, c, y, x) for x in range(3)] for y in range(3)]
                for l in range(2)
            ]
            u.append([[zero] * 3] * 3)
            for _step in range(2):
                u = hold(strip.step(u, co, ghosts, ghosts))
            got = [v * (1.0 / 9.0) for v in strip.pooled_step(u, co)]
            got[1] = pltpu.roll(got[1], 4, 0)
            for l in range(2):
                row = pl.multiple_of((l * CS + i) * M, M)
                to[pl.ds(row, M), :] = got[l]
                for side, sub in enumerate(((7, 3), (0, 4))):
                    row = base + (l * 2 + side) * CS + i
                    to[pl.ds(row, 1), :] = got[2][sub[l] : sub[l] + 1]
            return 0

        lax.fori_loop(0, CS, channel, 0, unroll=2)


def pick_band(z, anc, *refs):
    got, out = refs[: z.G], refs[z.G]
    g = lax.axis_index("grp")
    top = g // z.S * z.NB
    base, size = z.L * z.CS * z.M, z.CS * z.M
    for band in range(z.NB):
        n = nest_at(z, anc, top + band)
        of = n // z.L
        slot = jnp.bitwise_xor(of, g)
        first = n - of * z.L == 0
        for k in range(z.G):

            @pl.when(slot == k)
            def _(k=k, first=first, band=band):
                main = jnp.where(first, got[k][:size, :], got[k][size : 2 * size, :])
                edge = jnp.where(
                    first,
                    got[k][base : base + 2 * z.CS, :],
                    got[k][base + 2 * z.CS : base + 4 * z.CS, :],
                )
                for y in range(z.Y):
                    out[band * z.Y + y, :size, :] = main
                    out[band * z.Y + y, size:, :] = edge


def ring_parts(z, anc, parent, nest, buf, up, dn, tail, head, sem):
    fetch = [
        pltpu.make_async_copy(nest.at[:, :, z.H - 8 :, :], tail, sem.at[0]),
        pltpu.make_async_copy(nest.at[:, :, :8, :], head, sem.at[1]),
    ]
    for copy in fetch:
        copy.start()
    g, d = lax.axis_index("grp"), lax.axis_index("dev")
    row_base, col_base = g * z.TR, d * z.TC
    lane_t = iota((z.TR, LANES), 1)
    lane_f = iota((z.FR, LANES), 1)
    row_f = iota((z.FR, LANES), 0)
    lane_c = iota((z.C, LANES), 1)
    buf[...] = jnp.zeros_like(buf)

    def nest_ring(n, _):
        to = n // z.L
        l = n - to * z.L
        slot = to
        r, q = anc[0, n], anc[1, n]
        rows_meet = (r < row_base + z.TR) & (r + z.FR > row_base)
        cols_meet = (q < col_base + z.TC) & (q + z.FC > col_base)
        shift_r = lax.rem(row_base - r + 2 * z.G * z.TR, z.FR)
        shift_q = lax.rem(col_base - q + 2 * z.D * z.TC, z.FC)
        for side in range(2):
            col = (q - 1 if side == 0 else q + z.FC) - col_base
            first = (l * 2 + side) * z.C

            @pl.when(rows_meet & (col >= 0) & (col < z.TC))
            def _(col=col, first=first):
                acc = jnp.zeros((z.TR, LANES), F32)
                for c in range(z.C):
                    at = first + c
                    moved = pltpu.roll(parent[c], lax.rem(at - col + LANES, LANES), 1)
                    acc = jnp.where(lane_t == at, moved, acc)
                if z.FR > z.TR:
                    acc = jnp.concatenate([acc, jnp.zeros((z.FR - z.TR, LANES), F32)], axis=0)
                acc = pltpu.roll(acc, shift_r, 0)
                y = row_f + (r - row_base)
                good = (y >= 0) & (y < z.TR) & (lane_f >= first) & (lane_f < first + z.C)
                buf[slot, : z.FR, :] = jnp.where(good, acc, buf[slot, : z.FR, :])

            row = (r - 1 if side == 0 else r + z.FR) - row_base

            @pl.when(cols_meet & (row >= 0) & (row < z.TR))
            def _(row=row, first=first):
                rows = jnp.concatenate(
                    [parent[c, pl.ds(row, 1), :] for c in range(z.C)], axis=0
                )
                x = lane_c + (q - col_base)
                moved = jnp.where((x >= 0) & (x < z.TC), pltpu.roll(rows, shift_q, 1), 0.0)
                buf[slot, pl.ds(pl.multiple_of(z.FR + first, 8), z.C), :] = moved

        return 0

    lax.fori_loop(0, z.N, nest_ring, 0)
    for to in range(z.G):
        edge = jnp.where(to > g, z.TR - 1, 0)
        for c in range(z.C):
            buf[to, z.RING + c : z.RING + c + 1, :] = parent[c, pl.ds(edge, 1), :]
    first = jnp.zeros((z.TR, LANES), F32)
    last = first
    for c in range(z.C):
        first = jnp.where(lane_t == c, pltpu.roll(parent[c], c, 1) if c else parent[c], first)
        last = jnp.where(lane_t == c, pltpu.roll(parent[c], c + 1, 1), last)
    up[z.EDGE :, :] = last
    dn[z.EDGE :, :] = first
    for copy in fetch:
        copy.wait()
    for l in range(z.L):
        for c in range(z.C):
            for x in range(3):
                at = x * z.HALO + 3 * (l * z.C + c)
                lanes = slice(x * LANES, (x + 1) * LANES)
                up[at : at + 3, :] = tail[l, c, 5:8, lanes]
                dn[at : at + 3, :] = head[l, c, 0:3, lanes]


def ring_next(z, got, out, edges, slab):
    g, d = lax.axis_index("grp"), lax.axis_index("dev")
    C, L, FR, M = z.C, z.L, z.FR, z.M
    total = got[0, : z.RING, :]
    for k in range(1, z.G):
        total = total + got[k, : z.RING, :]
    slab[...] = total
    sub = iota((8, LANES), 0)
    for to in range(z.D):
        out[to, :M, :] = slab[to * M : (to + 1) * M, :]
        hi = min(to * M + M, FR - 1)
        lo = max(to * M - 1, 0)
        hi, lo = slab[hi : hi + 1, :], slab[lo : lo + 1, :]
        out[to, M:16, :] = jnp.where(sub == 0, hi, jnp.where(sub == 7, lo, 0.0))
        for l in range(L):
            at = 16 + l * C
            if to == 0 or to == z.D - 1:
                k = FR + (l * 2 + (0 if to == 0 else 1)) * C
                out[to, at : at + C, :] = slab[k : k + C, :]
            else:
                out[to, at : at + C, :] = jnp.zeros((C, LANES), F32)
    before, after = jnp.maximum(g - 1, 0), jnp.minimum(g + 1, z.G - 1)
    edges[:C, :] = jnp.where(g > 0, got[before, z.RING :, :], 0.0)
    edges[C:, :] = jnp.where(g < z.G - 1, got[after, z.RING :, :], 0.0)
    lane = iota((8, LANES), 1)
    first = jnp.zeros((8, LANES), F32)
    last = first
    for c in range(C):
        lo = edges[c : c + 1, :]
        hi = edges[C + c : C + c + 1, :]
        cap = jnp.where(sub == 0, hi, jnp.where(sub == 7, lo, 0.0))
        first = jnp.where(lane == c, pltpu.roll(cap, c, 1) if c else cap, first)
        last = jnp.where(lane == c, pltpu.roll(cap, c + 1, 1), last)
    for to in range(z.D):
        out[to, z.RG2 - 8 :, :] = jnp.where(to > d, last, first)


def nest_steps(z, diff, cour, phases, got, up_in, dn_in, out, back, ring, up, dn):
    d = lax.axis_index("dev")
    C, M = z.C, z.M
    strip = Strip()
    fine = lax.rem(iota((2 * z.W, z.W), 0), z.W)
    place = iota((2 * z.W, z.W), 1)
    deal = jnp.where(fine == lax.rem(place, LANES) * 3 + place // LANES, 1.0, 0.0).astype(BF16)
    for source, target in ((up_in, up), (dn_in, dn)):
        halo = [source[x * z.HALO : (x + 1) * z.HALO, :] for x in range(3)]
        dealt = split_dot(jnp.concatenate(halo, axis=1), deal)
        for x in range(3):
            target[x * z.HALO : (x + 1) * z.HALO, :] = dealt[:, x * LANES : (x + 1) * LANES]
    total = got[0]
    for k in range(1, z.D):
        total = total + got[k]
    ring[...] = total
    side_main = [ring[:M, :], pltpu.roll(ring[:M, :], 4, 0)]
    side_cap = jnp.where(
        strip.any_high, ring[M : M + 1, :], jnp.where(strip.any_low, ring[15:16, :], 0.0)
    )
    hold_low, hold_high = strip.any_low & (d == 0), strip.any_high & (d == z.D - 1)
    nest_1 = strip.high[1] | strip.low[1]

    def channel(c, _):
        co = weights(diff, cour, c, 3.0)
        u = [
            [[phase_rows(z, phases, l, c, y, x) for x in range(3)] for y in range(3)]
            for l in range(2)
        ]
        cap = []
        for y in range(3):
            row = []
            for x in range(3):
                v = jnp.zeros((8, LANES), F32)
                for l in range(2):
                    at = x * z.HALO + (l * C + c) * 3 + y
                    v = jnp.where(strip.high[l], dn[pl.ds(at, 1), :], v)
                    v = jnp.where(strip.low[l], up[pl.ds(at, 1), :], v)
                row.append(v)
            cap.append(row)
        u.append(cap)
        end = jnp.where(nest_1, ring[pl.ds(16 + C + c, 1), :], ring[pl.ds(16 + c, 1), :])
        west, east = [], []
        for side, lane, ghosts in ((0, 0, west), (1, LANES - 1, east)):
            turn = [lax.rem(lane - ((l * 2 + side) * C + c) + LANES, LANES) for l in range(2)]
            for l in range(2):
                ghosts.append(pltpu.roll(side_main[l], turn[l], 1))
            caps = [pltpu.roll(side_cap, turn[l], 1) for l in range(2)]
            ghosts.append(jnp.where(nest_1, caps[1], caps[0]))

        def hold(u):
            cap = [
                [jnp.where(hold_high, end, v) for v in u[2][0]],
                u[2][1],
                [jnp.where(hold_low, end, v) for v in u[2][2]],
            ]
            return [u[0], u[1], cap]

        u = hold(u)
        for k in range(3):
            u = strip.step(u, co, west, east)
            if k < 2:
                u = hold(u)
        for l in range(2):
            for y in range(3):
                for x in range(3):
                    v = u[l][y][x]
                    v = v if l == 0 else pltpu.roll(v, 4, 0)
                    back[x, pl.ds((l * C + c) * z.H + y, M, 3), :] = v
        return 0

    lax.fori_loop(0, C, channel, 0, unroll=2)
    fine = iota((2 * z.W, z.W), 1)
    place = lax.rem(iota((2 * z.W, z.W), 0), z.W)
    at = lax.rem(place, LANES) * 3 + place // LANES
    undeal = jnp.where(fine == at, 1.0, 0.0).astype(BF16)
    done = split_dot(jnp.concatenate([back[0], back[1], back[2]], axis=1), undeal)
    out[...] = done.reshape(z.L, C, z.H, z.W)


def parent_step(z, anc, diff, cour, parent, edges, up_in, dn_in, got, out):
    g, d = lax.axis_index("grp"), lax.axis_index("dev")
    C = z.C
    rows = z.TR + 8
    n = nest_at(z, anc, g // z.S * z.NB + d // z.Y)
    i = iota((z.TR, LANES), 0) + (g * z.TR - anc[0, n])
    j = iota((z.TR, LANES), 1) + (d * z.TC - anc[1, n])
    inside = (i >= 0) & (i < z.FR) & (j >= 0) & (j < z.FC)
    one = lambda cond: jnp.where(cond, 1.0, 0.0).astype(F32)
    on_w, on_e = one(inside & (j == 0)), one(inside & (j == z.FC - 1))
    on_s, on_n = one(inside & (i == 0)), one(inside & (i == z.FR - 1))
    i_end, j_end = one((i == 0) | (i == z.FR - 1)), one((j == 0) | (j == z.FC - 1))
    i_lo, i_hi = one(i > 0), one(i < z.FR - 1)
    j_lo, j_hi = one(j > 0), one(j < z.FC - 1)
    lane = iota((rows, LANES), 1)
    sub = iota((8, LANES), 0)

    cap_w = jnp.where(d > 0, got[jnp.maximum(d - 1, 0), z.RG2 - 8 :, :], 0.0)
    cap_e = jnp.where(d < z.D - 1, got[jnp.minimum(d + 1, z.D - 1), z.RG2 - 8 :, :], 0.0)
    col_w = jnp.concatenate([up_in[z.EDGE :, :], cap_w], axis=0)
    col_e = jnp.concatenate([dn_in[z.EDGE :, :], cap_e], axis=0)

    def channel(c, _):
        co = [v[:1] for v in weights(diff, cour, c, 1.0)]
        fm, fe, fw, fn, fs = [v[:1] for v in weights(diff, cour, c, 3.0)]
        lo = edges[pl.ds(c, 1), :]
        hi = edges[pl.ds(C + c, 1), :]
        cap = jnp.where(sub == 0, hi, jnp.where(sub == 7, lo, 0.0))
        full = jnp.concatenate([parent[c], cap], axis=0)
        w_in = pltpu.roll(col_w, lax.rem(LANES - c, LANES), 1)
        e_in = pltpu.roll(col_e, LANES - 1 - c, 1)
        w_all = jnp.where(lane == 0, w_in, pltpu.roll(full, 1, 1))
        e_all = jnp.where(lane == LANES - 1, e_in, pltpu.roll(full, LANES - 1, 1))
        up = lambda x: pltpu.roll(x, rows - 1, 0)[: z.TR]
        down = lambda x: pltpu.roll(x, 1, 0)[: z.TR]
        mid = full[: z.TR]
        w, e, n, s = w_all[: z.TR], e_all[: z.TR], up(full), down(full)
        w_up, w_down, e_up, e_down = up(w_all), down(w_all), up(e_all), down(e_all)
        step = (
            co[MID] * mid
            + (co[EAST] * e + co[WEST] * w)
            + (co[NORTH] * n + co[SOUTH] * s)
        )
        a, b, k, x = ghost_share(fw, fe, fm, fs, fn)
        share = on_w * ((a - x * i_end) * w + (b * i_lo) * w_down + (k * i_hi) * w_up)
        a, b, k, x = ghost_share(fe, fw, fm, fs, fn)
        share += on_e * ((a - x * i_end) * e + (b * i_lo) * e_down + (k * i_hi) * e_up)
        a, b, k, x = ghost_share(fs, fn, fm, fw, fe)
        share += on_s * ((a - x * j_end) * s + (b * j_lo) * w_down + (k * j_hi) * e_down)
        a, b, k, x = ghost_share(fn, fs, fm, fw, fe)
        share += on_n * ((a - x * j_end) * n + (b * j_lo) * w_up + (k * j_hi) * e_up)
        out[c] = jnp.where(inside, share, step)
        return 0

    lax.fori_loop(0, C, channel, 0, unroll=2)


def merge(z, which, anc, base, *refs):
    pieces, out, twice = refs[:-2], refs[-2], refs[-1]
    g, d = lax.axis_index("grp"), lax.axis_index("dev")
    n = nest_at(z, anc, g // z.S * z.NB + d // z.Y)
    r, q = anc[0, n], anc[1, n]
    start = lax.rem(g * z.TR - r + 2 * z.G * z.TR, z.FR)
    shift_q = lax.rem(q - d * z.TC + 2 * z.D * z.TC, z.FC)
    i = iota((z.TR, LANES), 0) + (g * z.TR - r)
    j = iota((z.TR, LANES), 1) + (d * z.TC - q)
    inside = (i >= 0) & (i < z.FR) & (j >= 0) & (j < z.FC)
    sub = iota((z.M, LANES), 0)
    part = lax.rem(g, z.S)
    size = z.CS * z.M
    for k in range(z.S):
        if k not in which:
            other = lax.rem(part - k + z.S, z.S) * z.CS
            out[pl.ds(other, z.CS)] = base[pl.ds(other, z.CS)]
    for piece, k in zip(pieces, which):
        first = lax.rem(part - k + z.S, z.S) * z.CS
        for c in range(z.CS):
            for m in range(z.D):
                x = piece[m, c * z.M : (c + 1) * z.M, :]
                if m + 1 < z.D:
                    row = piece[m + 1, size + c : size + c + 1, :]
                    x += jnp.where(sub == z.M - 1, row, 0.0)
                if m > 0:
                    row = piece[m - 1, size + z.CS + c : size + z.CS + c + 1, :]
                    x += jnp.where(sub == 0, row, 0.0)
                twice[c % 4, m * z.M : (m + 1) * z.M, :] = x
                if m * z.M < z.TR:
                    twice[c % 4, z.FR + m * z.M : z.FR + (m + 1) * z.M, :] = x
            x = pltpu.roll(twice[c % 4, pl.ds(start, z.TR), :], shift_q, 1)
            out[first + c] = base[first + c] + jnp.where(inside, x, 0.0)


def shards(parent, nest, anchor, diff, cour):
    z = Sizes(parent, nest, anchor, lax.axis_size("grp"), lax.axis_size("dev"))
    sds = lambda *shape: jax.ShapeDtypeStruct(shape, F32)
    vmem = lambda *shape: pltpu.VMEM(shape, F32)
    to_grp = lambda x, k: lax.ppermute(x, "grp", [(a, a ^ k) for a in range(z.G)])

    anchor = anchor.T
    message = sds(z.EDGE + z.TR, LANES)
    edge_tile = vmem(z.L, z.C, 8, z.W)
    ring, up, dn = call(
        functools.partial(ring_parts, z),
        [sds(z.G, z.RG, LANES), message, message],
        (anchor,),
        (parent,),
        [edge_tile, edge_tile, pltpu.SemaphoreType.DMA((2,))],
        (nest,),
    )
    nest, ring, up, dn = lax.optimization_barrier((nest, ring, up, dn))
    forward = [(k, k + 1) for k in range(z.D - 1)]
    up = lax.ppermute(up, "dev", forward)
    dn = lax.ppermute(dn, "dev", [(b, a) for a, b in forward])
    ring = lax.all_to_all(ring, "grp", 0, 0, tiled=True)
    *chunks, phases = call(
        functools.partial(partial_averages, z),
        [sds(z.R1, LANES)] * z.S + [sds(3, z.L * z.C * z.H, LANES)],
        (diff, cour),
        (),
        [pltpu.VMEM(nest.shape, F32), pltpu.SemaphoreType.DMA((z.L,))],
        (nest,),
    )
    chunks, ring, up, dn = lax.optimization_barrier((chunks, ring, up, dn))
    got = [chunks[0]] + [to_grp(chunks[k % z.S], k) for k in range(1, z.G)]
    ring, edges = call(
        functools.partial(ring_next, z),
        [sds(z.D, z.RG2, LANES), sds(2 * z.C, LANES)],
        (),
        (ring,),
        [vmem(z.RING, LANES)],
    )
    ring = lax.all_to_all(ring, "dev", 0, 0, tiled=True)
    got, ring, edges = lax.optimization_barrier((got, ring, edges))

    (avg,) = call(functools.partial(pick_band, z), [sds(z.D, z.R2, LANES)], (anchor,), got)
    avg, phases, edges = lax.optimization_barrier((avg, phases, edges))
    avg = lax.all_to_all(avg, "dev", 0, 0, tiled=True)
    (nest_out,) = call(
        functools.partial(nest_steps, z),
        [jax.ShapeDtypeStruct(nest.shape, F32)],
        (diff, cour),
        (phases, ring, up, dn),
        [
            vmem(3, z.L * z.C * z.H, LANES),
            vmem(z.RG2, LANES),
            vmem(z.EDGE, LANES),
            vmem(z.EDGE, LANES),
        ],
    )
    (out,) = call(
        functools.partial(parent_step, z),
        [jax.ShapeDtypeStruct(parent.shape, F32)],
        (anchor, diff, cour),
        (parent, edges, up, dn, ring),
    )
    avg, nest_out, out = lax.optimization_barrier((avg, nest_out, out))
    pieces = [avg]
    for k in range(1, z.S):
        pairs = [(a, a // z.S * z.S + (a + k) % z.S) for a in range(z.G)]
        pieces.append(lax.ppermute(avg, "grp", pairs))
    for which in ([0], list(range(1, z.S))):
        (out,) = call(
            functools.partial(merge, z, which),
            [jax.ShapeDtypeStruct(parent.shape, F32)],
            (anchor,),
            (out, *[pieces[k] for k in which]),
            [vmem(4, z.FR + z.TR, LANES)],
        )
    return out, nest_out


def solution(mesh):
    placed = (P(None, "grp", "dev"), P("grp", None, "dev", None), P(), P(), P())
    return jax.shard_map(
        shards,
        mesh=mesh,
        in_specs=placed,
        out_specs=(P(None, "grp", "dev"), P("grp", None, "dev", None)),
        check_vma=False,
    )
```

```python
import functools

import jax
import jax.numpy as jnp
from jax import lax
from jax.experimental import pallas as pl
from jax.experimental.pallas import tpu as pltpu
from jax.sharding import PartitionSpec as P

F32 = jnp.float32
BF16 = jnp.bfloat16
LANES = 128
VMEM_LIMIT = 63 * 1024 * 1024
MID, EAST, WEST, NORTH, SOUTH = range(5)


class Sizes:
    def __init__(self, parent, nest, anchor, grp_count, dev_count):
        self.C, self.TR, self.TC = parent.shape
        self.L, _, self.H, self.W = nest.shape
        self.N = anchor.shape[0]
        self.G, self.D = grp_count, dev_count
        self.M = self.H // 3
        self.FR, self.FC = self.M * self.D, self.W // 3
        self.S = self.G // 2
        self.NB = self.N // 2
        self.Y = self.D // self.NB
        self.CS = self.C // self.S
        self.BR, self.BC = self.S * self.TR, self.Y * self.TC
        self.R1 = self.L * self.CS * (self.M + 2)
        self.R2 = self.CS * (self.M + 2)
        self.RING = self.FR + self.L * 2 * self.C
        self.RG = self.RING + self.C
        self.RG2 = 16 + self.L * self.C + 8
        self.HALO = self.L * self.C * 3
        self.EDGE = 3 * self.HALO
        assert self.H == 24 and self.FC == LANES and self.TC == LANES
        assert self.FR >= self.TR and self.L == 2


def call(body, out_shape, smem, args, scratch=(), raw=(), early=None):
    moved = [*smem, *args]
    n_in, n_raw, n_out = len(moved), len(raw), len(out_shape)
    place = pl.BlockSpec(memory_space=pltpu.HBM)

    def kernel(*refs):
        source, refs = refs[:n_in], refs[n_in:]
        stay, refs = refs[:n_raw], refs[n_raw:]
        target, refs = refs[:n_out], refs[n_out:]
        inner, refs = refs[:n_in], refs[n_in:]
        result, refs = refs[:n_out], refs[n_out:]
        extra, sem = refs[:-1], refs[-1]
        fetch = [pltpu.make_async_copy(a, b, sem.at[k]) for k, (a, b) in enumerate(zip(source, inner))]
        for copy in fetch:
            copy.start()
        for copy in fetch:
            copy.wait()
        store = [
            pltpu.make_async_copy(a, b, sem.at[n_in + k]) for k, (a, b) in enumerate(zip(result, target))
        ]
        if early is None:
            body(*inner, *stay, *result, *extra)
        else:
            body(*inner, *stay, *result, *extra, store[early].start)
        for k, copy in enumerate(store):
            if k != early:
                copy.start()
        for copy in store:
            copy.wait()

    return pl.pallas_call(
        kernel,
        out_shape=list(out_shape),
        in_specs=[place] * (n_in + n_raw),
        out_specs=[place] * n_out,
        scratch_shapes=[
            *[pltpu.SMEM(x.shape, x.dtype) for x in smem],
            *[pltpu.VMEM(x.shape, x.dtype) for x in args],
            *[pltpu.VMEM(x.shape, x.dtype) for x in out_shape],
            *scratch,
            pltpu.SemaphoreType.DMA((n_in + n_out,)),
        ],
        compiler_params=pltpu.CompilerParams(vmem_limit_bytes=VMEM_LIMIT),
    )(*moved, *raw)


def iota(shape, dim):
    return lax.broadcasted_iota(jnp.int32, shape, dim)


def split_dot(x, table):
    high = x.astype(BF16)
    low = (x - high.astype(F32)).astype(BF16)
    return jnp.dot(jnp.concatenate([high, low], axis=1), table, preferred_element_type=F32)


def nest_at(z, anc, band):
    found = 0
    for n in range(z.N):
        found += jnp.where(anc[0, n] // z.BR * z.NB + anc[1, n] // z.BC == band, n, 0)
    return found


def weights(diff, cour, c, times):
    splat = lambda ref, k: jnp.full((8, LANES), ref[k, c], F32)
    east = times * splat(diff, 0)
    north = times * splat(diff, 1)
    west = east + splat(cour, 0)
    south = north + splat(cour, 1)
    return 1.0 - (east + west) - (north + south), east, west, north, south


def ghost_share(inject, back, mid, plus, minus):
    stay = mid + inject
    m0 = inject * (1.0 + stay + mid * stay + inject * (stay + back) + 2.0 * plus * minus)
    p1 = inject * plus * (1.0 + 2.0 * stay)
    p2 = inject * plus * plus
    n1 = inject * minus * (1.0 + 2.0 * stay)
    n2 = inject * minus * minus
    ninth = 1.0 / 9.0
    same = (3.0 * m0 + 2.0 * p1 + p2 + 2.0 * n1 + n2) * ninth
    return same, (p1 + 2.0 * p2) * ninth, (n1 + 2.0 * n2) * ninth, inject * plus * minus * ninth


class Strip:
    def __init__(self):
        sub = iota((8, LANES), 0)
        lane = iota((8, LANES), 1)
        self.high = [sub == 0, sub == 4]
        self.low = [sub == 7, sub == 3]
        self.any_high = (sub == 0) | (sub == 4)
        self.any_low = (sub == 7) | (sub == 3)
        self.first, self.last = lane == 0, lane == LANES - 1

    def east(self, x, ghost):
        return jnp.where(self.last, ghost, pltpu.roll(x, LANES - 1, 1))

    def west(self, x, ghost):
        return jnp.where(self.first, ghost, pltpu.roll(x, 1, 1))

    def north(self, mains, cap):
        up = [pltpu.roll(m, 7, 0) for m in mains]
        cap_up = pltpu.roll(cap, 7, 0)
        new = [jnp.where(self.low[l], cap_up, up[l]) for l in range(2)]
        return new, jnp.where(self.low[0], up[0], jnp.where(self.low[1], up[1], 0.0))

    def south(self, mains, cap):
        down = [pltpu.roll(m, 1, 0) for m in mains]
        cap_down = pltpu.roll(cap, 1, 0)
        new = [jnp.where(self.high[l], cap_down, down[l]) for l in range(2)]
        return new, jnp.where(self.high[0], down[0], jnp.where(self.high[1], down[1], 0.0))

    def step(self, u, co, west_ghost, east_ghost):
        n_in = [self.north([u[0][0][x], u[1][0][x]], u[2][0][x]) for x in range(3)]
        s_in = [self.south([u[0][2][x], u[1][2][x]], u[2][2][x]) for x in range(3)]
        pick = lambda pair, k: pair[1] if k == 2 else pair[0][k]
        new = []
        for k in range(3):
            rows = []
            for y in range(3):
                row = u[k][y]
                e = [row[1], row[2], self.east(row[0], east_ghost[k])]
                w = [self.west(row[2], west_ghost[k]), row[0], row[1]]
                cells = []
                for x in range(3):
                    n = u[k][y + 1][x] if y < 2 else pick(n_in[x], k)
                    s = u[k][y - 1][x] if y > 0 else pick(s_in[x], k)
                    cells.append(
                        co[MID] * row[x]
                        + (co[EAST] * e[x] + co[WEST] * w[x])
                        + (co[NORTH] * n + co[SOUTH] * s)
                    )
                rows.append(cells)
            new.append(rows)
        return new

    def pooled_step(self, u, co):
        ends = []
        for k in range(3):
            row = [u[k][y][0] + u[k][y][1] + u[k][y][2] for y in range(3)]
            col = [u[k][0][x] + u[k][1][x] + u[k][2][x] for x in (0, 2)]
            ends.append((row[0], row[2], col[0], col[1], row[0] + row[1] + row[2]))
        n_in = self.north([ends[0][0], ends[1][0]], ends[2][0])
        s_in = self.south([ends[0][1], ends[1][1]], ends[2][1])
        pick = lambda pair, k: pair[1] if k == 2 else pair[0][k]
        out = []
        for k in range(3):
            row0, row2, col0, col2, total = ends[k]
            flux_x = co[EAST] * (self.east(col0, 0.0) - col0)
            flux_x += co[WEST] * (self.west(col2, 0.0) - col2)
            flux_y = co[NORTH] * (pick(n_in, k) - row0) + co[SOUTH] * (pick(s_in, k) - row2)
            out.append(total + (flux_x + flux_y))
        return out


def phase_rows(z, ref, l, c, y, x):
    got = ref[x, pl.ds((l * z.C + c) * z.H + y, z.M, 3), :]
    return got if l == 0 else pltpu.roll(got, 4, 0)


def partial_averages(z, diff, cour, nest, *refs):
    out, (phases, strips, sem, store_phases) = refs[: z.S], refs[z.S :]
    fetch = [pltpu.make_async_copy(nest.at[l], strips.at[l], sem.at[l]) for l in range(z.L)]
    for copy in fetch:
        copy.start()
    d = lax.axis_index("dev")
    own = lax.rem(lax.axis_index("grp"), z.S)
    C, M, CS = z.C, z.M, z.CS
    fine = lax.rem(iota((2 * z.W, z.W), 0), z.W)
    place = iota((2 * z.W, z.W), 1)
    at = lax.rem(place, LANES) * 3 + place // LANES
    deal = jnp.where(fine == at, 1.0, 0.0).astype(BF16)
    rows = C * z.H
    for l in range(z.L):
        fetch[l].wait()
        dealt = split_dot(strips[l].reshape(rows, z.W), deal)
        for x in range(3):
            phases[x, l * rows : (l + 1) * rows, :] = dealt[:, x * LANES : (x + 1) * LANES]
    store_phases()
    strip = Strip()
    keep_high = strip.any_low | (strip.any_high & (d < z.D - 1))
    keep_low = strip.any_high | (strip.any_low & (d > 0))
    zero = jnp.zeros((8, LANES), F32)
    ghosts = [0.0] * 3
    base = z.L * CS * M

    def hold(u):
        cap = [
            [jnp.where(keep_high, v, 0.0) for v in u[2][0]],
            u[2][1],
            [jnp.where(keep_low, v, 0.0) for v in u[2][2]],
        ]
        return [u[0], u[1], cap]

    for part in range(z.S):

        def channel(i, _, to=out[part], first=jnp.bitwise_xor(own, part) * CS):
            c = first + i
            co = weights(diff, cour, c, 3.0)
            u = [
                [[phase_rows(z, phases, l, c, y, x) for x in range(3)] for y in range(3)]
                for l in range(2)
            ]
            u.append([[zero] * 3] * 3)
            for _step in range(2):
                u = hold(strip.step(u, co, ghosts, ghosts))
            got = [v * (1.0 / 9.0) for v in strip.pooled_step(u, co)]
            got[1] = pltpu.roll(got[1], 4, 0)
            for l in range(2):
                row = pl.multiple_of((l * CS + i) * M, M)
                to[pl.ds(row, M), :] = got[l]
                for side, sub in enumerate(((7, 3), (0, 4))):
                    row = base + (l * 2 + side) * CS + i
                    to[pl.ds(row, 1), :] = got[2][sub[l] : sub[l] + 1]
            return 0

        lax.fori_loop(0, CS, channel, 0, unroll=2)


def pick_band(z, anc, *refs):
    got, out = refs[: z.G], refs[z.G]
    g = lax.axis_index("grp")
    top = g // z.S * z.NB
    base, size = z.L * z.CS * z.M, z.CS * z.M
    for band in range(z.NB):
        n = nest_at(z, anc, top + band)
        of = n // z.L
        slot = jnp.bitwise_xor(of, g)
        first = n - of * z.L == 0
        for k in range(z.G):

            @pl.when(slot == k)
            def _(k=k, first=first, band=band):
                main = jnp.where(first, got[k][:size, :], got[k][size : 2 * size, :])
                edge = jnp.where(
                    first,
                    got[k][base : base + 2 * z.CS, :],
                    got[k][base + 2 * z.CS : base + 4 * z.CS, :],
                )
                for y in range(z.Y):
                    out[band * z.Y + y, :size, :] = main
                    out[band * z.Y + y, size:, :] = edge


def ring_parts(z, anc, parent, nest, buf, up, dn, tail, head, sem):
    fetch = [
        pltpu.make_async_copy(nest.at[:, :, z.H - 8 :, :], tail, sem.at[0]),
        pltpu.make_async_copy(nest.at[:, :, :8, :], head, sem.at[1]),
    ]
    for copy in fetch:
        copy.start()
    g, d = lax.axis_index("grp"), lax.axis_index("dev")
    row_base, col_base = g * z.TR, d * z.TC
    lane_t = iota((z.TR, LANES), 1)
    lane_f = iota((z.FR, LANES), 1)
    row_f = iota((z.FR, LANES), 0)
    lane_c = iota((z.C, LANES), 1)
    buf[...] = jnp.zeros_like(buf)

    def nest_ring(n, _):
        to = n // z.L
        l = n - to * z.L
        slot = to
        r, q = anc[0, n], anc[1, n]
        rows_meet = (r < row_base + z.TR) & (r + z.FR > row_base)
        cols_meet = (q < col_base + z.TC) & (q + z.FC > col_base)
        shift_r = lax.rem(row_base - r + 2 * z.G * z.TR, z.FR)
        shift_q = lax.rem(col_base - q + 2 * z.D * z.TC, z.FC)
        for side in range(2):
            col = (q - 1 if side == 0 else q + z.FC) - col_base
            first = (l * 2 + side) * z.C

            @pl.when(rows_meet & (col >= 0) & (col < z.TC))
            def _(col=col, first=first):
                acc = jnp.zeros((z.TR, LANES), F32)
                for c in range(z.C):
                    at = first + c
                    moved = pltpu.roll(parent[c], lax.rem(at - col + LANES, LANES), 1)
                    acc = jnp.where(lane_t == at, moved, acc)
                if z.FR > z.TR:
                    acc = jnp.concatenate([acc, jnp.zeros((z.FR - z.TR, LANES), F32)], axis=0)
                acc = pltpu.roll(acc, shift_r, 0)
                y = row_f + (r - row_base)
                good = (y >= 0) & (y < z.TR) & (lane_f >= first) & (lane_f < first + z.C)
                buf[slot, : z.FR, :] = jnp.where(good, acc, buf[slot, : z.FR, :])

            row = (r - 1 if side == 0 else r + z.FR) - row_base

            @pl.when(cols_meet & (row >= 0) & (row < z.TR))
            def _(row=row, first=first):
                rows = jnp.concatenate(
                    [parent[c, pl.ds(row, 1), :] for c in range(z.C)], axis=0
                )
                x = lane_c + (q - col_base)
                moved = jnp.where((x >= 0) & (x < z.TC), pltpu.roll(rows, shift_q, 1), 0.0)
                buf[slot, pl.ds(pl.multiple_of(z.FR + first, 8), z.C), :] = moved

        return 0

    lax.fori_loop(0, z.N, nest_ring, 0)
    for to in range(z.G):
        edge = jnp.where(to > g, z.TR - 1, 0)
        for c in range(z.C):
            buf[to, z.RING + c : z.RING + c + 1, :] = parent[c, pl.ds(edge, 1), :]
    first = jnp.zeros((z.TR, LANES), F32)
    last = first
    for c in range(z.C):
        first = jnp.where(lane_t == c, pltpu.roll(parent[c], c, 1) if c else parent[c], first)
        last = jnp.where(lane_t == c, pltpu.roll(parent[c], c + 1, 1), last)
    up[z.EDGE :, :] = last
    dn[z.EDGE :, :] = first
    for copy in fetch:
        copy.wait()
    for l in range(z.L):
        for c in range(z.C):
            for x in range(3):
                at = x * z.HALO + 3 * (l * z.C + c)
                lanes = slice(x * LANES, (x + 1) * LANES)
                up[at : at + 3, :] = tail[l, c, 5:8, lanes]
                dn[at : at + 3, :] = head[l, c, 0:3, lanes]


def ring_next(z, got, out, edges, slab):
    g, d = lax.axis_index("grp"), lax.axis_index("dev")
    C, L, FR, M = z.C, z.L, z.FR, z.M
    total = got[0, : z.RING, :]
    for k in range(1, z.G):
        total = total + got[k, : z.RING, :]
    slab[...] = total
    sub = iota((8, LANES), 0)
    for to in range(z.D):
        out[to, :M, :] = slab[to * M : (to + 1) * M, :]
        hi = min(to * M + M, FR - 1)
        lo = max(to * M - 1, 0)
        hi, lo = slab[hi : hi + 1, :], slab[lo : lo + 1, :]
        out[to, M:16, :] = jnp.where(sub == 0, hi, jnp.where(sub == 7, lo, 0.0))
        for l in range(L):
            at = 16 + l * C
            if to == 0 or to == z.D - 1:
                k = FR + (l * 2 + (0 if to == 0 else 1)) * C
                out[to, at : at + C, :] = slab[k : k + C, :]
            else:
                out[to, at : at + C, :] = jnp.zeros((C, LANES), F32)
    before, after = jnp.maximum(g - 1, 0), jnp.minimum(g + 1, z.G - 1)
    edges[:C, :] = jnp.where(g > 0, got[before, z.RING :, :], 0.0)
    edges[C:, :] = jnp.where(g < z.G - 1, got[after, z.RING :, :], 0.0)
    lane = iota((8, LANES), 1)
    first = jnp.zeros((8, LANES), F32)
    last = first
    for c in range(C):
        lo = edges[c : c + 1, :]
        hi = edges[C + c : C + c + 1, :]
        cap = jnp.where(sub == 0, hi, jnp.where(sub == 7, lo, 0.0))
        first = jnp.where(lane == c, pltpu.roll(cap, c, 1) if c else cap, first)
        last = jnp.where(lane == c, pltpu.roll(cap, c + 1, 1), last)
    for to in range(z.D):
        out[to, z.RG2 - 8 :, :] = jnp.where(to > d, last, first)


def nest_steps(z, diff, cour, phases, got, up_in, dn_in, out, back, ring, up, dn):
    d = lax.axis_index("dev")
    C, M = z.C, z.M
    strip = Strip()
    fine = lax.rem(iota((2 * z.W, z.W), 0), z.W)
    place = iota((2 * z.W, z.W), 1)
    deal = jnp.where(fine == lax.rem(place, LANES) * 3 + place // LANES, 1.0, 0.0).astype(BF16)
    for source, target in ((up_in, up), (dn_in, dn)):
        halo = [source[x * z.HALO : (x + 1) * z.HALO, :] for x in range(3)]
        dealt = split_dot(jnp.concatenate(halo, axis=1), deal)
        for x in range(3):
            target[x * z.HALO : (x + 1) * z.HALO, :] = dealt[:, x * LANES : (x + 1) * LANES]
    total = got[0]
    for k in range(1, z.D):
        total = total + got[k]
    ring[...] = total
    side_main = [ring[:M, :], pltpu.roll(ring[:M, :], 4, 0)]
    side_cap = jnp.where(
        strip.any_high, ring[M : M + 1, :], jnp.where(strip.any_low, ring[15:16, :], 0.0)
    )
    hold_low, hold_high = strip.any_low & (d == 0), strip.any_high & (d == z.D - 1)
    nest_1 = strip.high[1] | strip.low[1]

    def channel(c, _):
        co = weights(diff, cour, c, 3.0)
        u = [
            [[phase_rows(z, phases, l, c, y, x) for x in range(3)] for y in range(3)]
            for l in range(2)
        ]
        cap = []
        for y in range(3):
            row = []
            for x in range(3):
                v = jnp.zeros((8, LANES), F32)
                for l in range(2):
                    at = x * z.HALO + (l * C + c) * 3 + y
                    v = jnp.where(strip.high[l], dn[pl.ds(at, 1), :], v)
                    v = jnp.where(strip.low[l], up[pl.ds(at, 1), :], v)
                row.append(v)
            cap.append(row)
        u.append(cap)
        end = jnp.where(nest_1, ring[pl.ds(16 + C + c, 1), :], ring[pl.ds(16 + c, 1), :])
        west, east = [], []
        for side, lane, ghosts in ((0, 0, west), (1, LANES - 1, east)):
            turn = [lax.rem(lane - ((l * 2 + side) * C + c) + LANES, LANES) for l in range(2)]
            for l in range(2):
                ghosts.append(pltpu.roll(side_main[l], turn[l], 1))
            caps = [pltpu.roll(side_cap, turn[l], 1) for l in range(2)]
            ghosts.append(jnp.where(nest_1, caps[1], caps[0]))

        def hold(u):
            cap = [
                [jnp.where(hold_high, end, v) for v in u[2][0]],
                u[2][1],
                [jnp.where(hold_low, end, v) for v in u[2][2]],
            ]
            return [u[0], u[1], cap]

        u = hold(u)
        for k in range(3):
            u = strip.step(u, co, west, east)
            if k < 2:
                u = hold(u)
        for l in range(2):
            for y in range(3):
                for x in range(3):
                    v = u[l][y][x]
                    v = v if l == 0 else pltpu.roll(v, 4, 0)
                    back[x, pl.ds((l * C + c) * z.H + y, M, 3), :] = v
        return 0

    lax.fori_loop(0, C, channel, 0, unroll=2)
    fine = iota((2 * z.W, z.W), 1)
    place = lax.rem(iota((2 * z.W, z.W), 0), z.W)
    at = lax.rem(place, LANES) * 3 + place // LANES
    undeal = jnp.where(fine == at, 1.0, 0.0).astype(BF16)
    done = split_dot(jnp.concatenate([back[0], back[1], back[2]], axis=1), undeal)
    out[...] = done.reshape(z.L, C, z.H, z.W)


def parent_step(z, anc, diff, cour, parent, edges, up_in, dn_in, got, out):
    g, d = lax.axis_index("grp"), lax.axis_index("dev")
    C = z.C
    rows = z.TR + 8
    n = nest_at(z, anc, g // z.S * z.NB + d // z.Y)
    i = iota((z.TR, LANES), 0) + (g * z.TR - anc[0, n])
    j = iota((z.TR, LANES), 1) + (d * z.TC - anc[1, n])
    inside = (i >= 0) & (i < z.FR) & (j >= 0) & (j < z.FC)
    one = lambda cond: jnp.where(cond, 1.0, 0.0).astype(F32)
    on_w, on_e = one(inside & (j == 0)), one(inside & (j == z.FC - 1))
    on_s, on_n = one(inside & (i == 0)), one(inside & (i == z.FR - 1))
    i_end, j_end = one((i == 0) | (i == z.FR - 1)), one((j == 0) | (j == z.FC - 1))
    i_lo, i_hi = one(i > 0), one(i < z.FR - 1)
    j_lo, j_hi = one(j > 0), one(j < z.FC - 1)
    lane = iota((rows, LANES), 1)
    sub = iota((8, LANES), 0)

    cap_w = jnp.where(d > 0, got[jnp.maximum(d - 1, 0), z.RG2 - 8 :, :], 0.0)
    cap_e = jnp.where(d < z.D - 1, got[jnp.minimum(d + 1, z.D - 1), z.RG2 - 8 :, :], 0.0)
    col_w = jnp.concatenate([up_in[z.EDGE :, :], cap_w], axis=0)
    col_e = jnp.concatenate([dn_in[z.EDGE :, :], cap_e], axis=0)

    def channel(c, _):
        co = [v[:1] for v in weights(diff, cour, c, 1.0)]
        fm, fe, fw, fn, fs = [v[:1] for v in weights(diff, cour, c, 3.0)]
        lo = edges[pl.ds(c, 1), :]
        hi = edges[pl.ds(C + c, 1), :]
        cap = jnp.where(sub == 0, hi, jnp.where(sub == 7, lo, 0.0))
        full = jnp.concatenate([parent[c], cap], axis=0)
        w_in = pltpu.roll(col_w, lax.rem(LANES - c, LANES), 1)
        e_in = pltpu.roll(col_e, LANES - 1 - c, 1)
        w_all = jnp.where(lane == 0, w_in, pltpu.roll(full, 1, 1))
        e_all = jnp.where(lane == LANES - 1, e_in, pltpu.roll(full, LANES - 1, 1))
        up = lambda x: pltpu.roll(x, rows - 1, 0)[: z.TR]
        down = lambda x: pltpu.roll(x, 1, 0)[: z.TR]
        mid = full[: z.TR]
        w, e, n, s = w_all[: z.TR], e_all[: z.TR], up(full), down(full)
        w_up, w_down, e_up, e_down = up(w_all), down(w_all), up(e_all), down(e_all)
        step = (
            co[MID] * mid
            + (co[EAST] * e + co[WEST] * w)
            + (co[NORTH] * n + co[SOUTH] * s)
        )
        a, b, k, x = ghost_share(fw, fe, fm, fs, fn)
        share = on_w * ((a - x * i_end) * w + (b * i_lo) * w_down + (k * i_hi) * w_up)
        a, b, k, x = ghost_share(fe, fw, fm, fs, fn)
        share += on_e * ((a - x * i_end) * e + (b * i_lo) * e_down + (k * i_hi) * e_up)
        a, b, k, x = ghost_share(fs, fn, fm, fw, fe)
        share += on_s * ((a - x * j_end) * s + (b * j_lo) * w_down + (k * j_hi) * e_down)
        a, b, k, x = ghost_share(fn, fs, fm, fw, fe)
        share += on_n * ((a - x * j_end) * n + (b * j_lo) * w_up + (k * j_hi) * e_up)
        out[c] = jnp.where(inside, share, step)
        return 0

    lax.fori_loop(0, C, channel, 0, unroll=2)


def merge(z, which, anc, base, *refs):
    pieces, out, twice = refs[:-2], refs[-2], refs[-1]
    g, d = lax.axis_index("grp"), lax.axis_index("dev")
    n = nest_at(z, anc, g // z.S * z.NB + d // z.Y)
    r, q = anc[0, n], anc[1, n]
    start = lax.rem(g * z.TR - r + 2 * z.G * z.TR, z.FR)
    shift_q = lax.rem(q - d * z.TC + 2 * z.D * z.TC, z.FC)
    i = iota((z.TR, LANES), 0) + (g * z.TR - r)
    j = iota((z.TR, LANES), 1) + (d * z.TC - q)
    inside = (i >= 0) & (i < z.FR) & (j >= 0) & (j < z.FC)
    sub = iota((z.M, LANES), 0)
    part = lax.rem(g, z.S)
    size = z.CS * z.M
    for k in range(z.S):
        if k not in which:
            other = lax.rem(part - k + z.S, z.S) * z.CS
            out[pl.ds(other, z.CS)] = base[pl.ds(other, z.CS)]
    for piece, k in zip(pieces, which):
        first = lax.rem(part - k + z.S, z.S) * z.CS
        for c in range(z.CS):
            for m in range(z.D):
                x = piece[m, c * z.M : (c + 1) * z.M, :]
                if m + 1 < z.D:
                    row = piece[m + 1, size + c : size + c + 1, :]
                    x += jnp.where(sub == z.M - 1, row, 0.0)
                if m > 0:
                    row = piece[m - 1, size + z.CS + c : size + z.CS + c + 1, :]
                    x += jnp.where(sub == 0, row, 0.0)
                twice[c % 4, m * z.M : (m + 1) * z.M, :] = x
                if m * z.M < z.TR:
                    twice[c % 4, z.FR + m * z.M : z.FR + (m + 1) * z.M, :] = x
            x = pltpu.roll(twice[c % 4, pl.ds(start, z.TR), :], shift_q, 1)
            out[first + c] = base[first + c] + jnp.where(inside, x, 0.0)


def shards(parent, nest, anchor, diff, cour):
    z = Sizes(parent, nest, anchor, lax.axis_size("grp"), lax.axis_size("dev"))
    sds = lambda *shape: jax.ShapeDtypeStruct(shape, F32)
    vmem = lambda *shape: pltpu.VMEM(shape, F32)
    to_grp = lambda x, k: lax.ppermute(x, "grp", [(a, a ^ k) for a in range(z.G)])

    anchor = anchor.T
    *chunks, phases = call(
        functools.partial(partial_averages, z),
        [sds(z.R1, LANES)] * z.S + [sds(3, z.L * z.C * z.H, LANES)],
        (diff, cour),
        (),
        [pltpu.VMEM(nest.shape, F32), pltpu.SemaphoreType.DMA((z.L,))],
        (nest,),
        z.S,
    )
    parent, chunks = lax.optimization_barrier((parent, chunks))
    got = [chunks[0]] + [to_grp(chunks[k % z.S], k) for k in range(1, z.G)]
    message = sds(z.EDGE + z.TR, LANES)
    edge_tile = vmem(z.L, z.C, 8, z.W)
    ring, up, dn = call(
        functools.partial(ring_parts, z),
        [sds(z.G, z.RG, LANES), message, message],
        (anchor,),
        (parent,),
        [edge_tile, edge_tile, pltpu.SemaphoreType.DMA((2,))],
        (nest,),
    )
    got, ring, up, dn = lax.optimization_barrier((got, ring, up, dn))
    forward = [(k, k + 1) for k in range(z.D - 1)]
    up = lax.ppermute(up, "dev", forward)
    dn = lax.ppermute(dn, "dev", [(b, a) for a, b in forward])
    ring = lax.all_to_all(ring, "grp", 0, 0, tiled=True)
    ring, edges = call(
        functools.partial(ring_next, z),
        [sds(z.D, z.RG2, LANES), sds(2 * z.C, LANES)],
        (),
        (ring,),
        [vmem(z.RING, LANES)],
    )
    got, ring, edges = lax.optimization_barrier((got, ring, edges))
    ring = lax.all_to_all(ring, "dev", 0, 0, tiled=True)

    (avg,) = call(functools.partial(pick_band, z), [sds(z.D, z.R2, LANES)], (anchor,), got)
    avg, phases, edges, ring, up, dn = lax.optimization_barrier(
        (avg, phases, edges, ring, up, dn)
    )
    avg = lax.all_to_all(avg, "dev", 0, 0, tiled=True)
    (nest_out,) = call(
        functools.partial(nest_steps, z),
        [jax.ShapeDtypeStruct(nest.shape, F32)],
        (diff, cour),
        (phases, ring, up, dn),
        [
            vmem(3, z.L * z.C * z.H, LANES),
            vmem(z.RG2, LANES),
            vmem(z.EDGE, LANES),
            vmem(z.EDGE, LANES),
        ],
    )
    (out,) = call(
        functools.partial(parent_step, z),
        [jax.ShapeDtypeStruct(parent.shape, F32)],
        (anchor, diff, cour),
        (parent, edges, up, dn, ring),
    )
    avg, nest_out, out = lax.optimization_barrier((avg, nest_out, out))
    pieces = [avg]
    for k in range(1, z.S):
        pairs = [(a, a // z.S * z.S + (a + k) % z.S) for a in range(z.G)]
        pieces.append(lax.ppermute(avg, "grp", pairs))
    for which in ([0], list(range(1, z.S))):
        (out,) = call(
            functools.partial(merge, z, which),
            [jax.ShapeDtypeStruct(parent.shape, F32)],
            (anchor,),
            (out, *[pieces[k] for k in which]),
            [vmem(4, z.FR + z.TR, LANES)],
        )
    return out, nest_out


def solution(mesh):
    placed = (P(None, "grp", "dev"), P("grp", None, "dev", None), P(), P(), P())
    return jax.shard_map(
        shards,
        mesh=mesh,
        in_specs=placed,
        out_specs=(P(None, "grp", "dev"), P("grp", None, "dev", None)),
        check_vma=False,
    )
```

```python
import functools

import jax
import jax.numpy as jnp
from jax import lax
from jax.experimental import pallas as pl
from jax.experimental.pallas import tpu as pltpu
from jax.sharding import PartitionSpec as P

F32 = jnp.float32
BF16 = jnp.bfloat16
LANES = 128
VMEM_LIMIT = 63 * 1024 * 1024
MID, EAST, WEST, NORTH, SOUTH = range(5)


class Sizes:
    def __init__(self, parent, nest, anchor, grp_count, dev_count):
        self.C, self.TR, self.TC = parent.shape
        self.L, _, self.H, self.W = nest.shape
        self.N = anchor.shape[0]
        self.G, self.D = grp_count, dev_count
        self.M = self.H // 3
        self.FR, self.FC = self.M * self.D, self.W // 3
        self.S = self.G // 2
        self.NB = self.N // 2
        self.Y = self.D // self.NB
        self.CS = self.C // self.S
        self.BR, self.BC = self.S * self.TR, self.Y * self.TC
        self.R1 = self.L * self.CS * (self.M + 2)
        self.R2 = self.CS * (self.M + 2)
        self.RING = self.FR + self.L * 2 * self.C
        self.RG = self.RING + self.C
        self.RG2 = 16 + self.L * self.C + 8
        self.HALO = self.L * self.C * 3
        self.EDGE = 3 * self.HALO
        assert self.H == 24 and self.FC == LANES and self.TC == LANES
        assert self.FR >= self.TR and self.L == 2


def call(body, out_shape, smem, args, scratch=(), raw=(), early=None):
    moved = [*smem, *args]
    n_in, n_raw, n_out = len(moved), len(raw), len(out_shape)
    place = pl.BlockSpec(memory_space=pltpu.HBM)

    def kernel(*refs):
        source, refs = refs[:n_in], refs[n_in:]
        stay, refs = refs[:n_raw], refs[n_raw:]
        target, refs = refs[:n_out], refs[n_out:]
        inner, refs = refs[:n_in], refs[n_in:]
        result, refs = refs[:n_out], refs[n_out:]
        extra, sem = refs[:-1], refs[-1]
        fetch = [pltpu.make_async_copy(a, b, sem.at[k]) for k, (a, b) in enumerate(zip(source, inner))]
        for copy in fetch:
            copy.start()
        for copy in fetch:
            copy.wait()
        store = [
            pltpu.make_async_copy(a, b, sem.at[n_in + k]) for k, (a, b) in enumerate(zip(result, target))
        ]
        if early is None:
            body(*inner, *stay, *result, *extra)
        else:
            body(*inner, *stay, *result, *extra, store[early].start)
        for k, copy in enumerate(store):
            if k != early:
                copy.start()
        for copy in store:
            copy.wait()

    return pl.pallas_call(
        kernel,
        out_shape=list(out_shape),
        in_specs=[place] * (n_in + n_raw),
        out_specs=[place] * n_out,
        scratch_shapes=[
            *[pltpu.SMEM(x.shape, x.dtype) for x in smem],
            *[pltpu.VMEM(x.shape, x.dtype) for x in args],
            *[pltpu.VMEM(x.shape, x.dtype) for x in out_shape],
            *scratch,
            pltpu.SemaphoreType.DMA((n_in + n_out,)),
        ],
        compiler_params=pltpu.CompilerParams(vmem_limit_bytes=VMEM_LIMIT),
    )(*moved, *raw)


def iota(shape, dim):
    return lax.broadcasted_iota(jnp.int32, shape, dim)


def split_dot(x, table):
    high = x.astype(BF16)
    low = (x - high.astype(F32)).astype(BF16)
    return jnp.dot(jnp.concatenate([high, low], axis=1), table, preferred_element_type=F32)


def nest_at(z, anc, band):
    found = 0
    for n in range(z.N):
        found += jnp.where(anc[0, n] // z.BR * z.NB + anc[1, n] // z.BC == band, n, 0)
    return found


def weights(diff, cour, c, times):
    splat = lambda ref, k: jnp.full((8, LANES), ref[k, c], F32)
    east = times * splat(diff, 0)
    north = times * splat(diff, 1)
    west = east + splat(cour, 0)
    south = north + splat(cour, 1)
    return 1.0 - (east + west) - (north + south), east, west, north, south


def ghost_share(inject, back, mid, plus, minus):
    stay = mid + inject
    m0 = inject * (1.0 + stay + mid * stay + inject * (stay + back) + 2.0 * plus * minus)
    p1 = inject * plus * (1.0 + 2.0 * stay)
    p2 = inject * plus * plus
    n1 = inject * minus * (1.0 + 2.0 * stay)
    n2 = inject * minus * minus
    ninth = 1.0 / 9.0
    same = (3.0 * m0 + 2.0 * p1 + p2 + 2.0 * n1 + n2) * ninth
    return same, (p1 + 2.0 * p2) * ninth, (n1 + 2.0 * n2) * ninth, inject * plus * minus * ninth


class Strip:
    def __init__(self):
        sub = iota((8, LANES), 0)
        lane = iota((8, LANES), 1)
        self.high = [sub == 0, sub == 4]
        self.low = [sub == 7, sub == 3]
        self.any_high = (sub == 0) | (sub == 4)
        self.any_low = (sub == 7) | (sub == 3)
        self.first, self.last = lane == 0, lane == LANES - 1

    def east(self, x, ghost):
        return jnp.where(self.last, ghost, pltpu.roll(x, LANES - 1, 1))

    def west(self, x, ghost):
        return jnp.where(self.first, ghost, pltpu.roll(x, 1, 1))

    def north(self, mains, cap):
        up = [pltpu.roll(m, 7, 0) for m in mains]
        cap_up = pltpu.roll(cap, 7, 0)
        new = [jnp.where(self.low[l], cap_up, up[l]) for l in range(2)]
        return new, jnp.where(self.low[0], up[0], jnp.where(self.low[1], up[1], 0.0))

    def south(self, mains, cap):
        down = [pltpu.roll(m, 1, 0) for m in mains]
        cap_down = pltpu.roll(cap, 1, 0)
        new = [jnp.where(self.high[l], cap_down, down[l]) for l in range(2)]
        return new, jnp.where(self.high[0], down[0], jnp.where(self.high[1], down[1], 0.0))

    def step(self, u, co, west_ghost, east_ghost):
        n_in = [self.north([u[0][0][x], u[1][0][x]], u[2][0][x]) for x in range(3)]
        s_in = [self.south([u[0][2][x], u[1][2][x]], u[2][2][x]) for x in range(3)]
        pick = lambda pair, k: pair[1] if k == 2 else pair[0][k]
        new = []
        for k in range(3):
            rows = []
            for y in range(3):
                row = u[k][y]
                e = [row[1], row[2], self.east(row[0], east_ghost[k])]
                w = [self.west(row[2], west_ghost[k]), row[0], row[1]]
                cells = []
                for x in range(3):
                    n = u[k][y + 1][x] if y < 2 else pick(n_in[x], k)
                    s = u[k][y - 1][x] if y > 0 else pick(s_in[x], k)
                    cells.append(
                        co[MID] * row[x]
                        + (co[EAST] * e[x] + co[WEST] * w[x])
                        + (co[NORTH] * n + co[SOUTH] * s)
                    )
                rows.append(cells)
            new.append(rows)
        return new

    def pooled_step(self, u, co):
        ends = []
        for k in range(3):
            row = [u[k][y][0] + u[k][y][1] + u[k][y][2] for y in range(3)]
            col = [u[k][0][x] + u[k][1][x] + u[k][2][x] for x in (0, 2)]
            ends.append((row[0], row[2], col[0], col[1], row[0] + row[1] + row[2]))
        n_in = self.north([ends[0][0], ends[1][0]], ends[2][0])
        s_in = self.south([ends[0][1], ends[1][1]], ends[2][1])
        pick = lambda pair, k: pair[1] if k == 2 else pair[0][k]
        out = []
        for k in range(3):
            row0, row2, col0, col2, total = ends[k]
            flux_x = co[EAST] * (self.east(col0, 0.0) - col0)
            flux_x += co[WEST] * (self.west(col2, 0.0) - col2)
            flux_y = co[NORTH] * (pick(n_in, k) - row0) + co[SOUTH] * (pick(s_in, k) - row2)
            out.append(total + (flux_x + flux_y))
        return out


def phase_rows(z, ref, l, c, y, x):
    got = ref[x, pl.ds((l * z.C + c) * z.H + y, z.M, 3), :]
    return got if l == 0 else pltpu.roll(got, 4, 0)


def partial_averages(z, diff, cour, nest, *refs):
    out, (phases, strips, sem, store_phases) = refs[: z.S], refs[z.S :]
    fetch = [pltpu.make_async_copy(nest.at[l], strips.at[l], sem.at[l]) for l in range(z.L)]
    for copy in fetch:
        copy.start()
    d = lax.axis_index("dev")
    own = lax.rem(lax.axis_index("grp"), z.S)
    C, M, CS = z.C, z.M, z.CS
    fine = lax.rem(iota((2 * z.W, z.W), 0), z.W)
    place = iota((2 * z.W, z.W), 1)
    at = lax.rem(place, LANES) * 3 + place // LANES
    deal = jnp.where(fine == at, 1.0, 0.0).astype(BF16)
    rows = C * z.H
    for l in range(z.L):
        fetch[l].wait()
        dealt = split_dot(strips[l].reshape(rows, z.W), deal)
        for x in range(3):
            phases[x, l * rows : (l + 1) * rows, :] = dealt[:, x * LANES : (x + 1) * LANES]
    store_phases()
    strip = Strip()
    keep_high = strip.any_low | (strip.any_high & (d < z.D - 1))
    keep_low = strip.any_high | (strip.any_low & (d > 0))
    zero = jnp.zeros((8, LANES), F32)
    ghosts = [0.0] * 3
    base = z.L * CS * M

    def hold(u):
        cap = [
            [jnp.where(keep_high, v, 0.0) for v in u[2][0]],
            u[2][1],
            [jnp.where(keep_low, v, 0.0) for v in u[2][2]],
        ]
        return [u[0], u[1], cap]

    for part in range(z.S):

        def channel(i, _, to=out[part], first=jnp.bitwise_xor(own, part) * CS):
            c = first + i
            co = weights(diff, cour, c, 3.0)
            u = [
                [[phase_rows(z, phases, l, c, y, x) for x in range(3)] for y in range(3)]
                for l in range(2)
            ]
            u.append([[zero] * 3] * 3)
            for _step in range(2):
                u = hold(strip.step(u, co, ghosts, ghosts))
            got = [v * (1.0 / 9.0) for v in strip.pooled_step(u, co)]
            got[1] = pltpu.roll(got[1], 4, 0)
            for l in range(2):
                row = pl.multiple_of((l * CS + i) * M, M)
                to[pl.ds(row, M), :] = got[l]
                for side, sub in enumerate(((7, 3), (0, 4))):
                    row = base + (l * 2 + side) * CS + i
                    to[pl.ds(row, 1), :] = got[2][sub[l] : sub[l] + 1]
            return 0

        lax.fori_loop(0, CS, channel, 0, unroll=2)


def pick_band(z, anc, *refs):
    got, out = refs[: z.G], refs[z.G]
    g = lax.axis_index("grp")
    top = g // z.S * z.NB
    base, size = z.L * z.CS * z.M, z.CS * z.M
    for band in range(z.NB):
        n = nest_at(z, anc, top + band)
        of = n // z.L
        slot = jnp.bitwise_xor(of, g)
        first = n - of * z.L == 0
        for k in range(z.G):

            @pl.when(slot == k)
            def _(k=k, first=first, band=band):
                main = jnp.where(first, got[k][:size, :], got[k][size : 2 * size, :])
                edge = jnp.where(
                    first,
                    got[k][base : base + 2 * z.CS, :],
                    got[k][base + 2 * z.CS : base + 4 * z.CS, :],
                )
                for y in range(z.Y):
                    out[band * z.Y + y, :size, :] = main
                    out[band * z.Y + y, size:, :] = edge


def ring_parts(z, anc, parent, nest, buf, up, dn, tail, head, sem):
    fetch = [
        pltpu.make_async_copy(nest.at[:, :, z.H - 8 :, :], tail, sem.at[0]),
        pltpu.make_async_copy(nest.at[:, :, :8, :], head, sem.at[1]),
    ]
    for copy in fetch:
        copy.start()
    g, d = lax.axis_index("grp"), lax.axis_index("dev")
    row_base, col_base = g * z.TR, d * z.TC
    lane_t = iota((z.TR, LANES), 1)
    lane_f = iota((z.FR, LANES), 1)
    row_f = iota((z.FR, LANES), 0)
    lane_c = iota((z.C, LANES), 1)
    buf[...] = jnp.zeros_like(buf)

    def nest_ring(n, _):
        to = n // z.L
        l = n - to * z.L
        slot = to
        r, q = anc[0, n], anc[1, n]
        rows_meet = (r < row_base + z.TR) & (r + z.FR > row_base)
        cols_meet = (q < col_base + z.TC) & (q + z.FC > col_base)
        shift_r = lax.rem(row_base - r + 2 * z.G * z.TR, z.FR)
        shift_q = lax.rem(col_base - q + 2 * z.D * z.TC, z.FC)
        for side in range(2):
            col = (q - 1 if side == 0 else q + z.FC) - col_base
            first = (l * 2 + side) * z.C

            @pl.when(rows_meet & (col >= 0) & (col < z.TC))
            def _(col=col, first=first):
                acc = jnp.zeros((z.TR, LANES), F32)
                for c in range(z.C):
                    at = first + c
                    moved = pltpu.roll(parent[c], lax.rem(at - col + LANES, LANES), 1)
                    acc = jnp.where(lane_t == at, moved, acc)
                if z.FR > z.TR:
                    acc = jnp.concatenate([acc, jnp.zeros((z.FR - z.TR, LANES), F32)], axis=0)
                acc = pltpu.roll(acc, shift_r, 0)
                y = row_f + (r - row_base)
                good = (y >= 0) & (y < z.TR) & (lane_f >= first) & (lane_f < first + z.C)
                buf[slot, : z.FR, :] = jnp.where(good, acc, buf[slot, : z.FR, :])

            row = (r - 1 if side == 0 else r + z.FR) - row_base

            @pl.when(cols_meet & (row >= 0) & (row < z.TR))
            def _(row=row, first=first):
                rows = jnp.concatenate(
                    [parent[c, pl.ds(row, 1), :] for c in range(z.C)], axis=0
                )
                x = lane_c + (q - col_base)
                moved = jnp.where((x >= 0) & (x < z.TC), pltpu.roll(rows, shift_q, 1), 0.0)
                buf[slot, pl.ds(pl.multiple_of(z.FR + first, 8), z.C), :] = moved

        return 0

    lax.fori_loop(0, z.N, nest_ring, 0)
    for to in range(z.G):
        edge = jnp.where(to > g, z.TR - 1, 0)
        for c in range(z.C):
            buf[to, z.RING + c : z.RING + c + 1, :] = parent[c, pl.ds(edge, 1), :]
    first = jnp.zeros((z.TR, LANES), F32)
    last = first
    for c in range(z.C):
        first = jnp.where(lane_t == c, pltpu.roll(parent[c], c, 1) if c else parent[c], first)
        last = jnp.where(lane_t == c, pltpu.roll(parent[c], c + 1, 1), last)
    up[z.EDGE :, :] = last
    dn[z.EDGE :, :] = first
    for copy in fetch:
        copy.wait()
    for l in range(z.L):
        for c in range(z.C):
            for x in range(3):
                at = x * z.HALO + 3 * (l * z.C + c)
                lanes = slice(x * LANES, (x + 1) * LANES)
                up[at : at + 3, :] = tail[l, c, 5:8, lanes]
                dn[at : at + 3, :] = head[l, c, 0:3, lanes]


def ring_next(z, got, out, edges, slab):
    g, d = lax.axis_index("grp"), lax.axis_index("dev")
    C, L, FR, M = z.C, z.L, z.FR, z.M
    total = got[0, : z.RING, :]
    for k in range(1, z.G):
        total = total + got[k, : z.RING, :]
    slab[...] = total
    sub = iota((8, LANES), 0)
    for to in range(z.D):
        out[to, :M, :] = slab[to * M : (to + 1) * M, :]
        hi = min(to * M + M, FR - 1)
        lo = max(to * M - 1, 0)
        hi, lo = slab[hi : hi + 1, :], slab[lo : lo + 1, :]
        out[to, M:16, :] = jnp.where(sub == 0, hi, jnp.where(sub == 7, lo, 0.0))
        for l in range(L):
            at = 16 + l * C
            if to == 0 or to == z.D - 1:
                k = FR + (l * 2 + (0 if to == 0 else 1)) * C
                out[to, at : at + C, :] = slab[k : k + C, :]
            else:
                out[to, at : at + C, :] = jnp.zeros((C, LANES), F32)
    before, after = jnp.maximum(g - 1, 0), jnp.minimum(g + 1, z.G - 1)
    edges[:C, :] = jnp.where(g > 0, got[before, z.RING :, :], 0.0)
    edges[C:, :] = jnp.where(g < z.G - 1, got[after, z.RING :, :], 0.0)
    lane = iota((8, LANES), 1)
    first = jnp.zeros((8, LANES), F32)
    last = first
    for c in range(C):
        lo = edges[c : c + 1, :]
        hi = edges[C + c : C + c + 1, :]
        cap = jnp.where(sub == 0, hi, jnp.where(sub == 7, lo, 0.0))
        first = jnp.where(lane == c, pltpu.roll(cap, c, 1) if c else cap, first)
        last = jnp.where(lane == c, pltpu.roll(cap, c + 1, 1), last)
    for to in range(z.D):
        out[to, z.RG2 - 8 :, :] = jnp.where(to > d, last, first)


def nest_steps(z, diff, cour, phases, got, up_in, dn_in, out, back, ring, up, dn):
    d = lax.axis_index("dev")
    C, M = z.C, z.M
    strip = Strip()
    fine = lax.rem(iota((2 * z.W, z.W), 0), z.W)
    place = iota((2 * z.W, z.W), 1)
    deal = jnp.where(fine == lax.rem(place, LANES) * 3 + place // LANES, 1.0, 0.0).astype(BF16)
    for source, target in ((up_in, up), (dn_in, dn)):
        halo = [source[x * z.HALO : (x + 1) * z.HALO, :] for x in range(3)]
        dealt = split_dot(jnp.concatenate(halo, axis=1), deal)
        for x in range(3):
            target[x * z.HALO : (x + 1) * z.HALO, :] = dealt[:, x * LANES : (x + 1) * LANES]
    total = got[0]
    for k in range(1, z.D):
        total = total + got[k]
    ring[...] = total
    side_main = [ring[:M, :], pltpu.roll(ring[:M, :], 4, 0)]
    side_cap = jnp.where(
        strip.any_high, ring[M : M + 1, :], jnp.where(strip.any_low, ring[15:16, :], 0.0)
    )
    hold_low, hold_high = strip.any_low & (d == 0), strip.any_high & (d == z.D - 1)
    nest_1 = strip.high[1] | strip.low[1]

    def channel(c, _):
        co = weights(diff, cour, c, 3.0)
        u = [
            [[phase_rows(z, phases, l, c, y, x) for x in range(3)] for y in range(3)]
            for l in range(2)
        ]
        cap = []
        for y in range(3):
            row = []
            for x in range(3):
                v = jnp.zeros((8, LANES), F32)
                for l in range(2):
                    at = x * z.HALO + (l * C + c) * 3 + y
                    v = jnp.where(strip.high[l], dn[pl.ds(at, 1), :], v)
                    v = jnp.where(strip.low[l], up[pl.ds(at, 1), :], v)
                row.append(v)
            cap.append(row)
        u.append(cap)
        end = jnp.where(nest_1, ring[pl.ds(16 + C + c, 1), :], ring[pl.ds(16 + c, 1), :])
        west, east = [], []
        for side, lane, ghosts in ((0, 0, west), (1, LANES - 1, east)):
            turn = [lax.rem(lane - ((l * 2 + side) * C + c) + LANES, LANES) for l in range(2)]
            for l in range(2):
                ghosts.append(pltpu.roll(side_main[l], turn[l], 1))
            caps = [pltpu.roll(side_cap, turn[l], 1) for l in range(2)]
            ghosts.append(jnp.where(nest_1, caps[1], caps[0]))

        def hold(u):
            cap = [
                [jnp.where(hold_high, end, v) for v in u[2][0]],
                u[2][1],
                [jnp.where(hold_low, end, v) for v in u[2][2]],
            ]
            return [u[0], u[1], cap]

        u = hold(u)
        for k in range(3):
            u = strip.step(u, co, west, east)
            if k < 2:
                u = hold(u)
        for l in range(2):
            for y in range(3):
                for x in range(3):
                    v = u[l][y][x]
                    v = v if l == 0 else pltpu.roll(v, 4, 0)
                    back[x, pl.ds((l * C + c) * z.H + y, M, 3), :] = v
        return 0

    lax.fori_loop(0, C, channel, 0)
    fine = iota((2 * z.W, z.W), 1)
    place = lax.rem(iota((2 * z.W, z.W), 0), z.W)
    at = lax.rem(place, LANES) * 3 + place // LANES
    undeal = jnp.where(fine == at, 1.0, 0.0).astype(BF16)
    done = split_dot(jnp.concatenate([back[0], back[1], back[2]], axis=1), undeal)
    out[...] = done.reshape(z.L, C, z.H, z.W)


def parent_step(z, anc, diff, cour, parent, edges, up_in, dn_in, got, out):
    g, d = lax.axis_index("grp"), lax.axis_index("dev")
    C = z.C
    rows = z.TR + 8
    n = nest_at(z, anc, g // z.S * z.NB + d // z.Y)
    i = iota((z.TR, LANES), 0) + (g * z.TR - anc[0, n])
    j = iota((z.TR, LANES), 1) + (d * z.TC - anc[1, n])
    inside = (i >= 0) & (i < z.FR) & (j >= 0) & (j < z.FC)
    one = lambda cond: jnp.where(cond, 1.0, 0.0).astype(F32)
    on_w, on_e = one(inside & (j == 0)), one(inside & (j == z.FC - 1))
    on_s, on_n = one(inside & (i == 0)), one(inside & (i == z.FR - 1))
    i_end, j_end = one((i == 0) | (i == z.FR - 1)), one((j == 0) | (j == z.FC - 1))
    i_lo, i_hi = one(i > 0), one(i < z.FR - 1)
    j_lo, j_hi = one(j > 0), one(j < z.FC - 1)
    lane = iota((rows, LANES), 1)
    sub = iota((8, LANES), 0)

    cap_w = jnp.where(d > 0, got[jnp.maximum(d - 1, 0), z.RG2 - 8 :, :], 0.0)
    cap_e = jnp.where(d < z.D - 1, got[jnp.minimum(d + 1, z.D - 1), z.RG2 - 8 :, :], 0.0)
    col_w = jnp.concatenate([up_in[z.EDGE :, :], cap_w], axis=0)
    col_e = jnp.concatenate([dn_in[z.EDGE :, :], cap_e], axis=0)

    def channel(c, _):
        co = [v[:1] for v in weights(diff, cour, c, 1.0)]
        fm, fe, fw, fn, fs = [v[:1] for v in weights(diff, cour, c, 3.0)]
        lo = edges[pl.ds(c, 1), :]
        hi = edges[pl.ds(C + c, 1), :]
        cap = jnp.where(sub == 0, hi, jnp.where(sub == 7, lo, 0.0))
        full = jnp.concatenate([parent[c], cap], axis=0)
        w_in = pltpu.roll(col_w, lax.rem(LANES - c, LANES), 1)
        e_in = pltpu.roll(col_e, LANES - 1 - c, 1)
        w_all = jnp.where(lane == 0, w_in, pltpu.roll(full, 1, 1))
        e_all = jnp.where(lane == LANES - 1, e_in, pltpu.roll(full, LANES - 1, 1))
        up = lambda x: pltpu.roll(x, rows - 1, 0)[: z.TR]
        down = lambda x: pltpu.roll(x, 1, 0)[: z.TR]
        mid = full[: z.TR]
        w, e, n, s = w_all[: z.TR], e_all[: z.TR], up(full), down(full)
        w_up, w_down, e_up, e_down = up(w_all), down(w_all), up(e_all), down(e_all)
        step = (
            co[MID] * mid
            + (co[EAST] * e + co[WEST] * w)
            + (co[NORTH] * n + co[SOUTH] * s)
        )
        a, b, k, x = ghost_share(fw, fe, fm, fs, fn)
        share = on_w * ((a - x * i_end) * w + (b * i_lo) * w_down + (k * i_hi) * w_up)
        a, b, k, x = ghost_share(fe, fw, fm, fs, fn)
        share += on_e * ((a - x * i_end) * e + (b * i_lo) * e_down + (k * i_hi) * e_up)
        a, b, k, x = ghost_share(fs, fn, fm, fw, fe)
        share += on_s * ((a - x * j_end) * s + (b * j_lo) * w_down + (k * j_hi) * e_down)
        a, b, k, x = ghost_share(fn, fs, fm, fw, fe)
        share += on_n * ((a - x * j_end) * n + (b * j_lo) * w_up + (k * j_hi) * e_up)
        out[c] = jnp.where(inside, share, step)
        return 0

    lax.fori_loop(0, C, channel, 0, unroll=2)


def merge(z, which, anchor, base, pieces):
    count, size = len(which), z.CS * z.M

    def kernel(*refs):
        anc_in, base_in, refs = refs[0], refs[1], refs[2:]
        source, base_out, refs = refs[:count], refs[count], refs[count + 1 :]
        anc, refs = refs[0], refs[1:]
        inner, (old, new, twice, sem) = refs[:count], refs[count:]
        g, d = lax.axis_index("grp"), lax.axis_index("dev")
        part = lax.rem(g, z.S)
        firsts = [lax.rem(part - k + z.S, z.S) * z.CS for k in which]
        fetch = [pltpu.make_async_copy(anc_in, anc, sem.at[0])]
        for k in range(count):
            rows = base_in.at[pl.ds(firsts[k], z.CS)]
            fetch.append(pltpu.make_async_copy(source[k], inner[k], sem.at[1 + 2 * k]))
            fetch.append(pltpu.make_async_copy(rows, old.at[k], sem.at[2 + 2 * k]))
        for copy in fetch:
            copy.start()
        for copy in fetch:
            copy.wait()
        n = nest_at(z, anc, g // z.S * z.NB + d // z.Y)
        r, q = anc[0, n], anc[1, n]
        start = lax.rem(g * z.TR - r + 2 * z.G * z.TR, z.FR)
        shift_q = lax.rem(q - d * z.TC + 2 * z.D * z.TC, z.FC)
        i = iota((z.TR, LANES), 0) + (g * z.TR - r)
        j = iota((z.TR, LANES), 1) + (d * z.TC - q)
        inside = (i >= 0) & (i < z.FR) & (j >= 0) & (j < z.FC)
        sub = iota((z.M, LANES), 0)
        store = []
        for k in range(count):
            piece = inner[k]
            for c in range(z.CS):
                for m in range(z.D):
                    x = piece[m, c * z.M : (c + 1) * z.M, :]
                    if m + 1 < z.D:
                        row = piece[m + 1, size + c : size + c + 1, :]
                        x += jnp.where(sub == z.M - 1, row, 0.0)
                    if m > 0:
                        row = piece[m - 1, size + z.CS + c : size + z.CS + c + 1, :]
                        x += jnp.where(sub == 0, row, 0.0)
                    twice[c % 4, m * z.M : (m + 1) * z.M, :] = x
                    if m * z.M < z.TR:
                        twice[c % 4, z.FR + m * z.M : z.FR + (m + 1) * z.M, :] = x
                x = pltpu.roll(twice[c % 4, pl.ds(start, z.TR), :], shift_q, 1)
                new[k, c] = old[k, c] + jnp.where(inside, x, 0.0)
            rows = base_out.at[pl.ds(firsts[k], z.CS)]
            store.append(pltpu.make_async_copy(new.at[k], rows, sem.at[1 + 2 * k]))
            store[-1].start()
        for copy in store:
            copy.wait()

    place = pl.BlockSpec(memory_space=pltpu.HBM)
    half = pltpu.VMEM((count, z.CS, z.TR, LANES), F32)
    return pl.pallas_call(
        kernel,
        out_shape=jax.ShapeDtypeStruct(base.shape, F32),
        in_specs=[place] * (2 + count),
        out_specs=place,
        input_output_aliases={1: 0},
        scratch_shapes=[
            pltpu.SMEM(anchor.shape, anchor.dtype),
            *[pltpu.VMEM(x.shape, F32) for x in pieces],
            half,
            half,
            pltpu.VMEM((4, z.FR + z.TR, LANES), F32),
            pltpu.SemaphoreType.DMA((1 + 2 * count,)),
        ],
        compiler_params=pltpu.CompilerParams(vmem_limit_bytes=VMEM_LIMIT),
    )(anchor, base, *pieces)


def shards(parent, nest, anchor, diff, cour):
    z = Sizes(parent, nest, anchor, lax.axis_size("grp"), lax.axis_size("dev"))
    sds = lambda *shape: jax.ShapeDtypeStruct(shape, F32)
    vmem = lambda *shape: pltpu.VMEM(shape, F32)
    to_grp = lambda x, k: lax.ppermute(x, "grp", [(a, a ^ k) for a in range(z.G)])

    anchor = anchor.T
    message = sds(z.EDGE + z.TR, LANES)
    edge_tile = vmem(z.L, z.C, 8, z.W)
    ring, up, dn = call(
        functools.partial(ring_parts, z),
        [sds(z.G, z.RG, LANES), message, message],
        (anchor,),
        (parent,),
        [edge_tile, edge_tile, pltpu.SemaphoreType.DMA((2,))],
        (nest,),
    )
    nest, ring, up, dn = lax.optimization_barrier((nest, ring, up, dn))
    forward = [(k, k + 1) for k in range(z.D - 1)]
    up = lax.ppermute(up, "dev", forward)
    dn = lax.ppermute(dn, "dev", [(b, a) for a, b in forward])
    ring = lax.all_to_all(ring, "grp", 0, 0, tiled=True)
    *chunks, phases = call(
        functools.partial(partial_averages, z),
        [sds(z.R1, LANES)] * z.S + [sds(3, z.L * z.C * z.H, LANES)],
        (diff, cour),
        (),
        [pltpu.VMEM(nest.shape, F32), pltpu.SemaphoreType.DMA((z.L,))],
        (nest,),
        z.S,
    )
    chunks, ring, up, dn = lax.optimization_barrier((chunks, ring, up, dn))
    got = [chunks[0]] + [to_grp(chunks[k % z.S], k) for k in range(1, z.G)]
    ring, edges = call(
        functools.partial(ring_next, z),
        [sds(z.D, z.RG2, LANES), sds(2 * z.C, LANES)],
        (),
        (ring,),
        [vmem(z.RING, LANES)],
    )
    got, ring, edges = lax.optimization_barrier((got, ring, edges))
    ring = lax.all_to_all(ring, "dev", 0, 0, tiled=True)

    (avg,) = call(functools.partial(pick_band, z), [sds(z.D, z.R2, LANES)], (anchor,), got)
    avg, phases, edges, ring = lax.optimization_barrier((avg, phases, edges, ring))
    avg = lax.all_to_all(avg, "dev", 0, 0, tiled=True)
    (nest_out,) = call(
        functools.partial(nest_steps, z),
        [jax.ShapeDtypeStruct(nest.shape, F32)],
        (diff, cour),
        (phases, ring, up, dn),
        [
            vmem(3, z.L * z.C * z.H, LANES),
            vmem(z.RG2, LANES),
            vmem(z.EDGE, LANES),
            vmem(z.EDGE, LANES),
        ],
    )
    (out,) = call(
        functools.partial(parent_step, z),
        [jax.ShapeDtypeStruct(parent.shape, F32)],
        (anchor, diff, cour),
        (parent, edges, up, dn, ring),
    )
    avg, nest_out, out = lax.optimization_barrier((avg, nest_out, out))
    pieces = [avg]
    for k in range(1, z.S):
        pairs = [(a, a // z.S * z.S + (a + k) % z.S) for a in range(z.G)]
        pieces.append(lax.ppermute(avg, "grp", pairs))
    for which in ([0], list(range(1, z.S))):
        out = merge(z, which, anchor, out, [pieces[k] for k in which])
    return out, nest_out


def solution(mesh):
    placed = (P(None, "grp", "dev"), P("grp", None, "dev", None), P(), P(), P())
    return jax.shard_map(
        shards,
        mesh=mesh,
        in_specs=placed,
        out_specs=(P(None, "grp", "dev"), P("grp", None, "dev", None)),
        check_vma=False,
    )
```

```python
import functools

import jax
import jax.numpy as jnp
from jax import lax
from jax.experimental import pallas as pl
from jax.experimental.pallas import tpu as pltpu
from jax.sharding import PartitionSpec as P

F32 = jnp.float32
BF16 = jnp.bfloat16
LANES = 128
VMEM_LIMIT = 63 * 1024 * 1024
MID, EAST, WEST, NORTH, SOUTH = range(5)


class Sizes:
    def __init__(self, parent, nest, anchor, grp_count, dev_count):
        self.C, self.TR, self.TC = parent.shape
        self.L, _, self.H, self.W = nest.shape
        self.N = anchor.shape[0]
        self.G, self.D = grp_count, dev_count
        self.M = self.H // 3
        self.FR, self.FC = self.M * self.D, self.W // 3
        self.S = self.G // 2
        self.NB = self.N // 2
        self.Y = self.D // self.NB
        self.CS = self.C // self.S
        self.BR, self.BC = self.S * self.TR, self.Y * self.TC
        self.R1 = self.L * self.CS * (self.M + 2)
        self.R2 = self.CS * (self.M + 2)
        self.RING = self.FR + self.L * 2 * self.C
        self.RG = self.RING + self.C
        self.RG2 = 16 + self.L * self.C + 8
        self.HALO = self.L * self.C * 3
        self.EDGE = 3 * self.HALO
        assert self.H == 24 and self.FC == LANES and self.TC == LANES
        assert self.FR >= self.TR and self.L == 2


def call(body, out_shape, smem, args, scratch=(), raw=(), early=None):
    moved = [*smem, *args]
    n_in, n_raw, n_out = len(moved), len(raw), len(out_shape)
    place = pl.BlockSpec(memory_space=pltpu.HBM)

    def kernel(*refs):
        source, refs = refs[:n_in], refs[n_in:]
        stay, refs = refs[:n_raw], refs[n_raw:]
        target, refs = refs[:n_out], refs[n_out:]
        inner, refs = refs[:n_in], refs[n_in:]
        result, refs = refs[:n_out], refs[n_out:]
        extra, sem = refs[:-1], refs[-1]
        fetch = [pltpu.make_async_copy(a, b, sem.at[k]) for k, (a, b) in enumerate(zip(source, inner))]
        for copy in fetch:
            copy.start()
        for copy in fetch:
            copy.wait()
        store = [
            pltpu.make_async_copy(a, b, sem.at[n_in + k]) for k, (a, b) in enumerate(zip(result, target))
        ]
        if early is None:
            body(*inner, *stay, *result, *extra)
        else:
            body(*inner, *stay, *result, *extra, store[early].start)
        for k, copy in enumerate(store):
            if k != early:
                copy.start()
        for copy in store:
            copy.wait()

    return pl.pallas_call(
        kernel,
        out_shape=list(out_shape),
        in_specs=[place] * (n_in + n_raw),
        out_specs=[place] * n_out,
        scratch_shapes=[
            *[pltpu.SMEM(x.shape, x.dtype) for x in smem],
            *[pltpu.VMEM(x.shape, x.dtype) for x in args],
            *[pltpu.VMEM(x.shape, x.dtype) for x in out_shape],
            *scratch,
            pltpu.SemaphoreType.DMA((n_in + n_out,)),
        ],
        compiler_params=pltpu.CompilerParams(vmem_limit_bytes=VMEM_LIMIT),
    )(*moved, *raw)


def iota(shape, dim):
    return lax.broadcasted_iota(jnp.int32, shape, dim)


def split_dot(x, table):
    high = x.astype(BF16)
    low = (x - high.astype(F32)).astype(BF16)
    return jnp.dot(jnp.concatenate([high, low], axis=1), table, preferred_element_type=F32)


def nest_at(z, anc, band):
    found = 0
    for n in range(z.N):
        found += jnp.where(anc[0, n] // z.BR * z.NB + anc[1, n] // z.BC == band, n, 0)
    return found


def weights(diff, cour, c, times):
    splat = lambda ref, k: jnp.full((8, LANES), ref[k, c], F32)
    east = times * splat(diff, 0)
    north = times * splat(diff, 1)
    west = east + splat(cour, 0)
    south = north + splat(cour, 1)
    return 1.0 - (east + west) - (north + south), east, west, north, south


def ghost_share(inject, back, mid, plus, minus):
    stay = mid + inject
    m0 = inject * (1.0 + stay + mid * stay + inject * (stay + back) + 2.0 * plus * minus)
    p1 = inject * plus * (1.0 + 2.0 * stay)
    p2 = inject * plus * plus
    n1 = inject * minus * (1.0 + 2.0 * stay)
    n2 = inject * minus * minus
    ninth = 1.0 / 9.0
    same = (3.0 * m0 + 2.0 * p1 + p2 + 2.0 * n1 + n2) * ninth
    return same, (p1 + 2.0 * p2) * ninth, (n1 + 2.0 * n2) * ninth, inject * plus * minus * ninth


class Strip:
    def __init__(self):
        sub = iota((8, LANES), 0)
        lane = iota((8, LANES), 1)
        self.high = [sub == 0, sub == 4]
        self.low = [sub == 7, sub == 3]
        self.any_high = (sub == 0) | (sub == 4)
        self.any_low = (sub == 7) | (sub == 3)
        self.first, self.last = lane == 0, lane == LANES - 1

    def east(self, x, ghost):
        return jnp.where(self.last, ghost, pltpu.roll(x, LANES - 1, 1))

    def west(self, x, ghost):
        return jnp.where(self.first, ghost, pltpu.roll(x, 1, 1))

    def north(self, mains, cap):
        up = [pltpu.roll(m, 7, 0) for m in mains]
        cap_up = pltpu.roll(cap, 7, 0)
        new = [jnp.where(self.low[l], cap_up, up[l]) for l in range(2)]
        return new, jnp.where(self.low[0], up[0], jnp.where(self.low[1], up[1], 0.0))

    def south(self, mains, cap):
        down = [pltpu.roll(m, 1, 0) for m in mains]
        cap_down = pltpu.roll(cap, 1, 0)
        new = [jnp.where(self.high[l], cap_down, down[l]) for l in range(2)]
        return new, jnp.where(self.high[0], down[0], jnp.where(self.high[1], down[1], 0.0))

    def step(self, u, co, west_ghost, east_ghost):
        n_in = [self.north([u[0][0][x], u[1][0][x]], u[2][0][x]) for x in range(3)]
        s_in = [self.south([u[0][2][x], u[1][2][x]], u[2][2][x]) for x in range(3)]
        pick = lambda pair, k: pair[1] if k == 2 else pair[0][k]
        new = []
        for k in range(3):
            rows = []
            for y in range(3):
                row = u[k][y]
                e = [row[1], row[2], self.east(row[0], east_ghost[k])]
                w = [self.west(row[2], west_ghost[k]), row[0], row[1]]
                cells = []
                for x in range(3):
                    n = u[k][y + 1][x] if y < 2 else pick(n_in[x], k)
                    s = u[k][y - 1][x] if y > 0 else pick(s_in[x], k)
                    cells.append(
                        co[MID] * row[x]
                        + (co[EAST] * e[x] + co[WEST] * w[x])
                        + (co[NORTH] * n + co[SOUTH] * s)
                    )
                rows.append(cells)
            new.append(rows)
        return new

    def pooled_step(self, u, co):
        ends = []
        for k in range(3):
            row = [u[k][y][0] + u[k][y][1] + u[k][y][2] for y in range(3)]
            col = [u[k][0][x] + u[k][1][x] + u[k][2][x] for x in (0, 2)]
            ends.append((row[0], row[2], col[0], col[1], row[0] + row[1] + row[2]))
        n_in = self.north([ends[0][0], ends[1][0]], ends[2][0])
        s_in = self.south([ends[0][1], ends[1][1]], ends[2][1])
        pick = lambda pair, k: pair[1] if k == 2 else pair[0][k]
        out = []
        for k in range(3):
            row0, row2, col0, col2, total = ends[k]
            flux_x = co[EAST] * (self.east(col0, 0.0) - col0)
            flux_x += co[WEST] * (self.west(col2, 0.0) - col2)
            flux_y = co[NORTH] * (pick(n_in, k) - row0) + co[SOUTH] * (pick(s_in, k) - row2)
            out.append(total + (flux_x + flux_y))
        return out


def phase_rows(z, ref, l, c, y, x):
    got = ref[x, pl.ds((l * z.C + c) * z.H + y, z.M, 3), :]
    return got if l == 0 else pltpu.roll(got, 4, 0)


def partial_averages(z, diff, cour, nest, *refs):
    out, (phases, strips, sem, store_phases) = refs[: z.S], refs[z.S :]
    fetch = [pltpu.make_async_copy(nest.at[l], strips.at[l], sem.at[l]) for l in range(z.L)]
    for copy in fetch:
        copy.start()
    d = lax.axis_index("dev")
    own = lax.rem(lax.axis_index("grp"), z.S)
    C, M, CS = z.C, z.M, z.CS
    fine = lax.rem(iota((2 * z.W, z.W), 0), z.W)
    place = iota((2 * z.W, z.W), 1)
    at = lax.rem(place, LANES) * 3 + place // LANES
    deal = jnp.where(fine == at, 1.0, 0.0).astype(BF16)
    rows = C * z.H
    for l in range(z.L):
        fetch[l].wait()
        dealt = split_dot(strips[l].reshape(rows, z.W), deal)
        for x in range(3):
            phases[x, l * rows : (l + 1) * rows, :] = dealt[:, x * LANES : (x + 1) * LANES]
    store_phases()
    strip = Strip()
    keep_high = strip.any_low | (strip.any_high & (d < z.D - 1))
    keep_low = strip.any_high | (strip.any_low & (d > 0))
    zero = jnp.zeros((8, LANES), F32)
    ghosts = [0.0] * 3
    base = z.L * CS * M

    def hold(u):
        cap = [
            [jnp.where(keep_high, v, 0.0) for v in u[2][0]],
            u[2][1],
            [jnp.where(keep_low, v, 0.0) for v in u[2][2]],
        ]
        return [u[0], u[1], cap]

    for part in range(z.S):

        def channel(i, _, to=out[part], first=jnp.bitwise_xor(own, part) * CS):
            c = first + i
            co = weights(diff, cour, c, 3.0)
            u = [
                [[phase_rows(z, phases, l, c, y, x) for x in range(3)] for y in range(3)]
                for l in range(2)
            ]
            u.append([[zero] * 3] * 3)
            for _step in range(2):
                u = hold(strip.step(u, co, ghosts, ghosts))
            got = [v * (1.0 / 9.0) for v in strip.pooled_step(u, co)]
            got[1] = pltpu.roll(got[1], 4, 0)
            for l in range(2):
                row = pl.multiple_of((l * CS + i) * M, M)
                to[pl.ds(row, M), :] = got[l]
                for side, sub in enumerate(((7, 3), (0, 4))):
                    row = base + (l * 2 + side) * CS + i
                    to[pl.ds(row, 1), :] = got[2][sub[l] : sub[l] + 1]
            return 0

        lax.fori_loop(0, CS, channel, 0, unroll=2)


def pick_band(z, anc, *refs):
    got, out = refs[: z.G], refs[z.G]
    g = lax.axis_index("grp")
    top = g // z.S * z.NB
    base, size = z.L * z.CS * z.M, z.CS * z.M
    for band in range(z.NB):
        n = nest_at(z, anc, top + band)
        of = n // z.L
        slot = jnp.bitwise_xor(of, g)
        first = n - of * z.L == 0
        for k in range(z.G):

            @pl.when(slot == k)
            def _(k=k, first=first, band=band):
                main = jnp.where(first, got[k][:size, :], got[k][size : 2 * size, :])
                edge = jnp.where(
                    first,
                    got[k][base : base + 2 * z.CS, :],
                    got[k][base + 2 * z.CS : base + 4 * z.CS, :],
                )
                for y in range(z.Y):
                    out[band * z.Y + y, :size, :] = main
                    out[band * z.Y + y, size:, :] = edge


def ring_parts(z, anc, parent, nest, buf, up, dn, tail, head, sem):
    fetch = [
        pltpu.make_async_copy(nest.at[:, :, z.H - 8 :, :], tail, sem.at[0]),
        pltpu.make_async_copy(nest.at[:, :, :8, :], head, sem.at[1]),
    ]
    for copy in fetch:
        copy.start()
    g, d = lax.axis_index("grp"), lax.axis_index("dev")
    row_base, col_base = g * z.TR, d * z.TC
    lane_t = iota((z.TR, LANES), 1)
    lane_f = iota((z.FR, LANES), 1)
    row_f = iota((z.FR, LANES), 0)
    lane_c = iota((z.C, LANES), 1)
    buf[...] = jnp.zeros_like(buf)

    def nest_ring(n, _):
        to = n // z.L
        l = n - to * z.L
        slot = to
        r, q = anc[0, n], anc[1, n]
        rows_meet = (r < row_base + z.TR) & (r + z.FR > row_base)
        cols_meet = (q < col_base + z.TC) & (q + z.FC > col_base)
        shift_r = lax.rem(row_base - r + 2 * z.G * z.TR, z.FR)
        shift_q = lax.rem(col_base - q + 2 * z.D * z.TC, z.FC)
        for side in range(2):
            col = (q - 1 if side == 0 else q + z.FC) - col_base
            first = (l * 2 + side) * z.C

            @pl.when(rows_meet & (col >= 0) & (col < z.TC))
            def _(col=col, first=first):
                acc = jnp.zeros((z.TR, LANES), F32)
                for c in range(z.C):
                    at = first + c
                    moved = pltpu.roll(parent[c], lax.rem(at - col + LANES, LANES), 1)
                    acc = jnp.where(lane_t == at, moved, acc)
                if z.FR > z.TR:
                    acc = jnp.concatenate([acc, jnp.zeros((z.FR - z.TR, LANES), F32)], axis=0)
                acc = pltpu.roll(acc, shift_r, 0)
                y = row_f + (r - row_base)
                good = (y >= 0) & (y < z.TR) & (lane_f >= first) & (lane_f < first + z.C)
                buf[slot, : z.FR, :] = jnp.where(good, acc, buf[slot, : z.FR, :])

            row = (r - 1 if side == 0 else r + z.FR) - row_base

            @pl.when(cols_meet & (row >= 0) & (row < z.TR))
            def _(row=row, first=first):
                rows = jnp.concatenate(
                    [parent[c, pl.ds(row, 1), :] for c in range(z.C)], axis=0
                )
                x = lane_c + (q - col_base)
                moved = jnp.where((x >= 0) & (x < z.TC), pltpu.roll(rows, shift_q, 1), 0.0)
                buf[slot, pl.ds(pl.multiple_of(z.FR + first, 8), z.C), :] = moved

        return 0

    lax.fori_loop(0, z.N, nest_ring, 0)
    for to in range(z.G):
        edge = jnp.where(to > g, z.TR - 1, 0)
        for c in range(z.C):
            buf[to, z.RING + c : z.RING + c + 1, :] = parent[c, pl.ds(edge, 1), :]
    first = jnp.zeros((z.TR, LANES), F32)
    last = first
    for c in range(z.C):
        first = jnp.where(lane_t == c, pltpu.roll(parent[c], c, 1) if c else parent[c], first)
        last = jnp.where(lane_t == c, pltpu.roll(parent[c], c + 1, 1), last)
    up[z.EDGE :, :] = last
    dn[z.EDGE :, :] = first
    for copy in fetch:
        copy.wait()
    for l in range(z.L):
        for c in range(z.C):
            for x in range(3):
                at = x * z.HALO + 3 * (l * z.C + c)
                lanes = slice(x * LANES, (x + 1) * LANES)
                up[at : at + 3, :] = tail[l, c, 5:8, lanes]
                dn[at : at + 3, :] = head[l, c, 0:3, lanes]


def ring_next(z, got, out, edges, slab):
    g, d = lax.axis_index("grp"), lax.axis_index("dev")
    C, L, FR, M = z.C, z.L, z.FR, z.M
    total = got[0, : z.RING, :]
    for k in range(1, z.G):
        total = total + got[k, : z.RING, :]
    slab[...] = total
    sub = iota((8, LANES), 0)
    for to in range(z.D):
        out[to, :M, :] = slab[to * M : (to + 1) * M, :]
        hi = min(to * M + M, FR - 1)
        lo = max(to * M - 1, 0)
        hi, lo = slab[hi : hi + 1, :], slab[lo : lo + 1, :]
        out[to, M:16, :] = jnp.where(sub == 0, hi, jnp.where(sub == 7, lo, 0.0))
        for l in range(L):
            at = 16 + l * C
            if to == 0 or to == z.D - 1:
                k = FR + (l * 2 + (0 if to == 0 else 1)) * C
                out[to, at : at + C, :] = slab[k : k + C, :]
            else:
                out[to, at : at + C, :] = jnp.zeros((C, LANES), F32)
    before, after = jnp.maximum(g - 1, 0), jnp.minimum(g + 1, z.G - 1)
    edges[:C, :] = jnp.where(g > 0, got[before, z.RING :, :], 0.0)
    edges[C:, :] = jnp.where(g < z.G - 1, got[after, z.RING :, :], 0.0)
    lane = iota((8, LANES), 1)
    first = jnp.zeros((8, LANES), F32)
    last = first
    for c in range(C):
        lo = edges[c : c + 1, :]
        hi = edges[C + c : C + c + 1, :]
        cap = jnp.where(sub == 0, hi, jnp.where(sub == 7, lo, 0.0))
        first = jnp.where(lane == c, pltpu.roll(cap, c, 1) if c else cap, first)
        last = jnp.where(lane == c, pltpu.roll(cap, c + 1, 1), last)
    for to in range(z.D):
        out[to, z.RG2 - 8 :, :] = jnp.where(to > d, last, first)


def nest_steps(z, diff, cour, phases, got, up_in, dn_in, out, back, ring, up, dn):
    d = lax.axis_index("dev")
    C, M = z.C, z.M
    strip = Strip()
    fine = lax.rem(iota((2 * z.W, z.W), 0), z.W)
    place = iota((2 * z.W, z.W), 1)
    deal = jnp.where(fine == lax.rem(place, LANES) * 3 + place // LANES, 1.0, 0.0).astype(BF16)
    for source, target in ((up_in, up), (dn_in, dn)):
        halo = [source[x * z.HALO : (x + 1) * z.HALO, :] for x in range(3)]
        dealt = split_dot(jnp.concatenate(halo, axis=1), deal)
        for x in range(3):
            target[x * z.HALO : (x + 1) * z.HALO, :] = dealt[:, x * LANES : (x + 1) * LANES]
    total = got[0]
    for k in range(1, z.D):
        total = total + got[k]
    ring[...] = total
    side_main = [ring[:M, :], pltpu.roll(ring[:M, :], 4, 0)]
    side_cap = jnp.where(
        strip.any_high, ring[M : M + 1, :], jnp.where(strip.any_low, ring[15:16, :], 0.0)
    )
    hold_low, hold_high = strip.any_low & (d == 0), strip.any_high & (d == z.D - 1)
    nest_1 = strip.high[1] | strip.low[1]

    def channel(c, _):
        co = weights(diff, cour, c, 3.0)
        u = [
            [[phase_rows(z, phases, l, c, y, x) for x in range(3)] for y in range(3)]
            for l in range(2)
        ]
        cap = []
        for y in range(3):
            row = []
            for x in range(3):
                v = jnp.zeros((8, LANES), F32)
                for l in range(2):
                    at = x * z.HALO + (l * C + c) * 3 + y
                    v = jnp.where(strip.high[l], dn[pl.ds(at, 1), :], v)
                    v = jnp.where(strip.low[l], up[pl.ds(at, 1), :], v)
                row.append(v)
            cap.append(row)
        u.append(cap)
        end = jnp.where(nest_1, ring[pl.ds(16 + C + c, 1), :], ring[pl.ds(16 + c, 1), :])
        west, east = [], []
        for side, lane, ghosts in ((0, 0, west), (1, LANES - 1, east)):
            turn = [lax.rem(lane - ((l * 2 + side) * C + c) + LANES, LANES) for l in range(2)]
            for l in range(2):
                ghosts.append(pltpu.roll(side_main[l], turn[l], 1))
            caps = [pltpu.roll(side_cap, turn[l], 1) for l in range(2)]
            ghosts.append(jnp.where(nest_1, caps[1], caps[0]))

        def hold(u):
            cap = [
                [jnp.where(hold_high, end, v) for v in u[2][0]],
                u[2][1],
                [jnp.where(hold_low, end, v) for v in u[2][2]],
            ]
            return [u[0], u[1], cap]

        u = hold(u)
        for k in range(3):
            u = strip.step(u, co, west, east)
            if k < 2:
                u = hold(u)
        for l in range(2):
            for y in range(3):
                for x in range(3):
                    v = u[l][y][x]
                    v = v if l == 0 else pltpu.roll(v, 4, 0)
                    back[x, pl.ds((l * C + c) * z.H + y, M, 3), :] = v
        return 0

    lax.fori_loop(0, C, channel, 0, unroll=2)
    fine = iota((2 * z.W, z.W), 1)
    place = lax.rem(iota((2 * z.W, z.W), 0), z.W)
    at = lax.rem(place, LANES) * 3 + place // LANES
    undeal = jnp.where(fine == at, 1.0, 0.0).astype(BF16)
    done = split_dot(jnp.concatenate([back[0], back[1], back[2]], axis=1), undeal)
    out[...] = done.reshape(z.L, C, z.H, z.W)


def parent_step(z, anc, diff, cour, parent, edges, up_in, dn_in, got, out):
    g, d = lax.axis_index("grp"), lax.axis_index("dev")
    C = z.C
    rows = z.TR + 8
    n = nest_at(z, anc, g // z.S * z.NB + d // z.Y)
    i = iota((z.TR, LANES), 0) + (g * z.TR - anc[0, n])
    j = iota((z.TR, LANES), 1) + (d * z.TC - anc[1, n])
    inside = (i >= 0) & (i < z.FR) & (j >= 0) & (j < z.FC)
    one = lambda cond: jnp.where(cond, 1.0, 0.0).astype(F32)
    on_w, on_e = one(inside & (j == 0)), one(inside & (j == z.FC - 1))
    on_s, on_n = one(inside & (i == 0)), one(inside & (i == z.FR - 1))
    i_end, j_end = one((i == 0) | (i == z.FR - 1)), one((j == 0) | (j == z.FC - 1))
    i_lo, i_hi = one(i > 0), one(i < z.FR - 1)
    j_lo, j_hi = one(j > 0), one(j < z.FC - 1)
    lane = iota((rows, LANES), 1)
    sub = iota((8, LANES), 0)

    cap_w = jnp.where(d > 0, got[jnp.maximum(d - 1, 0), z.RG2 - 8 :, :], 0.0)
    cap_e = jnp.where(d < z.D - 1, got[jnp.minimum(d + 1, z.D - 1), z.RG2 - 8 :, :], 0.0)
    col_w = jnp.concatenate([up_in[z.EDGE :, :], cap_w], axis=0)
    col_e = jnp.concatenate([dn_in[z.EDGE :, :], cap_e], axis=0)

    def channel(c, _):
        co = [v[:1] for v in weights(diff, cour, c, 1.0)]
        fm, fe, fw, fn, fs = [v[:1] for v in weights(diff, cour, c, 3.0)]
        lo = edges[pl.ds(c, 1), :]
        hi = edges[pl.ds(C + c, 1), :]
        cap = jnp.where(sub == 0, hi, jnp.where(sub == 7, lo, 0.0))
        full = jnp.concatenate([parent[c], cap], axis=0)
        w_in = pltpu.roll(col_w, lax.rem(LANES - c, LANES), 1)
        e_in = pltpu.roll(col_e, LANES - 1 - c, 1)
        w_all = jnp.where(lane == 0, w_in, pltpu.roll(full, 1, 1))
        e_all = jnp.where(lane == LANES - 1, e_in, pltpu.roll(full, LANES - 1, 1))
        up = lambda x: pltpu.roll(x, rows - 1, 0)[: z.TR]
        down = lambda x: pltpu.roll(x, 1, 0)[: z.TR]
        mid = full[: z.TR]
        w, e, n, s = w_all[: z.TR], e_all[: z.TR], up(full), down(full)
        w_up, w_down, e_up, e_down = up(w_all), down(w_all), up(e_all), down(e_all)
        step = (
            co[MID] * mid
            + (co[EAST] * e + co[WEST] * w)
            + (co[NORTH] * n + co[SOUTH] * s)
        )
        a, b, k, x = ghost_share(fw, fe, fm, fs, fn)
        share = on_w * ((a - x * i_end) * w + (b * i_lo) * w_down + (k * i_hi) * w_up)
        a, b, k, x = ghost_share(fe, fw, fm, fs, fn)
        share += on_e * ((a - x * i_end) * e + (b * i_lo) * e_down + (k * i_hi) * e_up)
        a, b, k, x = ghost_share(fs, fn, fm, fw, fe)
        share += on_s * ((a - x * j_end) * s + (b * j_lo) * w_down + (k * j_hi) * e_down)
        a, b, k, x = ghost_share(fn, fs, fm, fw, fe)
        share += on_n * ((a - x * j_end) * n + (b * j_lo) * w_up + (k * j_hi) * e_up)
        out[c] = jnp.where(inside, share, step)
        return 0

    lax.fori_loop(0, C, channel, 0, unroll=2)


def merge(z, which, anchor, base, pieces):
    count, size = len(which), z.CS * z.M

    def kernel(*refs):
        anc_in, base_in, refs = refs[0], refs[1], refs[2:]
        source, base_out, refs = refs[:count], refs[count], refs[count + 1 :]
        anc, refs = refs[0], refs[1:]
        inner, (old, new, twice, sem) = refs[:count], refs[count:]
        g, d = lax.axis_index("grp"), lax.axis_index("dev")
        part = lax.rem(g, z.S)
        firsts = [lax.rem(part - k + z.S, z.S) * z.CS for k in which]
        fetch = [pltpu.make_async_copy(anc_in, anc, sem.at[0])]
        for k in range(count):
            rows = base_in.at[pl.ds(firsts[k], z.CS)]
            fetch.append(pltpu.make_async_copy(source[k], inner[k], sem.at[1 + 2 * k]))
            fetch.append(pltpu.make_async_copy(rows, old.at[k], sem.at[2 + 2 * k]))
        for copy in fetch:
            copy.start()
        for copy in fetch:
            copy.wait()
        n = nest_at(z, anc, g // z.S * z.NB + d // z.Y)
        r, q = anc[0, n], anc[1, n]
        start = lax.rem(g * z.TR - r + 2 * z.G * z.TR, z.FR)
        shift_q = lax.rem(q - d * z.TC + 2 * z.D * z.TC, z.FC)
        i = iota((z.TR, LANES), 0) + (g * z.TR - r)
        j = iota((z.TR, LANES), 1) + (d * z.TC - q)
        inside = (i >= 0) & (i < z.FR) & (j >= 0) & (j < z.FC)
        sub = iota((z.M, LANES), 0)
        store = []
        for k in range(count):
            piece = inner[k]
            for c in range(z.CS):
                for m in range(z.D):
                    x = piece[m, c * z.M : (c + 1) * z.M, :]
                    if m + 1 < z.D:
                        row = piece[m + 1, size + c : size + c + 1, :]
                        x += jnp.where(sub == z.M - 1, row, 0.0)
                    if m > 0:
                        row = piece[m - 1, size + z.CS + c : size + z.CS + c + 1, :]
                        x += jnp.where(sub == 0, row, 0.0)
                    twice[c % 4, m * z.M : (m + 1) * z.M, :] = x
                    if m * z.M < z.TR:
                        twice[c % 4, z.FR + m * z.M : z.FR + (m + 1) * z.M, :] = x
                x = pltpu.roll(twice[c % 4, pl.ds(start, z.TR), :], shift_q, 1)
                new[k, c] = old[k, c] + jnp.where(inside, x, 0.0)
            rows = base_out.at[pl.ds(firsts[k], z.CS)]
            store.append(pltpu.make_async_copy(new.at[k], rows, sem.at[1 + 2 * k]))
            store[-1].start()
        for copy in store:
            copy.wait()

    place = pl.BlockSpec(memory_space=pltpu.HBM)
    half = pltpu.VMEM((count, z.CS, z.TR, LANES), F32)
    return pl.pallas_call(
        kernel,
        out_shape=jax.ShapeDtypeStruct(base.shape, F32),
        in_specs=[place] * (2 + count),
        out_specs=place,
        input_output_aliases={1: 0},
        scratch_shapes=[
            pltpu.SMEM(anchor.shape, anchor.dtype),
            *[pltpu.VMEM(x.shape, F32) for x in pieces],
            half,
            half,
            pltpu.VMEM((4, z.FR + z.TR, LANES), F32),
            pltpu.SemaphoreType.DMA((1 + 2 * count,)),
        ],
        compiler_params=pltpu.CompilerParams(vmem_limit_bytes=VMEM_LIMIT),
    )(anchor, base, *pieces)


def shards(parent, nest, anchor, diff, cour):
    z = Sizes(parent, nest, anchor, lax.axis_size("grp"), lax.axis_size("dev"))
    sds = lambda *shape: jax.ShapeDtypeStruct(shape, F32)
    vmem = lambda *shape: pltpu.VMEM(shape, F32)
    to_grp = lambda x, k: lax.ppermute(x, "grp", [(a, a ^ k) for a in range(z.G)])

    anchor = anchor.T
    message = sds(z.EDGE + z.TR, LANES)
    edge_tile = vmem(z.L, z.C, 8, z.W)
    ring, up, dn = call(
        functools.partial(ring_parts, z),
        [sds(z.G, z.RG, LANES), message, message],
        (anchor,),
        (parent,),
        [edge_tile, edge_tile, pltpu.SemaphoreType.DMA((2,))],
        (nest,),
    )
    forward = [(k, k + 1) for k in range(z.D - 1)]
    up = lax.ppermute(up, "dev", forward)
    dn = lax.ppermute(dn, "dev", [(b, a) for a, b in forward])
    ring = lax.all_to_all(ring, "grp", 0, 0, tiled=True)
    ring, edges = call(
        functools.partial(ring_next, z),
        [sds(z.D, z.RG2, LANES), sds(2 * z.C, LANES)],
        (),
        (ring,),
        [vmem(z.RING, LANES)],
    )
    ring = lax.all_to_all(ring, "dev", 0, 0, tiled=True)
    nest, edges, up, dn = lax.optimization_barrier((nest, edges, up, dn))
    *chunks, phases = call(
        functools.partial(partial_averages, z),
        [sds(z.R1, LANES)] * z.S + [sds(3, z.L * z.C * z.H, LANES)],
        (diff, cour),
        (),
        [pltpu.VMEM(nest.shape, F32), pltpu.SemaphoreType.DMA((z.L,))],
        (nest,),
        z.S,
    )
    chunks, ring = lax.optimization_barrier((chunks, ring))
    got = [chunks[0]] + [to_grp(chunks[k % z.S], k) for k in range(1, z.G)]
    (out,) = call(
        functools.partial(parent_step, z),
        [jax.ShapeDtypeStruct(parent.shape, F32)],
        (anchor, diff, cour),
        (parent, edges, up, dn, ring),
    )
    got, out = lax.optimization_barrier((got, out))
    (avg,) = call(functools.partial(pick_band, z), [sds(z.D, z.R2, LANES)], (anchor,), got)
    avg, phases = lax.optimization_barrier((avg, phases))
    avg = lax.all_to_all(avg, "dev", 0, 0, tiled=True)
    (nest_out,) = call(
        functools.partial(nest_steps, z),
        [jax.ShapeDtypeStruct(nest.shape, F32)],
        (diff, cour),
        (phases, ring, up, dn),
        [
            vmem(3, z.L * z.C * z.H, LANES),
            vmem(z.RG2, LANES),
            vmem(z.EDGE, LANES),
            vmem(z.EDGE, LANES),
        ],
    )
    avg, nest_out, out = lax.optimization_barrier((avg, nest_out, out))
    pieces = [avg]
    for k in range(1, z.S):
        pairs = [(a, a // z.S * z.S + (a + k) % z.S) for a in range(z.G)]
        pieces.append(lax.ppermute(avg, "grp", pairs))
    for which in ([0], list(range(1, z.S))):
        out = merge(z, which, anchor, out, [pieces[k] for k in which])
    return out, nest_out


def solution(mesh):
    placed = (P(None, "grp", "dev"), P("grp", None, "dev", None), P(), P(), P())
    return jax.shard_map(
        shards,
        mesh=mesh,
        in_specs=placed,
        out_specs=(P(None, "grp", "dev"), P("grp", None, "dev", None)),
        check_vma=False,
    )
```

```python
import functools

import jax
import jax.numpy as jnp
from jax import lax
from jax.experimental import pallas as pl
from jax.experimental.pallas import tpu as pltpu
from jax.sharding import PartitionSpec as P

F32 = jnp.float32
BF16 = jnp.bfloat16
LANES = 128
VMEM_LIMIT = 63 * 1024 * 1024
MID, EAST, WEST, NORTH, SOUTH = range(5)


class Sizes:
    def __init__(self, parent, nest, anchor, grp_count, dev_count):
        self.C, self.TR, self.TC = parent.shape
        self.L, _, self.H, self.W = nest.shape
        self.N = anchor.shape[0]
        self.G, self.D = grp_count, dev_count
        self.M = self.H // 3
        self.FR, self.FC = self.M * self.D, self.W // 3
        self.S = self.G // 2
        self.NB = self.N // 2
        self.Y = self.D // self.NB
        self.CS = self.C // self.S
        self.BR, self.BC = self.S * self.TR, self.Y * self.TC
        self.R1 = self.L * self.CS * (self.M + 2)
        self.R2 = self.CS * (self.M + 2)
        self.RING = self.FR + self.L * 2 * self.C
        self.RG = self.RING + self.C
        self.RG2 = 16 + self.L * self.C + 8
        self.HALO = self.L * self.C * 3
        self.EDGE = 3 * self.HALO
        assert self.H == 24 and self.FC == LANES and self.TC == LANES
        assert self.FR >= self.TR and self.L == 2


def call(body, out_shape, smem, args, scratch=(), raw=(), early=None):
    moved = [*smem, *args]
    n_in, n_raw, n_out = len(moved), len(raw), len(out_shape)
    place = pl.BlockSpec(memory_space=pltpu.HBM)

    def kernel(*refs):
        source, refs = refs[:n_in], refs[n_in:]
        stay, refs = refs[:n_raw], refs[n_raw:]
        target, refs = refs[:n_out], refs[n_out:]
        inner, refs = refs[:n_in], refs[n_in:]
        result, refs = refs[:n_out], refs[n_out:]
        extra, sem = refs[:-1], refs[-1]
        fetch = [pltpu.make_async_copy(a, b, sem.at[k]) for k, (a, b) in enumerate(zip(source, inner))]
        for copy in fetch:
            copy.start()
        for copy in fetch:
            copy.wait()
        store = [
            pltpu.make_async_copy(a, b, sem.at[n_in + k]) for k, (a, b) in enumerate(zip(result, target))
        ]
        if early is None:
            body(*inner, *stay, *result, *extra)
        else:
            body(*inner, *stay, *result, *extra, store[early].start)
        for k, copy in enumerate(store):
            if k != early:
                copy.start()
        for copy in store:
            copy.wait()

    return pl.pallas_call(
        kernel,
        out_shape=list(out_shape),
        in_specs=[place] * (n_in + n_raw),
        out_specs=[place] * n_out,
        scratch_shapes=[
            *[pltpu.SMEM(x.shape, x.dtype) for x in smem],
            *[pltpu.VMEM(x.shape, x.dtype) for x in args],
            *[pltpu.VMEM(x.shape, x.dtype) for x in out_shape],
            *scratch,
            pltpu.SemaphoreType.DMA((n_in + n_out,)),
        ],
        compiler_params=pltpu.CompilerParams(vmem_limit_bytes=VMEM_LIMIT),
    )(*moved, *raw)


def iota(shape, dim):
    return lax.broadcasted_iota(jnp.int32, shape, dim)


def split_dot(x, table):
    high = x.astype(BF16)
    low = (x - high.astype(F32)).astype(BF16)
    return jnp.dot(jnp.concatenate([high, low], axis=1), table, preferred_element_type=F32)


def nest_at(z, anc, band):
    found = 0
    for n in range(z.N):
        found += jnp.where(anc[0, n] // z.BR * z.NB + anc[1, n] // z.BC == band, n, 0)
    return found


def weights(diff, cour, c, times):
    splat = lambda ref, k: jnp.full((8, LANES), ref[k, c], F32)
    east = times * splat(diff, 0)
    north = times * splat(diff, 1)
    west = east + splat(cour, 0)
    south = north + splat(cour, 1)
    return 1.0 - (east + west) - (north + south), east, west, north, south


def ghost_share(inject, back, mid, plus, minus):
    stay = mid + inject
    m0 = inject * (1.0 + stay + mid * stay + inject * (stay + back) + 2.0 * plus * minus)
    p1 = inject * plus * (1.0 + 2.0 * stay)
    p2 = inject * plus * plus
    n1 = inject * minus * (1.0 + 2.0 * stay)
    n2 = inject * minus * minus
    ninth = 1.0 / 9.0
    same = (3.0 * m0 + 2.0 * p1 + p2 + 2.0 * n1 + n2) * ninth
    return same, (p1 + 2.0 * p2) * ninth, (n1 + 2.0 * n2) * ninth, inject * plus * minus * ninth


class Strip:
    def __init__(self):
        sub = iota((8, LANES), 0)
        lane = iota((8, LANES), 1)
        self.high = [sub == 0, sub == 4]
        self.low = [sub == 7, sub == 3]
        self.any_high = (sub == 0) | (sub == 4)
        self.any_low = (sub == 7) | (sub == 3)
        self.first, self.last = lane == 0, lane == LANES - 1

    def east(self, x, ghost):
        return jnp.where(self.last, ghost, pltpu.roll(x, LANES - 1, 1))

    def west(self, x, ghost):
        return jnp.where(self.first, ghost, pltpu.roll(x, 1, 1))

    def north(self, mains, cap):
        up = [pltpu.roll(m, 7, 0) for m in mains]
        cap_up = pltpu.roll(cap, 7, 0)
        new = [jnp.where(self.low[l], cap_up, up[l]) for l in range(2)]
        return new, jnp.where(self.low[0], up[0], jnp.where(self.low[1], up[1], 0.0))

    def south(self, mains, cap):
        down = [pltpu.roll(m, 1, 0) for m in mains]
        cap_down = pltpu.roll(cap, 1, 0)
        new = [jnp.where(self.high[l], cap_down, down[l]) for l in range(2)]
        return new, jnp.where(self.high[0], down[0], jnp.where(self.high[1], down[1], 0.0))

    def step(self, u, co, west_ghost, east_ghost):
        n_in = [self.north([u[0][0][x], u[1][0][x]], u[2][0][x]) for x in range(3)]
        s_in = [self.south([u[0][2][x], u[1][2][x]], u[2][2][x]) for x in range(3)]
        pick = lambda pair, k: pair[1] if k == 2 else pair[0][k]
        new = []
        for k in range(3):
            rows = []
            for y in range(3):
                row = u[k][y]
                e = [row[1], row[2], self.east(row[0], east_ghost[k])]
                w = [self.west(row[2], west_ghost[k]), row[0], row[1]]
                cells = []
                for x in range(3):
                    n = u[k][y + 1][x] if y < 2 else pick(n_in[x], k)
                    s = u[k][y - 1][x] if y > 0 else pick(s_in[x], k)
                    cells.append(
                        co[MID] * row[x]
                        + (co[EAST] * e[x] + co[WEST] * w[x])
                        + (co[NORTH] * n + co[SOUTH] * s)
                    )
                rows.append(cells)
            new.append(rows)
        return new

    def pooled_step(self, u, co):
        ends = []
        for k in range(3):
            row = [u[k][y][0] + u[k][y][1] + u[k][y][2] for y in range(3)]
            col = [u[k][0][x] + u[k][1][x] + u[k][2][x] for x in (0, 2)]
            ends.append((row[0], row[2], col[0], col[1], row[0] + row[1] + row[2]))
        n_in = self.north([ends[0][0], ends[1][0]], ends[2][0])
        s_in = self.south([ends[0][1], ends[1][1]], ends[2][1])
        pick = lambda pair, k: pair[1] if k == 2 else pair[0][k]
        out = []
        for k in range(3):
            row0, row2, col0, col2, total = ends[k]
            flux_x = co[EAST] * (self.east(col0, 0.0) - col0)
            flux_x += co[WEST] * (self.west(col2, 0.0) - col2)
            flux_y = co[NORTH] * (pick(n_in, k) - row0) + co[SOUTH] * (pick(s_in, k) - row2)
            out.append(total + (flux_x + flux_y))
        return out


def phase_rows(z, ref, l, c, y, x):
    got = ref[x, pl.ds((l * z.C + c) * z.H + y, z.M, 3), :]
    return got if l == 0 else pltpu.roll(got, 4, 0)


def partial_averages(z, diff, cour, nest, *refs):
    out, (phases, strips, sem, store_phases) = refs[: z.S], refs[z.S :]
    fetch = [pltpu.make_async_copy(nest.at[l], strips.at[l], sem.at[l]) for l in range(z.L)]
    for copy in fetch:
        copy.start()
    d = lax.axis_index("dev")
    own = lax.rem(lax.axis_index("grp"), z.S)
    C, M, CS = z.C, z.M, z.CS
    fine = lax.rem(iota((2 * z.W, z.W), 0), z.W)
    place = iota((2 * z.W, z.W), 1)
    at = lax.rem(place, LANES) * 3 + place // LANES
    deal = jnp.where(fine == at, 1.0, 0.0).astype(BF16)
    rows = C * z.H
    for l in range(z.L):
        fetch[l].wait()
        dealt = split_dot(strips[l].reshape(rows, z.W), deal)
        for x in range(3):
            phases[x, l * rows : (l + 1) * rows, :] = dealt[:, x * LANES : (x + 1) * LANES]
    store_phases()
    strip = Strip()
    keep_high = strip.any_low | (strip.any_high & (d < z.D - 1))
    keep_low = strip.any_high | (strip.any_low & (d > 0))
    zero = jnp.zeros((8, LANES), F32)
    ghosts = [0.0] * 3
    base = z.L * CS * M

    def hold(u):
        cap = [
            [jnp.where(keep_high, v, 0.0) for v in u[2][0]],
            u[2][1],
            [jnp.where(keep_low, v, 0.0) for v in u[2][2]],
        ]
        return [u[0], u[1], cap]

    for part in range(z.S):

        def channel(i, _, to=out[part], first=jnp.bitwise_xor(own, part) * CS):
            c = first + i
            co = weights(diff, cour, c, 3.0)
            u = [
                [[phase_rows(z, phases, l, c, y, x) for x in range(3)] for y in range(3)]
                for l in range(2)
            ]
            u.append([[zero] * 3] * 3)
            for _step in range(2):
                u = hold(strip.step(u, co, ghosts, ghosts))
            got = [v * (1.0 / 9.0) for v in strip.pooled_step(u, co)]
            got[1] = pltpu.roll(got[1], 4, 0)
            for l in range(2):
                row = pl.multiple_of((l * CS + i) * M, M)
                to[pl.ds(row, M), :] = got[l]
                for side, sub in enumerate(((7, 3), (0, 4))):
                    row = base + (l * 2 + side) * CS + i
                    to[pl.ds(row, 1), :] = got[2][sub[l] : sub[l] + 1]
            return 0

        lax.fori_loop(0, CS, channel, 0, unroll=2)


def pick_band(z, anc, *refs):
    got, out = refs[: z.G], refs[z.G]
    g = lax.axis_index("grp")
    top = g // z.S * z.NB
    base, size = z.L * z.CS * z.M, z.CS * z.M
    for band in range(z.NB):
        n = nest_at(z, anc, top + band)
        of = n // z.L
        slot = jnp.bitwise_xor(of, g)
        first = n - of * z.L == 0
        for k in range(z.G):

            @pl.when(slot == k)
            def _(k=k, first=first, band=band):
                main = jnp.where(first, got[k][:size, :], got[k][size : 2 * size, :])
                edge = jnp.where(
                    first,
                    got[k][base : base + 2 * z.CS, :],
                    got[k][base + 2 * z.CS : base + 4 * z.CS, :],
                )
                for y in range(z.Y):
                    out[band * z.Y + y, :size, :] = main
                    out[band * z.Y + y, size:, :] = edge


def ring_parts(z, anc, parent, nest, buf, up, dn, tail, head, sem):
    fetch = [
        pltpu.make_async_copy(nest.at[:, :, z.H - 8 :, :], tail, sem.at[0]),
        pltpu.make_async_copy(nest.at[:, :, :8, :], head, sem.at[1]),
    ]
    for copy in fetch:
        copy.start()
    g, d = lax.axis_index("grp"), lax.axis_index("dev")
    row_base, col_base = g * z.TR, d * z.TC
    lane_t = iota((z.TR, LANES), 1)
    lane_f = iota((z.FR, LANES), 1)
    row_f = iota((z.FR, LANES), 0)
    lane_c = iota((z.C, LANES), 1)
    buf[...] = jnp.zeros_like(buf)

    def nest_ring(n, _):
        to = n // z.L
        l = n - to * z.L
        slot = to
        r, q = anc[0, n], anc[1, n]
        rows_meet = (r < row_base + z.TR) & (r + z.FR > row_base)
        cols_meet = (q < col_base + z.TC) & (q + z.FC > col_base)
        shift_r = lax.rem(row_base - r + 2 * z.G * z.TR, z.FR)
        shift_q = lax.rem(col_base - q + 2 * z.D * z.TC, z.FC)
        for side in range(2):
            col = (q - 1 if side == 0 else q + z.FC) - col_base
            first = (l * 2 + side) * z.C

            @pl.when(rows_meet & (col >= 0) & (col < z.TC))
            def _(col=col, first=first):
                acc = jnp.zeros((z.TR, LANES), F32)
                for c in range(z.C):
                    at = first + c
                    moved = pltpu.roll(parent[c], lax.rem(at - col + LANES, LANES), 1)
                    acc = jnp.where(lane_t == at, moved, acc)
                if z.FR > z.TR:
                    acc = jnp.concatenate([acc, jnp.zeros((z.FR - z.TR, LANES), F32)], axis=0)
                acc = pltpu.roll(acc, shift_r, 0)
                y = row_f + (r - row_base)
                good = (y >= 0) & (y < z.TR) & (lane_f >= first) & (lane_f < first + z.C)
                buf[slot, : z.FR, :] = jnp.where(good, acc, buf[slot, : z.FR, :])

            row = (r - 1 if side == 0 else r + z.FR) - row_base

            @pl.when(cols_meet & (row >= 0) & (row < z.TR))
            def _(row=row, first=first):
                rows = jnp.concatenate(
                    [parent[c, pl.ds(row, 1), :] for c in range(z.C)], axis=0
                )
                x = lane_c + (q - col_base)
                moved = jnp.where((x >= 0) & (x < z.TC), pltpu.roll(rows, shift_q, 1), 0.0)
                buf[slot, pl.ds(pl.multiple_of(z.FR + first, 8), z.C), :] = moved

        return 0

    lax.fori_loop(0, z.N, nest_ring, 0)
    for to in range(z.G):
        edge = jnp.where(to > g, z.TR - 1, 0)
        for c in range(z.C):
            buf[to, z.RING + c : z.RING + c + 1, :] = parent[c, pl.ds(edge, 1), :]
    first = jnp.zeros((z.TR, LANES), F32)
    last = first
    for c in range(z.C):
        first = jnp.where(lane_t == c, pltpu.roll(parent[c], c, 1) if c else parent[c], first)
        last = jnp.where(lane_t == c, pltpu.roll(parent[c], c + 1, 1), last)
    up[z.EDGE :, :] = last
    dn[z.EDGE :, :] = first
    for copy in fetch:
        copy.wait()
    for l in range(z.L):
        for c in range(z.C):
            for x in range(3):
                at = x * z.HALO + 3 * (l * z.C + c)
                lanes = slice(x * LANES, (x + 1) * LANES)
                up[at : at + 3, :] = tail[l, c, 5:8, lanes]
                dn[at : at + 3, :] = head[l, c, 0:3, lanes]


def ring_next(z, got, out, edges, slab):
    g, d = lax.axis_index("grp"), lax.axis_index("dev")
    C, L, FR, M = z.C, z.L, z.FR, z.M
    total = got[0, : z.RING, :]
    for k in range(1, z.G):
        total = total + got[k, : z.RING, :]
    slab[...] = total
    sub = iota((8, LANES), 0)
    for to in range(z.D):
        out[to, :M, :] = slab[to * M : (to + 1) * M, :]
        hi = min(to * M + M, FR - 1)
        lo = max(to * M - 1, 0)
        hi, lo = slab[hi : hi + 1, :], slab[lo : lo + 1, :]
        out[to, M:16, :] = jnp.where(sub == 0, hi, jnp.where(sub == 7, lo, 0.0))
        for l in range(L):
            at = 16 + l * C
            if to == 0 or to == z.D - 1:
                k = FR + (l * 2 + (0 if to == 0 else 1)) * C
                out[to, at : at + C, :] = slab[k : k + C, :]
            else:
                out[to, at : at + C, :] = jnp.zeros((C, LANES), F32)
    before, after = jnp.maximum(g - 1, 0), jnp.minimum(g + 1, z.G - 1)
    edges[:C, :] = jnp.where(g > 0, got[before, z.RING :, :], 0.0)
    edges[C:, :] = jnp.where(g < z.G - 1, got[after, z.RING :, :], 0.0)
    lane = iota((8, LANES), 1)
    first = jnp.zeros((8, LANES), F32)
    last = first
    for c in range(C):
        lo = edges[c : c + 1, :]
        hi = edges[C + c : C + c + 1, :]
        cap = jnp.where(sub == 0, hi, jnp.where(sub == 7, lo, 0.0))
        first = jnp.where(lane == c, pltpu.roll(cap, c, 1) if c else cap, first)
        last = jnp.where(lane == c, pltpu.roll(cap, c + 1, 1), last)
    for to in range(z.D):
        out[to, z.RG2 - 8 :, :] = jnp.where(to > d, last, first)


def nest_steps(z, diff, cour, phases, got, up_in, dn_in, out, back, ring, up, dn):
    d = lax.axis_index("dev")
    C, M = z.C, z.M
    strip = Strip()
    fine = lax.rem(iota((2 * z.W, z.W), 0), z.W)
    place = iota((2 * z.W, z.W), 1)
    deal = jnp.where(fine == lax.rem(place, LANES) * 3 + place // LANES, 1.0, 0.0).astype(BF16)
    for source, target in ((up_in, up), (dn_in, dn)):
        halo = [source[x * z.HALO : (x + 1) * z.HALO, :] for x in range(3)]
        dealt = split_dot(jnp.concatenate(halo, axis=1), deal)
        for x in range(3):
            target[x * z.HALO : (x + 1) * z.HALO, :] = dealt[:, x * LANES : (x + 1) * LANES]
    total = got[0]
    for k in range(1, z.D):
        total = total + got[k]
    ring[...] = total
    side_main = [ring[:M, :], pltpu.roll(ring[:M, :], 4, 0)]
    side_cap = jnp.where(
        strip.any_high, ring[M : M + 1, :], jnp.where(strip.any_low, ring[15:16, :], 0.0)
    )
    hold_low, hold_high = strip.any_low & (d == 0), strip.any_high & (d == z.D - 1)
    nest_1 = strip.high[1] | strip.low[1]

    def channel(c, _):
        co = weights(diff, cour, c, 3.0)
        u = [
            [[phase_rows(z, phases, l, c, y, x) for x in range(3)] for y in range(3)]
            for l in range(2)
        ]
        cap = []
        for y in range(3):
            row = []
            for x in range(3):
                v = jnp.zeros((8, LANES), F32)
                for l in range(2):
                    at = x * z.HALO + (l * C + c) * 3 + y
                    v = jnp.where(strip.high[l], dn[pl.ds(at, 1), :], v)
                    v = jnp.where(strip.low[l], up[pl.ds(at, 1), :], v)
                row.append(v)
            cap.append(row)
        u.append(cap)
        end = jnp.where(nest_1, ring[pl.ds(16 + C + c, 1), :], ring[pl.ds(16 + c, 1), :])
        west, east = [], []
        for side, lane, ghosts in ((0, 0, west), (1, LANES - 1, east)):
            turn = [lax.rem(lane - ((l * 2 + side) * C + c) + LANES, LANES) for l in range(2)]
            for l in range(2):
                ghosts.append(pltpu.roll(side_main[l], turn[l], 1))
            caps = [pltpu.roll(side_cap, turn[l], 1) for l in range(2)]
            ghosts.append(jnp.where(nest_1, caps[1], caps[0]))

        def hold(u):
            cap = [
                [jnp.where(hold_high, end, v) for v in u[2][0]],
                u[2][1],
                [jnp.where(hold_low, end, v) for v in u[2][2]],
            ]
            return [u[0], u[1], cap]

        u = hold(u)
        for k in range(3):
            u = strip.step(u, co, west, east)
            if k < 2:
                u = hold(u)
        for l in range(2):
            for y in range(3):
                for x in range(3):
                    v = u[l][y][x]
                    v = v if l == 0 else pltpu.roll(v, 4, 0)
                    back[x, pl.ds((l * C + c) * z.H + y, M, 3), :] = v
        return 0

    lax.fori_loop(0, C, channel, 0, unroll=2)
    fine = iota((2 * z.W, z.W), 1)
    place = lax.rem(iota((2 * z.W, z.W), 0), z.W)
    at = lax.rem(place, LANES) * 3 + place // LANES
    undeal = jnp.where(fine == at, 1.0, 0.0).astype(BF16)
    done = split_dot(jnp.concatenate([back[0], back[1], back[2]], axis=1), undeal)
    out[...] = done.reshape(z.L, C, z.H, z.W)


def parent_step(z, anc, diff, cour, parent, edges, up_in, dn_in, got, out):
    g, d = lax.axis_index("grp"), lax.axis_index("dev")
    C = z.C
    rows = z.TR + 8
    n = nest_at(z, anc, g // z.S * z.NB + d // z.Y)
    i = iota((z.TR, LANES), 0) + (g * z.TR - anc[0, n])
    j = iota((z.TR, LANES), 1) + (d * z.TC - anc[1, n])
    inside = (i >= 0) & (i < z.FR) & (j >= 0) & (j < z.FC)
    one = lambda cond: jnp.where(cond, 1.0, 0.0).astype(F32)
    on_w, on_e = one(inside & (j == 0)), one(inside & (j == z.FC - 1))
    on_s, on_n = one(inside & (i == 0)), one(inside & (i == z.FR - 1))
    i_end, j_end = one((i == 0) | (i == z.FR - 1)), one((j == 0) | (j == z.FC - 1))
    i_lo, i_hi = one(i > 0), one(i < z.FR - 1)
    j_lo, j_hi = one(j > 0), one(j < z.FC - 1)
    lane = iota((rows, LANES), 1)
    sub = iota((8, LANES), 0)

    cap_w = jnp.where(d > 0, got[jnp.maximum(d - 1, 0), z.RG2 - 8 :, :], 0.0)
    cap_e = jnp.where(d < z.D - 1, got[jnp.minimum(d + 1, z.D - 1), z.RG2 - 8 :, :], 0.0)
    col_w = jnp.concatenate([up_in[z.EDGE :, :], cap_w], axis=0)
    col_e = jnp.concatenate([dn_in[z.EDGE :, :], cap_e], axis=0)

    def channel(c, _):
        co = [v[:1] for v in weights(diff, cour, c, 1.0)]
        fm, fe, fw, fn, fs = [v[:1] for v in weights(diff, cour, c, 3.0)]
        lo = edges[pl.ds(c, 1), :]
        hi = edges[pl.ds(C + c, 1), :]
        cap = jnp.where(sub == 0, hi, jnp.where(sub == 7, lo, 0.0))
        full = jnp.concatenate([parent[c], cap], axis=0)
        w_in = pltpu.roll(col_w, lax.rem(LANES - c, LANES), 1)
        e_in = pltpu.roll(col_e, LANES - 1 - c, 1)
        w_all = jnp.where(lane == 0, w_in, pltpu.roll(full, 1, 1))
        e_all = jnp.where(lane == LANES - 1, e_in, pltpu.roll(full, LANES - 1, 1))
        up = lambda x: pltpu.roll(x, rows - 1, 0)[: z.TR]
        down = lambda x: pltpu.roll(x, 1, 0)[: z.TR]
        mid = full[: z.TR]
        w, e, n, s = w_all[: z.TR], e_all[: z.TR], up(full), down(full)
        w_up, w_down, e_up, e_down = up(w_all), down(w_all), up(e_all), down(e_all)
        step = (
            co[MID] * mid
            + (co[EAST] * e + co[WEST] * w)
            + (co[NORTH] * n + co[SOUTH] * s)
        )
        a, b, k, x = ghost_share(fw, fe, fm, fs, fn)
        share = on_w * ((a - x * i_end) * w + (b * i_lo) * w_down + (k * i_hi) * w_up)
        a, b, k, x = ghost_share(fe, fw, fm, fs, fn)
        share += on_e * ((a - x * i_end) * e + (b * i_lo) * e_down + (k * i_hi) * e_up)
        a, b, k, x = ghost_share(fs, fn, fm, fw, fe)
        share += on_s * ((a - x * j_end) * s + (b * j_lo) * w_down + (k * j_hi) * e_down)
        a, b, k, x = ghost_share(fn, fs, fm, fw, fe)
        share += on_n * ((a - x * j_end) * n + (b * j_lo) * w_up + (k * j_hi) * e_up)
        out[c] = jnp.where(inside, share, step)
        return 0

    lax.fori_loop(0, C, channel, 0, unroll=2)


def merge(z, which, anchor, base, pieces):
    count, size = len(which), z.CS * z.M

    def kernel(*refs):
        anc_in, base_in, refs = refs[0], refs[1], refs[2:]
        source, base_out, refs = refs[:count], refs[count], refs[count + 1 :]
        anc, refs = refs[0], refs[1:]
        inner, (old, new, twice, sem) = refs[:count], refs[count:]
        g, d = lax.axis_index("grp"), lax.axis_index("dev")
        part = lax.rem(g, z.S)
        firsts = [lax.rem(part - k + z.S, z.S) * z.CS for k in which]
        fetch = [pltpu.make_async_copy(anc_in, anc, sem.at[0])]
        for k in range(count):
            rows = base_in.at[pl.ds(firsts[k], z.CS)]
            fetch.append(pltpu.make_async_copy(source[k], inner[k], sem.at[1 + 2 * k]))
            fetch.append(pltpu.make_async_copy(rows, old.at[k], sem.at[2 + 2 * k]))
        for copy in fetch:
            copy.start()
        for copy in fetch:
            copy.wait()
        n = nest_at(z, anc, g // z.S * z.NB + d // z.Y)
        r, q = anc[0, n], anc[1, n]
        start = lax.rem(g * z.TR - r + 2 * z.G * z.TR, z.FR)
        shift_q = lax.rem(q - d * z.TC + 2 * z.D * z.TC, z.FC)
        i = iota((z.TR, LANES), 0) + (g * z.TR - r)
        j = iota((z.TR, LANES), 1) + (d * z.TC - q)
        inside = (i >= 0) & (i < z.FR) & (j >= 0) & (j < z.FC)
        sub = iota((z.M, LANES), 0)
        store = []
        for k in range(count):
            piece = inner[k]
            for c in range(z.CS):
                for m in range(z.D):
                    x = piece[m, c * z.M : (c + 1) * z.M, :]
                    if m + 1 < z.D:
                        row = piece[m + 1, size + c : size + c + 1, :]
                        x += jnp.where(sub == z.M - 1, row, 0.0)
                    if m > 0:
                        row = piece[m - 1, size + z.CS + c : size + z.CS + c + 1, :]
                        x += jnp.where(sub == 0, row, 0.0)
                    twice[c % 4, m * z.M : (m + 1) * z.M, :] = x
                    if m * z.M < z.TR:
                        twice[c % 4, z.FR + m * z.M : z.FR + (m + 1) * z.M, :] = x
                x = pltpu.roll(twice[c % 4, pl.ds(start, z.TR), :], shift_q, 1)
                new[k, c] = old[k, c] + jnp.where(inside, x, 0.0)
            rows = base_out.at[pl.ds(firsts[k], z.CS)]
            store.append(pltpu.make_async_copy(new.at[k], rows, sem.at[1 + 2 * k]))
            store[-1].start()
        for copy in store:
            copy.wait()

    place = pl.BlockSpec(memory_space=pltpu.HBM)
    half = pltpu.VMEM((count, z.CS, z.TR, LANES), F32)
    return pl.pallas_call(
        kernel,
        out_shape=jax.ShapeDtypeStruct(base.shape, F32),
        in_specs=[place] * (2 + count),
        out_specs=place,
        input_output_aliases={1: 0},
        scratch_shapes=[
            pltpu.SMEM(anchor.shape, anchor.dtype),
            *[pltpu.VMEM(x.shape, F32) for x in pieces],
            half,
            half,
            pltpu.VMEM((4, z.FR + z.TR, LANES), F32),
            pltpu.SemaphoreType.DMA((1 + 2 * count,)),
        ],
        compiler_params=pltpu.CompilerParams(vmem_limit_bytes=VMEM_LIMIT),
    )(anchor, base, *pieces)


def shards(parent, nest, anchor, diff, cour):
    z = Sizes(parent, nest, anchor, lax.axis_size("grp"), lax.axis_size("dev"))
    sds = lambda *shape: jax.ShapeDtypeStruct(shape, F32)
    vmem = lambda *shape: pltpu.VMEM(shape, F32)
    to_grp = lambda x, k: lax.ppermute(x, "grp", [(a, a ^ k) for a in range(z.G)])

    anchor = anchor.T
    message = sds(z.EDGE + z.TR, LANES)
    edge_tile = vmem(z.L, z.C, 8, z.W)
    ring, up, dn = call(
        functools.partial(ring_parts, z),
        [sds(z.G, z.RG, LANES), message, message],
        (anchor,),
        (parent,),
        [edge_tile, edge_tile, pltpu.SemaphoreType.DMA((2,))],
        (nest,),
    )
    nest, ring = lax.optimization_barrier((nest, ring))
    ring = lax.all_to_all(ring, "grp", 0, 0, tiled=True)
    *chunks, phases = call(
        functools.partial(partial_averages, z),
        [sds(z.R1, LANES)] * z.S + [sds(3, z.L * z.C * z.H, LANES)],
        (diff, cour),
        (),
        [pltpu.VMEM(nest.shape, F32), pltpu.SemaphoreType.DMA((z.L,))],
        (nest,),
        z.S,
    )
    chunks, ring, up, dn = lax.optimization_barrier((chunks, ring, up, dn))
    forward = [(k, k + 1) for k in range(z.D - 1)]
    up = lax.ppermute(up, "dev", forward)
    dn = lax.ppermute(dn, "dev", [(b, a) for a, b in forward])
    got = [chunks[0]] + [to_grp(chunks[k % z.S], k) for k in range(1, z.G)]
    ring, edges = call(
        functools.partial(ring_next, z),
        [sds(z.D, z.RG2, LANES), sds(2 * z.C, LANES)],
        (),
        (ring,),
        [vmem(z.RING, LANES)],
    )
    ring = lax.all_to_all(ring, "dev", 0, 0, tiled=True)
    (avg,) = call(functools.partial(pick_band, z), [sds(z.D, z.R2, LANES)], (anchor,), got)
    avg, phases, edges, ring, up, dn = lax.optimization_barrier(
        (avg, phases, edges, ring, up, dn)
    )
    avg = lax.all_to_all(avg, "dev", 0, 0, tiled=True)
    (out,) = call(
        functools.partial(parent_step, z),
        [jax.ShapeDtypeStruct(parent.shape, F32)],
        (anchor, diff, cour),
        (parent, edges, up, dn, ring),
    )
    (nest_out,) = call(
        functools.partial(nest_steps, z),
        [jax.ShapeDtypeStruct(nest.shape, F32)],
        (diff, cour),
        (phases, ring, up, dn),
        [
            vmem(3, z.L * z.C * z.H, LANES),
            vmem(z.RG2, LANES),
            vmem(z.EDGE, LANES),
            vmem(z.EDGE, LANES),
        ],
    )
    avg, nest_out, out = lax.optimization_barrier((avg, nest_out, out))
    pieces = [avg]
    for k in range(1, z.S):
        pairs = [(a, a // z.S * z.S + (a + k) % z.S) for a in range(z.G)]
        pieces.append(lax.ppermute(avg, "grp", pairs))
    for which in ([0], list(range(1, z.S))):
        out = merge(z, which, anchor, out, [pieces[k] for k in which])
    return out, nest_out


def solution(mesh):
    placed = (P(None, "grp", "dev"), P("grp", None, "dev", None), P(), P(), P())
    return jax.shard_map(
        shards,
        mesh=mesh,
        in_specs=placed,
        out_specs=(P(None, "grp", "dev"), P("grp", None, "dev", None)),
        check_vma=False,
    )
```

```python
import functools

import jax
import jax.numpy as jnp
from jax import lax
from jax.experimental import pallas as pl
from jax.experimental.pallas import tpu as pltpu
from jax.sharding import PartitionSpec as P

F32 = jnp.float32
BF16 = jnp.bfloat16
LANES = 128
VMEM_LIMIT = 65408 * 1024
MID, EAST, WEST, NORTH, SOUTH = range(5)


class Sizes:
    def __init__(self, parent, nest, anchor, grp_count, dev_count):
        self.C, self.TR, self.TC = parent.shape
        self.L, _, self.H, self.W = nest.shape
        self.N = anchor.shape[0]
        self.G, self.D = grp_count, dev_count
        self.M = self.H // 3
        self.FR, self.FC = self.M * self.D, self.W // 3
        self.S = self.G // 2
        self.NB = self.N // 2
        self.Y = self.D // self.NB
        self.CS = self.C // self.S
        self.BR, self.BC = self.S * self.TR, self.Y * self.TC
        self.R1 = self.L * self.CS * (self.M + 2)
        self.R2 = self.CS * (self.M + 2)
        self.RING = self.FR + self.L * 2 * self.C
        self.RG = self.RING + self.C
        self.RG2 = 16 + self.L * self.C + 8
        self.HALO = self.L * self.C * 3
        self.EDGE = 3 * self.HALO
        assert self.H == 24 and self.FC == LANES and self.TC == LANES
        assert self.FR >= self.TR and self.L == 2


def call(body, out_shape, smem, args, scratch=(), raw=(), early=None):
    moved = [*smem, *args]
    n_in, n_raw, n_out = len(moved), len(raw), len(out_shape)
    place = pl.BlockSpec(memory_space=pltpu.HBM)

    def kernel(*refs):
        source, refs = refs[:n_in], refs[n_in:]
        stay, refs = refs[:n_raw], refs[n_raw:]
        target, refs = refs[:n_out], refs[n_out:]
        inner, refs = refs[:n_in], refs[n_in:]
        result, refs = refs[:n_out], refs[n_out:]
        extra, sem = refs[:-1], refs[-1]
        fetch = [pltpu.make_async_copy(a, b, sem.at[k]) for k, (a, b) in enumerate(zip(source, inner))]
        for copy in fetch:
            copy.start()
        for copy in fetch:
            copy.wait()
        store = [
            pltpu.make_async_copy(a, b, sem.at[n_in + k]) for k, (a, b) in enumerate(zip(result, target))
        ]
        if early is None:
            body(*inner, *stay, *result, *extra)
        else:
            body(*inner, *stay, *result, *extra, store[early].start)
        for k, copy in enumerate(store):
            if k != early:
                copy.start()
        for copy in store:
            copy.wait()

    return pl.pallas_call(
        kernel,
        out_shape=list(out_shape),
        in_specs=[place] * (n_in + n_raw),
        out_specs=[place] * n_out,
        scratch_shapes=[
            *[pltpu.SMEM(x.shape, x.dtype) for x in smem],
            *[pltpu.VMEM(x.shape, x.dtype) for x in args],
            *[pltpu.VMEM(x.shape, x.dtype) for x in out_shape],
            *scratch,
            pltpu.SemaphoreType.DMA((n_in + n_out,)),
        ],
        compiler_params=pltpu.CompilerParams(vmem_limit_bytes=VMEM_LIMIT),
    )(*moved, *raw)


def iota(shape, dim):
    return lax.broadcasted_iota(jnp.int32, shape, dim)


def split_dot(x, table):
    high = x.astype(BF16)
    low = (x - high.astype(F32)).astype(BF16)
    return jnp.dot(jnp.concatenate([high, low], axis=1), table, preferred_element_type=F32)


def nest_at(z, anc, band):
    found = 0
    for n in range(z.N):
        found += jnp.where(anc[0, n] // z.BR * z.NB + anc[1, n] // z.BC == band, n, 0)
    return found


def weights(diff, cour, c, times):
    splat = lambda ref, k: jnp.full((8, LANES), ref[k, c], F32)
    east = times * splat(diff, 0)
    north = times * splat(diff, 1)
    west = east + splat(cour, 0)
    south = north + splat(cour, 1)
    return 1.0 - (east + west) - (north + south), east, west, north, south


def ghost_share(inject, back, mid, plus, minus):
    stay = mid + inject
    m0 = inject * (1.0 + stay + mid * stay + inject * (stay + back) + 2.0 * plus * minus)
    p1 = inject * plus * (1.0 + 2.0 * stay)
    p2 = inject * plus * plus
    n1 = inject * minus * (1.0 + 2.0 * stay)
    n2 = inject * minus * minus
    ninth = 1.0 / 9.0
    same = (3.0 * m0 + 2.0 * p1 + p2 + 2.0 * n1 + n2) * ninth
    return same, (p1 + 2.0 * p2) * ninth, (n1 + 2.0 * n2) * ninth, inject * plus * minus * ninth


class Strip:
    def __init__(self):
        sub = iota((8, LANES), 0)
        lane = iota((8, LANES), 1)
        self.high = [sub == 0, sub == 4]
        self.low = [sub == 7, sub == 3]
        self.any_high = (sub == 0) | (sub == 4)
        self.any_low = (sub == 7) | (sub == 3)
        self.first, self.last = lane == 0, lane == LANES - 1

    def east(self, x, ghost):
        return jnp.where(self.last, ghost, pltpu.roll(x, LANES - 1, 1))

    def west(self, x, ghost):
        return jnp.where(self.first, ghost, pltpu.roll(x, 1, 1))

    def north(self, mains, cap):
        up = [pltpu.roll(m, 7, 0) for m in mains]
        cap_up = pltpu.roll(cap, 7, 0)
        new = [jnp.where(self.low[l], cap_up, up[l]) for l in range(2)]
        return new, jnp.where(self.low[0], up[0], jnp.where(self.low[1], up[1], 0.0))

    def south(self, mains, cap):
        down = [pltpu.roll(m, 1, 0) for m in mains]
        cap_down = pltpu.roll(cap, 1, 0)
        new = [jnp.where(self.high[l], cap_down, down[l]) for l in range(2)]
        return new, jnp.where(self.high[0], down[0], jnp.where(self.high[1], down[1], 0.0))

    def step(self, u, co, west_ghost, east_ghost):
        n_in = [self.north([u[0][0][x], u[1][0][x]], u[2][0][x]) for x in range(3)]
        s_in = [self.south([u[0][2][x], u[1][2][x]], u[2][2][x]) for x in range(3)]
        pick = lambda pair, k: pair[1] if k == 2 else pair[0][k]
        new = []
        for k in range(3):
            rows = []
            for y in range(3):
                row = u[k][y]
                e = [row[1], row[2], self.east(row[0], east_ghost[k])]
                w = [self.west(row[2], west_ghost[k]), row[0], row[1]]
                cells = []
                for x in range(3):
                    n = u[k][y + 1][x] if y < 2 else pick(n_in[x], k)
                    s = u[k][y - 1][x] if y > 0 else pick(s_in[x], k)
                    cells.append(
                        co[MID] * row[x]
                        + (co[EAST] * e[x] + co[WEST] * w[x])
                        + (co[NORTH] * n + co[SOUTH] * s)
                    )
                rows.append(cells)
            new.append(rows)
        return new

    def pooled_step(self, u, co):
        ends = []
        for k in range(3):
            row = [u[k][y][0] + u[k][y][1] + u[k][y][2] for y in range(3)]
            col = [u[k][0][x] + u[k][1][x] + u[k][2][x] for x in (0, 2)]
            ends.append((row[0], row[2], col[0], col[1], row[0] + row[1] + row[2]))
        n_in = self.north([ends[0][0], ends[1][0]], ends[2][0])
        s_in = self.south([ends[0][1], ends[1][1]], ends[2][1])
        pick = lambda pair, k: pair[1] if k == 2 else pair[0][k]
        out = []
        for k in range(3):
            row0, row2, col0, col2, total = ends[k]
            flux_x = co[EAST] * (self.east(col0, 0.0) - col0)
            flux_x += co[WEST] * (self.west(col2, 0.0) - col2)
            flux_y = co[NORTH] * (pick(n_in, k) - row0) + co[SOUTH] * (pick(s_in, k) - row2)
            out.append(total + (flux_x + flux_y))
        return out


def phase_rows(z, ref, l, c, y, x):
    got = ref[x, pl.ds((l * z.C + c) * z.H + y, z.M, 3), :]
    return got if l == 0 else pltpu.roll(got, 4, 0)


def partial_averages(z, diff, cour, nest, *refs):
    out, (phases, strips, sem, store_phases) = refs[: z.S], refs[z.S :]
    fetch = [pltpu.make_async_copy(nest.at[l], strips.at[l], sem.at[l]) for l in range(z.L)]
    for copy in fetch:
        copy.start()
    d = lax.axis_index("dev")
    own = lax.rem(lax.axis_index("grp"), z.S)
    C, M, CS = z.C, z.M, z.CS
    fine = lax.rem(iota((2 * z.W, z.W), 0), z.W)
    place = iota((2 * z.W, z.W), 1)
    at = lax.rem(place, LANES) * 3 + place // LANES
    deal = jnp.where(fine == at, 1.0, 0.0).astype(BF16)
    rows = C * z.H
    for l in range(z.L):
        fetch[l].wait()
        dealt = split_dot(strips[l].reshape(rows, z.W), deal)
        for x in range(3):
            phases[x, l * rows : (l + 1) * rows, :] = dealt[:, x * LANES : (x + 1) * LANES]
    store_phases()
    strip = Strip()
    keep_high = strip.any_low | (strip.any_high & (d < z.D - 1))
    keep_low = strip.any_high | (strip.any_low & (d > 0))
    zero = jnp.zeros((8, LANES), F32)
    ghosts = [0.0] * 3
    base = z.L * CS * M

    def hold(u):
        cap = [
            [jnp.where(keep_high, v, 0.0) for v in u[2][0]],
            u[2][1],
            [jnp.where(keep_low, v, 0.0) for v in u[2][2]],
        ]
        return [u[0], u[1], cap]

    for part in range(z.S):

        def channel(i, _, to=out[part], first=jnp.bitwise_xor(own, part) * CS):
            c = first + i
            co = weights(diff, cour, c, 3.0)
            u = [
                [[phase_rows(z, phases, l, c, y, x) for x in range(3)] for y in range(3)]
                for l in range(2)
            ]
            u.append([[zero] * 3] * 3)
            for _step in range(2):
                u = hold(strip.step(u, co, ghosts, ghosts))
            got = [v * (1.0 / 9.0) for v in strip.pooled_step(u, co)]
            got[1] = pltpu.roll(got[1], 4, 0)
            for l in range(2):
                row = pl.multiple_of((l * CS + i) * M, M)
                to[pl.ds(row, M), :] = got[l]
                for side, sub in enumerate(((7, 3), (0, 4))):
                    row = base + (l * 2 + side) * CS + i
                    to[pl.ds(row, 1), :] = got[2][sub[l] : sub[l] + 1]
            return 0

        lax.fori_loop(0, CS, channel, 0, unroll=2)


def pick_band(z, anc, *refs):
    got, out = refs[: z.G], refs[z.G]
    g = lax.axis_index("grp")
    top = g // z.S * z.NB
    base, size = z.L * z.CS * z.M, z.CS * z.M
    for band in range(z.NB):
        n = nest_at(z, anc, top + band)
        of = n // z.L
        slot = jnp.bitwise_xor(of, g)
        first = n - of * z.L == 0
        for k in range(z.G):

            @pl.when(slot == k)
            def _(k=k, first=first, band=band):
                main = jnp.where(first, got[k][:size, :], got[k][size : 2 * size, :])
                edge = jnp.where(
                    first,
                    got[k][base : base + 2 * z.CS, :],
                    got[k][base + 2 * z.CS : base + 4 * z.CS, :],
                )
                for y in range(z.Y):
                    out[band * z.Y + y, :size, :] = main
                    out[band * z.Y + y, size:, :] = edge


def ring_parts(z, anc, parent, nest, buf, up, dn, tail, head, sem):
    fetch = [
        pltpu.make_async_copy(nest.at[:, :, z.H - 8 :, :], tail, sem.at[0]),
        pltpu.make_async_copy(nest.at[:, :, :8, :], head, sem.at[1]),
    ]
    for copy in fetch:
        copy.start()
    g, d = lax.axis_index("grp"), lax.axis_index("dev")
    row_base, col_base = g * z.TR, d * z.TC
    lane_t = iota((z.TR, LANES), 1)
    lane_f = iota((z.FR, LANES), 1)
    row_f = iota((z.FR, LANES), 0)
    lane_c = iota((z.C, LANES), 1)
    buf[...] = jnp.zeros_like(buf)

    def nest_ring(n, _):
        to = n // z.L
        l = n - to * z.L
        slot = to
        r, q = anc[0, n], anc[1, n]
        rows_meet = (r < row_base + z.TR) & (r + z.FR > row_base)
        cols_meet = (q < col_base + z.TC) & (q + z.FC > col_base)
        shift_r = lax.rem(row_base - r + 2 * z.G * z.TR, z.FR)
        shift_q = lax.rem(col_base - q + 2 * z.D * z.TC, z.FC)
        for side in range(2):
            col = (q - 1 if side == 0 else q + z.FC) - col_base
            first = (l * 2 + side) * z.C

            @pl.when(rows_meet & (col >= 0) & (col < z.TC))
            def _(col=col, first=first):
                acc = jnp.zeros((z.TR, LANES), F32)
                for c in range(z.C):
                    at = first + c
                    moved = pltpu.roll(parent[c], lax.rem(at - col + LANES, LANES), 1)
                    acc = jnp.where(lane_t == at, moved, acc)
                if z.FR > z.TR:
                    acc = jnp.concatenate([acc, jnp.zeros((z.FR - z.TR, LANES), F32)], axis=0)
                acc = pltpu.roll(acc, shift_r, 0)
                y = row_f + (r - row_base)
                good = (y >= 0) & (y < z.TR) & (lane_f >= first) & (lane_f < first + z.C)
                buf[slot, : z.FR, :] = jnp.where(good, acc, buf[slot, : z.FR, :])

            row = (r - 1 if side == 0 else r + z.FR) - row_base

            @pl.when(cols_meet & (row >= 0) & (row < z.TR))
            def _(row=row, first=first):
                rows = jnp.concatenate(
                    [parent[c, pl.ds(row, 1), :] for c in range(z.C)], axis=0
                )
                x = lane_c + (q - col_base)
                moved = jnp.where((x >= 0) & (x < z.TC), pltpu.roll(rows, shift_q, 1), 0.0)
                buf[slot, pl.ds(pl.multiple_of(z.FR + first, 8), z.C), :] = moved

        return 0

    lax.fori_loop(0, z.N, nest_ring, 0)
    for to in range(z.G):
        edge = jnp.where(to > g, z.TR - 1, 0)
        for c in range(z.C):
            buf[to, z.RING + c : z.RING + c + 1, :] = parent[c, pl.ds(edge, 1), :]
    first = jnp.zeros((z.TR, LANES), F32)
    last = first
    for c in range(z.C):
        first = jnp.where(lane_t == c, pltpu.roll(parent[c], c, 1) if c else parent[c], first)
        last = jnp.where(lane_t == c, pltpu.roll(parent[c], c + 1, 1), last)
    up[z.EDGE :, :] = last
    dn[z.EDGE :, :] = first
    for copy in fetch:
        copy.wait()
    for l in range(z.L):
        for c in range(z.C):
            for x in range(3):
                at = x * z.HALO + 3 * (l * z.C + c)
                lanes = slice(x * LANES, (x + 1) * LANES)
                up[at : at + 3, :] = tail[l, c, 5:8, lanes]
                dn[at : at + 3, :] = head[l, c, 0:3, lanes]


def ring_next(z, got, out, edges, slab):
    g, d = lax.axis_index("grp"), lax.axis_index("dev")
    C, L, FR, M = z.C, z.L, z.FR, z.M
    total = got[0, : z.RING, :]
    for k in range(1, z.G):
        total = total + got[k, : z.RING, :]
    slab[...] = total
    sub = iota((8, LANES), 0)
    for to in range(z.D):
        out[to, :M, :] = slab[to * M : (to + 1) * M, :]
        hi = min(to * M + M, FR - 1)
        lo = max(to * M - 1, 0)
        hi, lo = slab[hi : hi + 1, :], slab[lo : lo + 1, :]
        out[to, M:16, :] = jnp.where(sub == 0, hi, jnp.where(sub == 7, lo, 0.0))
        for l in range(L):
            at = 16 + l * C
            if to == 0 or to == z.D - 1:
                k = FR + (l * 2 + (0 if to == 0 else 1)) * C
                out[to, at : at + C, :] = slab[k : k + C, :]
            else:
                out[to, at : at + C, :] = jnp.zeros((C, LANES), F32)
    before, after = jnp.maximum(g - 1, 0), jnp.minimum(g + 1, z.G - 1)
    edges[:C, :] = jnp.where(g > 0, got[before, z.RING :, :], 0.0)
    edges[C:, :] = jnp.where(g < z.G - 1, got[after, z.RING :, :], 0.0)
    lane = iota((8, LANES), 1)
    first = jnp.zeros((8, LANES), F32)
    last = first
    for c in range(C):
        lo = edges[c : c + 1, :]
        hi = edges[C + c : C + c + 1, :]
        cap = jnp.where(sub == 0, hi, jnp.where(sub == 7, lo, 0.0))
        first = jnp.where(lane == c, pltpu.roll(cap, c, 1) if c else cap, first)
        last = jnp.where(lane == c, pltpu.roll(cap, c + 1, 1), last)
    for to in range(z.D):
        out[to, z.RG2 - 8 :, :] = jnp.where(to > d, last, first)


def nest_steps(z, diff, cour, phases, got, up_in, dn_in, out, back, ring, up, dn):
    d = lax.axis_index("dev")
    C, M = z.C, z.M
    strip = Strip()
    fine = lax.rem(iota((2 * z.W, z.W), 0), z.W)
    place = iota((2 * z.W, z.W), 1)
    deal = jnp.where(fine == lax.rem(place, LANES) * 3 + place // LANES, 1.0, 0.0).astype(BF16)
    for source, target in ((up_in, up), (dn_in, dn)):
        halo = [source[x * z.HALO : (x + 1) * z.HALO, :] for x in range(3)]
        dealt = split_dot(jnp.concatenate(halo, axis=1), deal)
        for x in range(3):
            target[x * z.HALO : (x + 1) * z.HALO, :] = dealt[:, x * LANES : (x + 1) * LANES]
    total = got[0]
    for k in range(1, z.D):
        total = total + got[k]
    ring[...] = total
    side_main = [ring[:M, :], pltpu.roll(ring[:M, :], 4, 0)]
    side_cap = jnp.where(
        strip.any_high, ring[M : M + 1, :], jnp.where(strip.any_low, ring[15:16, :], 0.0)
    )
    hold_low, hold_high = strip.any_low & (d == 0), strip.any_high & (d == z.D - 1)
    nest_1 = strip.high[1] | strip.low[1]

    def channel(c, _):
        co = weights(diff, cour, c, 3.0)
        u = [
            [[phase_rows(z, phases, l, c, y, x) for x in range(3)] for y in range(3)]
            for l in range(2)
        ]
        cap = []
        for y in range(3):
            row = []
            for x in range(3):
                v = jnp.zeros((8, LANES), F32)
                for l in range(2):
                    at = x * z.HALO + (l * C + c) * 3 + y
                    v = jnp.where(strip.high[l], dn[pl.ds(at, 1), :], v)
                    v = jnp.where(strip.low[l], up[pl.ds(at, 1), :], v)
                row.append(v)
            cap.append(row)
        u.append(cap)
        end = jnp.where(nest_1, ring[pl.ds(16 + C + c, 1), :], ring[pl.ds(16 + c, 1), :])
        west, east = [], []
        for side, lane, ghosts in ((0, 0, west), (1, LANES - 1, east)):
            turn = [lax.rem(lane - ((l * 2 + side) * C + c) + LANES, LANES) for l in range(2)]
            for l in range(2):
                ghosts.append(pltpu.roll(side_main[l], turn[l], 1))
            caps = [pltpu.roll(side_cap, turn[l], 1) for l in range(2)]
            ghosts.append(jnp.where(nest_1, caps[1], caps[0]))

        def hold(u):
            cap = [
                [jnp.where(hold_high, end, v) for v in u[2][0]],
                u[2][1],
                [jnp.where(hold_low, end, v) for v in u[2][2]],
            ]
            return [u[0], u[1], cap]

        u = hold(u)
        for k in range(3):
            u = strip.step(u, co, west, east)
            if k < 2:
                u = hold(u)
        for l in range(2):
            for y in range(3):
                for x in range(3):
                    v = u[l][y][x]
                    v = v if l == 0 else pltpu.roll(v, 4, 0)
                    back[x, pl.ds((l * C + c) * z.H + y, M, 3), :] = v
        return 0

    lax.fori_loop(0, C, channel, 0, unroll=2)
    fine = iota((2 * z.W, z.W), 1)
    place = lax.rem(iota((2 * z.W, z.W), 0), z.W)
    at = lax.rem(place, LANES) * 3 + place // LANES
    undeal = jnp.where(fine == at, 1.0, 0.0).astype(BF16)
    done = split_dot(jnp.concatenate([back[0], back[1], back[2]], axis=1), undeal)
    out[...] = done.reshape(z.L, C, z.H, z.W)


def parent_step(z, anc, diff, cour, parent, edges, up_in, dn_in, got, out):
    g, d = lax.axis_index("grp"), lax.axis_index("dev")
    C = z.C
    rows = z.TR + 8
    n = nest_at(z, anc, g // z.S * z.NB + d // z.Y)
    i = iota((z.TR, LANES), 0) + (g * z.TR - anc[0, n])
    j = iota((z.TR, LANES), 1) + (d * z.TC - anc[1, n])
    inside = (i >= 0) & (i < z.FR) & (j >= 0) & (j < z.FC)
    one = lambda cond: jnp.where(cond, 1.0, 0.0).astype(F32)
    on_w, on_e = one(inside & (j == 0)), one(inside & (j == z.FC - 1))
    on_s, on_n = one(inside & (i == 0)), one(inside & (i == z.FR - 1))
    i_end, j_end = one((i == 0) | (i == z.FR - 1)), one((j == 0) | (j == z.FC - 1))
    i_lo, i_hi = one(i > 0), one(i < z.FR - 1)
    j_lo, j_hi = one(j > 0), one(j < z.FC - 1)
    lane = iota((rows, LANES), 1)
    sub = iota((8, LANES), 0)

    cap_w = jnp.where(d > 0, got[jnp.maximum(d - 1, 0), z.RG2 - 8 :, :], 0.0)
    cap_e = jnp.where(d < z.D - 1, got[jnp.minimum(d + 1, z.D - 1), z.RG2 - 8 :, :], 0.0)
    col_w = jnp.concatenate([up_in[z.EDGE :, :], cap_w], axis=0)
    col_e = jnp.concatenate([dn_in[z.EDGE :, :], cap_e], axis=0)

    def channel(c, _):
        co = [v[:1] for v in weights(diff, cour, c, 1.0)]
        fm, fe, fw, fn, fs = [v[:1] for v in weights(diff, cour, c, 3.0)]
        lo = edges[pl.ds(c, 1), :]
        hi = edges[pl.ds(C + c, 1), :]
        cap = jnp.where(sub == 0, hi, jnp.where(sub == 7, lo, 0.0))
        full = jnp.concatenate([parent[c], cap], axis=0)
        w_in = pltpu.roll(col_w, lax.rem(LANES - c, LANES), 1)
        e_in = pltpu.roll(col_e, LANES - 1 - c, 1)
        w_all = jnp.where(lane == 0, w_in, pltpu.roll(full, 1, 1))
        e_all = jnp.where(lane == LANES - 1, e_in, pltpu.roll(full, LANES - 1, 1))
        up = lambda x: pltpu.roll(x, rows - 1, 0)[: z.TR]
        down = lambda x: pltpu.roll(x, 1, 0)[: z.TR]
        mid = full[: z.TR]
        w, e, n, s = w_all[: z.TR], e_all[: z.TR], up(full), down(full)
        w_up, w_down, e_up, e_down = up(w_all), down(w_all), up(e_all), down(e_all)
        step = (
            co[MID] * mid
            + (co[EAST] * e + co[WEST] * w)
            + (co[NORTH] * n + co[SOUTH] * s)
        )
        a, b, k, x = ghost_share(fw, fe, fm, fs, fn)
        share = on_w * ((a - x * i_end) * w + (b * i_lo) * w_down + (k * i_hi) * w_up)
        a, b, k, x = ghost_share(fe, fw, fm, fs, fn)
        share += on_e * ((a - x * i_end) * e + (b * i_lo) * e_down + (k * i_hi) * e_up)
        a, b, k, x = ghost_share(fs, fn, fm, fw, fe)
        share += on_s * ((a - x * j_end) * s + (b * j_lo) * w_down + (k * j_hi) * e_down)
        a, b, k, x = ghost_share(fn, fs, fm, fw, fe)
        share += on_n * ((a - x * j_end) * n + (b * j_lo) * w_up + (k * j_hi) * e_up)
        out[c] = jnp.where(inside, share, step)
        return 0

    lax.fori_loop(0, C, channel, 0, unroll=2)


def both_steps(
    z, anc, diff, cour, parent, edges, up, dn, ring, phases, out, nest_out, *scratch_and_store
):
    *scratch, store_parent = scratch_and_store
    parent_step(z, anc, diff, cour, parent, edges, up, dn, ring, out)
    store_parent()
    nest_steps(z, diff, cour, phases, ring, up, dn, nest_out, *scratch)


def merge(z, which, anchor, base, pieces):
    count, size = len(which), z.CS * z.M

    def kernel(*refs):
        anc_in, base_in, refs = refs[0], refs[1], refs[2:]
        source, base_out, refs = refs[:count], refs[count], refs[count + 1 :]
        anc, refs = refs[0], refs[1:]
        inner, (old, new, twice, sem) = refs[:count], refs[count:]
        g, d = lax.axis_index("grp"), lax.axis_index("dev")
        part = lax.rem(g, z.S)
        firsts = [lax.rem(part - k + z.S, z.S) * z.CS for k in which]
        fetch = [pltpu.make_async_copy(anc_in, anc, sem.at[0])]
        for k in range(count):
            rows = base_in.at[pl.ds(firsts[k], z.CS)]
            fetch.append(pltpu.make_async_copy(source[k], inner[k], sem.at[1 + 2 * k]))
            fetch.append(pltpu.make_async_copy(rows, old.at[k], sem.at[2 + 2 * k]))
        for copy in fetch:
            copy.start()
        for copy in fetch:
            copy.wait()
        n = nest_at(z, anc, g // z.S * z.NB + d // z.Y)
        r, q = anc[0, n], anc[1, n]
        start = lax.rem(g * z.TR - r + 2 * z.G * z.TR, z.FR)
        shift_q = lax.rem(q - d * z.TC + 2 * z.D * z.TC, z.FC)
        i = iota((z.TR, LANES), 0) + (g * z.TR - r)
        j = iota((z.TR, LANES), 1) + (d * z.TC - q)
        inside = (i >= 0) & (i < z.FR) & (j >= 0) & (j < z.FC)
        sub = iota((z.M, LANES), 0)
        store = []
        for k in range(count):
            piece = inner[k]
            for c in range(z.CS):
                for m in range(z.D):
                    x = piece[m, c * z.M : (c + 1) * z.M, :]
                    if m + 1 < z.D:
                        row = piece[m + 1, size + c : size + c + 1, :]
                        x += jnp.where(sub == z.M - 1, row, 0.0)
                    if m > 0:
                        row = piece[m - 1, size + z.CS + c : size + z.CS + c + 1, :]
                        x += jnp.where(sub == 0, row, 0.0)
                    twice[c % 4, m * z.M : (m + 1) * z.M, :] = x
                    if m * z.M < z.TR:
                        twice[c % 4, z.FR + m * z.M : z.FR + (m + 1) * z.M, :] = x
                x = pltpu.roll(twice[c % 4, pl.ds(start, z.TR), :], shift_q, 1)
                new[k, c] = old[k, c] + jnp.where(inside, x, 0.0)
            rows = base_out.at[pl.ds(firsts[k], z.CS)]
            store.append(pltpu.make_async_copy(new.at[k], rows, sem.at[1 + 2 * k]))
            store[-1].start()
        for copy in store:
            copy.wait()

    place = pl.BlockSpec(memory_space=pltpu.HBM)
    half = pltpu.VMEM((count, z.CS, z.TR, LANES), F32)
    return pl.pallas_call(
        kernel,
        out_shape=jax.ShapeDtypeStruct(base.shape, F32),
        in_specs=[place] * (2 + count),
        out_specs=place,
        input_output_aliases={1: 0},
        scratch_shapes=[
            pltpu.SMEM(anchor.shape, anchor.dtype),
            *[pltpu.VMEM(x.shape, F32) for x in pieces],
            half,
            half,
            pltpu.VMEM((4, z.FR + z.TR, LANES), F32),
            pltpu.SemaphoreType.DMA((1 + 2 * count,)),
        ],
        compiler_params=pltpu.CompilerParams(vmem_limit_bytes=VMEM_LIMIT),
    )(anchor, base, *pieces)


def shards(parent, nest, anchor, diff, cour):
    z = Sizes(parent, nest, anchor, lax.axis_size("grp"), lax.axis_size("dev"))
    sds = lambda *shape: jax.ShapeDtypeStruct(shape, F32)
    vmem = lambda *shape: pltpu.VMEM(shape, F32)
    to_grp = lambda x, k: lax.ppermute(x, "grp", [(a, a ^ k) for a in range(z.G)])

    anchor = anchor.T
    message = sds(z.EDGE + z.TR, LANES)
    edge_tile = vmem(z.L, z.C, 8, z.W)
    ring, up, dn = call(
        functools.partial(ring_parts, z),
        [sds(z.G, z.RG, LANES), message, message],
        (anchor,),
        (parent,),
        [edge_tile, edge_tile, pltpu.SemaphoreType.DMA((2,))],
        (nest,),
    )
    nest, ring = lax.optimization_barrier((nest, ring))
    ring = lax.all_to_all(ring, "grp", 0, 0, tiled=True)
    *chunks, phases = call(
        functools.partial(partial_averages, z),
        [sds(z.R1, LANES)] * z.S + [sds(3, z.L * z.C * z.H, LANES)],
        (diff, cour),
        (),
        [pltpu.VMEM(nest.shape, F32), pltpu.SemaphoreType.DMA((z.L,))],
        (nest,),
        z.S,
    )
    chunks, ring, up, dn = lax.optimization_barrier((chunks, ring, up, dn))
    forward = [(k, k + 1) for k in range(z.D - 1)]
    up = lax.ppermute(up, "dev", forward)
    dn = lax.ppermute(dn, "dev", [(b, a) for a, b in forward])
    got = [chunks[0]] + [to_grp(chunks[k % z.S], k) for k in range(1, z.G)]
    ring, edges = call(
        functools.partial(ring_next, z),
        [sds(z.D, z.RG2, LANES), sds(2 * z.C, LANES)],
        (),
        (ring,),
        [vmem(z.RING, LANES)],
    )
    ring = lax.all_to_all(ring, "dev", 0, 0, tiled=True)
    (avg,) = call(functools.partial(pick_band, z), [sds(z.D, z.R2, LANES)], (anchor,), got)
    avg, phases, edges, ring, up, dn = lax.optimization_barrier(
        (avg, phases, edges, ring, up, dn)
    )
    avg = lax.all_to_all(avg, "dev", 0, 0, tiled=True)
    out, nest_out = call(
        functools.partial(both_steps, z),
        [jax.ShapeDtypeStruct(parent.shape, F32), jax.ShapeDtypeStruct(nest.shape, F32)],
        (anchor, diff, cour),
        (parent, edges, up, dn, ring, phases),
        [
            vmem(3, z.L * z.C * z.H, LANES),
            vmem(z.RG2, LANES),
            vmem(z.EDGE, LANES),
            vmem(z.EDGE, LANES),
        ],
        (),
        0,
    )
    avg, nest_out, out = lax.optimization_barrier((avg, nest_out, out))
    pieces = [avg]
    for k in range(1, z.S):
        pairs = [(a, a // z.S * z.S + (a + k) % z.S) for a in range(z.G)]
        pieces.append(lax.ppermute(avg, "grp", pairs))
    for which in ([0], list(range(1, z.S))):
        out = merge(z, which, anchor, out, [pieces[k] for k in which])
    return out, nest_out


def solution(mesh):
    placed = (P(None, "grp", "dev"), P("grp", None, "dev", None), P(), P(), P())
    return jax.shard_map(
        shards,
        mesh=mesh,
        in_specs=placed,
        out_specs=(P(None, "grp", "dev"), P("grp", None, "dev", None)),
        check_vma=False,
    )
```

```python
import functools

import jax
import jax.numpy as jnp
from jax import lax
from jax.experimental import pallas as pl
from jax.experimental.pallas import tpu as pltpu
from jax.sharding import PartitionSpec as P

F32 = jnp.float32
BF16 = jnp.bfloat16
LANES = 128
VMEM_LIMIT = 65408 * 1024
MID, EAST, WEST, NORTH, SOUTH = range(5)


class Sizes:
    def __init__(self, parent, nest, anchor, grp_count, dev_count):
        self.C, self.TR, self.TC = parent.shape
        self.L, _, self.H, self.W = nest.shape
        self.N = anchor.shape[0]
        self.G, self.D = grp_count, dev_count
        self.M = self.H // 3
        self.FR, self.FC = self.M * self.D, self.W // 3
        self.S = self.G // 2
        self.NB = self.N // 2
        self.Y = self.D // self.NB
        self.CS = self.C // self.S
        self.BR, self.BC = self.S * self.TR, self.Y * self.TC
        self.R1 = self.L * self.CS * (self.M + 2)
        self.R2 = self.CS * (self.M + 2)
        self.RING = self.FR + self.L * 2 * self.C
        self.RG = self.RING + self.C
        self.RG2 = 16 + self.L * self.C + 8
        self.HALO = self.L * self.C * 3
        self.EDGE = 3 * self.HALO
        assert self.H == 24 and self.FC == LANES and self.TC == LANES
        assert self.FR >= self.TR and self.L == 2


def call(body, out_shape, smem, args, scratch=(), raw=(), early=None):
    moved = [*smem, *args]
    n_in, n_raw, n_out = len(moved), len(raw), len(out_shape)
    place = pl.BlockSpec(memory_space=pltpu.HBM)

    def kernel(*refs):
        source, refs = refs[:n_in], refs[n_in:]
        stay, refs = refs[:n_raw], refs[n_raw:]
        target, refs = refs[:n_out], refs[n_out:]
        inner, refs = refs[:n_in], refs[n_in:]
        result, refs = refs[:n_out], refs[n_out:]
        extra, sem = refs[:-1], refs[-1]
        fetch = [pltpu.make_async_copy(a, b, sem.at[k]) for k, (a, b) in enumerate(zip(source, inner))]
        for copy in fetch:
            copy.start()
        for copy in fetch:
            copy.wait()
        store = [
            pltpu.make_async_copy(a, b, sem.at[n_in + k]) for k, (a, b) in enumerate(zip(result, target))
        ]
        if early is None:
            body(*inner, *stay, *result, *extra)
        else:
            body(*inner, *stay, *result, *extra, store[early].start)
        for k, copy in enumerate(store):
            if k != early:
                copy.start()
        for copy in store:
            copy.wait()

    return pl.pallas_call(
        kernel,
        out_shape=list(out_shape),
        in_specs=[place] * (n_in + n_raw),
        out_specs=[place] * n_out,
        scratch_shapes=[
            *[pltpu.SMEM(x.shape, x.dtype) for x in smem],
            *[pltpu.VMEM(x.shape, x.dtype) for x in args],
            *[pltpu.VMEM(x.shape, x.dtype) for x in out_shape],
            *scratch,
            pltpu.SemaphoreType.DMA((n_in + n_out,)),
        ],
        compiler_params=pltpu.CompilerParams(vmem_limit_bytes=VMEM_LIMIT),
    )(*moved, *raw)


def iota(shape, dim):
    return lax.broadcasted_iota(jnp.int32, shape, dim)


def split_dot(x, table):
    high = x.astype(BF16)
    low = (x - high.astype(F32)).astype(BF16)
    return jnp.dot(jnp.concatenate([high, low], axis=1), table, preferred_element_type=F32)


def nest_at(z, anc, band):
    found = 0
    for n in range(z.N):
        found += jnp.where(anc[0, n] // z.BR * z.NB + anc[1, n] // z.BC == band, n, 0)
    return found


def weights(diff, cour, c, times):
    splat = lambda ref, k: jnp.full((8, LANES), ref[k, c], F32)
    east = times * splat(diff, 0)
    north = times * splat(diff, 1)
    west = east + splat(cour, 0)
    south = north + splat(cour, 1)
    return 1.0 - (east + west) - (north + south), east, west, north, south


def ghost_share(inject, back, mid, plus, minus):
    stay = mid + inject
    m0 = inject * (1.0 + stay + mid * stay + inject * (stay + back) + 2.0 * plus * minus)
    p1 = inject * plus * (1.0 + 2.0 * stay)
    p2 = inject * plus * plus
    n1 = inject * minus * (1.0 + 2.0 * stay)
    n2 = inject * minus * minus
    ninth = 1.0 / 9.0
    same = (3.0 * m0 + 2.0 * p1 + p2 + 2.0 * n1 + n2) * ninth
    return same, (p1 + 2.0 * p2) * ninth, (n1 + 2.0 * n2) * ninth, inject * plus * minus * ninth


class Strip:
    def __init__(self):
        sub = iota((8, LANES), 0)
        lane = iota((8, LANES), 1)
        self.high = [sub == 0, sub == 4]
        self.low = [sub == 7, sub == 3]
        self.any_high = (sub == 0) | (sub == 4)
        self.any_low = (sub == 7) | (sub == 3)
        self.first, self.last = lane == 0, lane == LANES - 1

    def east(self, x, ghost):
        return jnp.where(self.last, ghost, pltpu.roll(x, LANES - 1, 1))

    def west(self, x, ghost):
        return jnp.where(self.first, ghost, pltpu.roll(x, 1, 1))

    def north(self, mains, cap):
        up = [pltpu.roll(m, 7, 0) for m in mains]
        cap_up = pltpu.roll(cap, 7, 0)
        new = [jnp.where(self.low[l], cap_up, up[l]) for l in range(2)]
        return new, jnp.where(self.low[0], up[0], jnp.where(self.low[1], up[1], 0.0))

    def south(self, mains, cap):
        down = [pltpu.roll(m, 1, 0) for m in mains]
        cap_down = pltpu.roll(cap, 1, 0)
        new = [jnp.where(self.high[l], cap_down, down[l]) for l in range(2)]
        return new, jnp.where(self.high[0], down[0], jnp.where(self.high[1], down[1], 0.0))

    def step(self, u, co, west_ghost, east_ghost):
        n_in = [self.north([u[0][0][x], u[1][0][x]], u[2][0][x]) for x in range(3)]
        s_in = [self.south([u[0][2][x], u[1][2][x]], u[2][2][x]) for x in range(3)]
        pick = lambda pair, k: pair[1] if k == 2 else pair[0][k]
        new = []
        for k in range(3):
            rows = []
            for y in range(3):
                row = u[k][y]
                e = [row[1], row[2], self.east(row[0], east_ghost[k])]
                w = [self.west(row[2], west_ghost[k]), row[0], row[1]]
                cells = []
                for x in range(3):
                    n = u[k][y + 1][x] if y < 2 else pick(n_in[x], k)
                    s = u[k][y - 1][x] if y > 0 else pick(s_in[x], k)
                    cells.append(
                        co[MID] * row[x]
                        + (co[EAST] * e[x] + co[WEST] * w[x])
                        + (co[NORTH] * n + co[SOUTH] * s)
                    )
                rows.append(cells)
            new.append(rows)
        return new

    def pooled_step(self, u, co):
        ends = []
        for k in range(3):
            row = [u[k][y][0] + u[k][y][1] + u[k][y][2] for y in range(3)]
            col = [u[k][0][x] + u[k][1][x] + u[k][2][x] for x in (0, 2)]
            ends.append((row[0], row[2], col[0], col[1], row[0] + row[1] + row[2]))
        n_in = self.north([ends[0][0], ends[1][0]], ends[2][0])
        s_in = self.south([ends[0][1], ends[1][1]], ends[2][1])
        pick = lambda pair, k: pair[1] if k == 2 else pair[0][k]
        out = []
        for k in range(3):
            row0, row2, col0, col2, total = ends[k]
            flux_x = co[EAST] * (self.east(col0, 0.0) - col0)
            flux_x += co[WEST] * (self.west(col2, 0.0) - col2)
            flux_y = co[NORTH] * (pick(n_in, k) - row0) + co[SOUTH] * (pick(s_in, k) - row2)
            out.append(total + (flux_x + flux_y))
        return out


def phase_rows(z, ref, l, c, y, x):
    got = ref[x, pl.ds((l * z.C + c) * z.H + y, z.M, 3), :]
    return got if l == 0 else pltpu.roll(got, 4, 0)


def partial_averages(z, diff, cour, nest, *refs):
    out, (phases, strips, sem, store_phases) = refs[: z.S], refs[z.S :]
    fetch = [pltpu.make_async_copy(nest.at[l], strips.at[l], sem.at[l]) for l in range(z.L)]
    for copy in fetch:
        copy.start()
    d = lax.axis_index("dev")
    own = lax.rem(lax.axis_index("grp"), z.S)
    C, M, CS = z.C, z.M, z.CS
    fine = lax.rem(iota((2 * z.W, z.W), 0), z.W)
    place = iota((2 * z.W, z.W), 1)
    at = lax.rem(place, LANES) * 3 + place // LANES
    deal = jnp.where(fine == at, 1.0, 0.0).astype(BF16)
    rows = C * z.H
    for l in range(z.L):
        fetch[l].wait()
        dealt = split_dot(strips[l].reshape(rows, z.W), deal)
        for x in range(3):
            phases[x, l * rows : (l + 1) * rows, :] = dealt[:, x * LANES : (x + 1) * LANES]
    store_phases()
    strip = Strip()
    keep_high = strip.any_low | (strip.any_high & (d < z.D - 1))
    keep_low = strip.any_high | (strip.any_low & (d > 0))
    zero = jnp.zeros((8, LANES), F32)
    ghosts = [0.0] * 3
    base = z.L * CS * M

    def hold(u):
        cap = [
            [jnp.where(keep_high, v, 0.0) for v in u[2][0]],
            u[2][1],
            [jnp.where(keep_low, v, 0.0) for v in u[2][2]],
        ]
        return [u[0], u[1], cap]

    for part in range(z.S):

        def channel(i, _, to=out[part], first=jnp.bitwise_xor(own, part) * CS):
            c = first + i
            co = weights(diff, cour, c, 3.0)
            u = [
                [[phase_rows(z, phases, l, c, y, x) for x in range(3)] for y in range(3)]
                for l in range(2)
            ]
            u.append([[zero] * 3] * 3)
            for _step in range(2):
                u = hold(strip.step(u, co, ghosts, ghosts))
            got = [v * (1.0 / 9.0) for v in strip.pooled_step(u, co)]
            got[1] = pltpu.roll(got[1], 4, 0)
            for l in range(2):
                row = pl.multiple_of((l * CS + i) * M, M)
                to[pl.ds(row, M), :] = got[l]
                for side, sub in enumerate(((7, 3), (0, 4))):
                    row = base + (l * 2 + side) * CS + i
                    to[pl.ds(row, 1), :] = got[2][sub[l] : sub[l] + 1]
            return 0

        lax.fori_loop(0, CS, channel, 0, unroll=3)


def pick_band(z, anc, *refs):
    got, out = refs[: z.G], refs[z.G]
    g = lax.axis_index("grp")
    top = g // z.S * z.NB
    base, size = z.L * z.CS * z.M, z.CS * z.M
    for band in range(z.NB):
        n = nest_at(z, anc, top + band)
        of = n // z.L
        slot = jnp.bitwise_xor(of, g)
        first = n - of * z.L == 0
        for k in range(z.G):

            @pl.when(slot == k)
            def _(k=k, first=first, band=band):
                main = jnp.where(first, got[k][:size, :], got[k][size : 2 * size, :])
                edge = jnp.where(
                    first,
                    got[k][base : base + 2 * z.CS, :],
                    got[k][base + 2 * z.CS : base + 4 * z.CS, :],
                )
                for y in range(z.Y):
                    out[band * z.Y + y, :size, :] = main
                    out[band * z.Y + y, size:, :] = edge


def ring_parts(z, anc, parent, nest, buf, up, dn, tail, head, sem):
    fetch = [
        pltpu.make_async_copy(nest.at[:, :, z.H - 8 :, :], tail, sem.at[0]),
        pltpu.make_async_copy(nest.at[:, :, :8, :], head, sem.at[1]),
    ]
    for copy in fetch:
        copy.start()
    g, d = lax.axis_index("grp"), lax.axis_index("dev")
    row_base, col_base = g * z.TR, d * z.TC
    lane_t = iota((z.TR, LANES), 1)
    lane_f = iota((z.FR, LANES), 1)
    row_f = iota((z.FR, LANES), 0)
    lane_c = iota((z.C, LANES), 1)
    buf[...] = jnp.zeros_like(buf)

    def nest_ring(n, _):
        to = n // z.L
        l = n - to * z.L
        slot = to
        r, q = anc[0, n], anc[1, n]
        rows_meet = (r < row_base + z.TR) & (r + z.FR > row_base)
        cols_meet = (q < col_base + z.TC) & (q + z.FC > col_base)
        shift_r = lax.rem(row_base - r + 2 * z.G * z.TR, z.FR)
        shift_q = lax.rem(col_base - q + 2 * z.D * z.TC, z.FC)
        for side in range(2):
            col = (q - 1 if side == 0 else q + z.FC) - col_base
            first = (l * 2 + side) * z.C

            @pl.when(rows_meet & (col >= 0) & (col < z.TC))
            def _(col=col, first=first):
                acc = jnp.zeros((z.TR, LANES), F32)
                for c in range(z.C):
                    at = first + c
                    moved = pltpu.roll(parent[c], lax.rem(at - col + LANES, LANES), 1)
                    acc = jnp.where(lane_t == at, moved, acc)
                if z.FR > z.TR:
                    acc = jnp.concatenate([acc, jnp.zeros((z.FR - z.TR, LANES), F32)], axis=0)
                acc = pltpu.roll(acc, shift_r, 0)
                y = row_f + (r - row_base)
                good = (y >= 0) & (y < z.TR) & (lane_f >= first) & (lane_f < first + z.C)
                buf[slot, : z.FR, :] = jnp.where(good, acc, buf[slot, : z.FR, :])

            row = (r - 1 if side == 0 else r + z.FR) - row_base

            @pl.when(cols_meet & (row >= 0) & (row < z.TR))
            def _(row=row, first=first):
                rows = jnp.concatenate(
                    [parent[c, pl.ds(row, 1), :] for c in range(z.C)], axis=0
                )
                x = lane_c + (q - col_base)
                moved = jnp.where((x >= 0) & (x < z.TC), pltpu.roll(rows, shift_q, 1), 0.0)
                buf[slot, pl.ds(pl.multiple_of(z.FR + first, 8), z.C), :] = moved

        return 0

    lax.fori_loop(0, z.N, nest_ring, 0)
    for to in range(z.G):
        edge = jnp.where(to > g, z.TR - 1, 0)
        for c in range(z.C):
            buf[to, z.RING + c : z.RING + c + 1, :] = parent[c, pl.ds(edge, 1), :]
    first = jnp.zeros((z.TR, LANES), F32)
    last = first
    for c in range(z.C):
        first = jnp.where(lane_t == c, pltpu.roll(parent[c], c, 1) if c else parent[c], first)
        last = jnp.where(lane_t == c, pltpu.roll(parent[c], c + 1, 1), last)
    up[z.EDGE :, :] = last
    dn[z.EDGE :, :] = first
    for copy in fetch:
        copy.wait()
    for l in range(z.L):
        for c in range(z.C):
            for x in range(3):
                at = x * z.HALO + 3 * (l * z.C + c)
                lanes = slice(x * LANES, (x + 1) * LANES)
                up[at : at + 3, :] = tail[l, c, 5:8, lanes]
                dn[at : at + 3, :] = head[l, c, 0:3, lanes]


def ring_next(z, got, out, edges, slab):
    g, d = lax.axis_index("grp"), lax.axis_index("dev")
    C, L, FR, M = z.C, z.L, z.FR, z.M
    total = got[0, : z.RING, :]
    for k in range(1, z.G):
        total = total + got[k, : z.RING, :]
    slab[...] = total
    sub = iota((8, LANES), 0)
    for to in range(z.D):
        out[to, :M, :] = slab[to * M : (to + 1) * M, :]
        hi = min(to * M + M, FR - 1)
        lo = max(to * M - 1, 0)
        hi, lo = slab[hi : hi + 1, :], slab[lo : lo + 1, :]
        out[to, M:16, :] = jnp.where(sub == 0, hi, jnp.where(sub == 7, lo, 0.0))
        for l in range(L):
            at = 16 + l * C
            if to == 0 or to == z.D - 1:
                k = FR + (l * 2 + (0 if to == 0 else 1)) * C
                out[to, at : at + C, :] = slab[k : k + C, :]
            else:
                out[to, at : at + C, :] = jnp.zeros((C, LANES), F32)
    before, after = jnp.maximum(g - 1, 0), jnp.minimum(g + 1, z.G - 1)
    edges[:C, :] = jnp.where(g > 0, got[before, z.RING :, :], 0.0)
    edges[C:, :] = jnp.where(g < z.G - 1, got[after, z.RING :, :], 0.0)
    lane = iota((8, LANES), 1)
    first = jnp.zeros((8, LANES), F32)
    last = first
    for c in range(C):
        lo = edges[c : c + 1, :]
        hi = edges[C + c : C + c + 1, :]
        cap = jnp.where(sub == 0, hi, jnp.where(sub == 7, lo, 0.0))
        first = jnp.where(lane == c, pltpu.roll(cap, c, 1) if c else cap, first)
        last = jnp.where(lane == c, pltpu.roll(cap, c + 1, 1), last)
    for to in range(z.D):
        out[to, z.RG2 - 8 :, :] = jnp.where(to > d, last, first)


def nest_steps(z, diff, cour, phases, got, up_in, dn_in, out, back, ring, up, dn):
    d = lax.axis_index("dev")
    C, M = z.C, z.M
    strip = Strip()
    fine = lax.rem(iota((2 * z.W, z.W), 0), z.W)
    place = iota((2 * z.W, z.W), 1)
    deal = jnp.where(fine == lax.rem(place, LANES) * 3 + place // LANES, 1.0, 0.0).astype(BF16)
    for source, target in ((up_in, up), (dn_in, dn)):
        halo = [source[x * z.HALO : (x + 1) * z.HALO, :] for x in range(3)]
        dealt = split_dot(jnp.concatenate(halo, axis=1), deal)
        for x in range(3):
            target[x * z.HALO : (x + 1) * z.HALO, :] = dealt[:, x * LANES : (x + 1) * LANES]
    total = got[0]
    for k in range(1, z.D):
        total = total + got[k]
    ring[...] = total
    side_main = [ring[:M, :], pltpu.roll(ring[:M, :], 4, 0)]
    side_cap = jnp.where(
        strip.any_high, ring[M : M + 1, :], jnp.where(strip.any_low, ring[15:16, :], 0.0)
    )
    hold_low, hold_high = strip.any_low & (d == 0), strip.any_high & (d == z.D - 1)
    nest_1 = strip.high[1] | strip.low[1]

    def channel(c, _):
        co = weights(diff, cour, c, 3.0)
        u = [
            [[phase_rows(z, phases, l, c, y, x) for x in range(3)] for y in range(3)]
            for l in range(2)
        ]
        cap = []
        for y in range(3):
            row = []
            for x in range(3):
                v = jnp.zeros((8, LANES), F32)
                for l in range(2):
                    at = x * z.HALO + (l * C + c) * 3 + y
                    v = jnp.where(strip.high[l], dn[pl.ds(at, 1), :], v)
                    v = jnp.where(strip.low[l], up[pl.ds(at, 1), :], v)
                row.append(v)
            cap.append(row)
        u.append(cap)
        end = jnp.where(nest_1, ring[pl.ds(16 + C + c, 1), :], ring[pl.ds(16 + c, 1), :])
        west, east = [], []
        for side, lane, ghosts in ((0, 0, west), (1, LANES - 1, east)):
            turn = [lax.rem(lane - ((l * 2 + side) * C + c) + LANES, LANES) for l in range(2)]
            for l in range(2):
                ghosts.append(pltpu.roll(side_main[l], turn[l], 1))
            caps = [pltpu.roll(side_cap, turn[l], 1) for l in range(2)]
            ghosts.append(jnp.where(nest_1, caps[1], caps[0]))

        def hold(u):
            cap = [
                [jnp.where(hold_high, end, v) for v in u[2][0]],
                u[2][1],
                [jnp.where(hold_low, end, v) for v in u[2][2]],
            ]
            return [u[0], u[1], cap]

        u = hold(u)
        for k in range(3):
            u = strip.step(u, co, west, east)
            if k < 2:
                u = hold(u)
        for l in range(2):
            for y in range(3):
                for x in range(3):
                    v = u[l][y][x]
                    v = v if l == 0 else pltpu.roll(v, 4, 0)
                    back[x, pl.ds((l * C + c) * z.H + y, M, 3), :] = v
        return 0

    lax.fori_loop(0, C, channel, 0, unroll=3)
    fine = iota((2 * z.W, z.W), 1)
    place = lax.rem(iota((2 * z.W, z.W), 0), z.W)
    at = lax.rem(place, LANES) * 3 + place // LANES
    undeal = jnp.where(fine == at, 1.0, 0.0).astype(BF16)
    done = split_dot(jnp.concatenate([back[0], back[1], back[2]], axis=1), undeal)
    out[...] = done.reshape(z.L, C, z.H, z.W)


def parent_step(z, anc, diff, cour, parent, edges, up_in, dn_in, got, out):
    g, d = lax.axis_index("grp"), lax.axis_index("dev")
    C = z.C
    rows = z.TR + 8
    n = nest_at(z, anc, g // z.S * z.NB + d // z.Y)
    i = iota((z.TR, LANES), 0) + (g * z.TR - anc[0, n])
    j = iota((z.TR, LANES), 1) + (d * z.TC - anc[1, n])
    inside = (i >= 0) & (i < z.FR) & (j >= 0) & (j < z.FC)
    one = lambda cond: jnp.where(cond, 1.0, 0.0).astype(F32)
    on_w, on_e = one(inside & (j == 0)), one(inside & (j == z.FC - 1))
    on_s, on_n = one(inside & (i == 0)), one(inside & (i == z.FR - 1))
    i_end, j_end = one((i == 0) | (i == z.FR - 1)), one((j == 0) | (j == z.FC - 1))
    i_lo, i_hi = one(i > 0), one(i < z.FR - 1)
    j_lo, j_hi = one(j > 0), one(j < z.FC - 1)
    lane = iota((rows, LANES), 1)
    sub = iota((8, LANES), 0)

    cap_w = jnp.where(d > 0, got[jnp.maximum(d - 1, 0), z.RG2 - 8 :, :], 0.0)
    cap_e = jnp.where(d < z.D - 1, got[jnp.minimum(d + 1, z.D - 1), z.RG2 - 8 :, :], 0.0)
    col_w = jnp.concatenate([up_in[z.EDGE :, :], cap_w], axis=0)
    col_e = jnp.concatenate([dn_in[z.EDGE :, :], cap_e], axis=0)

    def channel(c, _):
        co = [v[:1] for v in weights(diff, cour, c, 1.0)]
        fm, fe, fw, fn, fs = [v[:1] for v in weights(diff, cour, c, 3.0)]
        lo = edges[pl.ds(c, 1), :]
        hi = edges[pl.ds(C + c, 1), :]
        cap = jnp.where(sub == 0, hi, jnp.where(sub == 7, lo, 0.0))
        full = jnp.concatenate([parent[c], cap], axis=0)
        w_in = pltpu.roll(col_w, lax.rem(LANES - c, LANES), 1)
        e_in = pltpu.roll(col_e, LANES - 1 - c, 1)
        w_all = jnp.where(lane == 0, w_in, pltpu.roll(full, 1, 1))
        e_all = jnp.where(lane == LANES - 1, e_in, pltpu.roll(full, LANES - 1, 1))
        up = lambda x: pltpu.roll(x, rows - 1, 0)[: z.TR]
        down = lambda x: pltpu.roll(x, 1, 0)[: z.TR]
        mid = full[: z.TR]
        w, e, n, s = w_all[: z.TR], e_all[: z.TR], up(full), down(full)
        w_up, w_down, e_up, e_down = up(w_all), down(w_all), up(e_all), down(e_all)
        step = (
            co[MID] * mid
            + (co[EAST] * e + co[WEST] * w)
            + (co[NORTH] * n + co[SOUTH] * s)
        )
        a, b, k, x = ghost_share(fw, fe, fm, fs, fn)
        share = on_w * ((a - x * i_end) * w + (b * i_lo) * w_down + (k * i_hi) * w_up)
        a, b, k, x = ghost_share(fe, fw, fm, fs, fn)
        share += on_e * ((a - x * i_end) * e + (b * i_lo) * e_down + (k * i_hi) * e_up)
        a, b, k, x = ghost_share(fs, fn, fm, fw, fe)
        share += on_s * ((a - x * j_end) * s + (b * j_lo) * w_down + (k * j_hi) * e_down)
        a, b, k, x = ghost_share(fn, fs, fm, fw, fe)
        share += on_n * ((a - x * j_end) * n + (b * j_lo) * w_up + (k * j_hi) * e_up)
        out[c] = jnp.where(inside, share, step)
        return 0

    lax.fori_loop(0, C, channel, 0, unroll=3)


def both_steps(
    z, anc, diff, cour, parent, edges, up, dn, ring, phases, out, nest_out, *scratch_and_store
):
    *scratch, store_parent = scratch_and_store
    parent_step(z, anc, diff, cour, parent, edges, up, dn, ring, out)
    store_parent()
    nest_steps(z, diff, cour, phases, ring, up, dn, nest_out, *scratch)


def merge(z, which, anchor, base, pieces):
    count, size = len(which), z.CS * z.M

    def kernel(*refs):
        anc_in, base_in, refs = refs[0], refs[1], refs[2:]
        source, base_out, refs = refs[:count], refs[count], refs[count + 1 :]
        anc, refs = refs[0], refs[1:]
        inner, (old, new, twice, sem) = refs[:count], refs[count:]
        g, d = lax.axis_index("grp"), lax.axis_index("dev")
        part = lax.rem(g, z.S)
        firsts = [lax.rem(part - k + z.S, z.S) * z.CS for k in which]
        fetch = [pltpu.make_async_copy(anc_in, anc, sem.at[0])]
        for k in range(count):
            rows = base_in.at[pl.ds(firsts[k], z.CS)]
            fetch.append(pltpu.make_async_copy(source[k], inner[k], sem.at[1 + 2 * k]))
            fetch.append(pltpu.make_async_copy(rows, old.at[k], sem.at[2 + 2 * k]))
        for copy in fetch:
            copy.start()
        for copy in fetch:
            copy.wait()
        n = nest_at(z, anc, g // z.S * z.NB + d // z.Y)
        r, q = anc[0, n], anc[1, n]
        start = lax.rem(g * z.TR - r + 2 * z.G * z.TR, z.FR)
        shift_q = lax.rem(q - d * z.TC + 2 * z.D * z.TC, z.FC)
        i = iota((z.TR, LANES), 0) + (g * z.TR - r)
        j = iota((z.TR, LANES), 1) + (d * z.TC - q)
        inside = (i >= 0) & (i < z.FR) & (j >= 0) & (j < z.FC)
        sub = iota((z.M, LANES), 0)
        store = []
        for k in range(count):
            piece = inner[k]
            for c in range(z.CS):
                for m in range(z.D):
                    x = piece[m, c * z.M : (c + 1) * z.M, :]
                    if m + 1 < z.D:
                        row = piece[m + 1, size + c : size + c + 1, :]
                        x += jnp.where(sub == z.M - 1, row, 0.0)
                    if m > 0:
                        row = piece[m - 1, size + z.CS + c : size + z.CS + c + 1, :]
                        x += jnp.where(sub == 0, row, 0.0)
                    twice[c % 4, m * z.M : (m + 1) * z.M, :] = x
                    if m * z.M < z.TR:
                        twice[c % 4, z.FR + m * z.M : z.FR + (m + 1) * z.M, :] = x
                x = pltpu.roll(twice[c % 4, pl.ds(start, z.TR), :], shift_q, 1)
                new[k, c] = old[k, c] + jnp.where(inside, x, 0.0)
            rows = base_out.at[pl.ds(firsts[k], z.CS)]
            store.append(pltpu.make_async_copy(new.at[k], rows, sem.at[1 + 2 * k]))
            store[-1].start()
        for copy in store:
            copy.wait()

    place = pl.BlockSpec(memory_space=pltpu.HBM)
    half = pltpu.VMEM((count, z.CS, z.TR, LANES), F32)
    return pl.pallas_call(
        kernel,
        out_shape=jax.ShapeDtypeStruct(base.shape, F32),
        in_specs=[place] * (2 + count),
        out_specs=place,
        input_output_aliases={1: 0},
        scratch_shapes=[
            pltpu.SMEM(anchor.shape, anchor.dtype),
            *[pltpu.VMEM(x.shape, F32) for x in pieces],
            half,
            half,
            pltpu.VMEM((4, z.FR + z.TR, LANES), F32),
            pltpu.SemaphoreType.DMA((1 + 2 * count,)),
        ],
        compiler_params=pltpu.CompilerParams(vmem_limit_bytes=VMEM_LIMIT),
    )(anchor, base, *pieces)


def shards(parent, nest, anchor, diff, cour):
    z = Sizes(parent, nest, anchor, lax.axis_size("grp"), lax.axis_size("dev"))
    sds = lambda *shape: jax.ShapeDtypeStruct(shape, F32)
    vmem = lambda *shape: pltpu.VMEM(shape, F32)
    to_grp = lambda x, k: lax.ppermute(x, "grp", [(a, a ^ k) for a in range(z.G)])

    anchor = anchor.T
    message = sds(z.EDGE + z.TR, LANES)
    edge_tile = vmem(z.L, z.C, 8, z.W)
    ring, up, dn = call(
        functools.partial(ring_parts, z),
        [sds(z.G, z.RG, LANES), message, message],
        (anchor,),
        (parent,),
        [edge_tile, edge_tile, pltpu.SemaphoreType.DMA((2,))],
        (nest,),
    )
    nest, ring = lax.optimization_barrier((nest, ring))
    ring = lax.all_to_all(ring, "grp", 0, 0, tiled=True)
    *chunks, phases = call(
        functools.partial(partial_averages, z),
        [sds(z.R1, LANES)] * z.S + [sds(3, z.L * z.C * z.H, LANES)],
        (diff, cour),
        (),
        [pltpu.VMEM(nest.shape, F32), pltpu.SemaphoreType.DMA((z.L,))],
        (nest,),
        z.S,
    )
    chunks, ring, up, dn = lax.optimization_barrier((chunks, ring, up, dn))
    forward = [(k, k + 1) for k in range(z.D - 1)]
    up = lax.ppermute(up, "dev", forward)
    dn = lax.ppermute(dn, "dev", [(b, a) for a, b in forward])
    got = [chunks[0]] + [to_grp(chunks[k % z.S], k) for k in range(1, z.G)]
    ring, edges = call(
        functools.partial(ring_next, z),
        [sds(z.D, z.RG2, LANES), sds(2 * z.C, LANES)],
        (),
        (ring,),
        [vmem(z.RING, LANES)],
    )
    ring = lax.all_to_all(ring, "dev", 0, 0, tiled=True)
    (avg,) = call(functools.partial(pick_band, z), [sds(z.D, z.R2, LANES)], (anchor,), got)
    avg, phases, edges, ring, up, dn = lax.optimization_barrier(
        (avg, phases, edges, ring, up, dn)
    )
    avg = lax.all_to_all(avg, "dev", 0, 0, tiled=True)
    out, nest_out = call(
        functools.partial(both_steps, z),
        [jax.ShapeDtypeStruct(parent.shape, F32), jax.ShapeDtypeStruct(nest.shape, F32)],
        (anchor, diff, cour),
        (parent, edges, up, dn, ring, phases),
        [
            vmem(3, z.L * z.C * z.H, LANES),
            vmem(z.RG2, LANES),
            vmem(z.EDGE, LANES),
            vmem(z.EDGE, LANES),
        ],
        (),
        0,
    )
    avg, nest_out, out = lax.optimization_barrier((avg, nest_out, out))
    pieces = [avg]
    for k in range(1, z.S):
        pairs = [(a, a // z.S * z.S + (a + k) % z.S) for a in range(z.G)]
        pieces.append(lax.ppermute(avg, "grp", pairs))
    for which in ([0], list(range(1, z.S))):
        out = merge(z, which, anchor, out, [pieces[k] for k in which])
    return out, nest_out


def solution(mesh):
    placed = (P(None, "grp", "dev"), P("grp", None, "dev", None), P(), P(), P())
    return jax.shard_map(
        shards,
        mesh=mesh,
        in_specs=placed,
        out_specs=(P(None, "grp", "dev"), P("grp", None, "dev", None)),
        check_vma=False,
    )
```

```python
import functools

import jax
import jax.numpy as jnp
from jax import lax
from jax.experimental import pallas as pl
from jax.experimental.pallas import tpu as pltpu
from jax.sharding import PartitionSpec as P

F32 = jnp.float32
BF16 = jnp.bfloat16
LANES = 128
VMEM_LIMIT = 65408 * 1024
MID, EAST, WEST, NORTH, SOUTH = range(5)


class Sizes:
    def __init__(self, parent, nest, anchor, grp_count, dev_count):
        self.C, self.TR, self.TC = parent.shape
        self.L, _, self.H, self.W = nest.shape
        self.N = anchor.shape[0]
        self.G, self.D = grp_count, dev_count
        self.M = self.H // 3
        self.FR, self.FC = self.M * self.D, self.W // 3
        self.S = self.G // 2
        self.NB = self.N // 2
        self.Y = self.D // self.NB
        self.CS = self.C // self.S
        self.BR, self.BC = self.S * self.TR, self.Y * self.TC
        self.R1 = self.L * self.CS * (self.M + 2)
        self.R2 = self.CS * (self.M + 2)
        self.RING = self.FR + self.L * 2 * self.C
        self.RG = self.RING + self.C
        self.RG2 = 16 + self.L * self.C + 8
        self.HALO = self.L * self.C * 3
        self.EDGE = 3 * self.HALO
        assert self.H == 24 and self.FC == LANES and self.TC == LANES
        assert self.FR >= self.TR and self.L == 2


def call(body, out_shape, smem, args, scratch=(), raw=(), early=None):
    moved = [*smem, *args]
    n_in, n_raw, n_out = len(moved), len(raw), len(out_shape)
    place = pl.BlockSpec(memory_space=pltpu.HBM)

    def kernel(*refs):
        source, refs = refs[:n_in], refs[n_in:]
        stay, refs = refs[:n_raw], refs[n_raw:]
        target, refs = refs[:n_out], refs[n_out:]
        inner, refs = refs[:n_in], refs[n_in:]
        result, refs = refs[:n_out], refs[n_out:]
        extra, sem = refs[:-1], refs[-1]
        fetch = [pltpu.make_async_copy(a, b, sem.at[k]) for k, (a, b) in enumerate(zip(source, inner))]
        for copy in fetch:
            copy.start()
        for copy in fetch:
            copy.wait()
        store = [
            pltpu.make_async_copy(a, b, sem.at[n_in + k]) for k, (a, b) in enumerate(zip(result, target))
        ]
        if early is None:
            body(*inner, *stay, *result, *extra)
        else:
            body(*inner, *stay, *result, *extra, store[early].start)
        for k, copy in enumerate(store):
            if k != early:
                copy.start()
        for copy in store:
            copy.wait()

    return pl.pallas_call(
        kernel,
        out_shape=list(out_shape),
        in_specs=[place] * (n_in + n_raw),
        out_specs=[place] * n_out,
        scratch_shapes=[
            *[pltpu.SMEM(x.shape, x.dtype) for x in smem],
            *[pltpu.VMEM(x.shape, x.dtype) for x in args],
            *[pltpu.VMEM(x.shape, x.dtype) for x in out_shape],
            *scratch,
            pltpu.SemaphoreType.DMA((n_in + n_out,)),
        ],
        compiler_params=pltpu.CompilerParams(vmem_limit_bytes=VMEM_LIMIT),
    )(*moved, *raw)


def iota(shape, dim):
    return lax.broadcasted_iota(jnp.int32, shape, dim)


def split_dot(x, table):
    high = x.astype(BF16)
    low = (x - high.astype(F32)).astype(BF16)
    return jnp.dot(jnp.concatenate([high, low], axis=1), table, preferred_element_type=F32)


def nest_at(z, anc, band):
    found = 0
    for n in range(z.N):
        found += jnp.where(anc[0, n] // z.BR * z.NB + anc[1, n] // z.BC == band, n, 0)
    return found


def deal_table(z, fine_dim):
    fine = iota((z.W, z.W), fine_dim)
    place = iota((z.W, z.W), 1 - fine_dim)
    at = jnp.bitwise_and(place, LANES - 1) * 3 + jnp.right_shift(place, 7)
    once = jnp.where(fine == at, 1.0, 0.0).astype(BF16)
    return jnp.concatenate([once, once], axis=0)


def weights(diff, cour, c, times):
    splat = lambda ref, k: jnp.full((8, LANES), ref[k, c], F32)
    east = times * splat(diff, 0)
    north = times * splat(diff, 1)
    west = east + splat(cour, 0)
    south = north + splat(cour, 1)
    return 1.0 - (east + west) - (north + south), east, west, north, south


def ghost_share(inject, back, mid, plus, minus):
    stay = mid + inject
    m0 = inject * (1.0 + stay + mid * stay + inject * (stay + back) + 2.0 * plus * minus)
    p1 = inject * plus * (1.0 + 2.0 * stay)
    p2 = inject * plus * plus
    n1 = inject * minus * (1.0 + 2.0 * stay)
    n2 = inject * minus * minus
    ninth = 1.0 / 9.0
    same = (3.0 * m0 + 2.0 * p1 + p2 + 2.0 * n1 + n2) * ninth
    return same, (p1 + 2.0 * p2) * ninth, (n1 + 2.0 * n2) * ninth, inject * plus * minus * ninth


class Strip:
    def __init__(self):
        sub = iota((8, LANES), 0)
        lane = iota((8, LANES), 1)
        self.high = [sub == 0, sub == 4]
        self.low = [sub == 7, sub == 3]
        self.any_high = (sub == 0) | (sub == 4)
        self.any_low = (sub == 7) | (sub == 3)
        self.first, self.last = lane == 0, lane == LANES - 1

    def east(self, x, ghost):
        return jnp.where(self.last, ghost, pltpu.roll(x, LANES - 1, 1))

    def west(self, x, ghost):
        return jnp.where(self.first, ghost, pltpu.roll(x, 1, 1))

    def north(self, mains, cap):
        up = [pltpu.roll(m, 7, 0) for m in mains]
        cap_up = pltpu.roll(cap, 7, 0)
        new = [jnp.where(self.low[l], cap_up, up[l]) for l in range(2)]
        return new, jnp.where(self.low[0], up[0], jnp.where(self.low[1], up[1], 0.0))

    def south(self, mains, cap):
        down = [pltpu.roll(m, 1, 0) for m in mains]
        cap_down = pltpu.roll(cap, 1, 0)
        new = [jnp.where(self.high[l], cap_down, down[l]) for l in range(2)]
        return new, jnp.where(self.high[0], down[0], jnp.where(self.high[1], down[1], 0.0))

    def step(self, u, co, west_ghost, east_ghost):
        n_in = [self.north([u[0][0][x], u[1][0][x]], u[2][0][x]) for x in range(3)]
        s_in = [self.south([u[0][2][x], u[1][2][x]], u[2][2][x]) for x in range(3)]
        pick = lambda pair, k: pair[1] if k == 2 else pair[0][k]
        new = []
        for k in range(3):
            rows = []
            for y in range(3):
                row = u[k][y]
                e = [row[1], row[2], self.east(row[0], east_ghost[k])]
                w = [self.west(row[2], west_ghost[k]), row[0], row[1]]
                cells = []
                for x in range(3):
                    n = u[k][y + 1][x] if y < 2 else pick(n_in[x], k)
                    s = u[k][y - 1][x] if y > 0 else pick(s_in[x], k)
                    cells.append(
                        co[MID] * row[x]
                        + (co[EAST] * e[x] + co[WEST] * w[x])
                        + (co[NORTH] * n + co[SOUTH] * s)
                    )
                rows.append(cells)
            new.append(rows)
        return new

    def pooled_step(self, u, co):
        ends = []
        for k in range(3):
            row = [u[k][y][0] + u[k][y][1] + u[k][y][2] for y in range(3)]
            col = [u[k][0][x] + u[k][1][x] + u[k][2][x] for x in (0, 2)]
            ends.append((row[0], row[2], col[0], col[1], row[0] + row[1] + row[2]))
        n_in = self.north([ends[0][0], ends[1][0]], ends[2][0])
        s_in = self.south([ends[0][1], ends[1][1]], ends[2][1])
        pick = lambda pair, k: pair[1] if k == 2 else pair[0][k]
        out = []
        for k in range(3):
            row0, row2, col0, col2, total = ends[k]
            flux_x = co[EAST] * (self.east(col0, 0.0) - col0)
            flux_x += co[WEST] * (self.west(col2, 0.0) - col2)
            flux_y = co[NORTH] * (pick(n_in, k) - row0) + co[SOUTH] * (pick(s_in, k) - row2)
            out.append(total + (flux_x + flux_y))
        return out


def phase_rows(z, ref, l, c, y, x):
    got = ref[x, pl.ds((l * z.C + c) * z.H + y, z.M, 3), :]
    return got if l == 0 else pltpu.roll(got, 4, 0)


def partial_averages(z, diff, cour, nest, *refs):
    out, (phases, strips, sem, store_phases) = refs[: z.S], refs[z.S :]
    fetch = [pltpu.make_async_copy(nest.at[l], strips.at[l], sem.at[l]) for l in range(z.L)]
    for copy in fetch:
        copy.start()
    d = lax.axis_index("dev")
    own = lax.rem(lax.axis_index("grp"), z.S)
    C, M, CS = z.C, z.M, z.CS
    deal = deal_table(z, 0)
    rows = C * z.H
    for l in range(z.L):
        fetch[l].wait()
        dealt = split_dot(strips[l].reshape(rows, z.W), deal)
        for x in range(3):
            phases[x, l * rows : (l + 1) * rows, :] = dealt[:, x * LANES : (x + 1) * LANES]
    store_phases()
    strip = Strip()
    keep_high = strip.any_low | (strip.any_high & (d < z.D - 1))
    keep_low = strip.any_high | (strip.any_low & (d > 0))
    zero = jnp.zeros((8, LANES), F32)
    ghosts = [0.0] * 3
    base = z.L * CS * M

    def hold(u):
        cap = [
            [jnp.where(keep_high, v, 0.0) for v in u[2][0]],
            u[2][1],
            [jnp.where(keep_low, v, 0.0) for v in u[2][2]],
        ]
        return [u[0], u[1], cap]

    for part in range(z.S):

        def channel(i, _, to=out[part], first=jnp.bitwise_xor(own, part) * CS):
            c = first + i
            co = weights(diff, cour, c, 3.0)
            u = [
                [[phase_rows(z, phases, l, c, y, x) for x in range(3)] for y in range(3)]
                for l in range(2)
            ]
            u.append([[zero] * 3] * 3)
            for _step in range(2):
                u = hold(strip.step(u, co, ghosts, ghosts))
            got = [v * (1.0 / 9.0) for v in strip.pooled_step(u, co)]
            got[1] = pltpu.roll(got[1], 4, 0)
            for l in range(2):
                row = pl.multiple_of((l * CS + i) * M, M)
                to[pl.ds(row, M), :] = got[l]
                for side, sub in enumerate(((7, 3), (0, 4))):
                    row = base + (l * 2 + side) * CS + i
                    to[pl.ds(row, 1), :] = got[2][sub[l] : sub[l] + 1]
            return 0

        lax.fori_loop(0, CS, channel, 0, unroll=3)


def pick_band(z, anc, *refs):
    got, out = refs[: z.G], refs[z.G]
    g = lax.axis_index("grp")
    top = g // z.S * z.NB
    base, size = z.L * z.CS * z.M, z.CS * z.M
    for band in range(z.NB):
        n = nest_at(z, anc, top + band)
        of = n // z.L
        slot = jnp.bitwise_xor(of, g)
        first = n - of * z.L == 0
        for k in range(z.G):

            @pl.when(slot == k)
            def _(k=k, first=first, band=band):
                main = jnp.where(first, got[k][:size, :], got[k][size : 2 * size, :])
                edge = jnp.where(
                    first,
                    got[k][base : base + 2 * z.CS, :],
                    got[k][base + 2 * z.CS : base + 4 * z.CS, :],
                )
                for y in range(z.Y):
                    out[band * z.Y + y, :size, :] = main
                    out[band * z.Y + y, size:, :] = edge


def ring_parts(z, anc, parent, nest, buf, up, dn, tail, head, sem):
    fetch = [
        pltpu.make_async_copy(nest.at[:, :, z.H - 8 :, :], tail, sem.at[0]),
        pltpu.make_async_copy(nest.at[:, :, :8, :], head, sem.at[1]),
    ]
    for copy in fetch:
        copy.start()
    g, d = lax.axis_index("grp"), lax.axis_index("dev")
    row_base, col_base = g * z.TR, d * z.TC
    lane_t = iota((z.TR, LANES), 1)
    lane_f = iota((z.FR, LANES), 1)
    row_f = iota((z.FR, LANES), 0)
    lane_c = iota((z.C, LANES), 1)
    buf[...] = jnp.zeros_like(buf)

    def nest_ring(n, _):
        to = n // z.L
        l = n - to * z.L
        slot = to
        r, q = anc[0, n], anc[1, n]
        rows_meet = (r < row_base + z.TR) & (r + z.FR > row_base)
        cols_meet = (q < col_base + z.TC) & (q + z.FC > col_base)
        shift_r = lax.rem(row_base - r + 2 * z.G * z.TR, z.FR)
        shift_q = lax.rem(col_base - q + 2 * z.D * z.TC, z.FC)
        for side in range(2):
            col = (q - 1 if side == 0 else q + z.FC) - col_base
            first = (l * 2 + side) * z.C

            @pl.when(rows_meet & (col >= 0) & (col < z.TC))
            def _(col=col, first=first):
                acc = jnp.zeros((z.TR, LANES), F32)
                for c in range(z.C):
                    at = first + c
                    moved = pltpu.roll(parent[c], lax.rem(at - col + LANES, LANES), 1)
                    acc = jnp.where(lane_t == at, moved, acc)
                if z.FR > z.TR:
                    acc = jnp.concatenate([acc, jnp.zeros((z.FR - z.TR, LANES), F32)], axis=0)
                acc = pltpu.roll(acc, shift_r, 0)
                y = row_f + (r - row_base)
                good = (y >= 0) & (y < z.TR) & (lane_f >= first) & (lane_f < first + z.C)
                buf[slot, : z.FR, :] = jnp.where(good, acc, buf[slot, : z.FR, :])

            row = (r - 1 if side == 0 else r + z.FR) - row_base

            @pl.when(cols_meet & (row >= 0) & (row < z.TR))
            def _(row=row, first=first):
                rows = jnp.concatenate(
                    [parent[c, pl.ds(row, 1), :] for c in range(z.C)], axis=0
                )
                x = lane_c + (q - col_base)
                moved = jnp.where((x >= 0) & (x < z.TC), pltpu.roll(rows, shift_q, 1), 0.0)
                buf[slot, pl.ds(pl.multiple_of(z.FR + first, 8), z.C), :] = moved

        return 0

    lax.fori_loop(0, z.N, nest_ring, 0)
    for to in range(z.G):
        edge = jnp.where(to > g, z.TR - 1, 0)
        for c in range(z.C):
            buf[to, z.RING + c : z.RING + c + 1, :] = parent[c, pl.ds(edge, 1), :]
    first = jnp.zeros((z.TR, LANES), F32)
    last = first
    for c in range(z.C):
        first = jnp.where(lane_t == c, pltpu.roll(parent[c], c, 1) if c else parent[c], first)
        last = jnp.where(lane_t == c, pltpu.roll(parent[c], c + 1, 1), last)
    up[z.EDGE :, :] = last
    dn[z.EDGE :, :] = first
    for copy in fetch:
        copy.wait()
    for l in range(z.L):
        for c in range(z.C):
            for x in range(3):
                at = x * z.HALO + 3 * (l * z.C + c)
                lanes = slice(x * LANES, (x + 1) * LANES)
                up[at : at + 3, :] = tail[l, c, 5:8, lanes]
                dn[at : at + 3, :] = head[l, c, 0:3, lanes]


def ring_next(z, got, out, edges, slab):
    g, d = lax.axis_index("grp"), lax.axis_index("dev")
    C, L, FR, M = z.C, z.L, z.FR, z.M
    total = got[0, : z.RING, :]
    for k in range(1, z.G):
        total = total + got[k, : z.RING, :]
    slab[...] = total
    sub = iota((8, LANES), 0)
    for to in range(z.D):
        out[to, :M, :] = slab[to * M : (to + 1) * M, :]
        hi = min(to * M + M, FR - 1)
        lo = max(to * M - 1, 0)
        hi, lo = slab[hi : hi + 1, :], slab[lo : lo + 1, :]
        out[to, M:16, :] = jnp.where(sub == 0, hi, jnp.where(sub == 7, lo, 0.0))
        for l in range(L):
            at = 16 + l * C
            if to == 0 or to == z.D - 1:
                k = FR + (l * 2 + (0 if to == 0 else 1)) * C
                out[to, at : at + C, :] = slab[k : k + C, :]
            else:
                out[to, at : at + C, :] = jnp.zeros((C, LANES), F32)
    before, after = jnp.maximum(g - 1, 0), jnp.minimum(g + 1, z.G - 1)
    edges[:C, :] = jnp.where(g > 0, got[before, z.RING :, :], 0.0)
    edges[C:, :] = jnp.where(g < z.G - 1, got[after, z.RING :, :], 0.0)
    lane = iota((8, LANES), 1)
    first = jnp.zeros((8, LANES), F32)
    last = first
    for c in range(C):
        lo = edges[c : c + 1, :]
        hi = edges[C + c : C + c + 1, :]
        cap = jnp.where(sub == 0, hi, jnp.where(sub == 7, lo, 0.0))
        first = jnp.where(lane == c, pltpu.roll(cap, c, 1) if c else cap, first)
        last = jnp.where(lane == c, pltpu.roll(cap, c + 1, 1), last)
    for to in range(z.D):
        out[to, z.RG2 - 8 :, :] = jnp.where(to > d, last, first)


def nest_steps(z, diff, cour, phases, got, up_in, dn_in, out, back, ring, up, dn):
    d = lax.axis_index("dev")
    C, M = z.C, z.M
    strip = Strip()
    deal = deal_table(z, 0)
    for source, target in ((up_in, up), (dn_in, dn)):
        halo = [source[x * z.HALO : (x + 1) * z.HALO, :] for x in range(3)]
        dealt = split_dot(jnp.concatenate(halo, axis=1), deal)
        for x in range(3):
            target[x * z.HALO : (x + 1) * z.HALO, :] = dealt[:, x * LANES : (x + 1) * LANES]
    total = got[0]
    for k in range(1, z.D):
        total = total + got[k]
    ring[...] = total
    side_main = [ring[:M, :], pltpu.roll(ring[:M, :], 4, 0)]
    side_cap = jnp.where(
        strip.any_high, ring[M : M + 1, :], jnp.where(strip.any_low, ring[15:16, :], 0.0)
    )
    hold_low, hold_high = strip.any_low & (d == 0), strip.any_high & (d == z.D - 1)
    nest_1 = strip.high[1] | strip.low[1]

    def channel(c, _):
        co = weights(diff, cour, c, 3.0)
        u = [
            [[phase_rows(z, phases, l, c, y, x) for x in range(3)] for y in range(3)]
            for l in range(2)
        ]
        cap = []
        for y in range(3):
            row = []
            for x in range(3):
                v = jnp.zeros((8, LANES), F32)
                for l in range(2):
                    at = x * z.HALO + (l * C + c) * 3 + y
                    v = jnp.where(strip.high[l], dn[pl.ds(at, 1), :], v)
                    v = jnp.where(strip.low[l], up[pl.ds(at, 1), :], v)
                row.append(v)
            cap.append(row)
        u.append(cap)
        end = jnp.where(nest_1, ring[pl.ds(16 + C + c, 1), :], ring[pl.ds(16 + c, 1), :])
        west, east = [], []
        for side, lane, ghosts in ((0, 0, west), (1, LANES - 1, east)):
            turn = [lax.rem(lane - ((l * 2 + side) * C + c) + LANES, LANES) for l in range(2)]
            for l in range(2):
                ghosts.append(pltpu.roll(side_main[l], turn[l], 1))
            caps = [pltpu.roll(side_cap, turn[l], 1) for l in range(2)]
            ghosts.append(jnp.where(nest_1, caps[1], caps[0]))

        def hold(u):
            cap = [
                [jnp.where(hold_high, end, v) for v in u[2][0]],
                u[2][1],
                [jnp.where(hold_low, end, v) for v in u[2][2]],
            ]
            return [u[0], u[1], cap]

        u = hold(u)
        for k in range(3):
            u = strip.step(u, co, west, east)
            if k < 2:
                u = hold(u)
        for l in range(2):
            for y in range(3):
                for x in range(3):
                    v = u[l][y][x]
                    v = v if l == 0 else pltpu.roll(v, 4, 0)
                    back[x, pl.ds((l * C + c) * z.H + y, M, 3), :] = v
        return 0

    lax.fori_loop(0, C, channel, 0, unroll=3)
    undeal = deal_table(z, 1)
    done = split_dot(jnp.concatenate([back[0], back[1], back[2]], axis=1), undeal)
    out[...] = done.reshape(z.L, C, z.H, z.W)


def parent_step(z, anc, diff, cour, parent, edges, up_in, dn_in, got, out):
    g, d = lax.axis_index("grp"), lax.axis_index("dev")
    C = z.C
    rows = z.TR + 8
    n = nest_at(z, anc, g // z.S * z.NB + d // z.Y)
    i = iota((z.TR, LANES), 0) + (g * z.TR - anc[0, n])
    j = iota((z.TR, LANES), 1) + (d * z.TC - anc[1, n])
    inside = (i >= 0) & (i < z.FR) & (j >= 0) & (j < z.FC)
    one = lambda cond: jnp.where(cond, 1.0, 0.0).astype(F32)
    on_w, on_e = one(inside & (j == 0)), one(inside & (j == z.FC - 1))
    on_s, on_n = one(inside & (i == 0)), one(inside & (i == z.FR - 1))
    i_end, j_end = one((i == 0) | (i == z.FR - 1)), one((j == 0) | (j == z.FC - 1))
    i_lo, i_hi = one(i > 0), one(i < z.FR - 1)
    j_lo, j_hi = one(j > 0), one(j < z.FC - 1)
    lane = iota((rows, LANES), 1)
    sub = iota((8, LANES), 0)

    cap_w = jnp.where(d > 0, got[jnp.maximum(d - 1, 0), z.RG2 - 8 :, :], 0.0)
    cap_e = jnp.where(d < z.D - 1, got[jnp.minimum(d + 1, z.D - 1), z.RG2 - 8 :, :], 0.0)
    col_w = jnp.concatenate([up_in[z.EDGE :, :], cap_w], axis=0)
    col_e = jnp.concatenate([dn_in[z.EDGE :, :], cap_e], axis=0)

    def channel(c, _):
        co = [v[:1] for v in weights(diff, cour, c, 1.0)]
        fm, fe, fw, fn, fs = [v[:1] for v in weights(diff, cour, c, 3.0)]
        lo = edges[pl.ds(c, 1), :]
        hi = edges[pl.ds(C + c, 1), :]
        cap = jnp.where(sub == 0, hi, jnp.where(sub == 7, lo, 0.0))
        full = jnp.concatenate([parent[c], cap], axis=0)
        w_in = pltpu.roll(col_w, lax.rem(LANES - c, LANES), 1)
        e_in = pltpu.roll(col_e, LANES - 1 - c, 1)
        w_all = jnp.where(lane == 0, w_in, pltpu.roll(full, 1, 1))
        e_all = jnp.where(lane == LANES - 1, e_in, pltpu.roll(full, LANES - 1, 1))
        up = lambda x: pltpu.roll(x, rows - 1, 0)[: z.TR]
        down = lambda x: pltpu.roll(x, 1, 0)[: z.TR]
        mid = full[: z.TR]
        w, e, n, s = w_all[: z.TR], e_all[: z.TR], up(full), down(full)
        w_up, w_down, e_up, e_down = up(w_all), down(w_all), up(e_all), down(e_all)
        step = (
            co[MID] * mid
            + (co[EAST] * e + co[WEST] * w)
            + (co[NORTH] * n + co[SOUTH] * s)
        )
        a, b, k, x = ghost_share(fw, fe, fm, fs, fn)
        share = on_w * ((a - x * i_end) * w + (b * i_lo) * w_down + (k * i_hi) * w_up)
        a, b, k, x = ghost_share(fe, fw, fm, fs, fn)
        share += on_e * ((a - x * i_end) * e + (b * i_lo) * e_down + (k * i_hi) * e_up)
        a, b, k, x = ghost_share(fs, fn, fm, fw, fe)
        share += on_s * ((a - x * j_end) * s + (b * j_lo) * w_down + (k * j_hi) * e_down)
        a, b, k, x = ghost_share(fn, fs, fm, fw, fe)
        share += on_n * ((a - x * j_end) * n + (b * j_lo) * w_up + (k * j_hi) * e_up)
        out[c] = jnp.where(inside, share, step)
        return 0

    lax.fori_loop(0, C, channel, 0, unroll=3)


def both_steps(
    z, anc, diff, cour, parent, edges, up, dn, ring, phases, out, nest_out, *scratch_and_store
):
    *scratch, store_parent = scratch_and_store
    parent_step(z, anc, diff, cour, parent, edges, up, dn, ring, out)
    store_parent()
    nest_steps(z, diff, cour, phases, ring, up, dn, nest_out, *scratch)


def merge(z, which, anchor, base, pieces):
    count, size = len(which), z.CS * z.M

    def kernel(*refs):
        anc_in, base_in, refs = refs[0], refs[1], refs[2:]
        source, base_out, refs = refs[:count], refs[count], refs[count + 1 :]
        anc, refs = refs[0], refs[1:]
        inner, (old, new, twice, sem) = refs[:count], refs[count:]
        g, d = lax.axis_index("grp"), lax.axis_index("dev")
        part = lax.rem(g, z.S)
        firsts = [lax.rem(part - k + z.S, z.S) * z.CS for k in which]
        fetch = [pltpu.make_async_copy(anc_in, anc, sem.at[0])]
        for k in range(count):
            rows = base_in.at[pl.ds(firsts[k], z.CS)]
            fetch.append(pltpu.make_async_copy(source[k], inner[k], sem.at[1 + 2 * k]))
            fetch.append(pltpu.make_async_copy(rows, old.at[k], sem.at[2 + 2 * k]))
        for copy in fetch:
            copy.start()
        for copy in fetch:
            copy.wait()
        n = nest_at(z, anc, g // z.S * z.NB + d // z.Y)
        r, q = anc[0, n], anc[1, n]
        start = lax.rem(g * z.TR - r + 2 * z.G * z.TR, z.FR)
        shift_q = lax.rem(q - d * z.TC + 2 * z.D * z.TC, z.FC)
        i = iota((z.TR, LANES), 0) + (g * z.TR - r)
        j = iota((z.TR, LANES), 1) + (d * z.TC - q)
        inside = (i >= 0) & (i < z.FR) & (j >= 0) & (j < z.FC)
        sub = iota((z.M, LANES), 0)
        store = []
        for k in range(count):
            piece = inner[k]
            for c in range(z.CS):
                for m in range(z.D):
                    x = piece[m, c * z.M : (c + 1) * z.M, :]
                    if m + 1 < z.D:
                        row = piece[m + 1, size + c : size + c + 1, :]
                        x += jnp.where(sub == z.M - 1, row, 0.0)
                    if m > 0:
                        row = piece[m - 1, size + z.CS + c : size + z.CS + c + 1, :]
                        x += jnp.where(sub == 0, row, 0.0)
                    twice[c % 4, m * z.M : (m + 1) * z.M, :] = x
                    if m * z.M < z.TR:
                        twice[c % 4, z.FR + m * z.M : z.FR + (m + 1) * z.M, :] = x
                x = pltpu.roll(twice[c % 4, pl.ds(start, z.TR), :], shift_q, 1)
                new[k, c] = old[k, c] + jnp.where(inside, x, 0.0)
            rows = base_out.at[pl.ds(firsts[k], z.CS)]
            store.append(pltpu.make_async_copy(new.at[k], rows, sem.at[1 + 2 * k]))
            store[-1].start()
        for copy in store:
            copy.wait()

    place = pl.BlockSpec(memory_space=pltpu.HBM)
    half = pltpu.VMEM((count, z.CS, z.TR, LANES), F32)
    return pl.pallas_call(
        kernel,
        out_shape=jax.ShapeDtypeStruct(base.shape, F32),
        in_specs=[place] * (2 + count),
        out_specs=place,
        input_output_aliases={1: 0},
        scratch_shapes=[
            pltpu.SMEM(anchor.shape, anchor.dtype),
            *[pltpu.VMEM(x.shape, F32) for x in pieces],
            half,
            half,
            pltpu.VMEM((4, z.FR + z.TR, LANES), F32),
            pltpu.SemaphoreType.DMA((1 + 2 * count,)),
        ],
        compiler_params=pltpu.CompilerParams(vmem_limit_bytes=VMEM_LIMIT),
    )(anchor, base, *pieces)


def shards(parent, nest, anchor, diff, cour):
    z = Sizes(parent, nest, anchor, lax.axis_size("grp"), lax.axis_size("dev"))
    sds = lambda *shape: jax.ShapeDtypeStruct(shape, F32)
    vmem = lambda *shape: pltpu.VMEM(shape, F32)
    to_grp = lambda x, k: lax.ppermute(x, "grp", [(a, a ^ k) for a in range(z.G)])

    anchor = anchor.T
    message = sds(z.EDGE + z.TR, LANES)
    edge_tile = vmem(z.L, z.C, 8, z.W)
    ring, up, dn = call(
        functools.partial(ring_parts, z),
        [sds(z.G, z.RG, LANES), message, message],
        (anchor,),
        (parent,),
        [edge_tile, edge_tile, pltpu.SemaphoreType.DMA((2,))],
        (nest,),
    )
    nest, ring = lax.optimization_barrier((nest, ring))
    ring = lax.all_to_all(ring, "grp", 0, 0, tiled=True)
    *chunks, phases = call(
        functools.partial(partial_averages, z),
        [sds(z.R1, LANES)] * z.S + [sds(3, z.L * z.C * z.H, LANES)],
        (diff, cour),
        (),
        [pltpu.VMEM(nest.shape, F32), pltpu.SemaphoreType.DMA((z.L,))],
        (nest,),
        z.S,
    )
    chunks, ring, up, dn = lax.optimization_barrier((chunks, ring, up, dn))
    forward = [(k, k + 1) for k in range(z.D - 1)]
    up = lax.ppermute(up, "dev", forward)
    dn = lax.ppermute(dn, "dev", [(b, a) for a, b in forward])
    got = [chunks[0]] + [to_grp(chunks[k % z.S], k) for k in range(1, z.G)]
    ring, edges = call(
        functools.partial(ring_next, z),
        [sds(z.D, z.RG2, LANES), sds(2 * z.C, LANES)],
        (),
        (ring,),
        [vmem(z.RING, LANES)],
    )
    ring = lax.all_to_all(ring, "dev", 0, 0, tiled=True)
    (avg,) = call(functools.partial(pick_band, z), [sds(z.D, z.R2, LANES)], (anchor,), got)
    avg, phases, edges, ring, up, dn = lax.optimization_barrier(
        (avg, phases, edges, ring, up, dn)
    )
    avg = lax.all_to_all(avg, "dev", 0, 0, tiled=True)
    out, nest_out = call(
        functools.partial(both_steps, z),
        [jax.ShapeDtypeStruct(parent.shape, F32), jax.ShapeDtypeStruct(nest.shape, F32)],
        (anchor, diff, cour),
        (parent, edges, up, dn, ring, phases),
        [
            vmem(3, z.L * z.C * z.H, LANES),
            vmem(z.RG2, LANES),
            vmem(z.EDGE, LANES),
            vmem(z.EDGE, LANES),
        ],
        (),
        0,
    )
    avg, nest_out, out = lax.optimization_barrier((avg, nest_out, out))
    pieces = [avg]
    for k in range(1, z.S):
        pairs = [(a, a // z.S * z.S + (a + k) % z.S) for a in range(z.G)]
        pieces.append(lax.ppermute(avg, "grp", pairs))
    for which in ([0], list(range(1, z.S))):
        out = merge(z, which, anchor, out, [pieces[k] for k in which])
    return out, nest_out


def solution(mesh):
    placed = (P(None, "grp", "dev"), P("grp", None, "dev", None), P(), P(), P())
    return jax.shard_map(
        shards,
        mesh=mesh,
        in_specs=placed,
        out_specs=(P(None, "grp", "dev"), P("grp", None, "dev", None)),
        check_vma=False,
    )
```
